32 devices in a mesh: groups: 2 (over y), ctx: 4 (over z), head: 4 (over x, core).
Axes of the slice: x: 2, y: 2, z: 4, core: 2. Of those that a mesh axis runs over, the one named last changes fastest.
Arguments:
- doc_lengths: int32 [32], P('groups'), parts along dimension 0, may hold values from 1 to 256, as said below
- owners: int32 [1024], P(('groups', 'ctx')), parts along dimension 0, may hold values from 0 to 3, as said below
- queries: bfloat16 [1024, 2048], P(('groups', 'ctx'), 'head'), parts along dimension 0, may hold values from -7 to 7
- key_head_rows: bfloat16 [1024, 512], P(('groups', 'ctx'), 'head'), parts along dimension 0, may hold values from -6 to 6
- value_head_rows: bfloat16 [1024, 512], P(('groups', 'ctx'), 'head'), parts along dimension 0, may hold values from -5 to 5
- forward_out: bfloat16 [1024, 2048], P(('groups', 'ctx'), 'head'), parts along dimension 0, may hold values from -5 to 5
- grad_out: bfloat16 [1024, 2048], P(('groups', 'ctx'), 'head'), parts along dimension 0, may hold values from -5 to 5
Outputs:
- grad_queries: float32 [1024, 2048], P(('groups', 'ctx'), 'head'), parts along dimension 0
- key_gradient_rows: float32 [1024, 512], P(('groups', 'ctx'), 'head'), parts along dimension 0
- value_gradient_rows: float32 [1024, 512], P(('groups', 'ctx'), 'head'), parts along dimension 0
The draws below stay inside these ranges and needn't reach their ends.
There are 2 independent parts, one for each index of `groups`. The reference program is written for one: setup_inputs(seed, part) draws one part's arguments, and reference() takes and returns one part's arrays. A program takes and returns all parts, laid end to end along the dimension named above; each array names one. Nothing has to cross between parts.
Inputs may be any that keep to these rules, and one draw needn't show every extreme that they name: `doc_lengths`: 16 lengths in sequence order that sum to 512; exactly one document has 256 tokens, all others fewer. Every owner is given exactly 128 tokens. Of the 128 tokens of one device at most 64 go to one owner, and every device gives exactly 64 tokens to some owner. The tokens of one device that go to one owner form one contiguous run, the runs following in the order of the owners.
All inputs are finite; a program needn't handle non-finite values.
Results may differ from the reference program's by a relative error of at most 0.0031.
Values may be sent and summed in bfloat16 or wider, within the bound.
No kernel may reach another device: no remote copies, remote signals or barrier semaphores. Data moves between devices by JAX's collectives and lax.ppermute only.
A program may use at most 64 MiB of HBM per device.

```python
import math
import jax
import jax.numpy as jnp
from jax import lax

HEAD_WIDTH = 128
HQ = 16
KEY_VALUE_HEADS = 4
ROWS = 128
DOCS = 16
GROUP = 4
SEQUENCE_LENGTH = 512
MOST = 256
N_CTX = 4


def packed_lengths(random_base_key):
    seed_key = jax.random.fold_in(random_base_key, 11)
    cut_key, slot_key = jax.random.split(seed_key)
    others = DOCS - 1
    spare_tokens = SEQUENCE_LENGTH // 2 - others
    cut_points = jnp.sort(jax.random.randint(cut_key, (others - 1,), 0, spare_tokens + 1)).astype(jnp.int32)
    boundaries = jnp.concatenate([jnp.zeros((1,), jnp.int32), cut_points, jnp.full((1,), spare_tokens, jnp.int32)])
    shorter = boundaries[1:] - boundaries[:-1] + 1
    longest = jax.random.randint(slot_key, (), 0, DOCS).astype(jnp.int32)
    places = jnp.arange(DOCS, dtype=jnp.int32)
    picked = jnp.clip(places - (places > longest).astype(jnp.int32), 0, others - 1)
    lengths = jnp.where(places == longest, MOST, shorter[picked]).astype(jnp.int32)
    return lengths


def draw_doc_lengths(key, part):
    return packed_lengths(key)


def draw_owners(key, part):
    key = jax.random.fold_in(key, 7)
    base_share = ROWS // N_CTX
    shuffle = jax.random.permutation(key, N_CTX).astype(jnp.int32)
    sources = jnp.arange(N_CTX, dtype=jnp.int32)
    owner_ids = jnp.arange(N_CTX, dtype=jnp.int32)
    fewer = shuffle[(sources + 1) % N_CTX]
    gains = (owner_ids[None, :] == shuffle[:, None]).astype(jnp.int32)
    losses = (owner_ids[None, :] == fewer[:, None]).astype(jnp.int32)
    counts = base_share + base_share * (gains - losses)
    bounds = jnp.cumsum(counts, axis=1)
    slot_rows = jnp.arange(ROWS, dtype=jnp.int32)
    slot_owner = jnp.sum((slot_rows[None, :, None] >= bounds[:, None, :]).astype(jnp.int32), axis=2)
    return slot_owner.reshape(SEQUENCE_LENGTH).astype(jnp.int32)


def draw_queries(key, part):
    key = jax.random.fold_in(key, 3)
    table_entries = jnp.clip(jax.random.normal(key, (SEQUENCE_LENGTH, HQ * HEAD_WIDTH), jnp.float32), -4.0, 4.0)
    return table_entries.astype(jnp.bfloat16)


def draw_key_head_rows(key, part):
    key = jax.random.fold_in(key, 5)
    table_entries = jnp.clip(jax.random.normal(key, (SEQUENCE_LENGTH, KEY_VALUE_HEADS * HEAD_WIDTH), jnp.float32), -4.0, 4.0)
    return table_entries.astype(jnp.bfloat16)


def block_levels(key, dims, shards, least, high):
    def one(axis_at, parts):
        heights = jax.random.uniform(jax.random.fold_in(jax.random.fold_in(key, 6), axis_at), (parts,), jnp.float32, least / len(shards), high / len(shards))
        return jnp.repeat(jnp.exp(heights), dims[axis_at] // parts).reshape((-1,) + (1,) * (len(dims) - axis_at - 1))

    factor_of = one(*shards[0])
    for cut in shards[1:]:
        factor_of = factor_of * one(*cut)
    return factor_of


def centred(stream_key, extent, deviation, most, shards=(), kind=jnp.bfloat16):
    values = deviation * jax.random.normal(stream_key, extent, jnp.float32)
    if shards:
        values = values * block_levels(stream_key, extent, shards, -0.22, 0.18)
    return jnp.clip(values, -most, most).astype(kind)


def setup_inputs(seed: int = 0, part: int = 0) -> dict:
    arg_keys = jax.random.split(jax.random.key(seed), 8)
    part_keys = jax.random.split(jax.random.fold_in(arg_keys[7], part), 8)
    return {
        "doc_lengths": draw_doc_lengths(jax.random.fold_in(jax.random.fold_in(arg_keys[7], part), 71), part),
        "owners": draw_owners(jax.random.fold_in(jax.random.fold_in(arg_keys[7], part), 71), part),
        "queries": draw_queries(jax.random.fold_in(jax.random.fold_in(arg_keys[7], part), 71), part),
        "key_head_rows": draw_key_head_rows(jax.random.fold_in(jax.random.fold_in(arg_keys[7], part), 71), part),
        "value_head_rows": centred(part_keys[4], (SEQUENCE_LENGTH, KEY_VALUE_HEADS * HEAD_WIDTH), 1.0, 5.0, ((0, 4), (1, 4))),
        "forward_out": centred(part_keys[5], (SEQUENCE_LENGTH, HQ * HEAD_WIDTH), 1.0, 5.0, ((0, 4), (1, 4))),
        "grad_out": centred(part_keys[6], (SEQUENCE_LENGTH, HQ * HEAD_WIDTH), 1.0, 5.0, ((0, 4), (1, 4))),
    }


NEG = -1e+30

def document_of(positions, doc_lengths):
    ends = jnp.cumsum(doc_lengths)
    return lax.optimization_barrier(jnp.sum((positions[:, None] >= ends[None, :]).astype(jnp.int32), axis=1))

def head_backward(query_head, key_head, value_head, saved_head, grad_head, positions, documents):
    score_scale = 1.0 / math.sqrt(HEAD_WIDTH)
    block = math.gcd(SEQUENCE_LENGTH, 512)
    delta_all = lax.optimization_barrier(jnp.sum(grad_head * saved_head, axis=1))

    def one_block(running, block_index):
        key_sum, value_sum = running
        first_row = block_index * block
        query_block = lax.dynamic_slice_in_dim(query_head, first_row, block, 0)
        grad_block = lax.dynamic_slice_in_dim(grad_head, first_row, block, 0)
        delta_block = lax.dynamic_slice_in_dim(delta_all, first_row, block, 0)
        block_positions = lax.dynamic_slice_in_dim(positions, first_row, block, 0)
        block_docs = lax.dynamic_slice_in_dim(documents, first_row, block, 0)
        scores = jnp.dot(query_block, key_head.T, preferred_element_type=jnp.float32) * score_scale
        allowed = (block_docs[:, None] == documents[None, :]) & (positions[None, :] <= block_positions[:, None])
        masked = jnp.where(allowed, scores, NEG)
        row_max = lax.optimization_barrier(jnp.max(masked, axis=1))
        totals = lax.optimization_barrier(jnp.sum(jnp.where(allowed, jnp.exp(masked - row_max[:, None]), 0.0), axis=1))
        log_norm = row_max + jnp.log(totals)
        weights = jnp.exp(masked - log_norm[:, None])
        grad_weights = jnp.dot(grad_block, value_head.T, preferred_element_type=jnp.float32)
        grad_scores = weights * (grad_weights - delta_block[:, None])
        rounded_weights = lax.optimization_barrier(weights.astype(jnp.bfloat16)).astype(jnp.float32)
        rounded_grads = lax.optimization_barrier(grad_scores.astype(jnp.bfloat16)).astype(jnp.float32)
        value_sum = value_sum + jnp.dot(rounded_weights.T, grad_block, preferred_element_type=jnp.float32)
        key_sum = key_sum + jnp.dot(rounded_grads.T, query_block, preferred_element_type=jnp.float32)
        query_part = jnp.dot(rounded_grads, key_head, preferred_element_type=jnp.float32) * score_scale
        return ((key_sum, value_sum), query_part)
    zeros = jnp.zeros((SEQUENCE_LENGTH, HEAD_WIDTH), jnp.float32)
    blocks = jnp.arange(SEQUENCE_LENGTH // block, dtype=jnp.int32)
    (key_sum, value_sum), query_parts = lax.scan(one_block, (zeros, zeros), blocks)
    return (query_parts.reshape(SEQUENCE_LENGTH, HEAD_WIDTH), key_sum * score_scale, value_sum)

def reference(doc_lengths, owners, queries, key_head_rows, value_head_rows, forward_out, grad_out):
    positions = jnp.arange(SEQUENCE_LENGTH, dtype=jnp.int32)
    documents = document_of(positions, doc_lengths)
    query_all = queries.astype(jnp.float32).reshape(SEQUENCE_LENGTH, HQ, HEAD_WIDTH)
    every_key_row = key_head_rows.astype(jnp.float32).reshape(SEQUENCE_LENGTH, KEY_VALUE_HEADS, HEAD_WIDTH)
    every_value_row = value_head_rows.astype(jnp.float32).reshape(SEQUENCE_LENGTH, KEY_VALUE_HEADS, HEAD_WIDTH)
    saved_all = forward_out.astype(jnp.float32).reshape(SEQUENCE_LENGTH, HQ, HEAD_WIDTH)
    grad_all = grad_out.astype(jnp.float32).reshape(SEQUENCE_LENGTH, HQ, HEAD_WIDTH)
    query_grads = []
    key_gradient_parts = []
    value_gradient_parts = []
    for key_value_head in range(KEY_VALUE_HEADS):
        key_total = jnp.zeros((SEQUENCE_LENGTH, HEAD_WIDTH), jnp.float32)
        value_total = jnp.zeros((SEQUENCE_LENGTH, HEAD_WIDTH), jnp.float32)
        for member in range(GROUP):
            head_number = key_value_head * GROUP + member
            query_part, key_part, value_part = head_backward(query_all[:, head_number], every_key_row[:, key_value_head], every_value_row[:, key_value_head], saved_all[:, head_number], grad_all[:, head_number], positions, documents)
            query_grads.append(query_part)
            key_total = key_total + key_part
            value_total = value_total + value_part
        key_gradient_parts.append(key_total)
        value_gradient_parts.append(value_total)
    row_arrangement = jnp.argsort(owners, stable=True).astype(jnp.int32)
    grad_queries = jnp.stack(query_grads, axis=1).reshape(SEQUENCE_LENGTH, HQ * HEAD_WIDTH)[row_arrangement]
    key_gradient_rows = jnp.stack(key_gradient_parts, axis=1).reshape(SEQUENCE_LENGTH, KEY_VALUE_HEADS * HEAD_WIDTH)[row_arrangement]
    value_gradient_rows = jnp.stack(value_gradient_parts, axis=1).reshape(SEQUENCE_LENGTH, KEY_VALUE_HEADS * HEAD_WIDTH)[row_arrangement]
    return (grad_queries, key_gradient_rows, value_gradient_rows)
```

```python
import functools
import math

import jax
import jax.numpy as jnp
from jax import lax
from jax.experimental import pallas as pl
from jax.experimental.pallas import tpu as pltpu
from jax.sharding import PartitionSpec as P

HEAD_WIDTH = 128
GROUP = 4


NEG = -1e30
BLOCK = 512


def shifted(value, axis, by):
    count = lax.axis_size(axis)
    return lax.ppermute(value, axis, [(i, (i + by) % count) for i in range(count)])


def document_of(positions, doc_lengths):
    ends = jnp.cumsum(doc_lengths)
    return jnp.sum((positions[:, None] >= ends[None, :]).astype(jnp.int32), axis=1)


def allowed_between(query_positions, query_docs, key_positions, key_docs):
    return (query_docs[:, None] == key_docs[None, :]) & (
        key_positions[None, :] <= query_positions[:, None]
    )


def head_rows(matrix, group_size, head_dim):
    row_count = matrix.shape[0]
    return matrix.reshape(row_count * group_size, head_dim)


def block_scores(query_flat, key_head, row_count, group_size, head_dim):
    scores = lax.dot_general(
        query_flat, key_head, (((1,), (1,)), ((), ())), preferred_element_type=jnp.float32
    )
    return (scores * (1.0 / math.sqrt(head_dim))).reshape(row_count, group_size, key_head.shape[0])


def update_stats(running, query_local, key_block, allowed, group_size, head_dim):
    running_max, totals = running
    row_count = query_local.shape[0]
    scores = block_scores(
        head_rows(query_local, group_size, head_dim), key_block, row_count, group_size, head_dim
    )
    masked = jnp.where(allowed[:, None, :], scores, NEG)
    new_max = jnp.maximum(running_max, jnp.max(masked, axis=2))
    weights = jnp.where(allowed[:, None, :], jnp.exp(masked - new_max[:, :, None]), 0.0)
    new_totals = [totals * jnp.exp(running_max - new_max) + jnp.sum(weights, axis=2)]
    new_maxima = [new_max]
    return (jnp.concatenate(new_maxima, axis=1), jnp.concatenate(new_totals, axis=1))


def backward_block(
    query_local,
    grad_local,
    log_norm,
    row_delta,
    key_block,
    value_block,
    allowed,
    group_size,
    head_dim,
):
    row_count = query_local.shape[0]
    query_flat = head_rows(query_local, group_size, head_dim)
    grad_flat = head_rows(grad_local, group_size, head_dim)
    scores = block_scores(query_flat, key_block, row_count, group_size, head_dim)
    masked = jnp.where(allowed[:, None, :], scores, NEG)
    weights = jnp.exp(masked - log_norm[:, 0:group_size, None])
    grad_weights = lax.dot_general(
        grad_flat, value_block, (((1,), (1,)), ((), ())), preferred_element_type=jnp.float32
    ).reshape(row_count, group_size, -1)
    grad_scores = weights * (grad_weights - row_delta[:, 0:group_size, None])
    rounded_weights = weights.astype(jnp.bfloat16).reshape(row_count * group_size, -1)
    rounded_grads = grad_scores.astype(jnp.bfloat16).reshape(row_count * group_size, -1)
    value_parts = [
        lax.dot_general(
            rounded_weights, grad_flat, (((0,), (0,)), ((), ())), preferred_element_type=jnp.float32
        )
    ]
    key_parts = [
        lax.dot_general(
            rounded_grads, query_flat, (((0,), (0,)), ((), ())), preferred_element_type=jnp.float32
        )
    ]
    query_parts = [
        jnp.dot(rounded_grads, key_block, preferred_element_type=jnp.float32).reshape(
            row_count, group_size * head_dim
        )
    ]
    return (
        jnp.concatenate(query_parts, axis=1),
        jnp.concatenate(key_parts, axis=1),
        jnp.concatenate(value_parts, axis=1),
    )


def ring_plan(doc_lengths, owners, queries, key_head_rows, value_head_rows, forward_out, grad_out):
    context_size = lax.axis_size("ctx")
    context_index = lax.axis_index("ctx")
    row_count = queries.shape[0]
    head_dim = HEAD_WIDTH
    group_size = GROUP
    query_heads = queries.shape[1] // head_dim
    slot_count = 2 * row_count // context_size
    everyone = lax.all_gather(owners, "ctx", axis=0, tiled=True)
    row_arrangement = jnp.argsort(everyone, stable=True)
    layout_docs = document_of(row_arrangement, doc_lengths)
    own_positions = lax.dynamic_slice_in_dim(
        row_arrangement, context_index * row_count, row_count, 0
    )
    own_documents = lax.dynamic_slice_in_dim(layout_docs, context_index * row_count, row_count, 0)
    owner_ids = jnp.arange(context_size, dtype=jnp.int32)
    owner_hot = (owners[:, None] == owner_ids[None, :]).astype(jnp.int32)
    earlier = jnp.cumsum(owner_hot, axis=0) - owner_hot
    rank_within = jnp.sum(earlier * owner_hot, axis=1)
    slot_rows = owners * slot_count + rank_within

    def packed(matrix):
        empty = jnp.zeros((context_size * slot_count,) + matrix.shape[1:], matrix.dtype)
        return empty.at[slot_rows].set(matrix)

    owner_grid = everyone.reshape(context_size, row_count)
    counts = jnp.sum((owner_grid == context_index).astype(jnp.int32), axis=1)
    count_ends = jnp.cumsum(counts)
    starts = count_ends - counts
    wanted = jnp.arange(row_count, dtype=jnp.int32)
    source = jnp.sum((wanted[:, None] >= count_ends[None, :]).astype(jnp.int32), axis=1)
    source_hot = (source[:, None] == owner_ids[None, :]).astype(jnp.int32)
    take_rows = source * slot_count + wanted - jnp.sum(source_hot * starts[None, :], axis=1)

    def compact(received):
        return jnp.take(received, take_rows, axis=0)

    local_delta = jnp.sum(
        (grad_out.astype(jnp.float32) * forward_out.astype(jnp.float32)).reshape(
            row_count, query_heads, head_dim
        ),
        axis=2,
    )
    arrived = (
        lax.all_to_all(packed(queries), "ctx", split_axis=0, concat_axis=0, tiled=True),
        lax.all_to_all(packed(key_head_rows), "ctx", split_axis=0, concat_axis=0, tiled=True),
        lax.all_to_all(packed(value_head_rows), "ctx", split_axis=0, concat_axis=0, tiled=True),
        lax.all_to_all(packed(grad_out), "ctx", split_axis=0, concat_axis=0, tiled=True),
    )
    query_local, key_local, value_local, grad_local = [compact(received) for received in arrived]
    row_delta = compact(
        lax.all_to_all(packed(local_delta), "ctx", split_axis=0, concat_axis=0, tiled=True)
    )

    def fold_keys(running, shard_rows, first_row):
        piece_count = shard_rows.shape[0]
        step_rows = math.gcd(piece_count, BLOCK) if piece_count > BLOCK else piece_count

        def one_block(partial_value, block_index):
            offset = first_row + block_index * step_rows
            key_block = lax.dynamic_slice_in_dim(shard_rows, block_index * step_rows, step_rows, 0)
            key_positions = lax.dynamic_slice_in_dim(row_arrangement, offset, step_rows, 0)
            key_docs = lax.dynamic_slice_in_dim(layout_docs, offset, step_rows, 0)
            allowed = allowed_between(own_positions, own_documents, key_positions, key_docs)
            return (
                update_stats(partial_value, query_local, key_block, allowed, group_size, head_dim),
                None,
            )

        if piece_count == step_rows:
            return one_block(running, 0)[0]
        return lax.scan(one_block, running, jnp.arange(piece_count // step_rows, dtype=jnp.int32))[
            0
        ]

    start_stats = (
        jnp.full((row_count, query_heads), NEG, jnp.float32),
        jnp.zeros((row_count, query_heads), jnp.float32),
    )
    top_scores, totals = fold_keys(
        start_stats, lax.all_gather(key_local, "ctx", axis=0, tiled=True), jnp.int32(0)
    )
    log_norm = top_scores + jnp.log(totals)

    def block_meta(owner_index, offset, size):
        first = owner_index * row_count + offset
        key_positions = lax.dynamic_slice_in_dim(row_arrangement, first, size, 0)
        key_docs = lax.dynamic_slice_in_dim(layout_docs, first, size, 0)
        return (key_positions, key_docs)

    query_zero = jnp.zeros(query_local.shape, jnp.float32)
    key_zero = jnp.zeros(key_local.shape, jnp.float32)

    def one_turn(turn_index, loop_state):
        key_moving, value_moving, key_grad, value_grad, query_grad = loop_state
        owner_index = (context_index - turn_index) % context_size
        key_positions, key_docs = block_meta(owner_index, 0, row_count)
        allowed = allowed_between(own_positions, own_documents, key_positions, key_docs)
        query_part, key_part, value_part = backward_block(
            query_local,
            grad_local,
            log_norm,
            row_delta,
            key_moving,
            value_moving,
            allowed,
            group_size,
            head_dim,
        )
        return (
            key_moving,
            value_moving,
            key_grad + key_part,
            value_grad + value_part,
            query_grad + query_part,
        )

    def moved_turn(turn_index, loop_state):
        key_moving, value_moving, key_grad, value_grad, query_grad = loop_state
        key_moving, value_moving = shifted((key_moving, value_moving), "ctx", 1)
        key_grad, value_grad = shifted((key_grad, value_grad), "ctx", 1)
        return one_turn(turn_index, (key_moving, value_moving, key_grad, value_grad, query_grad))

    loop_state = one_turn(0, (key_local, value_local, key_zero, key_zero, query_zero))
    loop_state = lax.fori_loop(1, context_size, moved_turn, loop_state)
    key_grad, value_grad = shifted((loop_state[2], loop_state[3]), "ctx", 1)
    query_grad = loop_state[4]
    inverse_root = 1.0 / math.sqrt(head_dim)
    return (query_grad * inverse_root, key_grad * inverse_root, value_grad)


META = 16


def contract(left, right, left_dim, right_dim, **kw):
    return lax.dot_general(
        left,
        right,
        (((left_dim,), (right_dim,)), ((), ())),
        preferred_element_type=jnp.float32,
        **kw,
    )


def attend_kernel(count, halo, docs, *refs):
    doc_ref, owner_ref, query_ref, grad_ref, saved_ref, key_ref, value_ref = refs[:7]
    near = refs[7 : 7 + halo]
    outs = refs[7 + halo :]
    rows, width = query_ref.shape
    depth = key_ref.shape[1]
    heads = width // depth
    slot = 2 * rows // count
    scale = 1.0 / math.sqrt(depth)
    index = lax.axis_index("ctx")
    lane = lax.broadcasted_iota(jnp.int32, (1, rows), 1)

    def stacked(ref):
        return jnp.concatenate([ref[:, h * depth : (h + 1) * depth] for h in range(heads)], axis=0)

    position = index * rows + lane
    first = jnp.zeros((1, rows), jnp.int32)
    end = jnp.int32(0)
    for d in range(docs):
        end = end + doc_ref[d]
        first = jnp.where(end <= position, end, first)
    key_rows = (halo + 1) * rows
    key_position = (index - halo) * rows + lax.broadcasted_iota(jnp.int32, (key_rows, rows), 0)
    allowed = (key_position >= first) & (key_position <= position)
    allowed = jnp.concatenate([allowed] * heads, axis=1)

    keys = jnp.concatenate([n[0:rows, :] for n in near[::-1]] + [key_ref[...]], axis=0)
    values = jnp.concatenate([n[rows : 2 * rows, :] for n in near[::-1]] + [value_ref[...]], axis=0)
    queries = stacked(query_ref)
    grads = stacked(grad_ref)
    product = grads.astype(jnp.float32) * stacked(saved_ref).astype(jnp.float32)
    delta = contract(
        jnp.ones((8, depth), jnp.float32), product, 1, 1, precision=lax.Precision.HIGHEST
    )[0:1, :]
    scores = jnp.where(allowed, contract(keys, queries, 1, 1) * scale, NEG)
    raised = jnp.exp(scores - jnp.max(scores, axis=0, keepdims=True))
    weights = raised * (1.0 / jnp.sum(raised, axis=0, keepdims=True))
    grad_scores = weights * (contract(values, grads, 1, 1) - delta)
    weights = weights.astype(jnp.bfloat16)
    grad_scores = grad_scores.astype(jnp.bfloat16)
    value_parts = contract(weights, grads, 1, 0).astype(jnp.bfloat16)
    key_parts = (contract(grad_scores, queries, 1, 0) * scale).astype(jnp.bfloat16)
    query_grad = (contract(keys, grad_scores, 0, 0) * scale).astype(jnp.bfloat16)

    def by_owner(owner):
        counts = [
            jnp.sum(jnp.where(owner == p, 1.0, 0.0), axis=1, keepdims=True) for p in range(count)
        ]
        before = jnp.zeros((1, rows), jnp.float32)
        for p in range(count - 1):
            before = before + jnp.where(owner > p, counts[p], 0.0)
        ahead = lax.rem(owner - index + count, count)
        target = ahead * slot + lane - before.astype(jnp.int32)
        places = lax.broadcasted_iota(jnp.int32, (count * slot, rows), 0)
        return counts, jnp.where(places == target, 1.0, 0.0).astype(jnp.bfloat16)

    counts, spread = by_owner(owner_ref[...])
    tall = jnp.concatenate(
        [query_grad[:, h * rows : (h + 1) * rows] for h in range(heads)], axis=0
    )
    query_slots = contract(spread, tall, 1, 1).astype(jnp.bfloat16)
    pieces = [query_slots[:, h * depth : (h + 1) * depth] for h in range(heads)]
    for back in range(halo + 1):
        if back:
            owner = near[back - 1][2 * rows : 2 * rows + 1, :].astype(jnp.int32)
            _, spread = by_owner(owner)
        at = slice((halo - back) * rows, (halo - back + 1) * rows)
        pieces.append(contract(spread, key_parts[at, :], 1, 0).astype(jnp.bfloat16))
        pieces.append(contract(spread, value_parts[at, :], 1, 0).astype(jnp.bfloat16))
    for ahead in range(count):
        owner = lax.rem(index + ahead, count)
        for n, piece in enumerate(pieces):
            outs[ahead][n * slot : (n + 1) * slot, :] = piece[ahead * slot : (ahead + 1) * slot, :]
        given = jnp.zeros((1, 1), jnp.float32)
        for p in range(count):
            given = jnp.where(owner == p, counts[p], given)
        outs[ahead][len(pieces) * slot :, :] = jnp.broadcast_to(given, (META, depth)).astype(
            jnp.bfloat16
        )


def place_kernel(count, halo, *refs):
    ins = refs[:count]
    query_out, key_out, value_out = refs[count:]
    rows, width = query_out.shape
    depth = key_out.shape[1]
    heads = width // depth
    slot = 2 * rows // count
    index = lax.axis_index("ctx")
    pieces = heads + 2 * (halo + 1)
    source = [lax.rem(index - k + count, count) for k in range(count)]
    given = [
        ins[k][pieces * slot : pieces * slot + 1, 0:1].astype(jnp.float32).astype(jnp.int32)
        for k in range(count)
    ]
    lane = lax.broadcasted_iota(jnp.int32, (1, count * slot), 1)
    target = jnp.full((1, count * slot), -1, jnp.int32)
    for k in range(count):
        before = jnp.zeros((1, 1), jnp.int32)
        for other in range(count):
            before = before + jnp.where(source[other] < source[k], given[other], 0)
        step = lane - k * slot
        inside = (step >= 0) & (step < given[k])
        target = jnp.where(inside, before + step, target)
    places = lax.broadcasted_iota(jnp.int32, (rows, count * slot), 0)
    spread = jnp.where(places == target, 1.0, 0.0).astype(jnp.bfloat16)

    def gathered(piece, back):
        return jnp.concatenate(
            [
                ins[(k - back) % count][piece * slot : (piece + 1) * slot, :]
                for k in range(count)
            ],
            axis=0,
        )

    for h in range(heads):
        query_out[:, h * depth : (h + 1) * depth] = contract(spread, gathered(h, 0), 1, 0)
    for n, out in enumerate((key_out, value_out)):
        total = contract(spread, gathered(heads + n, 0), 1, 0)
        for back in range(1, halo + 1):
            total = total + contract(spread, gathered(heads + 2 * back + n, back), 1, 0)
        out[...] = total


def near_plan(doc_lengths, owners, queries, key_head_rows, value_head_rows, forward_out, grad_out):
    count = lax.axis_size("ctx")
    rows, width = queries.shape
    depth = key_head_rows.shape[1]
    halo = count // 2
    slot = 2 * rows // count
    pieces = width // depth + 2 * (halo + 1)
    whole = pl.BlockSpec(memory_space=pltpu.VMEM)
    params = pltpu.CompilerParams(vmem_limit_bytes=40 * 1024 * 1024)
    packet = jnp.concatenate(
        [
            key_head_rows,
            value_head_rows,
            jnp.broadcast_to(owners.astype(jnp.bfloat16)[None, :], (META, rows)),
        ],
        axis=0,
    )
    near = [
        lax.ppermute(packet, "ctx", [(i, i + back) for i in range(count - back)])
        for back in range(1, halo + 1)
    ]
    sent = pl.pallas_call(
        functools.partial(attend_kernel, count, halo, doc_lengths.shape[0]),
        out_shape=[jax.ShapeDtypeStruct((pieces * slot + META, depth), jnp.bfloat16)] * count,
        in_specs=[pl.BlockSpec(memory_space=pltpu.SMEM)] + [whole] * (6 + halo),
        out_specs=[whole] * count,
        compiler_params=params,
    )(
        doc_lengths,
        owners.reshape(1, rows),
        queries,
        grad_out,
        forward_out,
        key_head_rows,
        value_head_rows,
        *near,
    )
    received = [sent[0]] + [
        lax.ppermute(sent[k], "ctx", [(i, (i + k) % count) for i in range(count)])
        for k in range(1, count)
    ]
    return pl.pallas_call(
        functools.partial(place_kernel, count, halo),
        out_shape=[
            jax.ShapeDtypeStruct((rows, width), jnp.float32),
            jax.ShapeDtypeStruct((rows, depth), jnp.float32),
            jax.ShapeDtypeStruct((rows, depth), jnp.float32),
        ],
        in_specs=[whole] * count,
        out_specs=[whole] * 3,
        compiler_params=params,
    )(*received)


def per_device(*args):
    if lax.axis_size("ctx") <= 4:
        return near_plan(*args)
    return ring_plan(*args)


def solution(mesh):
    return jax.shard_map(
        per_device,
        mesh=mesh,
        in_specs=(
            P("groups"),
            P(("groups", "ctx")),
            P(("groups", "ctx"), "head"),
            P(("groups", "ctx"), "head"),
            P(("groups", "ctx"), "head"),
            P(("groups", "ctx"), "head"),
            P(("groups", "ctx"), "head"),
        ),
        out_specs=(
            P(("groups", "ctx"), "head"),
            P(("groups", "ctx"), "head"),
            P(("groups", "ctx"), "head"),
        ),
        check_vma=False,
    )
```

```python
import functools
import math

import jax
import jax.numpy as jnp
from jax import lax
from jax.experimental import pallas as pl
from jax.experimental.pallas import tpu as pltpu
from jax.sharding import PartitionSpec as P

HEAD_WIDTH = 128
GROUP = 4


NEG = -1e30
BLOCK = 512


def shifted(value, axis, by):
    count = lax.axis_size(axis)
    return lax.ppermute(value, axis, [(i, (i + by) % count) for i in range(count)])


def document_of(positions, doc_lengths):
    ends = jnp.cumsum(doc_lengths)
    return jnp.sum((positions[:, None] >= ends[None, :]).astype(jnp.int32), axis=1)


def allowed_between(query_positions, query_docs, key_positions, key_docs):
    return (query_docs[:, None] == key_docs[None, :]) & (
        key_positions[None, :] <= query_positions[:, None]
    )


def head_rows(matrix, group_size, head_dim):
    row_count = matrix.shape[0]
    return matrix.reshape(row_count * group_size, head_dim)


def block_scores(query_flat, key_head, row_count, group_size, head_dim):
    scores = lax.dot_general(
        query_flat, key_head, (((1,), (1,)), ((), ())), preferred_element_type=jnp.float32
    )
    return (scores * (1.0 / math.sqrt(head_dim))).reshape(row_count, group_size, key_head.shape[0])


def update_stats(running, query_local, key_block, allowed, group_size, head_dim):
    running_max, totals = running
    row_count = query_local.shape[0]
    scores = block_scores(
        head_rows(query_local, group_size, head_dim), key_block, row_count, group_size, head_dim
    )
    masked = jnp.where(allowed[:, None, :], scores, NEG)
    new_max = jnp.maximum(running_max, jnp.max(masked, axis=2))
    weights = jnp.where(allowed[:, None, :], jnp.exp(masked - new_max[:, :, None]), 0.0)
    new_totals = [totals * jnp.exp(running_max - new_max) + jnp.sum(weights, axis=2)]
    new_maxima = [new_max]
    return (jnp.concatenate(new_maxima, axis=1), jnp.concatenate(new_totals, axis=1))


def backward_block(
    query_local,
    grad_local,
    log_norm,
    row_delta,
    key_block,
    value_block,
    allowed,
    group_size,
    head_dim,
):
    row_count = query_local.shape[0]
    query_flat = head_rows(query_local, group_size, head_dim)
    grad_flat = head_rows(grad_local, group_size, head_dim)
    scores = block_scores(query_flat, key_block, row_count, group_size, head_dim)
    masked = jnp.where(allowed[:, None, :], scores, NEG)
    weights = jnp.exp(masked - log_norm[:, 0:group_size, None])
    grad_weights = lax.dot_general(
        grad_flat, value_block, (((1,), (1,)), ((), ())), preferred_element_type=jnp.float32
    ).reshape(row_count, group_size, -1)
    grad_scores = weights * (grad_weights - row_delta[:, 0:group_size, None])
    rounded_weights = weights.astype(jnp.bfloat16).reshape(row_count * group_size, -1)
    rounded_grads = grad_scores.astype(jnp.bfloat16).reshape(row_count * group_size, -1)
    value_parts = [
        lax.dot_general(
            rounded_weights, grad_flat, (((0,), (0,)), ((), ())), preferred_element_type=jnp.float32
        )
    ]
    key_parts = [
        lax.dot_general(
            rounded_grads, query_flat, (((0,), (0,)), ((), ())), preferred_element_type=jnp.float32
        )
    ]
    query_parts = [
        jnp.dot(rounded_grads, key_block, preferred_element_type=jnp.float32).reshape(
            row_count, group_size * head_dim
        )
    ]
    return (
        jnp.concatenate(query_parts, axis=1),
        jnp.concatenate(key_parts, axis=1),
        jnp.concatenate(value_parts, axis=1),
    )


def ring_plan(doc_lengths, owners, queries, key_head_rows, value_head_rows, forward_out, grad_out):
    context_size = lax.axis_size("ctx")
    context_index = lax.axis_index("ctx")
    row_count = queries.shape[0]
    head_dim = HEAD_WIDTH
    group_size = GROUP
    query_heads = queries.shape[1] // head_dim
    slot_count = 2 * row_count // context_size
    everyone = lax.all_gather(owners, "ctx", axis=0, tiled=True)
    row_arrangement = jnp.argsort(everyone, stable=True)
    layout_docs = document_of(row_arrangement, doc_lengths)
    own_positions = lax.dynamic_slice_in_dim(
        row_arrangement, context_index * row_count, row_count, 0
    )
    own_documents = lax.dynamic_slice_in_dim(layout_docs, context_index * row_count, row_count, 0)
    owner_ids = jnp.arange(context_size, dtype=jnp.int32)
    owner_hot = (owners[:, None] == owner_ids[None, :]).astype(jnp.int32)
    earlier = jnp.cumsum(owner_hot, axis=0) - owner_hot
    rank_within = jnp.sum(earlier * owner_hot, axis=1)
    slot_rows = owners * slot_count + rank_within

    def packed(matrix):
        empty = jnp.zeros((context_size * slot_count,) + matrix.shape[1:], matrix.dtype)
        return empty.at[slot_rows].set(matrix)

    owner_grid = everyone.reshape(context_size, row_count)
    counts = jnp.sum((owner_grid == context_index).astype(jnp.int32), axis=1)
    count_ends = jnp.cumsum(counts)
    starts = count_ends - counts
    wanted = jnp.arange(row_count, dtype=jnp.int32)
    source = jnp.sum((wanted[:, None] >= count_ends[None, :]).astype(jnp.int32), axis=1)
    source_hot = (source[:, None] == owner_ids[None, :]).astype(jnp.int32)
    take_rows = source * slot_count + wanted - jnp.sum(source_hot * starts[None, :], axis=1)

    def compact(received):
        return jnp.take(received, take_rows, axis=0)

    local_delta = jnp.sum(
        (grad_out.astype(jnp.float32) * forward_out.astype(jnp.float32)).reshape(
            row_count, query_heads, head_dim
        ),
        axis=2,
    )
    arrived = (
        lax.all_to_all(packed(queries), "ctx", split_axis=0, concat_axis=0, tiled=True),
        lax.all_to_all(packed(key_head_rows), "ctx", split_axis=0, concat_axis=0, tiled=True),
        lax.all_to_all(packed(value_head_rows), "ctx", split_axis=0, concat_axis=0, tiled=True),
        lax.all_to_all(packed(grad_out), "ctx", split_axis=0, concat_axis=0, tiled=True),
    )
    query_local, key_local, value_local, grad_local = [compact(received) for received in arrived]
    row_delta = compact(
        lax.all_to_all(packed(local_delta), "ctx", split_axis=0, concat_axis=0, tiled=True)
    )

    def fold_keys(running, shard_rows, first_row):
        piece_count = shard_rows.shape[0]
        step_rows = math.gcd(piece_count, BLOCK) if piece_count > BLOCK else piece_count

        def one_block(partial_value, block_index):
            offset = first_row + block_index * step_rows
            key_block = lax.dynamic_slice_in_dim(shard_rows, block_index * step_rows, step_rows, 0)
            key_positions = lax.dynamic_slice_in_dim(row_arrangement, offset, step_rows, 0)
            key_docs = lax.dynamic_slice_in_dim(layout_docs, offset, step_rows, 0)
            allowed = allowed_between(own_positions, own_documents, key_positions, key_docs)
            return (
                update_stats(partial_value, query_local, key_block, allowed, group_size, head_dim),
                None,
            )

        if piece_count == step_rows:
            return one_block(running, 0)[0]
        return lax.scan(one_block, running, jnp.arange(piece_count // step_rows, dtype=jnp.int32))[
            0
        ]

    start_stats = (
        jnp.full((row_count, query_heads), NEG, jnp.float32),
        jnp.zeros((row_count, query_heads), jnp.float32),
    )
    top_scores, totals = fold_keys(
        start_stats, lax.all_gather(key_local, "ctx", axis=0, tiled=True), jnp.int32(0)
    )
    log_norm = top_scores + jnp.log(totals)

    def block_meta(owner_index, offset, size):
        first = owner_index * row_count + offset
        key_positions = lax.dynamic_slice_in_dim(row_arrangement, first, size, 0)
        key_docs = lax.dynamic_slice_in_dim(layout_docs, first, size, 0)
        return (key_positions, key_docs)

    query_zero = jnp.zeros(query_local.shape, jnp.float32)
    key_zero = jnp.zeros(key_local.shape, jnp.float32)

    def one_turn(turn_index, loop_state):
        key_moving, value_moving, key_grad, value_grad, query_grad = loop_state
        owner_index = (context_index - turn_index) % context_size
        key_positions, key_docs = block_meta(owner_index, 0, row_count)
        allowed = allowed_between(own_positions, own_documents, key_positions, key_docs)
        query_part, key_part, value_part = backward_block(
            query_local,
            grad_local,
            log_norm,
            row_delta,
            key_moving,
            value_moving,
            allowed,
            group_size,
            head_dim,
        )
        return (
            key_moving,
            value_moving,
            key_grad + key_part,
            value_grad + value_part,
            query_grad + query_part,
        )

    def moved_turn(turn_index, loop_state):
        key_moving, value_moving, key_grad, value_grad, query_grad = loop_state
        key_moving, value_moving = shifted((key_moving, value_moving), "ctx", 1)
        key_grad, value_grad = shifted((key_grad, value_grad), "ctx", 1)
        return one_turn(turn_index, (key_moving, value_moving, key_grad, value_grad, query_grad))

    loop_state = one_turn(0, (key_local, value_local, key_zero, key_zero, query_zero))
    loop_state = lax.fori_loop(1, context_size, moved_turn, loop_state)
    key_grad, value_grad = shifted((loop_state[2], loop_state[3]), "ctx", 1)
    query_grad = loop_state[4]
    inverse_root = 1.0 / math.sqrt(head_dim)
    return (query_grad * inverse_root, key_grad * inverse_root, value_grad)


META = 16


def contract(left, right, left_dim, right_dim, **kw):
    return lax.dot_general(
        left,
        right,
        (((left_dim,), (right_dim,)), ((), ())),
        preferred_element_type=jnp.float32,
        **kw,
    )


def one_hot(row_count, target):
    places = lax.broadcasted_iota(jnp.int32, (row_count, target.shape[1]), 0)
    return jnp.where(places == target, 1.0, 0.0).astype(jnp.bfloat16)


def side_by_side(stack, heads):
    rows = stack.shape[0] // heads
    return jnp.concatenate([stack[h * rows : (h + 1) * rows, :] for h in range(heads)], axis=1)


def end_to_end(matrix, heads):
    width = matrix.shape[1] // heads
    return jnp.concatenate([matrix[:, h * width : (h + 1) * width] for h in range(heads)], axis=0)


def own_kernel(
    docs,
    doc_ref,
    packet_ref,
    query_ref,
    grad_ref,
    saved_ref,
    query_out,
    grad_out,
    raised_out,
    change_out,
    row_out,
    query_in,
    grad_in,
    saved_in,
    sems,
):
    copies = [
        pltpu.make_async_copy(far, here, sems.at[n])
        for n, (far, here) in enumerate(
            ((query_ref, query_in), (grad_ref, grad_in), (saved_ref, saved_in))
        )
    ]
    for copy in copies:
        copy.start()
    rows, width = query_in.shape
    depth = packet_ref.shape[1]
    heads = width // depth
    index = lax.axis_index("ctx")
    lane = lax.broadcasted_iota(jnp.int32, (1, rows), 1)
    position = index * rows + lane
    first = jnp.zeros((1, rows), jnp.int32)
    end = jnp.int32(0)
    for d in range(docs):
        end = end + doc_ref[d]
        first = jnp.where(end <= position, end, first)
    key_position = index * rows + lax.broadcasted_iota(jnp.int32, (rows, rows), 0)
    allowed = (key_position >= first) & (key_position <= position)
    allowed = jnp.concatenate([allowed] * heads, axis=1)

    copies[0].wait()
    queries = end_to_end(query_in[...], heads)
    query_out[...] = queries
    scores = contract(packet_ref[0:rows, :], queries, 1, 1) * (1.0 / math.sqrt(depth))
    scores = jnp.where(allowed, scores, NEG)
    top = jnp.max(scores, axis=0, keepdims=True)
    raised = jnp.exp(scores - top)
    raised_out[...] = raised
    copies[1].wait()
    grads = end_to_end(grad_in[...], heads)
    grad_out[...] = grads
    copies[2].wait()
    product = grads.astype(jnp.float32) * end_to_end(saved_in[...], heads).astype(jnp.float32)
    delta = contract(
        jnp.ones((8, depth), jnp.float32), product, 1, 1, precision=lax.Precision.HIGHEST
    )[0:1, :]
    change_out[...] = contract(packet_ref[rows : 2 * rows, :], grads, 1, 1) - delta
    row_out[0:1, :] = delta
    row_out[1:2, :] = top
    row_out[2:3, :] = jnp.sum(raised, axis=0, keepdims=True)
    row_out[3:4, :] = jnp.concatenate([first.astype(jnp.float32)] * heads, axis=1)
    row_out[4:8, :] = jnp.zeros((4, width), jnp.float32)


def attend_kernel(count, halo, *refs):
    query_ref, grad_ref, raised_ref, change_ref, row_ref = refs[:5]
    own = refs[5]
    near = refs[6 : 6 + halo]
    outs = refs[6 + halo :]
    rows, columns = raised_ref.shape
    depth = query_ref.shape[1]
    heads = columns // rows
    slot = 2 * rows // count
    scale = 1.0 / math.sqrt(depth)
    index = lax.axis_index("ctx")
    before = near[::-1]
    delta, top, total = (row_ref[n : n + 1, :] for n in range(3))
    first = row_ref[3:4, :].astype(jnp.int32)

    key_position = (index - halo) * rows + lax.broadcasted_iota(
        jnp.int32, (halo * rows, columns), 0
    )
    queries = query_ref[...]
    grads = grad_ref[...]
    keys = jnp.concatenate([n[0:rows, :] for n in before], axis=0)
    values = jnp.concatenate([n[rows : 2 * rows, :] for n in before], axis=0)
    scores = jnp.where(key_position >= first, contract(keys, queries, 1, 1) * scale, NEG)
    new_top = jnp.maximum(top, jnp.max(scores, axis=0, keepdims=True))
    raised = jnp.exp(scores - new_top)
    shrink = jnp.exp(top - new_top)
    inverse = 1.0 / (total * shrink + jnp.sum(raised, axis=0, keepdims=True))
    weights = raised * inverse
    own_weights = raised_ref[...] * (shrink * inverse)
    grad_scores = weights * (contract(values, grads, 1, 1) - delta)
    own_grad_scores = own_weights * change_ref[...]
    weights = jnp.concatenate([weights, own_weights], axis=0).astype(jnp.bfloat16)
    grad_scores = jnp.concatenate([grad_scores, own_grad_scores], axis=0).astype(jnp.bfloat16)
    keys = jnp.concatenate([keys, own[0:rows, :]], axis=0)
    value_parts = contract(weights, grads, 1, 0).astype(jnp.bfloat16)
    key_parts = (contract(grad_scores, queries, 1, 0) * scale).astype(jnp.bfloat16)
    query_grad = (contract(keys, grad_scores, 0, 0) * scale).astype(jnp.bfloat16)

    lane = lax.broadcasted_iota(jnp.int32, (1, rows), 1)
    filled = jnp.zeros((count, 1), jnp.float32)
    targets = []
    for block, ref in enumerate(before + (own,)):
        hot = ref[2 * rows : 2 * rows + count, :].astype(jnp.float32)
        counts = jnp.sum(hot, axis=1, keepdims=True)
        owner = jnp.zeros((1, rows), jnp.int32)
        earlier = jnp.zeros((1, rows), jnp.float32)
        base = jnp.zeros((1, rows), jnp.float32)
        for p in range(count):
            mine = hot[p : p + 1, :] > 0.0
            owner = jnp.where(mine, p, owner)
            base = jnp.where(mine, filled[p : p + 1, :], base)
            for less in range(p):
                earlier = earlier + jnp.where(mine, counts[less : less + 1, :], 0.0)
        ahead = lax.rem(owner - index + count, count)
        rank = lane - earlier.astype(jnp.int32)
        target = ahead * rows + base.astype(jnp.int32) + rank
        targets.append(jnp.where(index - halo + block >= 0, target, -1))
        filled = filled + counts
    spread = one_hot(count * slot, ahead * slot + rank)
    query_slots = contract(spread, end_to_end(query_grad, heads), 1, 1).astype(jnp.bfloat16)
    spread = one_hot(count * rows, jnp.concatenate(targets, axis=1))
    key_slots = contract(spread, key_parts, 1, 0).astype(jnp.bfloat16)
    value_slots = contract(spread, value_parts, 1, 0).astype(jnp.bfloat16)
    for k in range(count):
        out = outs[k]
        for h in range(heads):
            out[h * slot : (h + 1) * slot, :] = query_slots[
                k * slot : (k + 1) * slot, h * depth : (h + 1) * depth
            ]
        at = heads * slot
        out[at : at + rows, :] = key_slots[k * rows : (k + 1) * rows, :]
        out[at + rows : at + 2 * rows, :] = value_slots[k * rows : (k + 1) * rows, :]
        owner = lax.rem(index + k, count)
        given = jnp.zeros((1, 1), jnp.float32)
        for p in range(count):
            given = jnp.where(owner == p, counts[p : p + 1, :], given)
        out[at + 2 * rows :, :] = jnp.broadcast_to(given, (META, depth)).astype(jnp.bfloat16)


def place_kernel(count, halo, *refs):
    ins = refs[:count]
    query_out, key_out, value_out = refs[count:]
    rows, width = query_out.shape
    depth = key_out.shape[1]
    heads = width // depth
    slot = 2 * rows // count
    at = heads * slot
    index = lax.axis_index("ctx")
    source = [lax.rem(index - k + count, count) for k in range(count)]
    given = [
        ref[at + 2 * rows : at + 2 * rows + 1, 0:1].astype(jnp.float32).astype(jnp.int32)
        for ref in ins
    ]
    query_targets = []
    key_targets = []
    for k in range(count):
        start = jnp.zeros((1, 1), jnp.int32)
        key_start = jnp.zeros((1, 1), jnp.int32)
        for other in range(count):
            start = start + jnp.where(source[other] < source[k], given[other], 0)
            key_start = key_start + jnp.where(source[other] < source[k] - halo, given[other], 0)
        query_targets.append(start)
        key_targets.append(key_start)

    def spread_of(starts, size, limits):
        lane = lax.broadcasted_iota(jnp.int32, (1, count * size), 1)
        target = jnp.full((1, count * size), -1, jnp.int32)
        for k in range(count):
            step = lane - k * size
            inside = (step >= 0) & (step < limits[k])
            target = jnp.where(inside, starts[k] + step, target)
        return one_hot(rows, target)

    spread = spread_of(query_targets, slot, given)
    for h in range(heads):
        taken = jnp.concatenate([ref[h * slot : (h + 1) * slot, :] for ref in ins], axis=0)
        query_out[:, h * depth : (h + 1) * depth] = contract(spread, taken, 1, 0)
    spread = spread_of(key_targets, rows, [rows] * count)
    for n, out in enumerate((key_out, value_out)):
        first = at + n * rows
        taken = jnp.concatenate([ref[first : first + rows, :] for ref in ins], axis=0)
        out[...] = contract(spread, taken, 1, 0)


def near_plan(doc_lengths, owners, queries, key_head_rows, value_head_rows, forward_out, grad_out):
    count = lax.axis_size("ctx")
    rows, width = queries.shape
    depth = key_head_rows.shape[1]
    heads = width // depth
    columns = heads * rows
    halo = count // 2
    slot = 2 * rows // count
    packet_rows = heads * slot + 2 * rows + META
    whole = pl.BlockSpec(memory_space=pltpu.VMEM)
    anywhere = pl.BlockSpec(memory_space=pltpu.HBM)
    params = pltpu.CompilerParams(vmem_limit_bytes=40 * 1024 * 1024)
    bf16, f32 = jnp.bfloat16, jnp.float32

    packet = jnp.concatenate(
        [
            key_head_rows,
            value_head_rows,
            (owners[None, :] == jnp.arange(META, dtype=jnp.int32)[:, None]).astype(bf16),
        ],
        axis=0,
    )
    near = [
        lax.ppermute(packet, "ctx", [(i, i + back) for i in range(count - back)])
        for back in range(1, halo + 1)
    ]
    own = pl.pallas_call(
        functools.partial(own_kernel, doc_lengths.shape[0]),
        out_shape=[
            jax.ShapeDtypeStruct((columns, depth), bf16),
            jax.ShapeDtypeStruct((columns, depth), bf16),
            jax.ShapeDtypeStruct((rows, columns), f32),
            jax.ShapeDtypeStruct((rows, columns), f32),
            jax.ShapeDtypeStruct((8, columns), f32),
        ],
        in_specs=[pl.BlockSpec(memory_space=pltpu.SMEM), whole] + [anywhere] * 3,
        out_specs=[whole] * 5,
        scratch_shapes=[pltpu.VMEM((rows, width), bf16)] * 3 + [pltpu.SemaphoreType.DMA((3,))],
        compiler_params=params,
    )(doc_lengths, packet, queries, grad_out, forward_out)
    sent = pl.pallas_call(
        functools.partial(attend_kernel, count, halo),
        out_shape=[jax.ShapeDtypeStruct((packet_rows, depth), bf16)] * count,
        in_specs=[whole] * (6 + halo),
        out_specs=[whole] * count,
        compiler_params=params,
    )(*own, packet, *near)
    received = [sent[0]] + [
        lax.ppermute(sent[k], "ctx", [(i, (i + k) % count) for i in range(count)])
        for k in range(1, count)
    ]
    return pl.pallas_call(
        functools.partial(place_kernel, count, halo),
        out_shape=[
            jax.ShapeDtypeStruct((rows, width), f32),
            jax.ShapeDtypeStruct((rows, depth), f32),
            jax.ShapeDtypeStruct((rows, depth), f32),
        ],
        in_specs=[whole] * count,
        out_specs=[whole] * 3,
        compiler_params=params,
    )(*received)


def per_device(*args):
    if lax.axis_size("ctx") <= 4:
        return near_plan(*args)
    return ring_plan(*args)


def solution(mesh):
    return jax.shard_map(
        per_device,
        mesh=mesh,
        in_specs=(
            P("groups"),
            P(("groups", "ctx")),
            P(("groups", "ctx"), "head"),
            P(("groups", "ctx"), "head"),
            P(("groups", "ctx"), "head"),
            P(("groups", "ctx"), "head"),
            P(("groups", "ctx"), "head"),
        ),
        out_specs=(
            P(("groups", "ctx"), "head"),
            P(("groups", "ctx"), "head"),
            P(("groups", "ctx"), "head"),
        ),
        check_vma=False,
    )
```

```python
import functools
import math

import jax
import jax.numpy as jnp
from jax import lax
from jax.experimental import pallas as pl
from jax.experimental.pallas import tpu as pltpu
from jax.sharding import PartitionSpec as P

HEAD_WIDTH = 128
GROUP = 4


NEG = -1e30
BLOCK = 512


def shifted(value, axis, by):
    count = lax.axis_size(axis)
    return lax.ppermute(value, axis, [(i, (i + by) % count) for i in range(count)])


def document_of(positions, doc_lengths):
    ends = jnp.cumsum(doc_lengths)
    return jnp.sum((positions[:, None] >= ends[None, :]).astype(jnp.int32), axis=1)


def allowed_between(query_positions, query_docs, key_positions, key_docs):
    return (query_docs[:, None] == key_docs[None, :]) & (
        key_positions[None, :] <= query_positions[:, None]
    )


def head_rows(matrix, group_size, head_dim):
    row_count = matrix.shape[0]
    return matrix.reshape(row_count * group_size, head_dim)


def block_scores(query_flat, key_head, row_count, group_size, head_dim):
    scores = lax.dot_general(
        query_flat, key_head, (((1,), (1,)), ((), ())), preferred_element_type=jnp.float32
    )
    return (scores * (1.0 / math.sqrt(head_dim))).reshape(row_count, group_size, key_head.shape[0])


def update_stats(running, query_local, key_block, allowed, group_size, head_dim):
    running_max, totals = running
    row_count = query_local.shape[0]
    scores = block_scores(
        head_rows(query_local, group_size, head_dim), key_block, row_count, group_size, head_dim
    )
    masked = jnp.where(allowed[:, None, :], scores, NEG)
    new_max = jnp.maximum(running_max, jnp.max(masked, axis=2))
    weights = jnp.where(allowed[:, None, :], jnp.exp(masked - new_max[:, :, None]), 0.0)
    new_totals = [totals * jnp.exp(running_max - new_max) + jnp.sum(weights, axis=2)]
    new_maxima = [new_max]
    return (jnp.concatenate(new_maxima, axis=1), jnp.concatenate(new_totals, axis=1))


def backward_block(
    query_local,
    grad_local,
    log_norm,
    row_delta,
    key_block,
    value_block,
    allowed,
    group_size,
    head_dim,
):
    row_count = query_local.shape[0]
    query_flat = head_rows(query_local, group_size, head_dim)
    grad_flat = head_rows(grad_local, group_size, head_dim)
    scores = block_scores(query_flat, key_block, row_count, group_size, head_dim)
    masked = jnp.where(allowed[:, None, :], scores, NEG)
    weights = jnp.exp(masked - log_norm[:, 0:group_size, None])
    grad_weights = lax.dot_general(
        grad_flat, value_block, (((1,), (1,)), ((), ())), preferred_element_type=jnp.float32
    ).reshape(row_count, group_size, -1)
    grad_scores = weights * (grad_weights - row_delta[:, 0:group_size, None])
    rounded_weights = weights.astype(jnp.bfloat16).reshape(row_count * group_size, -1)
    rounded_grads = grad_scores.astype(jnp.bfloat16).reshape(row_count * group_size, -1)
    value_parts = [
        lax.dot_general(
            rounded_weights, grad_flat, (((0,), (0,)), ((), ())), preferred_element_type=jnp.float32
        )
    ]
    key_parts = [
        lax.dot_general(
            rounded_grads, query_flat, (((0,), (0,)), ((), ())), preferred_element_type=jnp.float32
        )
    ]
    query_parts = [
        jnp.dot(rounded_grads, key_block, preferred_element_type=jnp.float32).reshape(
            row_count, group_size * head_dim
        )
    ]
    return (
        jnp.concatenate(query_parts, axis=1),
        jnp.concatenate(key_parts, axis=1),
        jnp.concatenate(value_parts, axis=1),
    )


def ring_plan(doc_lengths, owners, queries, key_head_rows, value_head_rows, forward_out, grad_out):
    context_size = lax.axis_size("ctx")
    context_index = lax.axis_index("ctx")
    row_count = queries.shape[0]
    head_dim = HEAD_WIDTH
    group_size = GROUP
    query_heads = queries.shape[1] // head_dim
    slot_count = 2 * row_count // context_size
    everyone = lax.all_gather(owners, "ctx", axis=0, tiled=True)
    row_arrangement = jnp.argsort(everyone, stable=True)
    layout_docs = document_of(row_arrangement, doc_lengths)
    own_positions = lax.dynamic_slice_in_dim(
        row_arrangement, context_index * row_count, row_count, 0
    )
    own_documents = lax.dynamic_slice_in_dim(layout_docs, context_index * row_count, row_count, 0)
    owner_ids = jnp.arange(context_size, dtype=jnp.int32)
    owner_hot = (owners[:, None] == owner_ids[None, :]).astype(jnp.int32)
    earlier = jnp.cumsum(owner_hot, axis=0) - owner_hot
    rank_within = jnp.sum(earlier * owner_hot, axis=1)
    slot_rows = owners * slot_count + rank_within

    def packed(matrix):
        empty = jnp.zeros((context_size * slot_count,) + matrix.shape[1:], matrix.dtype)
        return empty.at[slot_rows].set(matrix)

    owner_grid = everyone.reshape(context_size, row_count)
    counts = jnp.sum((owner_grid == context_index).astype(jnp.int32), axis=1)
    count_ends = jnp.cumsum(counts)
    starts = count_ends - counts
    wanted = jnp.arange(row_count, dtype=jnp.int32)
    source = jnp.sum((wanted[:, None] >= count_ends[None, :]).astype(jnp.int32), axis=1)
    source_hot = (source[:, None] == owner_ids[None, :]).astype(jnp.int32)
    take_rows = source * slot_count + wanted - jnp.sum(source_hot * starts[None, :], axis=1)

    def compact(received):
        return jnp.take(received, take_rows, axis=0)

    local_delta = jnp.sum(
        (grad_out.astype(jnp.float32) * forward_out.astype(jnp.float32)).reshape(
            row_count, query_heads, head_dim
        ),
        axis=2,
    )
    arrived = (
        lax.all_to_all(packed(queries), "ctx", split_axis=0, concat_axis=0, tiled=True),
        lax.all_to_all(packed(key_head_rows), "ctx", split_axis=0, concat_axis=0, tiled=True),
        lax.all_to_all(packed(value_head_rows), "ctx", split_axis=0, concat_axis=0, tiled=True),
        lax.all_to_all(packed(grad_out), "ctx", split_axis=0, concat_axis=0, tiled=True),
    )
    query_local, key_local, value_local, grad_local = [compact(received) for received in arrived]
    row_delta = compact(
        lax.all_to_all(packed(local_delta), "ctx", split_axis=0, concat_axis=0, tiled=True)
    )

    def fold_keys(running, shard_rows, first_row):
        piece_count = shard_rows.shape[0]
        step_rows = math.gcd(piece_count, BLOCK) if piece_count > BLOCK else piece_count

        def one_block(partial_value, block_index):
            offset = first_row + block_index * step_rows
            key_block = lax.dynamic_slice_in_dim(shard_rows, block_index * step_rows, step_rows, 0)
            key_positions = lax.dynamic_slice_in_dim(row_arrangement, offset, step_rows, 0)
            key_docs = lax.dynamic_slice_in_dim(layout_docs, offset, step_rows, 0)
            allowed = allowed_between(own_positions, own_documents, key_positions, key_docs)
            return (
                update_stats(partial_value, query_local, key_block, allowed, group_size, head_dim),
                None,
            )

        if piece_count == step_rows:
            return one_block(running, 0)[0]
        return lax.scan(one_block, running, jnp.arange(piece_count // step_rows, dtype=jnp.int32))[
            0
        ]

    start_stats = (
        jnp.full((row_count, query_heads), NEG, jnp.float32),
        jnp.zeros((row_count, query_heads), jnp.float32),
    )
    top_scores, totals = fold_keys(
        start_stats, lax.all_gather(key_local, "ctx", axis=0, tiled=True), jnp.int32(0)
    )
    log_norm = top_scores + jnp.log(totals)

    def block_meta(owner_index, offset, size):
        first = owner_index * row_count + offset
        key_positions = lax.dynamic_slice_in_dim(row_arrangement, first, size, 0)
        key_docs = lax.dynamic_slice_in_dim(layout_docs, first, size, 0)
        return (key_positions, key_docs)

    query_zero = jnp.zeros(query_local.shape, jnp.float32)
    key_zero = jnp.zeros(key_local.shape, jnp.float32)

    def one_turn(turn_index, loop_state):
        key_moving, value_moving, key_grad, value_grad, query_grad = loop_state
        owner_index = (context_index - turn_index) % context_size
        key_positions, key_docs = block_meta(owner_index, 0, row_count)
        allowed = allowed_between(own_positions, own_documents, key_positions, key_docs)
        query_part, key_part, value_part = backward_block(
            query_local,
            grad_local,
            log_norm,
            row_delta,
            key_moving,
            value_moving,
            allowed,
            group_size,
            head_dim,
        )
        return (
            key_moving,
            value_moving,
            key_grad + key_part,
            value_grad + value_part,
            query_grad + query_part,
        )

    def moved_turn(turn_index, loop_state):
        key_moving, value_moving, key_grad, value_grad, query_grad = loop_state
        key_moving, value_moving = shifted((key_moving, value_moving), "ctx", 1)
        key_grad, value_grad = shifted((key_grad, value_grad), "ctx", 1)
        return one_turn(turn_index, (key_moving, value_moving, key_grad, value_grad, query_grad))

    loop_state = one_turn(0, (key_local, value_local, key_zero, key_zero, query_zero))
    loop_state = lax.fori_loop(1, context_size, moved_turn, loop_state)
    key_grad, value_grad = shifted((loop_state[2], loop_state[3]), "ctx", 1)
    query_grad = loop_state[4]
    inverse_root = 1.0 / math.sqrt(head_dim)
    return (query_grad * inverse_root, key_grad * inverse_root, value_grad)


META = 16


def contract(left, right, left_dim, right_dim, **kw):
    return lax.dot_general(
        left,
        right,
        (((left_dim,), (right_dim,)), ((), ())),
        preferred_element_type=jnp.float32,
        **kw,
    )


def one_hot(row_count, target):
    places = lax.broadcasted_iota(jnp.int32, (row_count, target.shape[1]), 0)
    return jnp.where(places == target, 1.0, 0.0).astype(jnp.bfloat16)


def side_by_side(stack, heads):
    rows = stack.shape[0] // heads
    return jnp.concatenate([stack[h * rows : (h + 1) * rows, :] for h in range(heads)], axis=1)


def end_to_end(matrix, heads):
    width = matrix.shape[1] // heads
    return jnp.concatenate([matrix[:, h * width : (h + 1) * width] for h in range(heads)], axis=0)


def own_kernel(
    docs,
    doc_ref,
    packet_ref,
    query_ref,
    grad_ref,
    saved_ref,
    query_out,
    grad_out,
    raised_out,
    change_out,
    row_out,
):
    rows, width = query_ref.shape
    depth = packet_ref.shape[1]
    heads = width // depth
    index = lax.axis_index("ctx")
    lane = lax.broadcasted_iota(jnp.int32, (1, rows), 1)
    position = index * rows + lane
    first = jnp.zeros((1, rows), jnp.int32)
    end = jnp.int32(0)
    for d in range(docs):
        end = end + doc_ref[d]
        first = jnp.where(end <= position, end, first)
    key_position = index * rows + lax.broadcasted_iota(jnp.int32, (rows, rows), 0)
    allowed = (key_position >= first) & (key_position <= position)
    allowed = jnp.concatenate([allowed] * heads, axis=1)

    queries = end_to_end(query_ref[...], heads)
    query_out[...] = queries
    scores = contract(packet_ref[0:rows, :], queries, 1, 1) * (1.0 / math.sqrt(depth))
    scores = jnp.where(allowed, scores, NEG)
    top = jnp.max(scores, axis=0, keepdims=True)
    raised = jnp.exp(scores - top)
    raised_out[...] = raised
    grads = end_to_end(grad_ref[...], heads)
    grad_out[...] = grads
    product = grads.astype(jnp.float32) * end_to_end(saved_ref[...], heads).astype(jnp.float32)
    delta = contract(
        jnp.ones((8, depth), jnp.float32), product, 1, 1, precision=lax.Precision.HIGHEST
    )[0:1, :]
    change_out[...] = contract(packet_ref[rows : 2 * rows, :], grads, 1, 1) - delta
    row_out[0:1, :] = delta
    row_out[1:2, :] = top
    row_out[2:3, :] = jnp.sum(raised, axis=0, keepdims=True)
    row_out[3:4, :] = jnp.concatenate([first.astype(jnp.float32)] * heads, axis=1)
    row_out[4:8, :] = jnp.zeros((4, width), jnp.float32)


def attend_kernel(count, halo, *refs):
    query_ref, grad_ref, raised_ref, change_ref, row_ref = refs[:5]
    own = refs[5]
    near = refs[6 : 6 + halo]
    outs = refs[6 + halo :]
    rows, columns = raised_ref.shape
    depth = query_ref.shape[1]
    heads = columns // rows
    slot = 2 * rows // count
    scale = 1.0 / math.sqrt(depth)
    index = lax.axis_index("ctx")
    before = near[::-1]
    delta, top, total = (row_ref[n : n + 1, :] for n in range(3))
    first = row_ref[3:4, :].astype(jnp.int32)

    key_position = (index - halo) * rows + lax.broadcasted_iota(
        jnp.int32, (halo * rows, columns), 0
    )
    queries = query_ref[...]
    grads = grad_ref[...]
    keys = jnp.concatenate([n[0:rows, :] for n in before], axis=0)
    values = jnp.concatenate([n[rows : 2 * rows, :] for n in before], axis=0)
    scores = jnp.where(key_position >= first, contract(keys, queries, 1, 1) * scale, NEG)
    new_top = jnp.maximum(top, jnp.max(scores, axis=0, keepdims=True))
    raised = jnp.exp(scores - new_top)
    shrink = jnp.exp(top - new_top)
    inverse = 1.0 / (total * shrink + jnp.sum(raised, axis=0, keepdims=True))
    weights = raised * inverse
    own_weights = raised_ref[...] * (shrink * inverse)
    grad_scores = weights * (contract(values, grads, 1, 1) - delta)
    own_grad_scores = own_weights * change_ref[...]
    weights = jnp.concatenate([weights, own_weights], axis=0).astype(jnp.bfloat16)
    grad_scores = jnp.concatenate([grad_scores, own_grad_scores], axis=0).astype(jnp.bfloat16)
    keys = jnp.concatenate([keys, own[0:rows, :]], axis=0)
    value_parts = contract(weights, grads, 1, 0).astype(jnp.bfloat16)
    key_parts = (contract(grad_scores, queries, 1, 0) * scale).astype(jnp.bfloat16)
    query_grad = (contract(keys, grad_scores, 0, 0) * scale).astype(jnp.bfloat16)

    lane = lax.broadcasted_iota(jnp.int32, (1, rows), 1)
    filled = jnp.zeros((count, 1), jnp.float32)
    targets = []
    for block, ref in enumerate(before + (own,)):
        hot = ref[2 * rows : 2 * rows + count, :].astype(jnp.float32)
        hot = jnp.where(index - halo + block >= 0, hot, 0.0)
        counts = jnp.sum(hot, axis=1, keepdims=True)
        owner = jnp.zeros((1, rows), jnp.int32)
        earlier = jnp.zeros((1, rows), jnp.float32)
        base = jnp.zeros((1, rows), jnp.float32)
        for p in range(count):
            mine = hot[p : p + 1, :] > 0.0
            owner = jnp.where(mine, p, owner)
            base = jnp.where(mine, filled[p : p + 1, :], base)
            for less in range(p):
                earlier = earlier + jnp.where(mine, counts[less : less + 1, :], 0.0)
        ahead = lax.rem(owner - index + count, count)
        rank = lane - earlier.astype(jnp.int32)
        target = ahead * rows + base.astype(jnp.int32) + rank
        targets.append(jnp.where(index - halo + block >= 0, target, -1))
        filled = filled + counts
    spread = one_hot(count * slot, ahead * slot + rank)
    query_slots = contract(spread, end_to_end(query_grad, heads), 1, 1).astype(jnp.bfloat16)
    spread = one_hot(count * rows, jnp.concatenate(targets, axis=1))
    key_slots = contract(spread, key_parts, 1, 0).astype(jnp.bfloat16)
    value_slots = contract(spread, value_parts, 1, 0).astype(jnp.bfloat16)
    for k in range(count):
        out = outs[k]
        for h in range(heads):
            out[h * slot : (h + 1) * slot, :] = query_slots[
                k * slot : (k + 1) * slot, h * depth : (h + 1) * depth
            ]
        at = heads * slot
        out[at : at + rows, :] = key_slots[k * rows : (k + 1) * rows, :]
        out[at + rows : at + 2 * rows, :] = value_slots[k * rows : (k + 1) * rows, :]
        owner = lax.rem(index + k, count)
        given = jnp.zeros((1, 1), jnp.float32)
        for p in range(count):
            given = jnp.where(owner == p, counts[p : p + 1, :], given)
        out[at + 2 * rows :, :] = jnp.broadcast_to(given, (META, depth)).astype(jnp.bfloat16)


def place_kernel(count, halo, *refs):
    ins = refs[:count]
    query_out, key_out, value_out = refs[count:]
    rows, width = query_out.shape
    depth = key_out.shape[1]
    heads = width // depth
    slot = 2 * rows // count
    at = heads * slot
    index = lax.axis_index("ctx")
    source = [lax.rem(index - k + count, count) for k in range(count)]
    given = [
        ref[at + 2 * rows : at + 2 * rows + 1, 0:1].astype(jnp.float32).astype(jnp.int32)
        for ref in ins
    ]
    query_targets = []
    key_targets = []
    for k in range(count):
        start = jnp.zeros((1, 1), jnp.int32)
        key_start = jnp.zeros((1, 1), jnp.int32)
        for other in range(count):
            start = start + jnp.where(source[other] < source[k], given[other], 0)
            key_start = key_start + jnp.where(source[other] < source[k] - halo, given[other], 0)
        query_targets.append(start)
        key_targets.append(key_start)

    def spread_of(starts, size, limits):
        lane = lax.broadcasted_iota(jnp.int32, (1, count * size), 1)
        target = jnp.full((1, count * size), -1, jnp.int32)
        for k in range(count):
            step = lane - k * size
            inside = (step >= 0) & (step < limits[k])
            target = jnp.where(inside, starts[k] + step, target)
        return one_hot(rows, target)

    spread = spread_of(query_targets, slot, given)
    for h in range(heads):
        taken = jnp.concatenate([ref[h * slot : (h + 1) * slot, :] for ref in ins], axis=0)
        query_out[:, h * depth : (h + 1) * depth] = contract(spread, taken, 1, 0)
    spread = spread_of(key_targets, rows, [rows] * count)
    for n, out in enumerate((key_out, value_out)):
        first = at + n * rows
        taken = jnp.concatenate([ref[first : first + rows, :] for ref in ins], axis=0)
        out[...] = contract(spread, taken, 1, 0)


def near_plan(doc_lengths, owners, queries, key_head_rows, value_head_rows, forward_out, grad_out):
    count = lax.axis_size("ctx")
    rows, width = queries.shape
    depth = key_head_rows.shape[1]
    heads = width // depth
    columns = heads * rows
    halo = count // 2
    slot = 2 * rows // count
    packet_rows = heads * slot + 2 * rows + META
    whole = pl.BlockSpec(memory_space=pltpu.VMEM)
    params = pltpu.CompilerParams(vmem_limit_bytes=40 * 1024 * 1024)
    bf16, f32 = jnp.bfloat16, jnp.float32

    mark = lax.broadcasted_iota(jnp.int32, (2 * rows + META, rows), 0) - 2 * rows
    packet = jnp.where(
        mark < 0,
        jnp.pad(jnp.concatenate([key_head_rows, value_head_rows], axis=0), ((0, META), (0, 0))),
        (owners[None, :] == mark).astype(bf16),
    )
    near = [
        lax.ppermute(packet, "ctx", [(i, (i + back) % count) for i in range(count)])
        for back in range(1, halo + 1)
    ]
    own = pl.pallas_call(
        functools.partial(own_kernel, doc_lengths.shape[0]),
        out_shape=[
            jax.ShapeDtypeStruct((columns, depth), bf16),
            jax.ShapeDtypeStruct((columns, depth), bf16),
            jax.ShapeDtypeStruct((rows, columns), f32),
            jax.ShapeDtypeStruct((rows, columns), f32),
            jax.ShapeDtypeStruct((8, columns), f32),
        ],
        in_specs=[pl.BlockSpec(memory_space=pltpu.SMEM)] + [whole] * 4,
        out_specs=[whole] * 5,
        compiler_params=params,
    )(doc_lengths, packet, queries, grad_out, forward_out)
    sent = pl.pallas_call(
        functools.partial(attend_kernel, count, halo),
        out_shape=[jax.ShapeDtypeStruct((packet_rows, depth), bf16)] * count,
        in_specs=[whole] * (6 + halo),
        out_specs=[whole] * count,
        compiler_params=params,
    )(*own, packet, *near)
    received = [sent[0]] + [
        lax.ppermute(sent[k], "ctx", [(i, (i + k) % count) for i in range(count)])
        for k in range(1, count)
    ]
    return pl.pallas_call(
        functools.partial(place_kernel, count, halo),
        out_shape=[
            jax.ShapeDtypeStruct((rows, width), f32),
            jax.ShapeDtypeStruct((rows, depth), f32),
            jax.ShapeDtypeStruct((rows, depth), f32),
        ],
        in_specs=[whole] * count,
        out_specs=[whole] * 3,
        compiler_params=params,
    )(*received)


def per_device(*args):
    if lax.axis_size("ctx") <= 4:
        return near_plan(*args)
    return ring_plan(*args)


def solution(mesh):
    return jax.shard_map(
        per_device,
        mesh=mesh,
        in_specs=(
            P("groups"),
            P(("groups", "ctx")),
            P(("groups", "ctx"), "head"),
            P(("groups", "ctx"), "head"),
            P(("groups", "ctx"), "head"),
            P(("groups", "ctx"), "head"),
            P(("groups", "ctx"), "head"),
        ),
        out_specs=(
            P(("groups", "ctx"), "head"),
            P(("groups", "ctx"), "head"),
            P(("groups", "ctx"), "head"),
        ),
        check_vma=False,
    )
```

```python
import functools
import math

import jax
import jax.numpy as jnp
from jax import lax
from jax.experimental import pallas as pl
from jax.experimental.pallas import tpu as pltpu
from jax.sharding import PartitionSpec as P

HEAD_WIDTH = 128
GROUP = 4


NEG = -1e30
BLOCK = 512


def shifted(value, axis, by):
    count = lax.axis_size(axis)
    return lax.ppermute(value, axis, [(i, (i + by) % count) for i in range(count)])


def document_of(positions, doc_lengths):
    ends = jnp.cumsum(doc_lengths)
    return jnp.sum((positions[:, None] >= ends[None, :]).astype(jnp.int32), axis=1)


def allowed_between(query_positions, query_docs, key_positions, key_docs):
    return (query_docs[:, None] == key_docs[None, :]) & (
        key_positions[None, :] <= query_positions[:, None]
    )


def head_rows(matrix, group_size, head_dim):
    row_count = matrix.shape[0]
    return matrix.reshape(row_count * group_size, head_dim)


def block_scores(query_flat, key_head, row_count, group_size, head_dim):
    scores = lax.dot_general(
        query_flat, key_head, (((1,), (1,)), ((), ())), preferred_element_type=jnp.float32
    )
    return (scores * (1.0 / math.sqrt(head_dim))).reshape(row_count, group_size, key_head.shape[0])


def update_stats(running, query_local, key_block, allowed, group_size, head_dim):
    running_max, totals = running
    row_count = query_local.shape[0]
    scores = block_scores(
        head_rows(query_local, group_size, head_dim), key_block, row_count, group_size, head_dim
    )
    masked = jnp.where(allowed[:, None, :], scores, NEG)
    new_max = jnp.maximum(running_max, jnp.max(masked, axis=2))
    weights = jnp.where(allowed[:, None, :], jnp.exp(masked - new_max[:, :, None]), 0.0)
    new_totals = [totals * jnp.exp(running_max - new_max) + jnp.sum(weights, axis=2)]
    new_maxima = [new_max]
    return (jnp.concatenate(new_maxima, axis=1), jnp.concatenate(new_totals, axis=1))


def backward_block(
    query_local,
    grad_local,
    log_norm,
    row_delta,
    key_block,
    value_block,
    allowed,
    group_size,
    head_dim,
):
    row_count = query_local.shape[0]
    query_flat = head_rows(query_local, group_size, head_dim)
    grad_flat = head_rows(grad_local, group_size, head_dim)
    scores = block_scores(query_flat, key_block, row_count, group_size, head_dim)
    masked = jnp.where(allowed[:, None, :], scores, NEG)
    weights = jnp.exp(masked - log_norm[:, 0:group_size, None])
    grad_weights = lax.dot_general(
        grad_flat, value_block, (((1,), (1,)), ((), ())), preferred_element_type=jnp.float32
    ).reshape(row_count, group_size, -1)
    grad_scores = weights * (grad_weights - row_delta[:, 0:group_size, None])
    rounded_weights = weights.astype(jnp.bfloat16).reshape(row_count * group_size, -1)
    rounded_grads = grad_scores.astype(jnp.bfloat16).reshape(row_count * group_size, -1)
    value_parts = [
        lax.dot_general(
            rounded_weights, grad_flat, (((0,), (0,)), ((), ())), preferred_element_type=jnp.float32
        )
    ]
    key_parts = [
        lax.dot_general(
            rounded_grads, query_flat, (((0,), (0,)), ((), ())), preferred_element_type=jnp.float32
        )
    ]
    query_parts = [
        jnp.dot(rounded_grads, key_block, preferred_element_type=jnp.float32).reshape(
            row_count, group_size * head_dim
        )
    ]
    return (
        jnp.concatenate(query_parts, axis=1),
        jnp.concatenate(key_parts, axis=1),
        jnp.concatenate(value_parts, axis=1),
    )


def ring_plan(doc_lengths, owners, queries, key_head_rows, value_head_rows, forward_out, grad_out):
    context_size = lax.axis_size("ctx")
    context_index = lax.axis_index("ctx")
    row_count = queries.shape[0]
    head_dim = HEAD_WIDTH
    group_size = GROUP
    query_heads = queries.shape[1] // head_dim
    slot_count = 2 * row_count // context_size
    everyone = lax.all_gather(owners, "ctx", axis=0, tiled=True)
    row_arrangement = jnp.argsort(everyone, stable=True)
    layout_docs = document_of(row_arrangement, doc_lengths)
    own_positions = lax.dynamic_slice_in_dim(
        row_arrangement, context_index * row_count, row_count, 0
    )
    own_documents = lax.dynamic_slice_in_dim(layout_docs, context_index * row_count, row_count, 0)
    owner_ids = jnp.arange(context_size, dtype=jnp.int32)
    owner_hot = (owners[:, None] == owner_ids[None, :]).astype(jnp.int32)
    earlier = jnp.cumsum(owner_hot, axis=0) - owner_hot
    rank_within = jnp.sum(earlier * owner_hot, axis=1)
    slot_rows = owners * slot_count + rank_within

    def packed(matrix):
        empty = jnp.zeros((context_size * slot_count,) + matrix.shape[1:], matrix.dtype)
        return empty.at[slot_rows].set(matrix)

    owner_grid = everyone.reshape(context_size, row_count)
    counts = jnp.sum((owner_grid == context_index).astype(jnp.int32), axis=1)
    count_ends = jnp.cumsum(counts)
    starts = count_ends - counts
    wanted = jnp.arange(row_count, dtype=jnp.int32)
    source = jnp.sum((wanted[:, None] >= count_ends[None, :]).astype(jnp.int32), axis=1)
    source_hot = (source[:, None] == owner_ids[None, :]).astype(jnp.int32)
    take_rows = source * slot_count + wanted - jnp.sum(source_hot * starts[None, :], axis=1)

    def compact(received):
        return jnp.take(received, take_rows, axis=0)

    local_delta = jnp.sum(
        (grad_out.astype(jnp.float32) * forward_out.astype(jnp.float32)).reshape(
            row_count, query_heads, head_dim
        ),
        axis=2,
    )
    arrived = (
        lax.all_to_all(packed(queries), "ctx", split_axis=0, concat_axis=0, tiled=True),
        lax.all_to_all(packed(key_head_rows), "ctx", split_axis=0, concat_axis=0, tiled=True),
        lax.all_to_all(packed(value_head_rows), "ctx", split_axis=0, concat_axis=0, tiled=True),
        lax.all_to_all(packed(grad_out), "ctx", split_axis=0, concat_axis=0, tiled=True),
    )
    query_local, key_local, value_local, grad_local = [compact(received) for received in arrived]
    row_delta = compact(
        lax.all_to_all(packed(local_delta), "ctx", split_axis=0, concat_axis=0, tiled=True)
    )

    def fold_keys(running, shard_rows, first_row):
        piece_count = shard_rows.shape[0]
        step_rows = math.gcd(piece_count, BLOCK) if piece_count > BLOCK else piece_count

        def one_block(partial_value, block_index):
            offset = first_row + block_index * step_rows
            key_block = lax.dynamic_slice_in_dim(shard_rows, block_index * step_rows, step_rows, 0)
            key_positions = lax.dynamic_slice_in_dim(row_arrangement, offset, step_rows, 0)
            key_docs = lax.dynamic_slice_in_dim(layout_docs, offset, step_rows, 0)
            allowed = allowed_between(own_positions, own_documents, key_positions, key_docs)
            return (
                update_stats(partial_value, query_local, key_block, allowed, group_size, head_dim),
                None,
            )

        if piece_count == step_rows:
            return one_block(running, 0)[0]
        return lax.scan(one_block, running, jnp.arange(piece_count // step_rows, dtype=jnp.int32))[
            0
        ]

    start_stats = (
        jnp.full((row_count, query_heads), NEG, jnp.float32),
        jnp.zeros((row_count, query_heads), jnp.float32),
    )
    top_scores, totals = fold_keys(
        start_stats, lax.all_gather(key_local, "ctx", axis=0, tiled=True), jnp.int32(0)
    )
    log_norm = top_scores + jnp.log(totals)

    def block_meta(owner_index, offset, size):
        first = owner_index * row_count + offset
        key_positions = lax.dynamic_slice_in_dim(row_arrangement, first, size, 0)
        key_docs = lax.dynamic_slice_in_dim(layout_docs, first, size, 0)
        return (key_positions, key_docs)

    query_zero = jnp.zeros(query_local.shape, jnp.float32)
    key_zero = jnp.zeros(key_local.shape, jnp.float32)

    def one_turn(turn_index, loop_state):
        key_moving, value_moving, key_grad, value_grad, query_grad = loop_state
        owner_index = (context_index - turn_index) % context_size
        key_positions, key_docs = block_meta(owner_index, 0, row_count)
        allowed = allowed_between(own_positions, own_documents, key_positions, key_docs)
        query_part, key_part, value_part = backward_block(
            query_local,
            grad_local,
            log_norm,
            row_delta,
            key_moving,
            value_moving,
            allowed,
            group_size,
            head_dim,
        )
        return (
            key_moving,
            value_moving,
            key_grad + key_part,
            value_grad + value_part,
            query_grad + query_part,
        )

    def moved_turn(turn_index, loop_state):
        key_moving, value_moving, key_grad, value_grad, query_grad = loop_state
        key_moving, value_moving = shifted((key_moving, value_moving), "ctx", 1)
        key_grad, value_grad = shifted((key_grad, value_grad), "ctx", 1)
        return one_turn(turn_index, (key_moving, value_moving, key_grad, value_grad, query_grad))

    loop_state = one_turn(0, (key_local, value_local, key_zero, key_zero, query_zero))
    loop_state = lax.fori_loop(1, context_size, moved_turn, loop_state)
    key_grad, value_grad = shifted((loop_state[2], loop_state[3]), "ctx", 1)
    query_grad = loop_state[4]
    inverse_root = 1.0 / math.sqrt(head_dim)
    return (query_grad * inverse_root, key_grad * inverse_root, value_grad)


META = 16


def contract(left, right, left_dim, right_dim, **kw):
    return lax.dot_general(
        left,
        right,
        (((left_dim,), (right_dim,)), ((), ())),
        preferred_element_type=jnp.float32,
        **kw,
    )


def one_hot(row_count, target):
    places = lax.broadcasted_iota(jnp.int32, (row_count, target.shape[1]), 0)
    return jnp.where(places == target, 1.0, 0.0).astype(jnp.bfloat16)


def side_by_side(stack, heads):
    rows = stack.shape[0] // heads
    return jnp.concatenate([stack[h * rows : (h + 1) * rows, :] for h in range(heads)], axis=1)


def end_to_end(matrix, heads):
    width = matrix.shape[1] // heads
    return jnp.concatenate([matrix[:, h * width : (h + 1) * width] for h in range(heads)], axis=0)


def runs_of(hot):
    count, rows = hot.shape
    counts = jnp.sum(hot, axis=1, keepdims=True)
    owner = jnp.zeros((1, rows), jnp.int32)
    earlier = jnp.zeros((1, rows), jnp.float32)
    for p in range(count):
        mine = hot[p : p + 1, :] > 0.0
        owner = jnp.where(mine, p, owner)
        for less in range(p):
            earlier = earlier + jnp.where(mine, counts[less : less + 1, :], 0.0)
    lane = lax.broadcasted_iota(jnp.int32, (1, rows), 1)
    return owner, counts, lane - earlier.astype(jnp.int32)


def own_kernel(
    count,
    docs,
    doc_ref,
    packet_ref,
    query_ref,
    grad_ref,
    saved_ref,
    query_out,
    grad_out,
    raised_out,
    change_out,
    row_out,
    spread_out,
):
    rows, width = query_ref.shape
    depth = packet_ref.shape[1]
    heads = width // depth
    slot = 2 * rows // count
    index = lax.axis_index("ctx")
    lane = lax.broadcasted_iota(jnp.int32, (1, rows), 1)
    position = index * rows + lane
    first = jnp.zeros((1, rows), jnp.int32)
    end = jnp.int32(0)
    for d in range(docs):
        end = end + doc_ref[d]
        first = jnp.where(end <= position, end, first)
    key_position = index * rows + lax.broadcasted_iota(jnp.int32, (rows, rows), 0)
    allowed = (key_position >= first) & (key_position <= position)
    allowed = jnp.concatenate([allowed] * heads, axis=1)

    queries = end_to_end(query_ref[...], heads)
    query_out[...] = queries
    scores = contract(packet_ref[0:rows, :], queries, 1, 1) * (1.0 / math.sqrt(depth))
    scores = jnp.where(allowed, scores, NEG)
    top = jnp.max(scores, axis=0, keepdims=True)
    raised = jnp.exp(scores - top)
    raised_out[...] = raised
    grads = end_to_end(grad_ref[...], heads)
    grad_out[...] = grads
    product = grads.astype(jnp.float32) * end_to_end(saved_ref[...], heads).astype(jnp.float32)
    delta = contract(
        jnp.ones((8, depth), jnp.float32), product, 1, 1, precision=lax.Precision.HIGHEST
    )[0:1, :]
    change_out[...] = contract(packet_ref[rows : 2 * rows, :], grads, 1, 1) - delta
    row_out[0:1, :] = delta
    row_out[1:2, :] = top
    row_out[2:3, :] = jnp.sum(raised, axis=0, keepdims=True)
    row_out[3:4, :] = jnp.concatenate([first.astype(jnp.float32)] * heads, axis=1)
    row_out[4:8, :] = jnp.zeros((4, width), jnp.float32)
    owner, counts, rank = runs_of(packet_ref[2 * rows : 2 * rows + count, :].astype(jnp.float32))
    ahead = lax.rem(owner - index + count, count)
    spread_out[...] = one_hot(count * slot, ahead * slot + rank)


def attend_kernel(count, halo, *refs):
    query_ref, grad_ref, raised_ref, change_ref, row_ref, spread_ref = refs[:6]
    own = refs[6]
    before = refs[7 : 7 + halo][::-1]
    weight_out, change_out = refs[7 + halo : 9 + halo]
    outs = refs[9 + halo :]
    rows, columns = raised_ref.shape
    depth = query_ref.shape[1]
    heads = columns // rows
    slot = 2 * rows // count
    scale = 1.0 / math.sqrt(depth)
    index = lax.axis_index("ctx")
    delta, top, total = (row_ref[n : n + 1, :] for n in range(3))
    first = row_ref[3:4, :].astype(jnp.int32)

    key_position = (index - halo) * rows + lax.broadcasted_iota(
        jnp.int32, (halo * rows, columns), 0
    )
    keys = jnp.concatenate([n[0:rows, :] for n in before], axis=0)
    values = jnp.concatenate([n[rows : 2 * rows, :] for n in before], axis=0)
    scores = contract(keys, query_ref[...], 1, 1) * scale
    scores = jnp.where(key_position >= first, scores, NEG)
    new_top = jnp.maximum(top, jnp.max(scores, axis=0, keepdims=True))
    raised = jnp.exp(scores - new_top)
    shrink = jnp.exp(top - new_top)
    inverse = 1.0 / (total * shrink + jnp.sum(raised, axis=0, keepdims=True))
    weights = raised * inverse
    own_weights = raised_ref[...] * (shrink * inverse)
    changes = weights * (contract(values, grad_ref[...], 1, 1) - delta)
    own_changes = own_weights * change_ref[...]
    changes = jnp.concatenate([changes, own_changes], axis=0).astype(jnp.bfloat16)
    weight_out[0 : halo * rows, :] = weights.astype(jnp.bfloat16)
    weight_out[halo * rows :, :] = own_weights.astype(jnp.bfloat16)
    change_out[...] = changes
    keys = jnp.concatenate([keys, own[0:rows, :]], axis=0)
    query_grad = (contract(keys, changes, 0, 0) * scale).astype(jnp.bfloat16)

    slots = contract(spread_ref[...], end_to_end(query_grad, heads), 1, 1).astype(jnp.bfloat16)
    for k in range(count):
        for h in range(heads):
            outs[k][h * slot : (h + 1) * slot, :] = slots[
                k * slot : (k + 1) * slot, h * depth : (h + 1) * depth
            ]


def key_kernel(count, halo, _, *refs):
    query_ref, grad_ref, weight_ref, change_ref = refs[:4]
    own = refs[4]
    near = refs[5 : 5 + halo]
    given_out = refs[5 + halo]
    outs = refs[6 + halo :]
    depth = query_ref.shape[1]
    rows = weight_ref.shape[0] // (halo + 1)
    index = lax.axis_index("ctx")
    value_parts = contract(weight_ref[...], grad_ref[...], 1, 0).astype(jnp.bfloat16)
    key_parts = contract(change_ref[...], query_ref[...], 1, 0) * (1.0 / math.sqrt(depth))
    key_parts = key_parts.astype(jnp.bfloat16)

    filled = jnp.zeros((count, 1), jnp.float32)
    targets = []
    given = []
    for block, ref in enumerate(near[::-1] + (own,)):
        hot = ref[2 * rows : 2 * rows + count, :].astype(jnp.float32)
        owner, counts, rank = runs_of(hot)
        mine = jnp.zeros((1, 1), jnp.float32)
        base = jnp.zeros((1, rows), jnp.float32)
        for p in range(count):
            mine = jnp.where(index == p, counts[p : p + 1, :], mine)
            base = base + jnp.where(owner == p, filled[p : p + 1, :], 0.0)
        given.insert(0, mine)
        target = lax.rem(owner - index + count, count) * rows + base.astype(jnp.int32) + rank
        inside = index - halo + block >= 0
        targets.append(jnp.where(inside, target, -1))
        filled = filled + jnp.where(inside, counts, 0.0)
    spread = one_hot(count * rows, jnp.concatenate(targets, axis=1))
    key_slots = contract(spread, key_parts, 1, 0).astype(jnp.bfloat16)
    value_slots = contract(spread, value_parts, 1, 0).astype(jnp.bfloat16)
    for k in range(count):
        outs[k][0:rows, :] = key_slots[k * rows : (k + 1) * rows, :]
        outs[k][rows:, :] = value_slots[k * rows : (k + 1) * rows, :]

    if len(given) < count:
        given.append(rows - sum(given))
    for k in range(count):
        given_out[k : k + 1, :] = jnp.broadcast_to(given[k], (1, depth))
    given_out[count:, :] = jnp.zeros((8 - count, depth), jnp.float32)


def starts_of(given_ref, count, back):
    index = lax.axis_index("ctx")
    given = [given_ref[k : k + 1, 0:1].astype(jnp.int32) for k in range(count)]
    source = [lax.rem(index - k + count, count) for k in range(count)]
    starts = []
    for k in range(count):
        start = jnp.zeros((1, 1), jnp.int32)
        for other in range(count):
            start = start + jnp.where(source[other] < source[k] - back, given[other], 0)
        starts.append(start)
    return starts, given


def placement(rows, starts, size, limits):
    lane = lax.broadcasted_iota(jnp.int32, (1, len(starts) * size), 1)
    target = jnp.full(lane.shape, -1, jnp.int32)
    for k, start in enumerate(starts):
        step = lane - k * size
        target = jnp.where((step >= 0) & (step < limits[k]), start + step, target)
    return one_hot(rows, target)


def place_queries_kernel(count, given_ref, *refs):
    ins, out = refs[:count], refs[count]
    rows, width = out.shape
    slot = 2 * rows // count
    depth = width * slot // ins[0].shape[0]
    starts, given = starts_of(given_ref, count, 0)
    spread = placement(rows, starts, slot, given)
    for h in range(width // depth):
        taken = jnp.concatenate([ref[h * slot : (h + 1) * slot, :] for ref in ins], axis=0)
        out[:, h * depth : (h + 1) * depth] = contract(spread, taken, 1, 0)


def place_keys_kernel(count, halo, given_ref, *refs):
    ins, outs = refs[:count], refs[count:]
    rows = outs[0].shape[0]
    starts, _ = starts_of(given_ref, count, halo)
    spread = placement(rows, starts, rows, [rows] * count)
    for n, out in enumerate(outs):
        taken = jnp.concatenate([ref[n * rows : (n + 1) * rows, :] for ref in ins], axis=0)
        out[...] = contract(spread, taken, 1, 0)


def near_plan(doc_lengths, owners, queries, key_head_rows, value_head_rows, forward_out, grad_out):
    count = lax.axis_size("ctx")
    rows, width = queries.shape
    depth = key_head_rows.shape[1]
    heads = width // depth
    bf16, f32 = jnp.bfloat16, jnp.float32
    columns = heads * rows
    halo = count // 2
    slot = 2 * rows // count
    spread_shape = jax.ShapeDtypeStruct((count * slot, rows), bf16)
    whole = pl.BlockSpec(memory_space=pltpu.VMEM)
    params = pltpu.CompilerParams(vmem_limit_bytes=40 * 1024 * 1024)

    mark = lax.broadcasted_iota(jnp.int32, (2 * rows + META, rows), 0) - 2 * rows
    packet = jnp.where(
        mark < 0,
        jnp.pad(jnp.concatenate([key_head_rows, value_head_rows], axis=0), ((0, META), (0, 0))),
        (owners[None, :] == mark).astype(bf16),
    )
    near = [
        lax.ppermute(packet, "ctx", [(i, (i + back) % count) for i in range(count)])
        for back in range(1, halo + 1)
    ]
    own = pl.pallas_call(
        functools.partial(own_kernel, count, doc_lengths.shape[0]),
        out_shape=[
            jax.ShapeDtypeStruct((columns, depth), bf16),
            jax.ShapeDtypeStruct((columns, depth), bf16),
            jax.ShapeDtypeStruct((rows, columns), f32),
            jax.ShapeDtypeStruct((rows, columns), f32),
            jax.ShapeDtypeStruct((8, columns), f32),
            spread_shape,
        ],
        in_specs=[pl.BlockSpec(memory_space=pltpu.SMEM)] + [whole] * 4,
        out_specs=[whole] * 6,
        compiler_params=params,
    )(doc_lengths, packet, queries, grad_out, forward_out)
    weights, changes, *query_slots = pl.pallas_call(
        functools.partial(attend_kernel, count, halo),
        out_shape=[jax.ShapeDtypeStruct(((halo + 1) * rows, columns), bf16)] * 2
        + [jax.ShapeDtypeStruct((heads * slot, depth), bf16)] * count,
        in_specs=[whole] * (7 + halo),
        out_specs=[whole] * (2 + count),
        compiler_params=params,
    )(*own, packet, *near)

    def exchanged(slots):
        return [slots[0]] + [
            lax.ppermute(slots[k], "ctx", [(i, (i + k) % count) for i in range(count)])
            for k in range(1, count)
        ]

    query_slots = exchanged(query_slots)
    given, *key_slots = pl.pallas_call(
        functools.partial(key_kernel, count, halo),
        out_shape=[jax.ShapeDtypeStruct((8, depth), f32)]
        + [jax.ShapeDtypeStruct((2 * rows, depth), bf16)] * count,
        in_specs=[pl.BlockSpec(memory_space=pl.ANY)] + [whole] * (5 + halo),
        out_specs=[whole] * (1 + count),
        compiler_params=params,
    )(query_slots[1], own[0], own[1], weights, changes, packet, *near)
    key_slots = exchanged(key_slots)
    grad_queries = pl.pallas_call(
        functools.partial(place_queries_kernel, count),
        out_shape=jax.ShapeDtypeStruct((rows, width), f32),
        in_specs=[whole] * (1 + count),
        out_specs=whole,
        compiler_params=params,
    )(given, *query_slots)
    key_grads, value_grads = pl.pallas_call(
        functools.partial(place_keys_kernel, count, halo),
        out_shape=[jax.ShapeDtypeStruct((rows, depth), f32)] * 2,
        in_specs=[whole] * (1 + count),
        out_specs=[whole] * 2,
        compiler_params=params,
    )(given, *key_slots)
    return grad_queries, key_grads, value_grads


def per_device(*args):
    if lax.axis_size("ctx") <= 4:
        return near_plan(*args)
    return ring_plan(*args)


def solution(mesh):
    return jax.shard_map(
        per_device,
        mesh=mesh,
        in_specs=(
            P("groups"),
            P(("groups", "ctx")),
            P(("groups", "ctx"), "head"),
            P(("groups", "ctx"), "head"),
            P(("groups", "ctx"), "head"),
            P(("groups", "ctx"), "head"),
            P(("groups", "ctx"), "head"),
        ),
        out_specs=(
            P(("groups", "ctx"), "head"),
            P(("groups", "ctx"), "head"),
            P(("groups", "ctx"), "head"),
        ),
        check_vma=False,
    )
```

```python
import functools
import math

import jax
import jax.numpy as jnp
from jax import lax
from jax.experimental import pallas as pl
from jax.experimental.pallas import tpu as pltpu
from jax.sharding import PartitionSpec as P

HEAD_WIDTH = 128
GROUP = 4


NEG = -1e30
BLOCK = 512


def shifted(value, axis, by):
    count = lax.axis_size(axis)
    return lax.ppermute(value, axis, [(i, (i + by) % count) for i in range(count)])


def document_of(positions, doc_lengths):
    ends = jnp.cumsum(doc_lengths)
    return jnp.sum((positions[:, None] >= ends[None, :]).astype(jnp.int32), axis=1)


def allowed_between(query_positions, query_docs, key_positions, key_docs):
    return (query_docs[:, None] == key_docs[None, :]) & (
        key_positions[None, :] <= query_positions[:, None]
    )


def head_rows(matrix, group_size, head_dim):
    row_count = matrix.shape[0]
    return matrix.reshape(row_count * group_size, head_dim)


def block_scores(query_flat, key_head, row_count, group_size, head_dim):
    scores = lax.dot_general(
        query_flat, key_head, (((1,), (1,)), ((), ())), preferred_element_type=jnp.float32
    )
    return (scores * (1.0 / math.sqrt(head_dim))).reshape(row_count, group_size, key_head.shape[0])


def update_stats(running, query_local, key_block, allowed, group_size, head_dim):
    running_max, totals = running
    row_count = query_local.shape[0]
    scores = block_scores(
        head_rows(query_local, group_size, head_dim), key_block, row_count, group_size, head_dim
    )
    masked = jnp.where(allowed[:, None, :], scores, NEG)
    new_max = jnp.maximum(running_max, jnp.max(masked, axis=2))
    weights = jnp.where(allowed[:, None, :], jnp.exp(masked - new_max[:, :, None]), 0.0)
    new_totals = [totals * jnp.exp(running_max - new_max) + jnp.sum(weights, axis=2)]
    new_maxima = [new_max]
    return (jnp.concatenate(new_maxima, axis=1), jnp.concatenate(new_totals, axis=1))


def backward_block(
    query_local,
    grad_local,
    log_norm,
    row_delta,
    key_block,
    value_block,
    allowed,
    group_size,
    head_dim,
):
    row_count = query_local.shape[0]
    query_flat = head_rows(query_local, group_size, head_dim)
    grad_flat = head_rows(grad_local, group_size, head_dim)
    scores = block_scores(query_flat, key_block, row_count, group_size, head_dim)
    masked = jnp.where(allowed[:, None, :], scores, NEG)
    weights = jnp.exp(masked - log_norm[:, 0:group_size, None])
    grad_weights = lax.dot_general(
        grad_flat, value_block, (((1,), (1,)), ((), ())), preferred_element_type=jnp.float32
    ).reshape(row_count, group_size, -1)
    grad_scores = weights * (grad_weights - row_delta[:, 0:group_size, None])
    rounded_weights = weights.astype(jnp.bfloat16).reshape(row_count * group_size, -1)
    rounded_grads = grad_scores.astype(jnp.bfloat16).reshape(row_count * group_size, -1)
    value_parts = [
        lax.dot_general(
            rounded_weights, grad_flat, (((0,), (0,)), ((), ())), preferred_element_type=jnp.float32
        )
    ]
    key_parts = [
        lax.dot_general(
            rounded_grads, query_flat, (((0,), (0,)), ((), ())), preferred_element_type=jnp.float32
        )
    ]
    query_parts = [
        jnp.dot(rounded_grads, key_block, preferred_element_type=jnp.float32).reshape(
            row_count, group_size * head_dim
        )
    ]
    return (
        jnp.concatenate(query_parts, axis=1),
        jnp.concatenate(key_parts, axis=1),
        jnp.concatenate(value_parts, axis=1),
    )


def ring_plan(doc_lengths, owners, queries, key_head_rows, value_head_rows, forward_out, grad_out):
    context_size = lax.axis_size("ctx")
    context_index = lax.axis_index("ctx")
    row_count = queries.shape[0]
    head_dim = HEAD_WIDTH
    group_size = GROUP
    query_heads = queries.shape[1] // head_dim
    slot_count = 2 * row_count // context_size
    everyone = lax.all_gather(owners, "ctx", axis=0, tiled=True)
    row_arrangement = jnp.argsort(everyone, stable=True)
    layout_docs = document_of(row_arrangement, doc_lengths)
    own_positions = lax.dynamic_slice_in_dim(
        row_arrangement, context_index * row_count, row_count, 0
    )
    own_documents = lax.dynamic_slice_in_dim(layout_docs, context_index * row_count, row_count, 0)
    owner_ids = jnp.arange(context_size, dtype=jnp.int32)
    owner_hot = (owners[:, None] == owner_ids[None, :]).astype(jnp.int32)
    earlier = jnp.cumsum(owner_hot, axis=0) - owner_hot
    rank_within = jnp.sum(earlier * owner_hot, axis=1)
    slot_rows = owners * slot_count + rank_within

    def packed(matrix):
        empty = jnp.zeros((context_size * slot_count,) + matrix.shape[1:], matrix.dtype)
        return empty.at[slot_rows].set(matrix)

    owner_grid = everyone.reshape(context_size, row_count)
    counts = jnp.sum((owner_grid == context_index).astype(jnp.int32), axis=1)
    count_ends = jnp.cumsum(counts)
    starts = count_ends - counts
    wanted = jnp.arange(row_count, dtype=jnp.int32)
    source = jnp.sum((wanted[:, None] >= count_ends[None, :]).astype(jnp.int32), axis=1)
    source_hot = (source[:, None] == owner_ids[None, :]).astype(jnp.int32)
    take_rows = source * slot_count + wanted - jnp.sum(source_hot * starts[None, :], axis=1)

    def compact(received):
        return jnp.take(received, take_rows, axis=0)

    local_delta = jnp.sum(
        (grad_out.astype(jnp.float32) * forward_out.astype(jnp.float32)).reshape(
            row_count, query_heads, head_dim
        ),
        axis=2,
    )
    arrived = (
        lax.all_to_all(packed(queries), "ctx", split_axis=0, concat_axis=0, tiled=True),
        lax.all_to_all(packed(key_head_rows), "ctx", split_axis=0, concat_axis=0, tiled=True),
        lax.all_to_all(packed(value_head_rows), "ctx", split_axis=0, concat_axis=0, tiled=True),
        lax.all_to_all(packed(grad_out), "ctx", split_axis=0, concat_axis=0, tiled=True),
    )
    query_local, key_local, value_local, grad_local = [compact(received) for received in arrived]
    row_delta = compact(
        lax.all_to_all(packed(local_delta), "ctx", split_axis=0, concat_axis=0, tiled=True)
    )

    def fold_keys(running, shard_rows, first_row):
        piece_count = shard_rows.shape[0]
        step_rows = math.gcd(piece_count, BLOCK) if piece_count > BLOCK else piece_count

        def one_block(partial_value, block_index):
            offset = first_row + block_index * step_rows
            key_block = lax.dynamic_slice_in_dim(shard_rows, block_index * step_rows, step_rows, 0)
            key_positions = lax.dynamic_slice_in_dim(row_arrangement, offset, step_rows, 0)
            key_docs = lax.dynamic_slice_in_dim(layout_docs, offset, step_rows, 0)
            allowed = allowed_between(own_positions, own_documents, key_positions, key_docs)
            return (
                update_stats(partial_value, query_local, key_block, allowed, group_size, head_dim),
                None,
            )

        if piece_count == step_rows:
            return one_block(running, 0)[0]
        return lax.scan(one_block, running, jnp.arange(piece_count // step_rows, dtype=jnp.int32))[
            0
        ]

    start_stats = (
        jnp.full((row_count, query_heads), NEG, jnp.float32),
        jnp.zeros((row_count, query_heads), jnp.float32),
    )
    top_scores, totals = fold_keys(
        start_stats, lax.all_gather(key_local, "ctx", axis=0, tiled=True), jnp.int32(0)
    )
    log_norm = top_scores + jnp.log(totals)

    def block_meta(owner_index, offset, size):
        first = owner_index * row_count + offset
        key_positions = lax.dynamic_slice_in_dim(row_arrangement, first, size, 0)
        key_docs = lax.dynamic_slice_in_dim(layout_docs, first, size, 0)
        return (key_positions, key_docs)

    query_zero = jnp.zeros(query_local.shape, jnp.float32)
    key_zero = jnp.zeros(key_local.shape, jnp.float32)

    def one_turn(turn_index, loop_state):
        key_moving, value_moving, key_grad, value_grad, query_grad = loop_state
        owner_index = (context_index - turn_index) % context_size
        key_positions, key_docs = block_meta(owner_index, 0, row_count)
        allowed = allowed_between(own_positions, own_documents, key_positions, key_docs)
        query_part, key_part, value_part = backward_block(
            query_local,
            grad_local,
            log_norm,
            row_delta,
            key_moving,
            value_moving,
            allowed,
            group_size,
            head_dim,
        )
        return (
            key_moving,
            value_moving,
            key_grad + key_part,
            value_grad + value_part,
            query_grad + query_part,
        )

    def moved_turn(turn_index, loop_state):
        key_moving, value_moving, key_grad, value_grad, query_grad = loop_state
        key_moving, value_moving = shifted((key_moving, value_moving), "ctx", 1)
        key_grad, value_grad = shifted((key_grad, value_grad), "ctx", 1)
        return one_turn(turn_index, (key_moving, value_moving, key_grad, value_grad, query_grad))

    loop_state = one_turn(0, (key_local, value_local, key_zero, key_zero, query_zero))
    loop_state = lax.fori_loop(1, context_size, moved_turn, loop_state)
    key_grad, value_grad = shifted((loop_state[2], loop_state[3]), "ctx", 1)
    query_grad = loop_state[4]
    inverse_root = 1.0 / math.sqrt(head_dim)
    return (query_grad * inverse_root, key_grad * inverse_root, value_grad)


META = 16


def contract(left, right, left_dim, right_dim, **kw):
    return lax.dot_general(
        left,
        right,
        (((left_dim,), (right_dim,)), ((), ())),
        preferred_element_type=jnp.float32,
        **kw,
    )


def one_hot(row_count, target):
    places = lax.broadcasted_iota(jnp.int32, (row_count, target.shape[1]), 0)
    return jnp.where(places == target, 1.0, 0.0).astype(jnp.bfloat16)


def side_by_side(stack, heads):
    rows = stack.shape[0] // heads
    return jnp.concatenate([stack[h * rows : (h + 1) * rows, :] for h in range(heads)], axis=1)


def end_to_end(matrix, heads):
    width = matrix.shape[1] // heads
    return jnp.concatenate([matrix[:, h * width : (h + 1) * width] for h in range(heads)], axis=0)


def runs_of(hot):
    count, rows = hot.shape
    counts = jnp.sum(hot, axis=1, keepdims=True)
    owner = jnp.zeros((1, rows), jnp.int32)
    earlier = jnp.zeros((1, rows), jnp.float32)
    for p in range(count):
        mine = hot[p : p + 1, :] > 0.0
        owner = jnp.where(mine, p, owner)
        for less in range(p):
            earlier = earlier + jnp.where(mine, counts[less : less + 1, :], 0.0)
    lane = lax.broadcasted_iota(jnp.int32, (1, rows), 1)
    return owner, counts, lane - earlier.astype(jnp.int32)


def own_kernel(
    count,
    docs,
    doc_ref,
    packet_ref,
    query_ref,
    grad_ref,
    saved_ref,
    query_out,
    grad_out,
    raised_out,
    change_out,
    row_out,
    spread_out,
):
    rows, width = query_ref.shape
    depth = packet_ref.shape[1]
    heads = width // depth
    slot = 2 * rows // count
    index = lax.axis_index("ctx")
    lane = lax.broadcasted_iota(jnp.int32, (1, rows), 1)
    position = index * rows + lane
    first = jnp.zeros((1, rows), jnp.int32)
    end = jnp.int32(0)
    for d in range(docs):
        end = end + doc_ref[d]
        first = jnp.where(end <= position, end, first)
    key_position = index * rows + lax.broadcasted_iota(jnp.int32, (rows, rows), 0)
    allowed = (key_position >= first) & (key_position <= position)
    allowed = jnp.concatenate([allowed] * heads, axis=1)

    queries = end_to_end(query_ref[...], heads)
    query_out[...] = queries
    scores = contract(packet_ref[0:rows, :], queries, 1, 1) * (1.0 / math.sqrt(depth))
    scores = jnp.where(allowed, scores, NEG)
    top = jnp.max(scores, axis=0, keepdims=True)
    raised = jnp.exp(scores - top)
    raised_out[...] = raised
    grads = end_to_end(grad_ref[...], heads)
    grad_out[...] = grads
    product = grads.astype(jnp.float32) * end_to_end(saved_ref[...], heads).astype(jnp.float32)
    delta = contract(
        jnp.ones((8, depth), jnp.float32), product, 1, 1, precision=lax.Precision.HIGHEST
    )[0:1, :]
    change_out[...] = contract(packet_ref[rows : 2 * rows, :], grads, 1, 1) - delta
    row_out[0:1, :] = delta
    row_out[1:2, :] = top
    row_out[2:3, :] = jnp.sum(raised, axis=0, keepdims=True)
    row_out[3:4, :] = jnp.concatenate([first.astype(jnp.float32)] * heads, axis=1)
    row_out[4:8, :] = jnp.zeros((4, width), jnp.float32)
    owner, counts, rank = runs_of(packet_ref[2 * rows : 2 * rows + count, :].astype(jnp.float32))
    ahead = lax.rem(owner - index + count, count)
    spread_out[...] = one_hot(count * slot, ahead * slot + rank)


def attend_kernel(count, halo, *refs):
    query_ref, grad_ref, raised_ref, change_ref, row_ref, spread_ref = refs[:6]
    own = refs[6]
    before = refs[7 : 7 + halo]
    outs = refs[7 + halo :]
    rows, columns = raised_ref.shape
    depth = query_ref.shape[1]
    heads = columns // rows
    slot = 2 * rows // count
    scale = 1.0 / math.sqrt(depth)
    index = lax.axis_index("ctx")
    delta, top, total = (row_ref[n : n + 1, :] for n in range(3))
    first = row_ref[3:4, :].astype(jnp.int32)
    queries = query_ref[...]
    grads = grad_ref[...]

    key_position = (index - halo) * rows + lax.broadcasted_iota(
        jnp.int32, (halo * rows, columns), 0
    )
    keys = jnp.concatenate([n[0:rows, :] for n in before], axis=0)
    values = jnp.concatenate([n[rows : 2 * rows, :] for n in before], axis=0)
    scores = jnp.where(key_position >= first, contract(keys, queries, 1, 1) * scale, NEG)
    new_top = jnp.maximum(top, jnp.max(scores, axis=0, keepdims=True))
    raised = jnp.exp(scores - new_top)
    shrink = jnp.exp(top - new_top)
    inverse = 1.0 / (total * shrink + jnp.sum(raised, axis=0, keepdims=True))
    weights = raised * inverse
    own_weights = raised_ref[...] * (shrink * inverse)
    changes = weights * (contract(values, grads, 1, 1) - delta)
    own_changes = own_weights * change_ref[...]
    weights = jnp.concatenate([weights, own_weights], axis=0).astype(jnp.bfloat16)
    changes = jnp.concatenate([changes, own_changes], axis=0).astype(jnp.bfloat16)
    keys = jnp.concatenate([keys, own[0:rows, :]], axis=0)
    query_grad = (contract(keys, changes, 0, 0) * scale).astype(jnp.bfloat16)
    value_parts = contract(weights, grads, 1, 0).astype(jnp.bfloat16)
    key_parts = (contract(changes, queries, 1, 0) * scale).astype(jnp.bfloat16)

    query_slots = contract(spread_ref[...], end_to_end(query_grad, heads), 1, 1)
    query_slots = query_slots.astype(jnp.bfloat16)
    filled = jnp.zeros((count, 1), jnp.float32)
    targets = []
    for block, ref in enumerate(before + (own,)):
        owner, counts, rank = runs_of(ref[2 * rows : 2 * rows + count, :].astype(jnp.float32))
        base = jnp.zeros((1, rows), jnp.float32)
        for p in range(count):
            base = base + jnp.where(owner == p, filled[p : p + 1, :], 0.0)
        target = lax.rem(owner - index + count, count) * rows + base.astype(jnp.int32) + rank
        inside = index - halo + block >= 0
        targets.append(jnp.where(inside, target, -1))
        filled = filled + jnp.where(inside, counts, 0.0)
    spread = one_hot(count * rows, jnp.concatenate(targets, axis=1))
    key_slots = contract(spread, key_parts, 1, 0).astype(jnp.bfloat16)
    value_slots = contract(spread, value_parts, 1, 0).astype(jnp.bfloat16)
    at = heads * slot
    for k in range(count):
        out = outs[k]
        for h in range(heads):
            out[h * slot : (h + 1) * slot, :] = query_slots[
                k * slot : (k + 1) * slot, h * depth : (h + 1) * depth
            ]
        out[at : at + rows, :] = key_slots[k * rows : (k + 1) * rows, :]
        out[at + rows :, :] = value_slots[k * rows : (k + 1) * rows, :]


def order_kernel(count, halo, _, *refs):
    packets = refs[:1] + refs[1 : 1 + halo][::-1]
    query_out, key_out = refs[1 + halo :]
    rows = query_out.shape[0]
    index = lax.axis_index("ctx")
    given = []
    for ref in packets:
        hot = ref[2 * rows : 2 * rows + count, :].astype(jnp.float32)
        counts = jnp.sum(hot, axis=1, keepdims=True)
        mine = jnp.zeros((1, 1), jnp.float32)
        for p in range(count):
            mine = jnp.where(index == p, counts[p : p + 1, :], mine)
        given.append(mine.astype(jnp.int32))
    if len(given) < count:
        given.append(rows - sum(given))
    source = [lax.rem(index - k + count, count) for k in range(count)]

    def placement(size, back, whole):
        lane = lax.broadcasted_iota(jnp.int32, (1, count * size), 1)
        target = jnp.full(lane.shape, -1, jnp.int32)
        for k in range(count):
            start = jnp.zeros((1, 1), jnp.int32)
            for other in range(count):
                start = start + jnp.where(source[other] < source[k] - back, given[other], 0)
            step = lane - k * size
            inside = (step >= 0) & (step < (size if whole else given[k]))
            target = jnp.where(inside, start + step, target)
        return one_hot(rows, target)

    query_out[...] = placement(2 * rows // count, 0, False)
    key_out[...] = placement(rows, halo, True)


def place_kernel(count, query_spread, key_spread, *refs):
    ins = refs[:count]
    query_out, key_out, value_out = refs[count:]
    rows, width = query_out.shape
    depth = key_out.shape[1]
    heads = width // depth
    slot = 2 * rows // count
    for h in range(heads):
        taken = jnp.concatenate([ref[h * slot : (h + 1) * slot, :] for ref in ins], axis=0)
        query_out[:, h * depth : (h + 1) * depth] = contract(query_spread[...], taken, 1, 0)
    for n, out in enumerate((key_out, value_out)):
        at = heads * slot + n * rows
        taken = jnp.concatenate([ref[at : at + rows, :] for ref in ins], axis=0)
        out[...] = contract(key_spread[...], taken, 1, 0)


def near_plan(doc_lengths, owners, queries, key_head_rows, value_head_rows, forward_out, grad_out):
    count = lax.axis_size("ctx")
    rows, width = queries.shape
    depth = key_head_rows.shape[1]
    heads = width // depth
    bf16, f32 = jnp.bfloat16, jnp.float32
    columns = heads * rows
    halo = count // 2
    slot = 2 * rows // count
    spread_shape = jax.ShapeDtypeStruct((count * slot, rows), bf16)
    whole = pl.BlockSpec(memory_space=pltpu.VMEM)
    params = pltpu.CompilerParams(vmem_limit_bytes=40 * 1024 * 1024)

    mark = lax.broadcasted_iota(jnp.int32, (2 * rows + META, rows), 0) - 2 * rows
    packet = jnp.where(
        mark < 0,
        jnp.pad(jnp.concatenate([key_head_rows, value_head_rows], axis=0), ((0, META), (0, 0))),
        (owners[None, :] == mark).astype(bf16),
    )
    near = [
        lax.ppermute(packet, "ctx", [(i, (i + back) % count) for i in range(count)])
        for back in range(halo, 0, -1)
    ]
    own = pl.pallas_call(
        functools.partial(own_kernel, count, doc_lengths.shape[0]),
        out_shape=[
            jax.ShapeDtypeStruct((columns, depth), bf16),
            jax.ShapeDtypeStruct((columns, depth), bf16),
            jax.ShapeDtypeStruct((rows, columns), f32),
            jax.ShapeDtypeStruct((rows, columns), f32),
            jax.ShapeDtypeStruct((8, columns), f32),
            spread_shape,
        ],
        in_specs=[pl.BlockSpec(memory_space=pltpu.SMEM)] + [whole] * 4,
        out_specs=[whole] * 6,
        compiler_params=params,
    )(doc_lengths, packet, queries, grad_out, forward_out)
    sent = pl.pallas_call(
        functools.partial(attend_kernel, count, halo),
        out_shape=[jax.ShapeDtypeStruct((heads * slot + 2 * rows, depth), bf16)] * count,
        in_specs=[whole] * (7 + halo),
        out_specs=[whole] * count,
        compiler_params=params,
    )(*own, packet, *near)
    received = [sent[0]] + [
        lax.ppermute(sent[k], "ctx", [(i, (i + k) % count) for i in range(count)])
        for k in range(1, count)
    ]
    spreads = pl.pallas_call(
        functools.partial(order_kernel, count, halo),
        out_shape=[
            jax.ShapeDtypeStruct((rows, count * slot), bf16),
            jax.ShapeDtypeStruct((rows, count * rows), bf16),
        ],
        in_specs=[pl.BlockSpec(memory_space=pl.ANY)] + [whole] * (1 + halo),
        out_specs=[whole] * 2,
        compiler_params=params,
    )(received[1], packet, *near)
    return pl.pallas_call(
        functools.partial(place_kernel, count),
        out_shape=[
            jax.ShapeDtypeStruct((rows, width), f32),
            jax.ShapeDtypeStruct((rows, depth), f32),
            jax.ShapeDtypeStruct((rows, depth), f32),
        ],
        in_specs=[whole] * (2 + count),
        out_specs=[whole] * 3,
        compiler_params=params,
    )(*spreads, *received)


def per_device(*args):
    if lax.axis_size("ctx") <= 4:
        return near_plan(*args)
    return ring_plan(*args)


def solution(mesh):
    return jax.shard_map(
        per_device,
        mesh=mesh,
        in_specs=(
            P("groups"),
            P(("groups", "ctx")),
            P(("groups", "ctx"), "head"),
            P(("groups", "ctx"), "head"),
            P(("groups", "ctx"), "head"),
            P(("groups", "ctx"), "head"),
            P(("groups", "ctx"), "head"),
        ),
        out_specs=(
            P(("groups", "ctx"), "head"),
            P(("groups", "ctx"), "head"),
            P(("groups", "ctx"), "head"),
        ),
        check_vma=False,
    )
```

```python
import functools
import math

import jax
import jax.numpy as jnp
from jax import lax
from jax.experimental import pallas as pl
from jax.experimental.pallas import tpu as pltpu
from jax.sharding import PartitionSpec as P

HEAD_WIDTH = 128
GROUP = 4


NEG = -1e30
BLOCK = 512


def shifted(value, axis, by):
    count = lax.axis_size(axis)
    return lax.ppermute(value, axis, [(i, (i + by) % count) for i in range(count)])


def document_of(positions, doc_lengths):
    ends = jnp.cumsum(doc_lengths)
    return jnp.sum((positions[:, None] >= ends[None, :]).astype(jnp.int32), axis=1)


def allowed_between(query_positions, query_docs, key_positions, key_docs):
    return (query_docs[:, None] == key_docs[None, :]) & (
        key_positions[None, :] <= query_positions[:, None]
    )


def head_rows(matrix, group_size, head_dim):
    row_count = matrix.shape[0]
    return matrix.reshape(row_count * group_size, head_dim)


def block_scores(query_flat, key_head, row_count, group_size, head_dim):
    scores = lax.dot_general(
        query_flat, key_head, (((1,), (1,)), ((), ())), preferred_element_type=jnp.float32
    )
    return (scores * (1.0 / math.sqrt(head_dim))).reshape(row_count, group_size, key_head.shape[0])


def update_stats(running, query_local, key_block, allowed, group_size, head_dim):
    running_max, totals = running
    row_count = query_local.shape[0]
    scores = block_scores(
        head_rows(query_local, group_size, head_dim), key_block, row_count, group_size, head_dim
    )
    masked = jnp.where(allowed[:, None, :], scores, NEG)
    new_max = jnp.maximum(running_max, jnp.max(masked, axis=2))
    weights = jnp.where(allowed[:, None, :], jnp.exp(masked - new_max[:, :, None]), 0.0)
    new_totals = [totals * jnp.exp(running_max - new_max) + jnp.sum(weights, axis=2)]
    new_maxima = [new_max]
    return (jnp.concatenate(new_maxima, axis=1), jnp.concatenate(new_totals, axis=1))


def backward_block(
    query_local,
    grad_local,
    log_norm,
    row_delta,
    key_block,
    value_block,
    allowed,
    group_size,
    head_dim,
):
    row_count = query_local.shape[0]
    query_flat = head_rows(query_local, group_size, head_dim)
    grad_flat = head_rows(grad_local, group_size, head_dim)
    scores = block_scores(query_flat, key_block, row_count, group_size, head_dim)
    masked = jnp.where(allowed[:, None, :], scores, NEG)
    weights = jnp.exp(masked - log_norm[:, 0:group_size, None])
    grad_weights = lax.dot_general(
        grad_flat, value_block, (((1,), (1,)), ((), ())), preferred_element_type=jnp.float32
    ).reshape(row_count, group_size, -1)
    grad_scores = weights * (grad_weights - row_delta[:, 0:group_size, None])
    rounded_weights = weights.astype(jnp.bfloat16).reshape(row_count * group_size, -1)
    rounded_grads = grad_scores.astype(jnp.bfloat16).reshape(row_count * group_size, -1)
    value_parts = [
        lax.dot_general(
            rounded_weights, grad_flat, (((0,), (0,)), ((), ())), preferred_element_type=jnp.float32
        )
    ]
    key_parts = [
        lax.dot_general(
            rounded_grads, query_flat, (((0,), (0,)), ((), ())), preferred_element_type=jnp.float32
        )
    ]
    query_parts = [
        jnp.dot(rounded_grads, key_block, preferred_element_type=jnp.float32).reshape(
            row_count, group_size * head_dim
        )
    ]
    return (
        jnp.concatenate(query_parts, axis=1),
        jnp.concatenate(key_parts, axis=1),
        jnp.concatenate(value_parts, axis=1),
    )


def ring_plan(doc_lengths, owners, queries, key_head_rows, value_head_rows, forward_out, grad_out):
    context_size = lax.axis_size("ctx")
    context_index = lax.axis_index("ctx")
    row_count = queries.shape[0]
    head_dim = HEAD_WIDTH
    group_size = GROUP
    query_heads = queries.shape[1] // head_dim
    slot_count = 2 * row_count // context_size
    everyone = lax.all_gather(owners, "ctx", axis=0, tiled=True)
    row_arrangement = jnp.argsort(everyone, stable=True)
    layout_docs = document_of(row_arrangement, doc_lengths)
    own_positions = lax.dynamic_slice_in_dim(
        row_arrangement, context_index * row_count, row_count, 0
    )
    own_documents = lax.dynamic_slice_in_dim(layout_docs, context_index * row_count, row_count, 0)
    owner_ids = jnp.arange(context_size, dtype=jnp.int32)
    owner_hot = (owners[:, None] == owner_ids[None, :]).astype(jnp.int32)
    earlier = jnp.cumsum(owner_hot, axis=0) - owner_hot
    rank_within = jnp.sum(earlier * owner_hot, axis=1)
    slot_rows = owners * slot_count + rank_within

    def packed(matrix):
        empty = jnp.zeros((context_size * slot_count,) + matrix.shape[1:], matrix.dtype)
        return empty.at[slot_rows].set(matrix)

    owner_grid = everyone.reshape(context_size, row_count)
    counts = jnp.sum((owner_grid == context_index).astype(jnp.int32), axis=1)
    count_ends = jnp.cumsum(counts)
    starts = count_ends - counts
    wanted = jnp.arange(row_count, dtype=jnp.int32)
    source = jnp.sum((wanted[:, None] >= count_ends[None, :]).astype(jnp.int32), axis=1)
    source_hot = (source[:, None] == owner_ids[None, :]).astype(jnp.int32)
    take_rows = source * slot_count + wanted - jnp.sum(source_hot * starts[None, :], axis=1)

    def compact(received):
        return jnp.take(received, take_rows, axis=0)

    local_delta = jnp.sum(
        (grad_out.astype(jnp.float32) * forward_out.astype(jnp.float32)).reshape(
            row_count, query_heads, head_dim
        ),
        axis=2,
    )
    arrived = (
        lax.all_to_all(packed(queries), "ctx", split_axis=0, concat_axis=0, tiled=True),
        lax.all_to_all(packed(key_head_rows), "ctx", split_axis=0, concat_axis=0, tiled=True),
        lax.all_to_all(packed(value_head_rows), "ctx", split_axis=0, concat_axis=0, tiled=True),
        lax.all_to_all(packed(grad_out), "ctx", split_axis=0, concat_axis=0, tiled=True),
    )
    query_local, key_local, value_local, grad_local = [compact(received) for received in arrived]
    row_delta = compact(
        lax.all_to_all(packed(local_delta), "ctx", split_axis=0, concat_axis=0, tiled=True)
    )

    def fold_keys(running, shard_rows, first_row):
        piece_count = shard_rows.shape[0]
        step_rows = math.gcd(piece_count, BLOCK) if piece_count > BLOCK else piece_count

        def one_block(partial_value, block_index):
            offset = first_row + block_index * step_rows
            key_block = lax.dynamic_slice_in_dim(shard_rows, block_index * step_rows, step_rows, 0)
            key_positions = lax.dynamic_slice_in_dim(row_arrangement, offset, step_rows, 0)
            key_docs = lax.dynamic_slice_in_dim(layout_docs, offset, step_rows, 0)
            allowed = allowed_between(own_positions, own_documents, key_positions, key_docs)
            return (
                update_stats(partial_value, query_local, key_block, allowed, group_size, head_dim),
                None,
            )

        if piece_count == step_rows:
            return one_block(running, 0)[0]
        return lax.scan(one_block, running, jnp.arange(piece_count // step_rows, dtype=jnp.int32))[
            0
        ]

    start_stats = (
        jnp.full((row_count, query_heads), NEG, jnp.float32),
        jnp.zeros((row_count, query_heads), jnp.float32),
    )
    top_scores, totals = fold_keys(
        start_stats, lax.all_gather(key_local, "ctx", axis=0, tiled=True), jnp.int32(0)
    )
    log_norm = top_scores + jnp.log(totals)

    def block_meta(owner_index, offset, size):
        first = owner_index * row_count + offset
        key_positions = lax.dynamic_slice_in_dim(row_arrangement, first, size, 0)
        key_docs = lax.dynamic_slice_in_dim(layout_docs, first, size, 0)
        return (key_positions, key_docs)

    query_zero = jnp.zeros(query_local.shape, jnp.float32)
    key_zero = jnp.zeros(key_local.shape, jnp.float32)

    def one_turn(turn_index, loop_state):
        key_moving, value_moving, key_grad, value_grad, query_grad = loop_state
        owner_index = (context_index - turn_index) % context_size
        key_positions, key_docs = block_meta(owner_index, 0, row_count)
        allowed = allowed_between(own_positions, own_documents, key_positions, key_docs)
        query_part, key_part, value_part = backward_block(
            query_local,
            grad_local,
            log_norm,
            row_delta,
            key_moving,
            value_moving,
            allowed,
            group_size,
            head_dim,
        )
        return (
            key_moving,
            value_moving,
            key_grad + key_part,
            value_grad + value_part,
            query_grad + query_part,
        )

    def moved_turn(turn_index, loop_state):
        key_moving, value_moving, key_grad, value_grad, query_grad = loop_state
        key_moving, value_moving = shifted((key_moving, value_moving), "ctx", 1)
        key_grad, value_grad = shifted((key_grad, value_grad), "ctx", 1)
        return one_turn(turn_index, (key_moving, value_moving, key_grad, value_grad, query_grad))

    loop_state = one_turn(0, (key_local, value_local, key_zero, key_zero, query_zero))
    loop_state = lax.fori_loop(1, context_size, moved_turn, loop_state)
    key_grad, value_grad = shifted((loop_state[2], loop_state[3]), "ctx", 1)
    query_grad = loop_state[4]
    inverse_root = 1.0 / math.sqrt(head_dim)
    return (query_grad * inverse_root, key_grad * inverse_root, value_grad)


META = 16


def contract(left, right, left_dim, right_dim, **kw):
    return lax.dot_general(
        left,
        right,
        (((left_dim,), (right_dim,)), ((), ())),
        preferred_element_type=jnp.float32,
        **kw,
    )


def one_hot(row_count, target):
    places = lax.broadcasted_iota(jnp.int32, (row_count, target.shape[1]), 0)
    return jnp.where(places == target, 1.0, 0.0).astype(jnp.bfloat16)


def side_by_side(stack, heads):
    rows = stack.shape[0] // heads
    return jnp.concatenate([stack[h * rows : (h + 1) * rows, :] for h in range(heads)], axis=1)


def end_to_end(matrix, heads):
    width = matrix.shape[1] // heads
    return jnp.concatenate([matrix[:, h * width : (h + 1) * width] for h in range(heads)], axis=0)


def runs_of(hot):
    count, rows = hot.shape
    counts = jnp.sum(hot, axis=1, keepdims=True)
    owner = jnp.zeros((1, rows), jnp.int32)
    earlier = jnp.zeros((1, rows), jnp.float32)
    for p in range(count):
        mine = hot[p : p + 1, :] > 0.0
        owner = jnp.where(mine, p, owner)
        for less in range(p):
            earlier = earlier + jnp.where(mine, counts[less : less + 1, :], 0.0)
    lane = lax.broadcasted_iota(jnp.int32, (1, rows), 1)
    return owner, counts, lane - earlier.astype(jnp.int32)


def own_kernel(
    count,
    docs,
    doc_ref,
    packet_ref,
    query_ref,
    grad_ref,
    saved_ref,
    query_out,
    grad_out,
    raised_out,
    change_out,
    row_out,
    spread_out,
):
    rows, width = query_ref.shape
    depth = packet_ref.shape[1]
    heads = width // depth
    slot = 2 * rows // count
    index = lax.axis_index("ctx")
    lane = lax.broadcasted_iota(jnp.int32, (1, rows), 1)
    position = index * rows + lane
    first = jnp.zeros((1, rows), jnp.int32)
    end = jnp.int32(0)
    for d in range(docs):
        end = end + doc_ref[d]
        first = jnp.where(end <= position, end, first)
    key_position = index * rows + lax.broadcasted_iota(jnp.int32, (rows, rows), 0)
    allowed = (key_position >= first) & (key_position <= position)
    allowed = jnp.concatenate([allowed] * heads, axis=1)

    queries = end_to_end(query_ref[...], heads)
    query_out[...] = queries
    scores = contract(packet_ref[0:rows, :], queries, 1, 1) * (1.0 / math.sqrt(depth))
    scores = jnp.where(allowed, scores, NEG)
    top = jnp.max(scores, axis=0, keepdims=True)
    raised = jnp.exp(scores - top)
    raised_out[...] = raised
    grads = end_to_end(grad_ref[...], heads)
    grad_out[...] = grads
    product = grads.astype(jnp.float32) * end_to_end(saved_ref[...], heads).astype(jnp.float32)
    delta = contract(
        jnp.ones((8, depth), jnp.float32), product, 1, 1, precision=lax.Precision.HIGHEST
    )[0:1, :]
    change_out[...] = contract(packet_ref[rows : 2 * rows, :], grads, 1, 1) - delta
    row_out[0:1, :] = delta
    row_out[1:2, :] = top
    row_out[2:3, :] = jnp.sum(raised, axis=0, keepdims=True)
    row_out[3:4, :] = jnp.concatenate([first.astype(jnp.float32)] * heads, axis=1)
    row_out[4:8, :] = jnp.zeros((4, width), jnp.float32)
    owner, counts, rank = runs_of(packet_ref[2 * rows : 2 * rows + count, :].astype(jnp.float32))
    spread_out[...] = one_hot(count * slot, (owner ^ index) * slot + rank)


def attend_kernel(count, halo, *refs):
    query_ref, grad_ref, raised_ref, change_ref, row_ref, spread_ref = refs[:6]
    own = refs[6]
    before = refs[7 : 7 + halo]
    outs = refs[7 + halo :]
    rows, columns = raised_ref.shape
    depth = query_ref.shape[1]
    heads = columns // rows
    slot = 2 * rows // count
    scale = 1.0 / math.sqrt(depth)
    index = lax.axis_index("ctx")
    delta, top, total = (row_ref[n : n + 1, :] for n in range(3))
    first = row_ref[3:4, :].astype(jnp.int32)
    queries = query_ref[...]
    grads = grad_ref[...]

    key_position = (index - halo) * rows + lax.broadcasted_iota(
        jnp.int32, (halo * rows, columns), 0
    )
    keys = jnp.concatenate([n[0:rows, :] for n in before], axis=0)
    values = jnp.concatenate([n[rows : 2 * rows, :] for n in before], axis=0)
    scores = jnp.where(key_position >= first, contract(keys, queries, 1, 1) * scale, NEG)
    new_top = jnp.maximum(top, jnp.max(scores, axis=0, keepdims=True))
    raised = jnp.exp(scores - new_top)
    shrink = jnp.exp(top - new_top)
    inverse = 1.0 / (total * shrink + jnp.sum(raised, axis=0, keepdims=True))
    weights = raised * inverse
    own_weights = raised_ref[...] * (shrink * inverse)
    changes = weights * (contract(values, grads, 1, 1) - delta)
    own_changes = own_weights * change_ref[...]
    weights = jnp.concatenate([weights, own_weights], axis=0).astype(jnp.bfloat16)
    changes = jnp.concatenate([changes, own_changes], axis=0).astype(jnp.bfloat16)
    keys = jnp.concatenate([keys, own[0:rows, :]], axis=0)
    query_grad = (contract(keys, changes, 0, 0) * scale).astype(jnp.bfloat16)
    value_parts = contract(weights, grads, 1, 0).astype(jnp.bfloat16)
    key_parts = (contract(changes, queries, 1, 0) * scale).astype(jnp.bfloat16)

    query_slots = contract(spread_ref[...], end_to_end(query_grad, heads), 1, 1)
    query_slots = query_slots.astype(jnp.bfloat16)
    filled = jnp.zeros((count, 1), jnp.float32)
    targets = []
    for block, ref in enumerate(before + (own,)):
        owner, counts, rank = runs_of(ref[2 * rows : 2 * rows + count, :].astype(jnp.float32))
        base = jnp.zeros((1, rows), jnp.float32)
        for p in range(count):
            base = base + jnp.where(owner == p, filled[p : p + 1, :], 0.0)
        target = (owner ^ index) * rows + base.astype(jnp.int32) + rank
        inside = index - halo + block >= 0
        targets.append(jnp.where(inside, target, -1))
        filled = filled + jnp.where(inside, counts, 0.0)
    spread = one_hot(count * rows, jnp.concatenate(targets, axis=1))
    key_slots = contract(spread, key_parts, 1, 0).astype(jnp.bfloat16)
    value_slots = contract(spread, value_parts, 1, 0).astype(jnp.bfloat16)
    at = heads * slot
    for k in range(count):
        out = outs[k]
        for h in range(heads):
            out[h * slot : (h + 1) * slot, :] = query_slots[
                k * slot : (k + 1) * slot, h * depth : (h + 1) * depth
            ]
        out[at : at + rows, :] = key_slots[k * rows : (k + 1) * rows, :]
        out[at + rows :, :] = value_slots[k * rows : (k + 1) * rows, :]


def order_kernel(count, halo, _, *refs):
    packets = refs[:1] + refs[1 : 1 + halo][::-1]
    query_out, key_out = refs[1 + halo :]
    rows = query_out.shape[0]
    index = lax.axis_index("ctx")
    given = []
    for ref in packets:
        hot = ref[2 * rows : 2 * rows + count, :].astype(jnp.float32)
        counts = jnp.sum(hot, axis=1, keepdims=True)
        mine = jnp.zeros((1, 1), jnp.float32)
        for p in range(count):
            mine = jnp.where(index == p, counts[p : p + 1, :], mine)
        given.append(mine.astype(jnp.int32))
    if len(given) < count:
        given.append(rows - sum(given))
    giver = [lax.rem(index - d + count, count) for d in range(count)]

    def placement(size, back, whole):
        lane = lax.broadcasted_iota(jnp.int32, (1, count * size), 1)
        target = jnp.full(lane.shape, -1, jnp.int32)
        for k in range(count):
            start = jnp.zeros((1, 1), jnp.int32)
            limit = jnp.full((1, 1), size, jnp.int32)
            for d in range(count):
                start = start + jnp.where(giver[d] < (index ^ k) - back, given[d], 0)
                if not whole:
                    limit = jnp.where(giver[d] == (index ^ k), given[d], limit)
            step = lane - k * size
            target = jnp.where((step >= 0) & (step < limit), start + step, target)
        return one_hot(rows, target)

    query_out[...] = placement(2 * rows // count, 0, False)
    key_out[...] = placement(rows, halo, True)


def place_kernel(count, query_spread, key_spread, *refs):
    ins = refs[:count]
    query_out, key_out, value_out = refs[count : count + 3]
    query_here, key_here, value_here, sems = refs[count + 3 :]
    rows, width = query_here.shape
    depth = key_here.shape[1]
    heads = width // depth
    slot = 2 * rows // count
    copies = []

    def leave(here, out):
        copies.append(pltpu.make_async_copy(here, out, sems.at[len(copies)]))
        copies[-1].start()

    for h in range(heads):
        at = slice(h * depth, (h + 1) * depth)
        taken = jnp.concatenate([ref[h * slot : (h + 1) * slot, :] for ref in ins], axis=0)
        query_here[:, at] = contract(query_spread[...], taken, 1, 0)
        leave(query_here.at[:, at], query_out.at[:, at])
    for n, (here, out) in enumerate(((key_here, key_out), (value_here, value_out))):
        at = heads * slot + n * rows
        taken = jnp.concatenate([ref[at : at + rows, :] for ref in ins], axis=0)
        here[...] = contract(key_spread[...], taken, 1, 0)
        leave(here, out)
    for copy in copies:
        copy.wait()


def near_plan(doc_lengths, owners, queries, key_head_rows, value_head_rows, forward_out, grad_out):
    count = lax.axis_size("ctx")
    rows, width = queries.shape
    depth = key_head_rows.shape[1]
    heads = width // depth
    bf16, f32 = jnp.bfloat16, jnp.float32
    columns = heads * rows
    halo = count // 2
    slot = 2 * rows // count
    spread_shape = jax.ShapeDtypeStruct((count * slot, rows), bf16)
    whole = pl.BlockSpec(memory_space=pltpu.VMEM)
    params = pltpu.CompilerParams(vmem_limit_bytes=40 * 1024 * 1024)

    mark = lax.broadcasted_iota(jnp.int32, (2 * rows + META, rows), 0) - 2 * rows
    packet = jnp.where(
        mark < 0,
        jnp.pad(jnp.concatenate([key_head_rows, value_head_rows], axis=0), ((0, META), (0, 0))),
        (owners[None, :] == mark).astype(bf16),
    )
    near = [
        lax.ppermute(packet, "ctx", [(i, (i + back) % count) for i in range(count)])
        for back in range(halo, 0, -1)
    ]
    own = pl.pallas_call(
        functools.partial(own_kernel, count, doc_lengths.shape[0]),
        out_shape=[
            jax.ShapeDtypeStruct((columns, depth), bf16),
            jax.ShapeDtypeStruct((columns, depth), bf16),
            jax.ShapeDtypeStruct((rows, columns), f32),
            jax.ShapeDtypeStruct((rows, columns), f32),
            jax.ShapeDtypeStruct((8, columns), f32),
            spread_shape,
        ],
        in_specs=[pl.BlockSpec(memory_space=pltpu.SMEM)] + [whole] * 4,
        out_specs=[whole] * 6,
        compiler_params=params,
    )(doc_lengths, packet, queries, grad_out, forward_out)
    sent = pl.pallas_call(
        functools.partial(attend_kernel, count, halo),
        out_shape=[jax.ShapeDtypeStruct((heads * slot + 2 * rows, depth), bf16)] * count,
        in_specs=[whole] * (7 + halo),
        out_specs=[whole] * count,
        compiler_params=params,
    )(*own, packet, *near)
    received = [sent[0]] + [
        lax.ppermute(sent[k], "ctx", [(i, i ^ k) for i in range(count)]) for k in range(1, count)
    ]
    spreads = pl.pallas_call(
        functools.partial(order_kernel, count, halo),
        out_shape=[
            jax.ShapeDtypeStruct((rows, count * slot), bf16),
            jax.ShapeDtypeStruct((rows, count * rows), bf16),
        ],
        in_specs=[pl.BlockSpec(memory_space=pl.ANY)] + [whole] * (1 + halo),
        out_specs=[whole] * 2,
        compiler_params=params,
    )(received[-1], packet, *near)
    return pl.pallas_call(
        functools.partial(place_kernel, count),
        out_shape=[
            jax.ShapeDtypeStruct((rows, width), f32),
            jax.ShapeDtypeStruct((rows, depth), f32),
            jax.ShapeDtypeStruct((rows, depth), f32),
        ],
        in_specs=[whole] * (2 + count),
        out_specs=[pl.BlockSpec(memory_space=pl.ANY)] * 3,
        scratch_shapes=[
            pltpu.VMEM((rows, width), f32),
            pltpu.VMEM((rows, depth), f32),
            pltpu.VMEM((rows, depth), f32),
            pltpu.SemaphoreType.DMA((heads + 2,)),
        ],
        compiler_params=params,
    )(*spreads, *received)


def per_device(*args):
    if lax.axis_size("ctx") in (2, 4):
        return near_plan(*args)
    return ring_plan(*args)


def solution(mesh):
    return jax.shard_map(
        per_device,
        mesh=mesh,
        in_specs=(
            P("groups"),
            P(("groups", "ctx")),
            P(("groups", "ctx"), "head"),
            P(("groups", "ctx"), "head"),
            P(("groups", "ctx"), "head"),
            P(("groups", "ctx"), "head"),
            P(("groups", "ctx"), "head"),
        ),
        out_specs=(
            P(("groups", "ctx"), "head"),
            P(("groups", "ctx"), "head"),
            P(("groups", "ctx"), "head"),
        ),
        check_vma=False,
    )
```

```python
import functools
import math

import jax
import jax.numpy as jnp
from jax import lax
from jax.experimental import pallas as pl
from jax.experimental.pallas import tpu as pltpu
from jax.sharding import PartitionSpec as P

HEAD_WIDTH = 128
GROUP = 4


NEG = -1e30
BLOCK = 512


def shifted(value, axis, by):
    count = lax.axis_size(axis)
    return lax.ppermute(value, axis, [(i, (i + by) % count) for i in range(count)])


def document_of(positions, doc_lengths):
    ends = jnp.cumsum(doc_lengths)
    return jnp.sum((positions[:, None] >= ends[None, :]).astype(jnp.int32), axis=1)


def allowed_between(query_positions, query_docs, key_positions, key_docs):
    return (query_docs[:, None] == key_docs[None, :]) & (
        key_positions[None, :] <= query_positions[:, None]
    )


def head_rows(matrix, group_size, head_dim):
    row_count = matrix.shape[0]
    return matrix.reshape(row_count * group_size, head_dim)


def block_scores(query_flat, key_head, row_count, group_size, head_dim):
    scores = lax.dot_general(
        query_flat, key_head, (((1,), (1,)), ((), ())), preferred_element_type=jnp.float32
    )
    return (scores * (1.0 / math.sqrt(head_dim))).reshape(row_count, group_size, key_head.shape[0])


def update_stats(running, query_local, key_block, allowed, group_size, head_dim):
    running_max, totals = running
    row_count = query_local.shape[0]
    scores = block_scores(
        head_rows(query_local, group_size, head_dim), key_block, row_count, group_size, head_dim
    )
    masked = jnp.where(allowed[:, None, :], scores, NEG)
    new_max = jnp.maximum(running_max, jnp.max(masked, axis=2))
    weights = jnp.where(allowed[:, None, :], jnp.exp(masked - new_max[:, :, None]), 0.0)
    new_totals = [totals * jnp.exp(running_max - new_max) + jnp.sum(weights, axis=2)]
    new_maxima = [new_max]
    return (jnp.concatenate(new_maxima, axis=1), jnp.concatenate(new_totals, axis=1))


def backward_block(
    query_local,
    grad_local,
    log_norm,
    row_delta,
    key_block,
    value_block,
    allowed,
    group_size,
    head_dim,
):
    row_count = query_local.shape[0]
    query_flat = head_rows(query_local, group_size, head_dim)
    grad_flat = head_rows(grad_local, group_size, head_dim)
    scores = block_scores(query_flat, key_block, row_count, group_size, head_dim)
    masked = jnp.where(allowed[:, None, :], scores, NEG)
    weights = jnp.exp(masked - log_norm[:, 0:group_size, None])
    grad_weights = lax.dot_general(
        grad_flat, value_block, (((1,), (1,)), ((), ())), preferred_element_type=jnp.float32
    ).reshape(row_count, group_size, -1)
    grad_scores = weights * (grad_weights - row_delta[:, 0:group_size, None])
    rounded_weights = weights.astype(jnp.bfloat16).reshape(row_count * group_size, -1)
    rounded_grads = grad_scores.astype(jnp.bfloat16).reshape(row_count * group_size, -1)
    value_parts = [
        lax.dot_general(
            rounded_weights, grad_flat, (((0,), (0,)), ((), ())), preferred_element_type=jnp.float32
        )
    ]
    key_parts = [
        lax.dot_general(
            rounded_grads, query_flat, (((0,), (0,)), ((), ())), preferred_element_type=jnp.float32
        )
    ]
    query_parts = [
        jnp.dot(rounded_grads, key_block, preferred_element_type=jnp.float32).reshape(
            row_count, group_size * head_dim
        )
    ]
    return (
        jnp.concatenate(query_parts, axis=1),
        jnp.concatenate(key_parts, axis=1),
        jnp.concatenate(value_parts, axis=1),
    )


def ring_plan(doc_lengths, owners, queries, key_head_rows, value_head_rows, forward_out, grad_out):
    context_size = lax.axis_size("ctx")
    context_index = lax.axis_index("ctx")
    row_count = queries.shape[0]
    head_dim = HEAD_WIDTH
    group_size = GROUP
    query_heads = queries.shape[1] // head_dim
    slot_count = 2 * row_count // context_size
    everyone = lax.all_gather(owners, "ctx", axis=0, tiled=True)
    row_arrangement = jnp.argsort(everyone, stable=True)
    layout_docs = document_of(row_arrangement, doc_lengths)
    own_positions = lax.dynamic_slice_in_dim(
        row_arrangement, context_index * row_count, row_count, 0
    )
    own_documents = lax.dynamic_slice_in_dim(layout_docs, context_index * row_count, row_count, 0)
    owner_ids = jnp.arange(context_size, dtype=jnp.int32)
    owner_hot = (owners[:, None] == owner_ids[None, :]).astype(jnp.int32)
    earlier = jnp.cumsum(owner_hot, axis=0) - owner_hot
    rank_within = jnp.sum(earlier * owner_hot, axis=1)
    slot_rows = owners * slot_count + rank_within

    def packed(matrix):
        empty = jnp.zeros((context_size * slot_count,) + matrix.shape[1:], matrix.dtype)
        return empty.at[slot_rows].set(matrix)

    owner_grid = everyone.reshape(context_size, row_count)
    counts = jnp.sum((owner_grid == context_index).astype(jnp.int32), axis=1)
    count_ends = jnp.cumsum(counts)
    starts = count_ends - counts
    wanted = jnp.arange(row_count, dtype=jnp.int32)
    source = jnp.sum((wanted[:, None] >= count_ends[None, :]).astype(jnp.int32), axis=1)
    source_hot = (source[:, None] == owner_ids[None, :]).astype(jnp.int32)
    take_rows = source * slot_count + wanted - jnp.sum(source_hot * starts[None, :], axis=1)

    def compact(received):
        return jnp.take(received, take_rows, axis=0)

    local_delta = jnp.sum(
        (grad_out.astype(jnp.float32) * forward_out.astype(jnp.float32)).reshape(
            row_count, query_heads, head_dim
        ),
        axis=2,
    )
    arrived = (
        lax.all_to_all(packed(queries), "ctx", split_axis=0, concat_axis=0, tiled=True),
        lax.all_to_all(packed(key_head_rows), "ctx", split_axis=0, concat_axis=0, tiled=True),
        lax.all_to_all(packed(value_head_rows), "ctx", split_axis=0, concat_axis=0, tiled=True),
        lax.all_to_all(packed(grad_out), "ctx", split_axis=0, concat_axis=0, tiled=True),
    )
    query_local, key_local, value_local, grad_local = [compact(received) for received in arrived]
    row_delta = compact(
        lax.all_to_all(packed(local_delta), "ctx", split_axis=0, concat_axis=0, tiled=True)
    )

    def fold_keys(running, shard_rows, first_row):
        piece_count = shard_rows.shape[0]
        step_rows = math.gcd(piece_count, BLOCK) if piece_count > BLOCK else piece_count

        def one_block(partial_value, block_index):
            offset = first_row + block_index * step_rows
            key_block = lax.dynamic_slice_in_dim(shard_rows, block_index * step_rows, step_rows, 0)
            key_positions = lax.dynamic_slice_in_dim(row_arrangement, offset, step_rows, 0)
            key_docs = lax.dynamic_slice_in_dim(layout_docs, offset, step_rows, 0)
            allowed = allowed_between(own_positions, own_documents, key_positions, key_docs)
            return (
                update_stats(partial_value, query_local, key_block, allowed, group_size, head_dim),
                None,
            )

        if piece_count == step_rows:
            return one_block(running, 0)[0]
        return lax.scan(one_block, running, jnp.arange(piece_count // step_rows, dtype=jnp.int32))[
            0
        ]

    start_stats = (
        jnp.full((row_count, query_heads), NEG, jnp.float32),
        jnp.zeros((row_count, query_heads), jnp.float32),
    )
    top_scores, totals = fold_keys(
        start_stats, lax.all_gather(key_local, "ctx", axis=0, tiled=True), jnp.int32(0)
    )
    log_norm = top_scores + jnp.log(totals)

    def block_meta(owner_index, offset, size):
        first = owner_index * row_count + offset
        key_positions = lax.dynamic_slice_in_dim(row_arrangement, first, size, 0)
        key_docs = lax.dynamic_slice_in_dim(layout_docs, first, size, 0)
        return (key_positions, key_docs)

    query_zero = jnp.zeros(query_local.shape, jnp.float32)
    key_zero = jnp.zeros(key_local.shape, jnp.float32)

    def one_turn(turn_index, loop_state):
        key_moving, value_moving, key_grad, value_grad, query_grad = loop_state
        owner_index = (context_index - turn_index) % context_size
        key_positions, key_docs = block_meta(owner_index, 0, row_count)
        allowed = allowed_between(own_positions, own_documents, key_positions, key_docs)
        query_part, key_part, value_part = backward_block(
            query_local,
            grad_local,
            log_norm,
            row_delta,
            key_moving,
            value_moving,
            allowed,
            group_size,
            head_dim,
        )
        return (
            key_moving,
            value_moving,
            key_grad + key_part,
            value_grad + value_part,
            query_grad + query_part,
        )

    def moved_turn(turn_index, loop_state):
        key_moving, value_moving, key_grad, value_grad, query_grad = loop_state
        key_moving, value_moving = shifted((key_moving, value_moving), "ctx", 1)
        key_grad, value_grad = shifted((key_grad, value_grad), "ctx", 1)
        return one_turn(turn_index, (key_moving, value_moving, key_grad, value_grad, query_grad))

    loop_state = one_turn(0, (key_local, value_local, key_zero, key_zero, query_zero))
    loop_state = lax.fori_loop(1, context_size, moved_turn, loop_state)
    key_grad, value_grad = shifted((loop_state[2], loop_state[3]), "ctx", 1)
    query_grad = loop_state[4]
    inverse_root = 1.0 / math.sqrt(head_dim)
    return (query_grad * inverse_root, key_grad * inverse_root, value_grad)


META = 16


def contract(left, right, left_dim, right_dim, **kw):
    return lax.dot_general(
        left,
        right,
        (((left_dim,), (right_dim,)), ((), ())),
        preferred_element_type=jnp.float32,
        **kw,
    )


def one_hot(row_count, target):
    places = lax.broadcasted_iota(jnp.int32, (row_count, target.shape[1]), 0)
    return jnp.where(places == target, 1.0, 0.0).astype(jnp.bfloat16)


def side_by_side(stack, heads):
    rows = stack.shape[0] // heads
    return jnp.concatenate([stack[h * rows : (h + 1) * rows, :] for h in range(heads)], axis=1)


def end_to_end(matrix, heads):
    width = matrix.shape[1] // heads
    return jnp.concatenate([matrix[:, h * width : (h + 1) * width] for h in range(heads)], axis=0)


def runs_of(hot):
    count, rows = hot.shape
    counts = jnp.sum(hot, axis=1, keepdims=True)
    owner = jnp.zeros((1, rows), jnp.int32)
    earlier = jnp.zeros((1, rows), jnp.float32)
    for p in range(count):
        mine = hot[p : p + 1, :] > 0.0
        owner = jnp.where(mine, p, owner)
        for less in range(p):
            earlier = earlier + jnp.where(mine, counts[less : less + 1, :], 0.0)
    lane = lax.broadcasted_iota(jnp.int32, (1, rows), 1)
    return owner, counts, lane - earlier.astype(jnp.int32)


def own_kernel(
    count,
    docs,
    doc_ref,
    packet_ref,
    query_ref,
    grad_ref,
    saved_ref,
    query_out,
    grad_out,
    raised_out,
    change_out,
    row_out,
    spread_out,
    target_out,
    filled_out,
):
    rows, width = query_ref.shape
    depth = packet_ref.shape[1]
    heads = width // depth
    slot = 2 * rows // count
    index = lax.axis_index("ctx")
    lane = lax.broadcasted_iota(jnp.int32, (1, rows), 1)
    position = index * rows + lane
    first = jnp.zeros((1, rows), jnp.int32)
    end = jnp.int32(0)
    for d in range(docs):
        end = end + doc_ref[d]
        first = jnp.where(end <= position, end, first)
    key_position = index * rows + lax.broadcasted_iota(jnp.int32, (rows, rows), 0)
    allowed = (key_position >= first) & (key_position <= position)
    allowed = jnp.concatenate([allowed] * heads, axis=1)

    queries = end_to_end(query_ref[...], heads)
    query_out[...] = queries
    scores = contract(packet_ref[0:rows, :], queries, 1, 1) * (1.0 / math.sqrt(depth))
    scores = jnp.where(allowed, scores, NEG)
    top = jnp.max(scores, axis=0, keepdims=True)
    raised = jnp.exp(scores - top)
    raised_out[...] = raised
    grads = end_to_end(grad_ref[...], heads)
    grad_out[...] = grads
    product = grads.astype(jnp.float32) * end_to_end(saved_ref[...], heads).astype(jnp.float32)
    delta = contract(
        jnp.ones((8, depth), jnp.float32), product, 1, 1, precision=lax.Precision.HIGHEST
    )[0:1, :]
    change_out[...] = contract(packet_ref[rows : 2 * rows, :], grads, 1, 1) - delta
    row_out[0:1, :] = delta
    row_out[1:2, :] = top
    row_out[2:3, :] = jnp.sum(raised, axis=0, keepdims=True)
    row_out[3:4, :] = jnp.concatenate([first.astype(jnp.float32)] * heads, axis=1)
    row_out[4:8, :] = jnp.ones((4, width), jnp.float32)
    owner, counts, rank = runs_of(packet_ref[2 * rows : 2 * rows + count, :].astype(jnp.float32))
    spread_out[...] = one_hot(count * slot, (owner ^ index) * slot + rank)
    target_out[...] = one_hot(count * rows, (owner ^ index) * rows + rank)
    filled_out[0:count, :] = jnp.broadcast_to(counts, (count, rows))
    filled_out[count:, :] = jnp.zeros((8 - count, rows), jnp.float32)


def fold(count, back, packet, queries, grads, row, filled):
    rows = packet.shape[1]
    index = lax.axis_index("ctx")
    delta, top, total = (row[n : n + 1, :] for n in range(3))
    first = row[3:4, :].astype(jnp.int32)
    position = (index - back) * rows + lax.broadcasted_iota(jnp.int32, (rows, row.shape[1]), 0)
    scores = contract(packet[0:rows, :], queries, 1, 1) * (1.0 / math.sqrt(queries.shape[1]))
    scores = jnp.where(position >= first, scores, NEG)
    new_top = jnp.maximum(top, jnp.max(scores, axis=0, keepdims=True))
    raised = jnp.exp(scores - new_top)
    shrink = jnp.exp(top - new_top)
    total = total * shrink + jnp.sum(raised, axis=0, keepdims=True)
    change = contract(packet[rows : 2 * rows, :], grads, 1, 1) - delta
    factors = row[4:8, :] * jnp.where(
        lax.broadcasted_iota(jnp.int32, (4, row.shape[1]), 0) < back, shrink, 1.0
    )
    owner, counts, rank = runs_of(packet[2 * rows : 2 * rows + count, :].astype(jnp.float32))
    base = jnp.zeros((1, rows), jnp.float32)
    for p in range(count):
        base = base + jnp.where(owner == p, filled[p : p + 1, :], 0.0)
    inside = index >= back
    target = jnp.where(inside, (owner ^ index) * rows + base.astype(jnp.int32) + rank, -1)
    filled = filled[0:count, :] + jnp.where(inside, counts, 0.0)
    return raised, change, (new_top, total, factors), one_hot(count * rows, target), filled


def step_kernel(count, back, *refs):
    query_ref, grad_ref, row_ref, filled_ref, packet_ref = refs[:5]
    raised_out, change_out, row_out, target_out, filled_out = refs[5:]
    raised, change, (top, total, factors), target, filled = fold(
        count, back, packet_ref, query_ref[...], grad_ref[...], row_ref, filled_ref
    )
    raised_out[...] = raised
    change_out[...] = change
    row_out[0:1, :] = row_ref[0:1, :]
    row_out[1:2, :] = top
    row_out[2:3, :] = total
    row_out[3:4, :] = row_ref[3:4, :]
    row_out[4:8, :] = factors
    target_out[...] = target
    filled_out[0:count, :] = filled
    filled_out[count:, :] = jnp.zeros_like(filled_out[count:, :])


def attend_kernel(count, halo, *refs):
    query_ref, grad_ref, row_ref, filled_ref, spread_ref = refs[:5]
    raised_refs = refs[5 : 5 + halo]
    change_refs = refs[5 + halo : 5 + 2 * halo]
    target_refs = refs[5 + 2 * halo : 5 + 3 * halo]
    packets = refs[5 + 3 * halo : 6 + 4 * halo]
    outs = refs[6 + 4 * halo :]
    rows = packets[0].shape[1]
    depth = query_ref.shape[1]
    heads = query_ref.shape[0] // rows
    slot = 2 * rows // count
    scale = 1.0 / math.sqrt(depth)
    queries = query_ref[...]
    grads = grad_ref[...]
    raised, change, (_, total, factors), target, _ = fold(
        count, halo, packets[halo], queries, grads, row_ref, filled_ref
    )
    factors = factors * (1.0 / total)
    weights = []
    changes = []
    for block in range(halo + 1):
        mine = raised if block == halo else raised_refs[block][...]
        mine = mine * factors[block : block + 1, :]
        weights.append(mine.astype(jnp.bfloat16))
        mine = mine * (change if block == halo else change_refs[block][...])
        changes.append(mine.astype(jnp.bfloat16))
    weights = jnp.concatenate(weights, axis=0)
    changes = jnp.concatenate(changes, axis=0)
    keys = jnp.concatenate([packet[0:rows, :] for packet in packets], axis=0)
    query_grad = (contract(keys, changes, 0, 0) * scale).astype(jnp.bfloat16)
    value_parts = contract(weights, grads, 1, 0).astype(jnp.bfloat16)
    key_parts = (contract(changes, queries, 1, 0) * scale).astype(jnp.bfloat16)

    query_slots = contract(spread_ref[...], end_to_end(query_grad, heads), 1, 1)
    query_slots = query_slots.astype(jnp.bfloat16)
    spread = jnp.concatenate([ref[...] for ref in target_refs] + [target], axis=1)
    key_slots = contract(spread, key_parts, 1, 0).astype(jnp.bfloat16)
    value_slots = contract(spread, value_parts, 1, 0).astype(jnp.bfloat16)
    at = heads * slot
    for k in range(count):
        out = outs[k]
        for h in range(heads):
            out[h * slot : (h + 1) * slot, :] = query_slots[
                k * slot : (k + 1) * slot, h * depth : (h + 1) * depth
            ]
        out[at : at + rows, :] = key_slots[k * rows : (k + 1) * rows, :]
        out[at + rows :, :] = value_slots[k * rows : (k + 1) * rows, :]


def order_kernel(count, halo, _, *refs):
    packets = refs[: 1 + halo]
    query_out, key_out = refs[1 + halo :]
    rows = query_out.shape[0]
    index = lax.axis_index("ctx")
    given = []
    for ref in packets:
        hot = ref[2 * rows : 2 * rows + count, :].astype(jnp.float32)
        counts = jnp.sum(hot, axis=1, keepdims=True)
        mine = jnp.zeros((1, 1), jnp.float32)
        for p in range(count):
            mine = jnp.where(index == p, counts[p : p + 1, :], mine)
        given.append(mine.astype(jnp.int32))
    if len(given) < count:
        given.append(rows - sum(given))
    giver = [lax.rem(index - d + count, count) for d in range(count)]

    def placement(size, halo):
        lane = lax.broadcasted_iota(jnp.int32, (1, count * size), 1)
        target = jnp.full(lane.shape, -1, jnp.int32)
        for k in range(count):
            step = lane - k * size
            for back in range(halo + 1):
                block = (index ^ k) - back
                start = jnp.zeros((1, 1), jnp.int32)
                length = jnp.zeros((1, 1), jnp.int32)
                for d in range(count):
                    start = start + jnp.where(giver[d] < block, given[d], 0)
                    length = length + jnp.where(giver[d] == block, given[d], 0)
                target = jnp.where((step >= 0) & (step < length), start + step, target)
                step = step - length
        return one_hot(rows, target)

    query_out[...] = placement(2 * rows // count, 0)
    key_out[...] = placement(rows, halo)


def place_kernel(count, query_spread, key_spread, *refs):
    ins = refs[:count]
    query_out, key_out, value_out = refs[count : count + 3]
    query_here, key_here, value_here, sems = refs[count + 3 :]
    rows, width = query_here.shape
    depth = key_here.shape[1]
    heads = width // depth
    slot = 2 * rows // count
    copies = []

    def leave(here, out):
        copies.append(pltpu.make_async_copy(here, out, sems.at[len(copies)]))
        copies[-1].start()

    for h in range(heads):
        at = slice(h * depth, (h + 1) * depth)
        taken = jnp.concatenate([ref[h * slot : (h + 1) * slot, :] for ref in ins], axis=0)
        query_here[:, at] = contract(query_spread[...], taken, 1, 0)
        leave(query_here.at[:, at], query_out.at[:, at])
    for n, (here, out) in enumerate(((key_here, key_out), (value_here, value_out))):
        at = heads * slot + n * rows
        taken = jnp.concatenate([ref[at : at + rows, :] for ref in ins], axis=0)
        here[...] = contract(key_spread[...], taken, 1, 0)
        leave(here, out)
    for copy in copies:
        copy.wait()


def near_plan(doc_lengths, owners, queries, key_head_rows, value_head_rows, forward_out, grad_out):
    count = lax.axis_size("ctx")
    rows, width = queries.shape
    depth = key_head_rows.shape[1]
    heads = width // depth
    bf16, f32 = jnp.bfloat16, jnp.float32
    columns = heads * rows
    halo = count // 2
    slot = 2 * rows // count
    whole = pl.BlockSpec(memory_space=pltpu.VMEM)
    params = pltpu.CompilerParams(vmem_limit_bytes=40 * 1024 * 1024)

    mark = lax.broadcasted_iota(jnp.int32, (2 * rows + META, rows), 0) - 2 * rows
    packet = jnp.where(
        mark < 0,
        jnp.pad(jnp.concatenate([key_head_rows, value_head_rows], axis=0), ((0, META), (0, 0))),
        (owners[None, :] == mark).astype(bf16),
    )
    near = [
        lax.ppermute(packet, "ctx", [(i, (i + back) % count) for i in range(count)])
        for back in range(1, halo + 1)
    ]
    block_shapes = [jax.ShapeDtypeStruct((rows, columns), f32)] * 2
    row_shape = jax.ShapeDtypeStruct((8, columns), f32)
    target_shape = jax.ShapeDtypeStruct((count * rows, rows), bf16)
    filled_shape = jax.ShapeDtypeStruct((8, rows), f32)
    query_rows, grad_rows, raised, change, row, spread, target, filled = pl.pallas_call(
        functools.partial(own_kernel, count, doc_lengths.shape[0]),
        out_shape=[jax.ShapeDtypeStruct((columns, depth), bf16)] * 2
        + block_shapes
        + [row_shape, jax.ShapeDtypeStruct((count * slot, rows), bf16), target_shape, filled_shape],
        in_specs=[pl.BlockSpec(memory_space=pltpu.SMEM)] + [whole] * 4,
        out_specs=[whole] * 8,
        compiler_params=params,
    )(doc_lengths, packet, queries, grad_out, forward_out)
    raised, change, target = [raised], [change], [target]
    for back in range(1, halo):
        found = pl.pallas_call(
            functools.partial(step_kernel, count, back),
            out_shape=block_shapes + [row_shape, target_shape, filled_shape],
            in_specs=[whole] * 5,
            out_specs=[whole] * 5,
            compiler_params=params,
        )(query_rows, grad_rows, row, filled, near[back - 1])
        raised.append(found[0])
        change.append(found[1])
        row = found[2]
        target.append(found[3])
        filled = found[4]
    sent = pl.pallas_call(
        functools.partial(attend_kernel, count, halo),
        out_shape=[jax.ShapeDtypeStruct((heads * slot + 2 * rows, depth), bf16)] * count,
        in_specs=[whole] * (6 + 4 * halo),
        out_specs=[whole] * count,
        compiler_params=params,
    )(query_rows, grad_rows, row, filled, spread, *raised, *change, *target, packet, *near)
    received = [sent[0]] + [
        lax.ppermute(sent[k], "ctx", [(i, i ^ k) for i in range(count)]) for k in range(1, count)
    ]
    spreads = pl.pallas_call(
        functools.partial(order_kernel, count, halo),
        out_shape=[
            jax.ShapeDtypeStruct((rows, count * slot), bf16),
            jax.ShapeDtypeStruct((rows, count * rows), bf16),
        ],
        in_specs=[pl.BlockSpec(memory_space=pl.ANY)] + [whole] * (1 + halo),
        out_specs=[whole] * 2,
        compiler_params=params,
    )(received[-1], packet, *near)
    return pl.pallas_call(
        functools.partial(place_kernel, count),
        out_shape=[
            jax.ShapeDtypeStruct((rows, width), f32),
            jax.ShapeDtypeStruct((rows, depth), f32),
            jax.ShapeDtypeStruct((rows, depth), f32),
        ],
        in_specs=[whole] * (2 + count),
        out_specs=[pl.BlockSpec(memory_space=pl.ANY)] * 3,
        scratch_shapes=[
            pltpu.VMEM((rows, width), f32),
            pltpu.VMEM((rows, depth), f32),
            pltpu.VMEM((rows, depth), f32),
            pltpu.SemaphoreType.DMA((heads + 2,)),
        ],
        compiler_params=params,
    )(*spreads, *received)


def per_device(*args):
    if lax.axis_size("ctx") in (2, 4):
        return near_plan(*args)
    return ring_plan(*args)


def solution(mesh):
    return jax.shard_map(
        per_device,
        mesh=mesh,
        in_specs=(
            P("groups"),
            P(("groups", "ctx")),
            P(("groups", "ctx"), "head"),
            P(("groups", "ctx"), "head"),
            P(("groups", "ctx"), "head"),
            P(("groups", "ctx"), "head"),
            P(("groups", "ctx"), "head"),
        ),
        out_specs=(
            P(("groups", "ctx"), "head"),
            P(("groups", "ctx"), "head"),
            P(("groups", "ctx"), "head"),
        ),
        check_vma=False,
    )
```

```python
import functools
import math

import jax
import jax.numpy as jnp
from jax import lax
from jax.experimental import pallas as pl
from jax.experimental.pallas import tpu as pltpu
from jax.sharding import PartitionSpec as P

HEAD_WIDTH = 128
GROUP = 4


NEG = -1e30
BLOCK = 512


def shifted(value, axis, by):
    count = lax.axis_size(axis)
    return lax.ppermute(value, axis, [(i, (i + by) % count) for i in range(count)])


def document_of(positions, doc_lengths):
    ends = jnp.cumsum(doc_lengths)
    return jnp.sum((positions[:, None] >= ends[None, :]).astype(jnp.int32), axis=1)


def allowed_between(query_positions, query_docs, key_positions, key_docs):
    return (query_docs[:, None] == key_docs[None, :]) & (
        key_positions[None, :] <= query_positions[:, None]
    )


def head_rows(matrix, group_size, head_dim):
    row_count = matrix.shape[0]
    return matrix.reshape(row_count * group_size, head_dim)


def block_scores(query_flat, key_head, row_count, group_size, head_dim):
    scores = lax.dot_general(
        query_flat, key_head, (((1,), (1,)), ((), ())), preferred_element_type=jnp.float32
    )
    return (scores * (1.0 / math.sqrt(head_dim))).reshape(row_count, group_size, key_head.shape[0])


def update_stats(running, query_local, key_block, allowed, group_size, head_dim):
    running_max, totals = running
    row_count = query_local.shape[0]
    scores = block_scores(
        head_rows(query_local, group_size, head_dim), key_block, row_count, group_size, head_dim
    )
    masked = jnp.where(allowed[:, None, :], scores, NEG)
    new_max = jnp.maximum(running_max, jnp.max(masked, axis=2))
    weights = jnp.where(allowed[:, None, :], jnp.exp(masked - new_max[:, :, None]), 0.0)
    new_totals = [totals * jnp.exp(running_max - new_max) + jnp.sum(weights, axis=2)]
    new_maxima = [new_max]
    return (jnp.concatenate(new_maxima, axis=1), jnp.concatenate(new_totals, axis=1))


def backward_block(
    query_local,
    grad_local,
    log_norm,
    row_delta,
    key_block,
    value_block,
    allowed,
    group_size,
    head_dim,
):
    row_count = query_local.shape[0]
    query_flat = head_rows(query_local, group_size, head_dim)
    grad_flat = head_rows(grad_local, group_size, head_dim)
    scores = block_scores(query_flat, key_block, row_count, group_size, head_dim)
    masked = jnp.where(allowed[:, None, :], scores, NEG)
    weights = jnp.exp(masked - log_norm[:, 0:group_size, None])
    grad_weights = lax.dot_general(
        grad_flat, value_block, (((1,), (1,)), ((), ())), preferred_element_type=jnp.float32
    ).reshape(row_count, group_size, -1)
    grad_scores = weights * (grad_weights - row_delta[:, 0:group_size, None])
    rounded_weights = weights.astype(jnp.bfloat16).reshape(row_count * group_size, -1)
    rounded_grads = grad_scores.astype(jnp.bfloat16).reshape(row_count * group_size, -1)
    value_parts = [
        lax.dot_general(
            rounded_weights, grad_flat, (((0,), (0,)), ((), ())), preferred_element_type=jnp.float32
        )
    ]
    key_parts = [
        lax.dot_general(
            rounded_grads, query_flat, (((0,), (0,)), ((), ())), preferred_element_type=jnp.float32
        )
    ]
    query_parts = [
        jnp.dot(rounded_grads, key_block, preferred_element_type=jnp.float32).reshape(
            row_count, group_size * head_dim
        )
    ]
    return (
        jnp.concatenate(query_parts, axis=1),
        jnp.concatenate(key_parts, axis=1),
        jnp.concatenate(value_parts, axis=1),
    )


def ring_plan(doc_lengths, owners, queries, key_head_rows, value_head_rows, forward_out, grad_out):
    context_size = lax.axis_size("ctx")
    context_index = lax.axis_index("ctx")
    row_count = queries.shape[0]
    head_dim = HEAD_WIDTH
    group_size = GROUP
    query_heads = queries.shape[1] // head_dim
    slot_count = 2 * row_count // context_size
    everyone = lax.all_gather(owners, "ctx", axis=0, tiled=True)
    row_arrangement = jnp.argsort(everyone, stable=True)
    layout_docs = document_of(row_arrangement, doc_lengths)
    own_positions = lax.dynamic_slice_in_dim(
        row_arrangement, context_index * row_count, row_count, 0
    )
    own_documents = lax.dynamic_slice_in_dim(layout_docs, context_index * row_count, row_count, 0)
    owner_ids = jnp.arange(context_size, dtype=jnp.int32)
    owner_hot = (owners[:, None] == owner_ids[None, :]).astype(jnp.int32)
    earlier = jnp.cumsum(owner_hot, axis=0) - owner_hot
    rank_within = jnp.sum(earlier * owner_hot, axis=1)
    slot_rows = owners * slot_count + rank_within

    def packed(matrix):
        empty = jnp.zeros((context_size * slot_count,) + matrix.shape[1:], matrix.dtype)
        return empty.at[slot_rows].set(matrix)

    owner_grid = everyone.reshape(context_size, row_count)
    counts = jnp.sum((owner_grid == context_index).astype(jnp.int32), axis=1)
    count_ends = jnp.cumsum(counts)
    starts = count_ends - counts
    wanted = jnp.arange(row_count, dtype=jnp.int32)
    source = jnp.sum((wanted[:, None] >= count_ends[None, :]).astype(jnp.int32), axis=1)
    source_hot = (source[:, None] == owner_ids[None, :]).astype(jnp.int32)
    take_rows = source * slot_count + wanted - jnp.sum(source_hot * starts[None, :], axis=1)

    def compact(received):
        return jnp.take(received, take_rows, axis=0)

    local_delta = jnp.sum(
        (grad_out.astype(jnp.float32) * forward_out.astype(jnp.float32)).reshape(
            row_count, query_heads, head_dim
        ),
        axis=2,
    )
    arrived = (
        lax.all_to_all(packed(queries), "ctx", split_axis=0, concat_axis=0, tiled=True),
        lax.all_to_all(packed(key_head_rows), "ctx", split_axis=0, concat_axis=0, tiled=True),
        lax.all_to_all(packed(value_head_rows), "ctx", split_axis=0, concat_axis=0, tiled=True),
        lax.all_to_all(packed(grad_out), "ctx", split_axis=0, concat_axis=0, tiled=True),
    )
    query_local, key_local, value_local, grad_local = [compact(received) for received in arrived]
    row_delta = compact(
        lax.all_to_all(packed(local_delta), "ctx", split_axis=0, concat_axis=0, tiled=True)
    )

    def fold_keys(running, shard_rows, first_row):
        piece_count = shard_rows.shape[0]
        step_rows = math.gcd(piece_count, BLOCK) if piece_count > BLOCK else piece_count

        def one_block(partial_value, block_index):
            offset = first_row + block_index * step_rows
            key_block = lax.dynamic_slice_in_dim(shard_rows, block_index * step_rows, step_rows, 0)
            key_positions = lax.dynamic_slice_in_dim(row_arrangement, offset, step_rows, 0)
            key_docs = lax.dynamic_slice_in_dim(layout_docs, offset, step_rows, 0)
            allowed = allowed_between(own_positions, own_documents, key_positions, key_docs)
            return (
                update_stats(partial_value, query_local, key_block, allowed, group_size, head_dim),
                None,
            )

        if piece_count == step_rows:
            return one_block(running, 0)[0]
        return lax.scan(one_block, running, jnp.arange(piece_count // step_rows, dtype=jnp.int32))[
            0
        ]

    start_stats = (
        jnp.full((row_count, query_heads), NEG, jnp.float32),
        jnp.zeros((row_count, query_heads), jnp.float32),
    )
    top_scores, totals = fold_keys(
        start_stats, lax.all_gather(key_local, "ctx", axis=0, tiled=True), jnp.int32(0)
    )
    log_norm = top_scores + jnp.log(totals)

    def block_meta(owner_index, offset, size):
        first = owner_index * row_count + offset
        key_positions = lax.dynamic_slice_in_dim(row_arrangement, first, size, 0)
        key_docs = lax.dynamic_slice_in_dim(layout_docs, first, size, 0)
        return (key_positions, key_docs)

    query_zero = jnp.zeros(query_local.shape, jnp.float32)
    key_zero = jnp.zeros(key_local.shape, jnp.float32)

    def one_turn(turn_index, loop_state):
        key_moving, value_moving, key_grad, value_grad, query_grad = loop_state
        owner_index = (context_index - turn_index) % context_size
        key_positions, key_docs = block_meta(owner_index, 0, row_count)
        allowed = allowed_between(own_positions, own_documents, key_positions, key_docs)
        query_part, key_part, value_part = backward_block(
            query_local,
            grad_local,
            log_norm,
            row_delta,
            key_moving,
            value_moving,
            allowed,
            group_size,
            head_dim,
        )
        return (
            key_moving,
            value_moving,
            key_grad + key_part,
            value_grad + value_part,
            query_grad + query_part,
        )

    def moved_turn(turn_index, loop_state):
        key_moving, value_moving, key_grad, value_grad, query_grad = loop_state
        key_moving, value_moving = shifted((key_moving, value_moving), "ctx", 1)
        key_grad, value_grad = shifted((key_grad, value_grad), "ctx", 1)
        return one_turn(turn_index, (key_moving, value_moving, key_grad, value_grad, query_grad))

    loop_state = one_turn(0, (key_local, value_local, key_zero, key_zero, query_zero))
    loop_state = lax.fori_loop(1, context_size, moved_turn, loop_state)
    key_grad, value_grad = shifted((loop_state[2], loop_state[3]), "ctx", 1)
    query_grad = loop_state[4]
    inverse_root = 1.0 / math.sqrt(head_dim)
    return (query_grad * inverse_root, key_grad * inverse_root, value_grad)


META = 16


def contract(left, right, left_dim, right_dim, **kw):
    return lax.dot_general(
        left,
        right,
        (((left_dim,), (right_dim,)), ((), ())),
        preferred_element_type=jnp.float32,
        **kw,
    )


def one_hot(row_count, target):
    places = lax.broadcasted_iota(jnp.int32, (row_count, target.shape[1]), 0)
    return jnp.where(places == target, 1.0, 0.0).astype(jnp.bfloat16)


def side_by_side(stack, heads):
    rows = stack.shape[0] // heads
    return jnp.concatenate([stack[h * rows : (h + 1) * rows, :] for h in range(heads)], axis=1)


def end_to_end(matrix, heads):
    width = matrix.shape[1] // heads
    return jnp.concatenate([matrix[:, h * width : (h + 1) * width] for h in range(heads)], axis=0)


def runs_of(hot):
    count, rows = hot.shape
    counts = jnp.sum(hot, axis=1, keepdims=True)
    owner = jnp.zeros((1, rows), jnp.int32)
    earlier = jnp.zeros((1, rows), jnp.float32)
    for p in range(count):
        mine = hot[p : p + 1, :] > 0.0
        owner = jnp.where(mine, p, owner)
        for less in range(p):
            earlier = earlier + jnp.where(mine, counts[less : less + 1, :], 0.0)
    lane = lax.broadcasted_iota(jnp.int32, (1, rows), 1)
    return owner, counts, lane - earlier.astype(jnp.int32)


def own_kernel(
    count,
    docs,
    doc_ref,
    packet_ref,
    query_ref,
    grad_ref,
    saved_ref,
    query_out,
    grad_out,
    raised_out,
    change_out,
    row_out,
    spread_out,
    target_out,
    filled_out,
):
    rows, width = query_ref.shape
    depth = packet_ref.shape[1]
    heads = width // depth
    slot = 2 * rows // count
    index = lax.axis_index("ctx")
    lane = lax.broadcasted_iota(jnp.int32, (1, rows), 1)
    position = index * rows + lane
    first = jnp.zeros((1, rows), jnp.int32)
    end = jnp.int32(0)
    for d in range(docs):
        end = end + doc_ref[d]
        first = jnp.where(end <= position, end, first)
    key_position = index * rows + lax.broadcasted_iota(jnp.int32, (rows, rows), 0)
    allowed = (key_position >= first) & (key_position <= position)
    allowed = jnp.concatenate([allowed] * heads, axis=1)

    queries = end_to_end(query_ref[...], heads)
    query_out[...] = queries
    scores = contract(packet_ref[0:rows, :], queries, 1, 1) * (1.0 / math.sqrt(depth))
    scores = jnp.where(allowed, scores, NEG)
    top = jnp.max(scores, axis=0, keepdims=True)
    raised = jnp.exp(scores - top)
    raised_out[...] = raised
    grads = end_to_end(grad_ref[...], heads)
    grad_out[...] = grads
    product = grads.astype(jnp.float32) * end_to_end(saved_ref[...], heads).astype(jnp.float32)
    delta = contract(
        jnp.ones((8, depth), jnp.float32), product, 1, 1, precision=lax.Precision.HIGHEST
    )[0:1, :]
    change_out[...] = contract(packet_ref[rows : 2 * rows, :], grads, 1, 1) - delta
    row_out[0:1, :] = delta
    row_out[1:2, :] = top
    row_out[2:3, :] = jnp.sum(raised, axis=0, keepdims=True)
    row_out[3:4, :] = jnp.concatenate([first.astype(jnp.float32)] * heads, axis=1)
    row_out[4:8, :] = jnp.ones((4, width), jnp.float32)
    owner, counts, rank = runs_of(packet_ref[2 * rows : 2 * rows + count, :].astype(jnp.float32))
    spread_out[...] = one_hot(count * slot, (owner ^ index) * slot + rank)
    target_out[...] = one_hot(count * rows, (owner ^ index) * rows + rank)
    filled_out[0:count, :] = jnp.broadcast_to(counts, (count, rows))
    filled_out[count:, :] = jnp.zeros((8 - count, rows), jnp.float32)


def packets_of(refs, halo):
    even = lax.rem(lax.axis_index("ctx"), 2) == 0
    packets = [ref[...] for ref in refs[: 1 + min(halo, 1)]]
    for n in range(2, 2 * halo, 2):
        packets.append(jnp.where(even, refs[n][...], refs[n + 1][...]))
    return packets


def fold(count, back, packet, queries, grads, row, filled):
    rows = packet.shape[1]
    index = lax.axis_index("ctx")
    delta, top, total = (row[n : n + 1, :] for n in range(3))
    first = row[3:4, :].astype(jnp.int32)
    position = (index - back) * rows + lax.broadcasted_iota(jnp.int32, (rows, row.shape[1]), 0)
    scores = contract(packet[0:rows, :], queries, 1, 1) * (1.0 / math.sqrt(queries.shape[1]))
    scores = jnp.where(position >= first, scores, NEG)
    new_top = jnp.maximum(top, jnp.max(scores, axis=0, keepdims=True))
    raised = jnp.exp(scores - new_top)
    shrink = jnp.exp(top - new_top)
    total = total * shrink + jnp.sum(raised, axis=0, keepdims=True)
    change = contract(packet[rows : 2 * rows, :], grads, 1, 1) - delta
    factors = row[4:8, :] * jnp.where(
        lax.broadcasted_iota(jnp.int32, (4, row.shape[1]), 0) < back, shrink, 1.0
    )
    owner, counts, rank = runs_of(packet[2 * rows : 2 * rows + count, :].astype(jnp.float32))
    base = jnp.zeros((1, rows), jnp.float32)
    for p in range(count):
        base = base + jnp.where(owner == p, filled[p : p + 1, :], 0.0)
    inside = index >= back
    target = jnp.where(inside, (owner ^ index) * rows + base.astype(jnp.int32) + rank, -1)
    filled = filled[0:count, :] + jnp.where(inside, counts, 0.0)
    return raised, change, (new_top, total, factors), one_hot(count * rows, target), filled


def step_kernel(count, back, *refs):
    query_ref, grad_ref, row_ref, filled_ref, packet_ref = refs[:5]
    raised_out, change_out, row_out, target_out, filled_out = refs[-5:]
    raised, change, (top, total, factors), target, filled = fold(
        count, back, packet_ref[...], query_ref[...], grad_ref[...], row_ref, filled_ref
    )
    raised_out[...] = raised
    change_out[...] = change
    row_out[0:1, :] = row_ref[0:1, :]
    row_out[1:2, :] = top
    row_out[2:3, :] = total
    row_out[3:4, :] = row_ref[3:4, :]
    row_out[4:8, :] = factors
    target_out[...] = target
    filled_out[0:count, :] = filled
    filled_out[count:, :] = jnp.zeros_like(filled_out[count:, :])


def attend_kernel(count, halo, *refs):
    query_ref, grad_ref, row_ref, filled_ref, spread_ref = refs[:5]
    raised_refs = refs[5 : 5 + halo]
    change_refs = refs[5 + halo : 5 + 2 * halo]
    target_refs = refs[5 + 2 * halo : 5 + 3 * halo]
    outs = refs[-count:]
    packets = packets_of(refs[5 + 3 * halo : -count], halo)
    rows = packets[0].shape[1]
    depth = query_ref.shape[1]
    heads = query_ref.shape[0] // rows
    slot = 2 * rows // count
    scale = 1.0 / math.sqrt(depth)
    queries = query_ref[...]
    grads = grad_ref[...]
    raised, change, (_, total, factors), target, _ = fold(
        count, halo, packets[halo], queries, grads, row_ref, filled_ref
    )
    factors = factors * (1.0 / total)
    weights = []
    changes = []
    for block in range(halo + 1):
        mine = raised if block == halo else raised_refs[block][...]
        mine = mine * factors[block : block + 1, :]
        weights.append(mine.astype(jnp.bfloat16))
        mine = mine * (change if block == halo else change_refs[block][...])
        changes.append(mine.astype(jnp.bfloat16))
    weights = jnp.concatenate(weights, axis=0)
    changes = jnp.concatenate(changes, axis=0)
    keys = jnp.concatenate([packet[0:rows, :] for packet in packets], axis=0)
    query_grad = (contract(keys, changes, 0, 0) * scale).astype(jnp.bfloat16)
    value_parts = contract(weights, grads, 1, 0).astype(jnp.bfloat16)
    key_parts = (contract(changes, queries, 1, 0) * scale).astype(jnp.bfloat16)

    query_slots = contract(spread_ref[...], end_to_end(query_grad, heads), 1, 1)
    query_slots = query_slots.astype(jnp.bfloat16)
    spread = jnp.concatenate([ref[...] for ref in target_refs] + [target], axis=1)
    key_slots = contract(spread, key_parts, 1, 0).astype(jnp.bfloat16)
    value_slots = contract(spread, value_parts, 1, 0).astype(jnp.bfloat16)
    at = heads * slot
    for k in range(count):
        out = outs[k]
        for h in range(heads):
            out[h * slot : (h + 1) * slot, :] = query_slots[
                k * slot : (k + 1) * slot, h * depth : (h + 1) * depth
            ]
        out[at : at + rows, :] = key_slots[k * rows : (k + 1) * rows, :]
        out[at + rows :, :] = value_slots[k * rows : (k + 1) * rows, :]


def order_kernel(count, halo, _, *refs):
    query_out, key_out = refs[-2:]
    packets = packets_of(refs[:-2], halo)
    rows = query_out.shape[0]
    index = lax.axis_index("ctx")
    given = []
    for packet in packets:
        hot = packet[2 * rows : 2 * rows + count, :].astype(jnp.float32)
        counts = jnp.sum(hot, axis=1, keepdims=True)
        mine = jnp.zeros((1, 1), jnp.float32)
        for p in range(count):
            mine = jnp.where(index == p, counts[p : p + 1, :], mine)
        given.append(mine.astype(jnp.int32))
    if len(given) < count:
        given.append(rows - sum(given))
    giver = [lax.rem(index - d + count, count) for d in range(count)]

    def placement(size, halo):
        lane = lax.broadcasted_iota(jnp.int32, (1, count * size), 1)
        target = jnp.full(lane.shape, -1, jnp.int32)
        for k in range(count):
            step = lane - k * size
            for back in range(halo + 1):
                block = (index ^ k) - back
                start = jnp.zeros((1, 1), jnp.int32)
                length = jnp.zeros((1, 1), jnp.int32)
                for d in range(count):
                    start = start + jnp.where(giver[d] < block, given[d], 0)
                    length = length + jnp.where(giver[d] == block, given[d], 0)
                target = jnp.where((step >= 0) & (step < length), start + step, target)
                step = step - length
        return one_hot(rows, target)

    query_out[...] = placement(2 * rows // count, 0)
    key_out[...] = placement(rows, halo)


def place_kernel(count, query_spread, key_spread, *refs):
    ins = refs[:count]
    query_out, key_out, value_out = refs[count : count + 3]
    query_here, key_here, value_here, sems = refs[count + 3 :]
    rows, width = query_here.shape
    depth = key_here.shape[1]
    heads = width // depth
    slot = 2 * rows // count
    copies = []

    def leave(here, out):
        copies.append(pltpu.make_async_copy(here, out, sems.at[len(copies)]))
        copies[-1].start()

    for h in range(heads):
        at = slice(h * depth, (h + 1) * depth)
        taken = jnp.concatenate([ref[h * slot : (h + 1) * slot, :] for ref in ins], axis=0)
        query_here[:, at] = contract(query_spread[...], taken, 1, 0)
        leave(query_here.at[:, at], query_out.at[:, at])
    for n, (here, out) in enumerate(((key_here, key_out), (value_here, value_out))):
        at = heads * slot + n * rows
        taken = jnp.concatenate([ref[at : at + rows, :] for ref in ins], axis=0)
        here[...] = contract(key_spread[...], taken, 1, 0)
        leave(here, out)
    for copy in copies:
        copy.wait()


def near_plan(doc_lengths, owners, queries, key_head_rows, value_head_rows, forward_out, grad_out):
    count = lax.axis_size("ctx")
    rows, width = queries.shape
    depth = key_head_rows.shape[1]
    heads = width // depth
    bf16, f32 = jnp.bfloat16, jnp.float32
    columns = heads * rows
    halo = count // 2
    slot = 2 * rows // count
    whole = pl.BlockSpec(memory_space=pltpu.VMEM)
    params = pltpu.CompilerParams(vmem_limit_bytes=40 * 1024 * 1024)

    mark = lax.broadcasted_iota(jnp.int32, (2 * rows + META, rows), 0) - 2 * rows
    packet = jnp.where(
        mark < 0,
        jnp.pad(jnp.concatenate([key_head_rows, value_head_rows], axis=0), ((0, META), (0, 0))),
        (owners[None, :] == mark).astype(bf16),
    )
    near = [lax.ppermute(packet, "ctx", [(i, (i + 1) % count) for i in range(count)])]
    for back in range(2, halo + 1):
        for part in range(2):
            pairs = [(i, (i + back) % count if i % 2 == part else i) for i in range(count)]
            near.append(lax.ppermute(packet, "ctx", pairs))
    block_shapes = [jax.ShapeDtypeStruct((rows, columns), f32)] * 2
    row_shape = jax.ShapeDtypeStruct((8, columns), f32)
    target_shape = jax.ShapeDtypeStruct((count * rows, rows), bf16)
    filled_shape = jax.ShapeDtypeStruct((8, rows), f32)
    query_rows, grad_rows, raised, change, row, spread, target, filled = pl.pallas_call(
        functools.partial(own_kernel, count, doc_lengths.shape[0]),
        out_shape=[jax.ShapeDtypeStruct((columns, depth), bf16)] * 2
        + block_shapes
        + [row_shape, jax.ShapeDtypeStruct((count * slot, rows), bf16), target_shape, filled_shape],
        in_specs=[pl.BlockSpec(memory_space=pltpu.SMEM)] + [whole] * 4,
        out_specs=[whole] * 8,
        compiler_params=params,
    )(doc_lengths, packet, queries, grad_out, forward_out)
    raised, change, target = [raised], [change], [target]
    for back in range(1, halo):
        found = pl.pallas_call(
            functools.partial(step_kernel, count, back),
            out_shape=block_shapes + [row_shape, target_shape, filled_shape],
            in_specs=[whole] * 5 + [pl.BlockSpec(memory_space=pl.ANY)],
            out_specs=[whole] * 5,
            compiler_params=params,
        )(query_rows, grad_rows, row, filled, near[back - 1], near[1])
        raised.append(found[0])
        change.append(found[1])
        row = found[2]
        target.append(found[3])
        filled = found[4]
    sent = pl.pallas_call(
        functools.partial(attend_kernel, count, halo),
        out_shape=[jax.ShapeDtypeStruct((heads * slot + 2 * rows, depth), bf16)] * count,
        in_specs=[whole] * (6 + 3 * halo + len(near)),
        out_specs=[whole] * count,
        compiler_params=params,
    )(query_rows, grad_rows, row, filled, spread, *raised, *change, *target, packet, *near)
    received = [sent[0]] + [
        lax.ppermute(sent[k], "ctx", [(i, i ^ k) for i in range(count)]) for k in range(1, count)
    ]
    spreads = pl.pallas_call(
        functools.partial(order_kernel, count, halo),
        out_shape=[
            jax.ShapeDtypeStruct((rows, count * slot), bf16),
            jax.ShapeDtypeStruct((rows, count * rows), bf16),
        ],
        in_specs=[pl.BlockSpec(memory_space=pl.ANY)] + [whole] * (1 + len(near)),
        out_specs=[whole] * 2,
        compiler_params=params,
    )(received[-1], packet, *near)
    return pl.pallas_call(
        functools.partial(place_kernel, count),
        out_shape=[
            jax.ShapeDtypeStruct((rows, width), f32),
            jax.ShapeDtypeStruct((rows, depth), f32),
            jax.ShapeDtypeStruct((rows, depth), f32),
        ],
        in_specs=[whole] * (2 + count),
        out_specs=[pl.BlockSpec(memory_space=pl.ANY)] * 3,
        scratch_shapes=[
            pltpu.VMEM((rows, width), f32),
            pltpu.VMEM((rows, depth), f32),
            pltpu.VMEM((rows, depth), f32),
            pltpu.SemaphoreType.DMA((heads + 2,)),
        ],
        compiler_params=params,
    )(*spreads, *received)


def per_device(*args):
    if lax.axis_size("ctx") in (2, 4):
        return near_plan(*args)
    return ring_plan(*args)


def solution(mesh):
    return jax.shard_map(
        per_device,
        mesh=mesh,
        in_specs=(
            P("groups"),
            P(("groups", "ctx")),
            P(("groups", "ctx"), "head"),
            P(("groups", "ctx"), "head"),
            P(("groups", "ctx"), "head"),
            P(("groups", "ctx"), "head"),
            P(("groups", "ctx"), "head"),
        ),
        out_specs=(
            P(("groups", "ctx"), "head"),
            P(("groups", "ctx"), "head"),
            P(("groups", "ctx"), "head"),
        ),
        check_vma=False,
    )
```

```python
import functools
import math

import jax
import jax.numpy as jnp
from jax import lax
from jax.experimental import pallas as pl
from jax.experimental.pallas import tpu as pltpu
from jax.sharding import PartitionSpec as P

HEAD_WIDTH = 128
GROUP = 4


NEG = -1e30
BLOCK = 512


def shifted(value, axis, by):
    count = lax.axis_size(axis)
    return lax.ppermute(value, axis, [(i, (i + by) % count) for i in range(count)])


def document_of(positions, doc_lengths):
    ends = jnp.cumsum(doc_lengths)
    return jnp.sum((positions[:, None] >= ends[None, :]).astype(jnp.int32), axis=1)


def allowed_between(query_positions, query_docs, key_positions, key_docs):
    return (query_docs[:, None] == key_docs[None, :]) & (
        key_positions[None, :] <= query_positions[:, None]
    )


def head_rows(matrix, group_size, head_dim):
    row_count = matrix.shape[0]
    return matrix.reshape(row_count * group_size, head_dim)


def block_scores(query_flat, key_head, row_count, group_size, head_dim):
    scores = lax.dot_general(
        query_flat, key_head, (((1,), (1,)), ((), ())), preferred_element_type=jnp.float32
    )
    return (scores * (1.0 / math.sqrt(head_dim))).reshape(row_count, group_size, key_head.shape[0])


def update_stats(running, query_local, key_block, allowed, group_size, head_dim):
    running_max, totals = running
    row_count = query_local.shape[0]
    scores = block_scores(
        head_rows(query_local, group_size, head_dim), key_block, row_count, group_size, head_dim
    )
    masked = jnp.where(allowed[:, None, :], scores, NEG)
    new_max = jnp.maximum(running_max, jnp.max(masked, axis=2))
    weights = jnp.where(allowed[:, None, :], jnp.exp(masked - new_max[:, :, None]), 0.0)
    new_totals = [totals * jnp.exp(running_max - new_max) + jnp.sum(weights, axis=2)]
    new_maxima = [new_max]
    return (jnp.concatenate(new_maxima, axis=1), jnp.concatenate(new_totals, axis=1))


def backward_block(
    query_local,
    grad_local,
    log_norm,
    row_delta,
    key_block,
    value_block,
    allowed,
    group_size,
    head_dim,
):
    row_count = query_local.shape[0]
    query_flat = head_rows(query_local, group_size, head_dim)
    grad_flat = head_rows(grad_local, group_size, head_dim)
    scores = block_scores(query_flat, key_block, row_count, group_size, head_dim)
    masked = jnp.where(allowed[:, None, :], scores, NEG)
    weights = jnp.exp(masked - log_norm[:, 0:group_size, None])
    grad_weights = lax.dot_general(
        grad_flat, value_block, (((1,), (1,)), ((), ())), preferred_element_type=jnp.float32
    ).reshape(row_count, group_size, -1)
    grad_scores = weights * (grad_weights - row_delta[:, 0:group_size, None])
    rounded_weights = weights.astype(jnp.bfloat16).reshape(row_count * group_size, -1)
    rounded_grads = grad_scores.astype(jnp.bfloat16).reshape(row_count * group_size, -1)
    value_parts = [
        lax.dot_general(
            rounded_weights, grad_flat, (((0,), (0,)), ((), ())), preferred_element_type=jnp.float32
        )
    ]
    key_parts = [
        lax.dot_general(
            rounded_grads, query_flat, (((0,), (0,)), ((), ())), preferred_element_type=jnp.float32
        )
    ]
    query_parts = [
        jnp.dot(rounded_grads, key_block, preferred_element_type=jnp.float32).reshape(
            row_count, group_size * head_dim
        )
    ]
    return (
        jnp.concatenate(query_parts, axis=1),
        jnp.concatenate(key_parts, axis=1),
        jnp.concatenate(value_parts, axis=1),
    )


def ring_plan(doc_lengths, owners, queries, key_head_rows, value_head_rows, forward_out, grad_out):
    context_size = lax.axis_size("ctx")
    context_index = lax.axis_index("ctx")
    row_count = queries.shape[0]
    head_dim = HEAD_WIDTH
    group_size = GROUP
    query_heads = queries.shape[1] // head_dim
    slot_count = 2 * row_count // context_size
    everyone = lax.all_gather(owners, "ctx", axis=0, tiled=True)
    row_arrangement = jnp.argsort(everyone, stable=True)
    layout_docs = document_of(row_arrangement, doc_lengths)
    own_positions = lax.dynamic_slice_in_dim(
        row_arrangement, context_index * row_count, row_count, 0
    )
    own_documents = lax.dynamic_slice_in_dim(layout_docs, context_index * row_count, row_count, 0)
    owner_ids = jnp.arange(context_size, dtype=jnp.int32)
    owner_hot = (owners[:, None] == owner_ids[None, :]).astype(jnp.int32)
    earlier = jnp.cumsum(owner_hot, axis=0) - owner_hot
    rank_within = jnp.sum(earlier * owner_hot, axis=1)
    slot_rows = owners * slot_count + rank_within

    def packed(matrix):
        empty = jnp.zeros((context_size * slot_count,) + matrix.shape[1:], matrix.dtype)
        return empty.at[slot_rows].set(matrix)

    owner_grid = everyone.reshape(context_size, row_count)
    counts = jnp.sum((owner_grid == context_index).astype(jnp.int32), axis=1)
    count_ends = jnp.cumsum(counts)
    starts = count_ends - counts
    wanted = jnp.arange(row_count, dtype=jnp.int32)
    source = jnp.sum((wanted[:, None] >= count_ends[None, :]).astype(jnp.int32), axis=1)
    source_hot = (source[:, None] == owner_ids[None, :]).astype(jnp.int32)
    take_rows = source * slot_count + wanted - jnp.sum(source_hot * starts[None, :], axis=1)

    def compact(received):
        return jnp.take(received, take_rows, axis=0)

    local_delta = jnp.sum(
        (grad_out.astype(jnp.float32) * forward_out.astype(jnp.float32)).reshape(
            row_count, query_heads, head_dim
        ),
        axis=2,
    )
    arrived = (
        lax.all_to_all(packed(queries), "ctx", split_axis=0, concat_axis=0, tiled=True),
        lax.all_to_all(packed(key_head_rows), "ctx", split_axis=0, concat_axis=0, tiled=True),
        lax.all_to_all(packed(value_head_rows), "ctx", split_axis=0, concat_axis=0, tiled=True),
        lax.all_to_all(packed(grad_out), "ctx", split_axis=0, concat_axis=0, tiled=True),
    )
    query_local, key_local, value_local, grad_local = [compact(received) for received in arrived]
    row_delta = compact(
        lax.all_to_all(packed(local_delta), "ctx", split_axis=0, concat_axis=0, tiled=True)
    )

    def fold_keys(running, shard_rows, first_row):
        piece_count = shard_rows.shape[0]
        step_rows = math.gcd(piece_count, BLOCK) if piece_count > BLOCK else piece_count

        def one_block(partial_value, block_index):
            offset = first_row + block_index * step_rows
            key_block = lax.dynamic_slice_in_dim(shard_rows, block_index * step_rows, step_rows, 0)
            key_positions = lax.dynamic_slice_in_dim(row_arrangement, offset, step_rows, 0)
            key_docs = lax.dynamic_slice_in_dim(layout_docs, offset, step_rows, 0)
            allowed = allowed_between(own_positions, own_documents, key_positions, key_docs)
            return (
                update_stats(partial_value, query_local, key_block, allowed, group_size, head_dim),
                None,
            )

        if piece_count == step_rows:
            return one_block(running, 0)[0]
        return lax.scan(one_block, running, jnp.arange(piece_count // step_rows, dtype=jnp.int32))[
            0
        ]

    start_stats = (
        jnp.full((row_count, query_heads), NEG, jnp.float32),
        jnp.zeros((row_count, query_heads), jnp.float32),
    )
    top_scores, totals = fold_keys(
        start_stats, lax.all_gather(key_local, "ctx", axis=0, tiled=True), jnp.int32(0)
    )
    log_norm = top_scores + jnp.log(totals)

    def block_meta(owner_index, offset, size):
        first = owner_index * row_count + offset
        key_positions = lax.dynamic_slice_in_dim(row_arrangement, first, size, 0)
        key_docs = lax.dynamic_slice_in_dim(layout_docs, first, size, 0)
        return (key_positions, key_docs)

    query_zero = jnp.zeros(query_local.shape, jnp.float32)
    key_zero = jnp.zeros(key_local.shape, jnp.float32)

    def one_turn(turn_index, loop_state):
        key_moving, value_moving, key_grad, value_grad, query_grad = loop_state
        owner_index = (context_index - turn_index) % context_size
        key_positions, key_docs = block_meta(owner_index, 0, row_count)
        allowed = allowed_between(own_positions, own_documents, key_positions, key_docs)
        query_part, key_part, value_part = backward_block(
            query_local,
            grad_local,
            log_norm,
            row_delta,
            key_moving,
            value_moving,
            allowed,
            group_size,
            head_dim,
        )
        return (
            key_moving,
            value_moving,
            key_grad + key_part,
            value_grad + value_part,
            query_grad + query_part,
        )

    def moved_turn(turn_index, loop_state):
        key_moving, value_moving, key_grad, value_grad, query_grad = loop_state
        key_moving, value_moving = shifted((key_moving, value_moving), "ctx", 1)
        key_grad, value_grad = shifted((key_grad, value_grad), "ctx", 1)
        return one_turn(turn_index, (key_moving, value_moving, key_grad, value_grad, query_grad))

    loop_state = one_turn(0, (key_local, value_local, key_zero, key_zero, query_zero))
    loop_state = lax.fori_loop(1, context_size, moved_turn, loop_state)
    key_grad, value_grad = shifted((loop_state[2], loop_state[3]), "ctx", 1)
    query_grad = loop_state[4]
    inverse_root = 1.0 / math.sqrt(head_dim)
    return (query_grad * inverse_root, key_grad * inverse_root, value_grad)


META = 8


def contract(left, right, left_dim, right_dim, **kw):
    return lax.dot_general(
        left,
        right,
        (((left_dim,), (right_dim,)), ((), ())),
        preferred_element_type=jnp.float32,
        **kw,
    )


def one_hot(row_count, target):
    places = lax.broadcasted_iota(jnp.int32, (row_count, target.shape[1]), 0)
    return jnp.where(places == target, 1.0, 0.0).astype(jnp.bfloat16)


def side_by_side(stack, heads):
    rows = stack.shape[0] // heads
    return jnp.concatenate([stack[h * rows : (h + 1) * rows, :] for h in range(heads)], axis=1)


def end_to_end(matrix, heads):
    width = matrix.shape[1] // heads
    return jnp.concatenate([matrix[:, h * width : (h + 1) * width] for h in range(heads)], axis=0)


def runs_of(hot):
    count, rows = hot.shape
    counts = jnp.sum(hot, axis=1, keepdims=True)
    owner = jnp.zeros((1, rows), jnp.int32)
    earlier = jnp.zeros((1, rows), jnp.float32)
    for p in range(count):
        mine = hot[p : p + 1, :] > 0.0
        owner = jnp.where(mine, p, owner)
        for less in range(p):
            earlier = earlier + jnp.where(mine, counts[less : less + 1, :], 0.0)
    lane = lax.broadcasted_iota(jnp.int32, (1, rows), 1)
    return owner, counts, lane - earlier.astype(jnp.int32)


def own_kernel(
    count,
    docs,
    doc_ref,
    packet_ref,
    query_ref,
    grad_ref,
    saved_ref,
    query_out,
    grad_out,
    raised_out,
    change_out,
    row_out,
    spread_out,
    target_out,
    filled_out,
):
    rows, width = query_ref.shape
    depth = packet_ref.shape[1]
    heads = width // depth
    slot = 2 * rows // count
    index = lax.axis_index("ctx")
    lane = lax.broadcasted_iota(jnp.int32, (1, rows), 1)
    position = index * rows + lane
    first = jnp.zeros((1, rows), jnp.int32)
    end = jnp.int32(0)
    for d in range(docs):
        end = end + doc_ref[d]
        first = jnp.where(end <= position, end, first)
    key_position = index * rows + lax.broadcasted_iota(jnp.int32, (rows, rows), 0)
    allowed = (key_position >= first) & (key_position <= position)
    allowed = jnp.concatenate([allowed] * heads, axis=1)

    queries = end_to_end(query_ref[...], heads)
    query_out[...] = queries
    scores = contract(packet_ref[0:rows, :], queries, 1, 1) * (1.0 / math.sqrt(depth))
    scores = jnp.where(allowed, scores, NEG)
    top = jnp.max(scores, axis=0, keepdims=True)
    raised = jnp.exp(scores - top)
    raised_out[...] = raised
    grads = end_to_end(grad_ref[...], heads)
    grad_out[...] = grads
    product = grads.astype(jnp.float32) * end_to_end(saved_ref[...], heads).astype(jnp.float32)
    delta = contract(
        jnp.ones((8, depth), jnp.float32), product, 1, 1, precision=lax.Precision.HIGHEST
    )[0:1, :]
    change_out[...] = contract(packet_ref[rows : 2 * rows, :], grads, 1, 1) - delta
    row_out[0:1, :] = delta
    row_out[1:2, :] = top
    row_out[2:3, :] = jnp.sum(raised, axis=0, keepdims=True)
    row_out[3:4, :] = jnp.concatenate([first.astype(jnp.float32)] * heads, axis=1)
    row_out[4:8, :] = jnp.ones((4, width), jnp.float32)
    owner, counts, rank = runs_of(packet_ref[2 * rows : 2 * rows + count, :].astype(jnp.float32))
    spread_out[...] = one_hot(count * slot, (owner ^ index) * slot + rank)
    target_out[...] = one_hot(count * rows, (owner ^ index) * rows + rank)
    filled_out[0:count, :] = jnp.broadcast_to(counts, (count, rows))
    filled_out[count:, :] = jnp.zeros((8 - count, rows), jnp.float32)


def fold(count, back, packet, queries, grads, row, filled):
    rows = packet.shape[1]
    index = lax.axis_index("ctx")
    delta, top, total = (row[n : n + 1, :] for n in range(3))
    first = row[3:4, :].astype(jnp.int32)
    position = (index - back) * rows + lax.broadcasted_iota(jnp.int32, (rows, row.shape[1]), 0)
    scores = contract(packet[0:rows, :], queries, 1, 1) * (1.0 / math.sqrt(queries.shape[1]))
    scores = jnp.where(position >= first, scores, NEG)
    new_top = jnp.maximum(top, jnp.max(scores, axis=0, keepdims=True))
    raised = jnp.exp(scores - new_top)
    shrink = jnp.exp(top - new_top)
    total = total * shrink + jnp.sum(raised, axis=0, keepdims=True)
    change = contract(packet[rows : 2 * rows, :], grads, 1, 1) - delta
    factors = row[4:8, :] * jnp.where(
        lax.broadcasted_iota(jnp.int32, (4, row.shape[1]), 0) < back, shrink, 1.0
    )
    owner, counts, rank = runs_of(packet[2 * rows : 2 * rows + count, :].astype(jnp.float32))
    base = jnp.zeros((1, rows), jnp.float32)
    for p in range(count):
        base = base + jnp.where(owner == p, filled[p : p + 1, :], 0.0)
    inside = index >= back
    target = jnp.where(inside, (owner ^ index) * rows + base.astype(jnp.int32) + rank, -1)
    filled = filled[0:count, :] + jnp.where(inside, counts, 0.0)
    return raised, change, (new_top, total, factors), one_hot(count * rows, target), filled


def step_kernel(count, back, *refs):
    query_ref, grad_ref, row_ref, filled_ref, packet_ref = refs[:5]
    raised_out, change_out, row_out, target_out, filled_out = refs[5:]
    raised, change, (top, total, factors), target, filled = fold(
        count, back, packet_ref, query_ref[...], grad_ref[...], row_ref, filled_ref
    )
    raised_out[...] = raised
    change_out[...] = change
    row_out[0:1, :] = row_ref[0:1, :]
    row_out[1:2, :] = top
    row_out[2:3, :] = total
    row_out[3:4, :] = row_ref[3:4, :]
    row_out[4:8, :] = factors
    target_out[...] = target
    filled_out[0:count, :] = filled
    filled_out[count:, :] = jnp.zeros_like(filled_out[count:, :])


def attend_kernel(count, halo, *refs):
    query_ref, grad_ref, row_ref, filled_ref, spread_ref = refs[:5]
    raised_refs = refs[5 : 5 + halo]
    change_refs = refs[5 + halo : 5 + 2 * halo]
    target_refs = refs[5 + 2 * halo : 5 + 3 * halo]
    packets = refs[5 + 3 * halo : 6 + 4 * halo]
    outs = refs[6 + 4 * halo :]
    rows = packets[0].shape[1]
    depth = query_ref.shape[1]
    heads = query_ref.shape[0] // rows
    slot = 2 * rows // count
    scale = 1.0 / math.sqrt(depth)
    queries = query_ref[...]
    grads = grad_ref[...]
    raised, change, (_, total, factors), target, _ = fold(
        count, halo, packets[halo], queries, grads, row_ref, filled_ref
    )
    factors = factors * (1.0 / total)
    weights = []
    changes = []
    for block in range(halo + 1):
        mine = raised if block == halo else raised_refs[block][...]
        mine = mine * factors[block : block + 1, :]
        weights.append(mine.astype(jnp.bfloat16))
        mine = mine * (change if block == halo else change_refs[block][...])
        changes.append(mine.astype(jnp.bfloat16))
    weights = jnp.concatenate(weights, axis=0)
    changes = jnp.concatenate(changes, axis=0)
    keys = jnp.concatenate([packet[0:rows, :] for packet in packets], axis=0)
    query_grad = (contract(keys, changes, 0, 0) * scale).astype(jnp.bfloat16)
    key_parts = contract(changes, queries, 1, 0) * scale
    value_parts = contract(weights, grads, 1, 0)
    parts = jnp.concatenate([key_parts, value_parts], axis=1).astype(jnp.bfloat16)

    query_slots = contract(spread_ref[...], end_to_end(query_grad, heads), 1, 1)
    query_slots = query_slots.astype(jnp.bfloat16)
    spread = jnp.concatenate([ref[...] for ref in target_refs] + [target], axis=1)
    part_slots = contract(spread, parts, 1, 0).astype(jnp.bfloat16)
    at = heads * slot
    for k in range(count):
        out = outs[k]
        for h in range(heads):
            out[h * slot : (h + 1) * slot, :] = query_slots[
                k * slot : (k + 1) * slot, h * depth : (h + 1) * depth
            ]
        for n in range(2):
            out[at + n * rows : at + (n + 1) * rows, :] = part_slots[
                k * rows : (k + 1) * rows, n * depth : (n + 1) * depth
            ]


def order_kernel(count, halo, _, *refs):
    packets = refs[: 1 + halo]
    query_out, key_out = refs[1 + halo :]
    rows = query_out.shape[0]
    index = lax.axis_index("ctx")
    given = []
    for ref in packets:
        hot = ref[2 * rows : 2 * rows + count, :].astype(jnp.float32)
        counts = jnp.sum(hot, axis=1, keepdims=True)
        mine = jnp.zeros((1, 1), jnp.float32)
        for p in range(count):
            mine = jnp.where(index == p, counts[p : p + 1, :], mine)
        given.append(mine.astype(jnp.int32))
    if len(given) < count:
        given.append(rows - sum(given))
    giver = [lax.rem(index - d + count, count) for d in range(count)]

    def placement(size, halo):
        lane = lax.broadcasted_iota(jnp.int32, (1, count * size), 1)
        target = jnp.full(lane.shape, -1, jnp.int32)
        for k in range(count):
            step = lane - k * size
            for back in range(halo + 1):
                block = (index ^ k) - back
                start = jnp.zeros((1, 1), jnp.int32)
                length = jnp.zeros((1, 1), jnp.int32)
                for d in range(count):
                    start = start + jnp.where(giver[d] < block, given[d], 0)
                    length = length + jnp.where(giver[d] == block, given[d], 0)
                target = jnp.where((step >= 0) & (step < length), start + step, target)
                step = step - length
        return one_hot(rows, target)

    query_out[...] = placement(2 * rows // count, 0)
    key_out[...] = placement(rows, halo)


def place_kernel(count, query_spread, key_spread, *refs):
    ins = refs[:count]
    query_out, key_out, value_out = refs[count : count + 3]
    query_here, key_here, value_here, sems = refs[count + 3 :]
    rows, width = query_here.shape
    depth = key_here.shape[1]
    heads = width // depth
    slot = 2 * rows // count
    copies = []

    def leave(here, out):
        copies.append(pltpu.make_async_copy(here, out, sems.at[len(copies)]))
        copies[-1].start()

    def taken(first, size, pieces):
        return jnp.concatenate(
            [
                jnp.concatenate(
                    [ref[first + n * size : first + (n + 1) * size, :] for n in range(pieces)],
                    axis=1,
                )
                for ref in ins
            ],
            axis=0,
        )

    query_here[...] = contract(query_spread[...], taken(0, slot, heads), 1, 0)
    leave(query_here, query_out)
    both = contract(key_spread[...], taken(heads * slot, rows, 2), 1, 0)
    for n, (here, out) in enumerate(((key_here, key_out), (value_here, value_out))):
        here[...] = both[:, n * depth : (n + 1) * depth]
        leave(here, out)
    for copy in copies:
        copy.wait()


def near_plan(doc_lengths, owners, queries, key_head_rows, value_head_rows, forward_out, grad_out):
    count = lax.axis_size("ctx")
    rows, width = queries.shape
    depth = key_head_rows.shape[1]
    heads = width // depth
    bf16, f32 = jnp.bfloat16, jnp.float32
    columns = heads * rows
    halo = count // 2
    slot = 2 * rows // count
    whole = pl.BlockSpec(memory_space=pltpu.VMEM)
    params = pltpu.CompilerParams(vmem_limit_bytes=40 * 1024 * 1024)

    mark = lax.broadcasted_iota(jnp.int32, (2 * rows + META, rows), 0) - 2 * rows
    packet = jnp.where(
        mark < 0,
        jnp.pad(jnp.concatenate([key_head_rows, value_head_rows], axis=0), ((0, META), (0, 0))),
        (owners[None, :] == mark).astype(bf16),
    )
    near = [
        lax.ppermute(packet, "ctx", [(i, (i + back) % count) for i in range(count)])
        for back in range(1, halo + 1)
    ]
    block_shapes = [jax.ShapeDtypeStruct((rows, columns), f32)] * 2
    row_shape = jax.ShapeDtypeStruct((8, columns), f32)
    target_shape = jax.ShapeDtypeStruct((count * rows, rows), bf16)
    filled_shape = jax.ShapeDtypeStruct((8, rows), f32)
    query_rows, grad_rows, raised, change, row, spread, target, filled = pl.pallas_call(
        functools.partial(own_kernel, count, doc_lengths.shape[0]),
        out_shape=[jax.ShapeDtypeStruct((columns, depth), bf16)] * 2
        + block_shapes
        + [row_shape, jax.ShapeDtypeStruct((count * slot, rows), bf16), target_shape, filled_shape],
        in_specs=[pl.BlockSpec(memory_space=pltpu.SMEM)] + [whole] * 4,
        out_specs=[whole] * 8,
        compiler_params=params,
    )(doc_lengths, packet, queries, grad_out, forward_out)
    raised, change, target = [raised], [change], [target]
    for back in range(1, halo):
        found = pl.pallas_call(
            functools.partial(step_kernel, count, back),
            out_shape=block_shapes + [row_shape, target_shape, filled_shape],
            in_specs=[whole] * 5,
            out_specs=[whole] * 5,
            compiler_params=params,
        )(query_rows, grad_rows, row, filled, near[back - 1])
        raised.append(found[0])
        change.append(found[1])
        row = found[2]
        target.append(found[3])
        filled = found[4]
    sent = pl.pallas_call(
        functools.partial(attend_kernel, count, halo),
        out_shape=[jax.ShapeDtypeStruct((heads * slot + 2 * rows, depth), bf16)] * count,
        in_specs=[whole] * (6 + 4 * halo),
        out_specs=[whole] * count,
        compiler_params=params,
    )(query_rows, grad_rows, row, filled, spread, *raised, *change, *target, packet, *near)
    received = [sent[0]] + [
        lax.ppermute(sent[k], "ctx", [(i, i ^ k) for i in range(count)]) for k in range(1, count)
    ]
    spreads = pl.pallas_call(
        functools.partial(order_kernel, count, halo),
        out_shape=[
            jax.ShapeDtypeStruct((rows, count * slot), bf16),
            jax.ShapeDtypeStruct((rows, count * rows), bf16),
        ],
        in_specs=[pl.BlockSpec(memory_space=pl.ANY)] + [whole] * (1 + halo),
        out_specs=[whole] * 2,
        compiler_params=params,
    )(received[-1], packet, *near)
    return pl.pallas_call(
        functools.partial(place_kernel, count),
        out_shape=[
            jax.ShapeDtypeStruct((rows, width), f32),
            jax.ShapeDtypeStruct((rows, depth), f32),
            jax.ShapeDtypeStruct((rows, depth), f32),
        ],
        in_specs=[whole] * (2 + count),
        out_specs=[pl.BlockSpec(memory_space=pl.ANY)] * 3,
        scratch_shapes=[
            pltpu.VMEM((rows, width), f32),
            pltpu.VMEM((rows, depth), f32),
            pltpu.VMEM((rows, depth), f32),
            pltpu.SemaphoreType.DMA((3,)),
        ],
        compiler_params=params,
    )(*spreads, *received)


def per_device(*args):
    if lax.axis_size("ctx") in (2, 4):
        return near_plan(*args)
    return ring_plan(*args)


def solution(mesh):
    return jax.shard_map(
        per_device,
        mesh=mesh,
        in_specs=(
            P("groups"),
            P(("groups", "ctx")),
            P(("groups", "ctx"), "head"),
            P(("groups", "ctx"), "head"),
            P(("groups", "ctx"), "head"),
            P(("groups", "ctx"), "head"),
            P(("groups", "ctx"), "head"),
        ),
        out_specs=(
            P(("groups", "ctx"), "head"),
            P(("groups", "ctx"), "head"),
            P(("groups", "ctx"), "head"),
        ),
        check_vma=False,
    )
```

```python
import functools
import math

import jax
import jax.numpy as jnp
from jax import lax
from jax.experimental import pallas as pl
from jax.experimental.pallas import tpu as pltpu
from jax.sharding import PartitionSpec as P

HEAD_WIDTH = 128
GROUP = 4


NEG = -1e30
BLOCK = 512


def shifted(value, axis, by):
    count = lax.axis_size(axis)
    return lax.ppermute(value, axis, [(i, (i + by) % count) for i in range(count)])


def document_of(positions, doc_lengths):
    ends = jnp.cumsum(doc_lengths)
    return jnp.sum((positions[:, None] >= ends[None, :]).astype(jnp.int32), axis=1)


def allowed_between(query_positions, query_docs, key_positions, key_docs):
    return (query_docs[:, None] == key_docs[None, :]) & (
        key_positions[None, :] <= query_positions[:, None]
    )


def head_rows(matrix, group_size, head_dim):
    row_count = matrix.shape[0]
    return matrix.reshape(row_count * group_size, head_dim)


def block_scores(query_flat, key_head, row_count, group_size, head_dim):
    scores = lax.dot_general(
        query_flat, key_head, (((1,), (1,)), ((), ())), preferred_element_type=jnp.float32
    )
    return (scores * (1.0 / math.sqrt(head_dim))).reshape(row_count, group_size, key_head.shape[0])


def update_stats(running, query_local, key_block, allowed, group_size, head_dim):
    running_max, totals = running
    row_count = query_local.shape[0]
    scores = block_scores(
        head_rows(query_local, group_size, head_dim), key_block, row_count, group_size, head_dim
    )
    masked = jnp.where(allowed[:, None, :], scores, NEG)
    new_max = jnp.maximum(running_max, jnp.max(masked, axis=2))
    weights = jnp.where(allowed[:, None, :], jnp.exp(masked - new_max[:, :, None]), 0.0)
    new_totals = [totals * jnp.exp(running_max - new_max) + jnp.sum(weights, axis=2)]
    new_maxima = [new_max]
    return (jnp.concatenate(new_maxima, axis=1), jnp.concatenate(new_totals, axis=1))


def backward_block(
    query_local,
    grad_local,
    log_norm,
    row_delta,
    key_block,
    value_block,
    allowed,
    group_size,
    head_dim,
):
    row_count = query_local.shape[0]
    query_flat = head_rows(query_local, group_size, head_dim)
    grad_flat = head_rows(grad_local, group_size, head_dim)
    scores = block_scores(query_flat, key_block, row_count, group_size, head_dim)
    masked = jnp.where(allowed[:, None, :], scores, NEG)
    weights = jnp.exp(masked - log_norm[:, 0:group_size, None])
    grad_weights = lax.dot_general(
        grad_flat, value_block, (((1,), (1,)), ((), ())), preferred_element_type=jnp.float32
    ).reshape(row_count, group_size, -1)
    grad_scores = weights * (grad_weights - row_delta[:, 0:group_size, None])
    rounded_weights = weights.astype(jnp.bfloat16).reshape(row_count * group_size, -1)
    rounded_grads = grad_scores.astype(jnp.bfloat16).reshape(row_count * group_size, -1)
    value_parts = [
        lax.dot_general(
            rounded_weights, grad_flat, (((0,), (0,)), ((), ())), preferred_element_type=jnp.float32
        )
    ]
    key_parts = [
        lax.dot_general(
            rounded_grads, query_flat, (((0,), (0,)), ((), ())), preferred_element_type=jnp.float32
        )
    ]
    query_parts = [
        jnp.dot(rounded_grads, key_block, preferred_element_type=jnp.float32).reshape(
            row_count, group_size * head_dim
        )
    ]
    return (
        jnp.concatenate(query_parts, axis=1),
        jnp.concatenate(key_parts, axis=1),
        jnp.concatenate(value_parts, axis=1),
    )


def ring_plan(doc_lengths, owners, queries, key_head_rows, value_head_rows, forward_out, grad_out):
    context_size = lax.axis_size("ctx")
    context_index = lax.axis_index("ctx")
    row_count = queries.shape[0]
    head_dim = HEAD_WIDTH
    group_size = GROUP
    query_heads = queries.shape[1] // head_dim
    slot_count = 2 * row_count // context_size
    everyone = lax.all_gather(owners, "ctx", axis=0, tiled=True)
    row_arrangement = jnp.argsort(everyone, stable=True)
    layout_docs = document_of(row_arrangement, doc_lengths)
    own_positions = lax.dynamic_slice_in_dim(
        row_arrangement, context_index * row_count, row_count, 0
    )
    own_documents = lax.dynamic_slice_in_dim(layout_docs, context_index * row_count, row_count, 0)
    owner_ids = jnp.arange(context_size, dtype=jnp.int32)
    owner_hot = (owners[:, None] == owner_ids[None, :]).astype(jnp.int32)
    earlier = jnp.cumsum(owner_hot, axis=0) - owner_hot
    rank_within = jnp.sum(earlier * owner_hot, axis=1)
    slot_rows = owners * slot_count + rank_within

    def packed(matrix):
        empty = jnp.zeros((context_size * slot_count,) + matrix.shape[1:], matrix.dtype)
        return empty.at[slot_rows].set(matrix)

    owner_grid = everyone.reshape(context_size, row_count)
    counts = jnp.sum((owner_grid == context_index).astype(jnp.int32), axis=1)
    count_ends = jnp.cumsum(counts)
    starts = count_ends - counts
    wanted = jnp.arange(row_count, dtype=jnp.int32)
    source = jnp.sum((wanted[:, None] >= count_ends[None, :]).astype(jnp.int32), axis=1)
    source_hot = (source[:, None] == owner_ids[None, :]).astype(jnp.int32)
    take_rows = source * slot_count + wanted - jnp.sum(source_hot * starts[None, :], axis=1)

    def compact(received):
        return jnp.take(received, take_rows, axis=0)

    local_delta = jnp.sum(
        (grad_out.astype(jnp.float32) * forward_out.astype(jnp.float32)).reshape(
            row_count, query_heads, head_dim
        ),
        axis=2,
    )
    arrived = (
        lax.all_to_all(packed(queries), "ctx", split_axis=0, concat_axis=0, tiled=True),
        lax.all_to_all(packed(key_head_rows), "ctx", split_axis=0, concat_axis=0, tiled=True),
        lax.all_to_all(packed(value_head_rows), "ctx", split_axis=0, concat_axis=0, tiled=True),
        lax.all_to_all(packed(grad_out), "ctx", split_axis=0, concat_axis=0, tiled=True),
    )
    query_local, key_local, value_local, grad_local = [compact(received) for received in arrived]
    row_delta = compact(
        lax.all_to_all(packed(local_delta), "ctx", split_axis=0, concat_axis=0, tiled=True)
    )

    def fold_keys(running, shard_rows, first_row):
        piece_count = shard_rows.shape[0]
        step_rows = math.gcd(piece_count, BLOCK) if piece_count > BLOCK else piece_count

        def one_block(partial_value, block_index):
            offset = first_row + block_index * step_rows
            key_block = lax.dynamic_slice_in_dim(shard_rows, block_index * step_rows, step_rows, 0)
            key_positions = lax.dynamic_slice_in_dim(row_arrangement, offset, step_rows, 0)
            key_docs = lax.dynamic_slice_in_dim(layout_docs, offset, step_rows, 0)
            allowed = allowed_between(own_positions, own_documents, key_positions, key_docs)
            return (
                update_stats(partial_value, query_local, key_block, allowed, group_size, head_dim),
                None,
            )

        if piece_count == step_rows:
            return one_block(running, 0)[0]
        return lax.scan(one_block, running, jnp.arange(piece_count // step_rows, dtype=jnp.int32))[
            0
        ]

    start_stats = (
        jnp.full((row_count, query_heads), NEG, jnp.float32),
        jnp.zeros((row_count, query_heads), jnp.float32),
    )
    top_scores, totals = fold_keys(
        start_stats, lax.all_gather(key_local, "ctx", axis=0, tiled=True), jnp.int32(0)
    )
    log_norm = top_scores + jnp.log(totals)

    def block_meta(owner_index, offset, size):
        first = owner_index * row_count + offset
        key_positions = lax.dynamic_slice_in_dim(row_arrangement, first, size, 0)
        key_docs = lax.dynamic_slice_in_dim(layout_docs, first, size, 0)
        return (key_positions, key_docs)

    query_zero = jnp.zeros(query_local.shape, jnp.float32)
    key_zero = jnp.zeros(key_local.shape, jnp.float32)

    def one_turn(turn_index, loop_state):
        key_moving, value_moving, key_grad, value_grad, query_grad = loop_state
        owner_index = (context_index - turn_index) % context_size
        key_positions, key_docs = block_meta(owner_index, 0, row_count)
        allowed = allowed_between(own_positions, own_documents, key_positions, key_docs)
        query_part, key_part, value_part = backward_block(
            query_local,
            grad_local,
            log_norm,
            row_delta,
            key_moving,
            value_moving,
            allowed,
            group_size,
            head_dim,
        )
        return (
            key_moving,
            value_moving,
            key_grad + key_part,
            value_grad + value_part,
            query_grad + query_part,
        )

    def moved_turn(turn_index, loop_state):
        key_moving, value_moving, key_grad, value_grad, query_grad = loop_state
        key_moving, value_moving = shifted((key_moving, value_moving), "ctx", 1)
        key_grad, value_grad = shifted((key_grad, value_grad), "ctx", 1)
        return one_turn(turn_index, (key_moving, value_moving, key_grad, value_grad, query_grad))

    loop_state = one_turn(0, (key_local, value_local, key_zero, key_zero, query_zero))
    loop_state = lax.fori_loop(1, context_size, moved_turn, loop_state)
    key_grad, value_grad = shifted((loop_state[2], loop_state[3]), "ctx", 1)
    query_grad = loop_state[4]
    inverse_root = 1.0 / math.sqrt(head_dim)
    return (query_grad * inverse_root, key_grad * inverse_root, value_grad)


META = 8


def contract(left, right, left_dim, right_dim, **kw):
    return lax.dot_general(
        left,
        right,
        (((left_dim,), (right_dim,)), ((), ())),
        preferred_element_type=jnp.float32,
        **kw,
    )


def one_hot(row_count, target):
    places = lax.broadcasted_iota(jnp.int32, (row_count, target.shape[1]), 0)
    return jnp.where(places == target, 1.0, 0.0).astype(jnp.bfloat16)


def side_by_side(stack, heads):
    rows = stack.shape[0] // heads
    return jnp.concatenate([stack[h * rows : (h + 1) * rows, :] for h in range(heads)], axis=1)


def end_to_end(matrix, heads):
    width = matrix.shape[1] // heads
    return jnp.concatenate([matrix[:, h * width : (h + 1) * width] for h in range(heads)], axis=0)


def runs_of(hot):
    count, rows = hot.shape
    counts = jnp.sum(hot, axis=1, keepdims=True)
    owner = jnp.zeros((1, rows), jnp.int32)
    earlier = jnp.zeros((1, rows), jnp.float32)
    for p in range(count):
        mine = hot[p : p + 1, :] > 0.0
        owner = jnp.where(mine, p, owner)
        for less in range(p):
            earlier = earlier + jnp.where(mine, counts[less : less + 1, :], 0.0)
    lane = lax.broadcasted_iota(jnp.int32, (1, rows), 1)
    return owner, counts, lane - earlier.astype(jnp.int32)


def own_kernel(
    count,
    docs,
    doc_ref,
    packet_ref,
    query_ref,
    grad_ref,
    saved_ref,
    query_out,
    grad_out,
    raised_out,
    change_out,
    row_out,
    spread_out,
    target_out,
    filled_out,
):
    rows, width = query_ref.shape
    depth = packet_ref.shape[1]
    heads = width // depth
    slot = 2 * rows // count
    index = lax.axis_index("ctx")
    lane = lax.broadcasted_iota(jnp.int32, (1, rows), 1)
    position = index * rows + lane
    first = jnp.zeros((1, rows), jnp.int32)
    end = jnp.int32(0)
    for d in range(docs):
        end = end + doc_ref[d]
        first = jnp.where(end <= position, end, first)
    key_position = index * rows + lax.broadcasted_iota(jnp.int32, (rows, rows), 0)
    allowed = (key_position >= first) & (key_position <= position)
    allowed = jnp.concatenate([allowed] * heads, axis=1)

    queries = end_to_end(query_ref[...], heads)
    query_out[...] = queries
    scores = contract(packet_ref[0:rows, :], queries, 1, 1) * (1.0 / math.sqrt(depth))
    scores = jnp.where(allowed, scores, NEG)
    top = jnp.max(scores, axis=0, keepdims=True)
    raised = jnp.exp(scores - top)
    raised_out[...] = raised
    grads = end_to_end(grad_ref[...], heads)
    grad_out[...] = grads
    product = grads.astype(jnp.float32) * end_to_end(saved_ref[...], heads).astype(jnp.float32)
    delta = contract(
        jnp.ones((8, depth), jnp.float32), product, 1, 1, precision=lax.Precision.HIGHEST
    )[0:1, :]
    change_out[...] = contract(packet_ref[rows : 2 * rows, :], grads, 1, 1) - delta
    row_out[0:1, :] = delta
    row_out[1:2, :] = top
    row_out[2:3, :] = jnp.sum(raised, axis=0, keepdims=True)
    row_out[3:4, :] = jnp.concatenate([first.astype(jnp.float32)] * heads, axis=1)
    row_out[4:8, :] = jnp.ones((4, width), jnp.float32)
    owner, counts, rank = runs_of(packet_ref[2 * rows : 2 * rows + count, :].astype(jnp.float32))
    spread_out[...] = one_hot(count * slot, (owner ^ index) * slot + rank)
    target_out[...] = one_hot(count * rows, (owner ^ index) * rows + rank)
    filled_out[0:count, :] = jnp.broadcast_to(counts, (count, rows))
    filled_out[count:, :] = jnp.zeros((8 - count, rows), jnp.float32)


def fold(count, back, packet, queries, grads, row, filled):
    rows = packet.shape[1]
    index = lax.axis_index("ctx")
    delta, top, total = (row[n : n + 1, :] for n in range(3))
    first = row[3:4, :].astype(jnp.int32)
    position = (index - back) * rows + lax.broadcasted_iota(jnp.int32, (rows, row.shape[1]), 0)
    scores = contract(packet[0:rows, :], queries, 1, 1) * (1.0 / math.sqrt(queries.shape[1]))
    scores = jnp.where(position >= first, scores, NEG)
    new_top = jnp.maximum(top, jnp.max(scores, axis=0, keepdims=True))
    raised = jnp.exp(scores - new_top)
    shrink = jnp.exp(top - new_top)
    total = total * shrink + jnp.sum(raised, axis=0, keepdims=True)
    change = contract(packet[rows : 2 * rows, :], grads, 1, 1) - delta
    factors = row[4:8, :] * jnp.where(
        lax.broadcasted_iota(jnp.int32, (4, row.shape[1]), 0) < back, shrink, 1.0
    )
    owner, counts, rank = runs_of(packet[2 * rows : 2 * rows + count, :].astype(jnp.float32))
    base = jnp.zeros((1, rows), jnp.float32)
    for p in range(count):
        base = base + jnp.where(owner == p, filled[p : p + 1, :], 0.0)
    inside = index >= back
    target = jnp.where(inside, (owner ^ index) * rows + base.astype(jnp.int32) + rank, -1)
    filled = filled[0:count, :] + jnp.where(inside, counts, 0.0)
    return raised, change, (new_top, total, factors), one_hot(count * rows, target), filled


def step_kernel(count, back, *refs):
    query_ref, grad_ref, row_ref, filled_ref, packet_ref = refs[:5]
    raised_out, change_out, row_out, target_out, filled_out = refs[5:]
    raised, change, (top, total, factors), target, filled = fold(
        count, back, packet_ref, query_ref[...], grad_ref[...], row_ref, filled_ref
    )
    raised_out[...] = raised
    change_out[...] = change
    row_out[0:1, :] = row_ref[0:1, :]
    row_out[1:2, :] = top
    row_out[2:3, :] = total
    row_out[3:4, :] = row_ref[3:4, :]
    row_out[4:8, :] = factors
    target_out[...] = target
    filled_out[0:count, :] = filled
    filled_out[count:, :] = jnp.zeros_like(filled_out[count:, :])


def attend_kernel(count, halo, *refs):
    query_ref, grad_ref, row_ref, filled_ref, spread_ref, given_ref = refs[:6]
    raised_refs = refs[6 : 6 + halo]
    change_refs = refs[6 + halo : 6 + 2 * halo]
    target_refs = refs[6 + 2 * halo : 6 + 3 * halo]
    packets = refs[6 + 3 * halo : 7 + 4 * halo]
    outs = refs[7 + 4 * halo :]
    rows = packets[0].shape[1]
    depth = query_ref.shape[1]
    heads = query_ref.shape[0] // rows
    slot = 2 * rows // count
    scale = 1.0 / math.sqrt(depth)
    index = lax.axis_index("ctx")
    queries = query_ref[...]
    grads = grad_ref[...]
    raised, change, (_, total, factors), target, _ = fold(
        count, halo, packets[halo], queries, grads, row_ref, filled_ref
    )
    factors = factors * (1.0 / total)
    weights = []
    changes = []
    for block in range(halo + 1):
        mine = raised if block == halo else raised_refs[block][...]
        mine = mine * factors[block : block + 1, :]
        weights.append(mine.astype(jnp.bfloat16))
        mine = mine * (change if block == halo else change_refs[block][...])
        changes.append(mine.astype(jnp.bfloat16))
    weights = jnp.concatenate(weights, axis=0)
    changes = jnp.concatenate(changes, axis=0)
    keys = jnp.concatenate([packet[0:rows, :] for packet in packets], axis=0)
    query_grad = (contract(keys, changes, 0, 0) * scale).astype(jnp.bfloat16)
    key_parts = contract(changes, queries, 1, 0) * scale
    value_parts = contract(weights, grads, 1, 0)
    parts = jnp.concatenate([key_parts, value_parts], axis=1).astype(jnp.bfloat16)

    query_slots = contract(spread_ref[...], end_to_end(query_grad, heads), 1, 1)
    query_slots = query_slots.astype(jnp.bfloat16)
    spread = jnp.concatenate([ref[...] for ref in target_refs] + [target], axis=1)
    part_slots = contract(spread, parts, 1, 0).astype(jnp.bfloat16)
    at = heads * slot
    for k in range(count):
        out = outs[k]
        for h in range(heads):
            out[h * slot : (h + 1) * slot, :] = query_slots[
                k * slot : (k + 1) * slot, h * depth : (h + 1) * depth
            ]
        for n in range(2):
            out[at + n * rows : at + (n + 1) * rows, :] = part_slots[
                k * rows : (k + 1) * rows, n * depth : (n + 1) * depth
            ]
        given = jnp.zeros((1, rows), jnp.float32)
        for p in range(count):
            given = jnp.where((index ^ k) == p, given_ref[p : p + 1, :], given)
        out[at + 2 * rows :, :] = jnp.broadcast_to(given[:, :depth], (META, depth)).astype(
            jnp.bfloat16
        )


def order_kernel(count, halo, last, packet_ref, *refs):
    ins = refs[:-2]
    query_out, key_out = refs[-2:]
    rows = query_out.shape[0]
    index = lax.axis_index("ctx")
    hot = packet_ref[2 * rows : 2 * rows + count, :].astype(jnp.float32)
    counts = jnp.sum(hot, axis=1, keepdims=True)
    mine = jnp.zeros((1, 1), jnp.float32)
    for p in range(count):
        mine = jnp.where(index == p, counts[p : p + 1, :], mine)
    given = [mine.astype(jnp.int32)]
    for ref in ins[::-1]:
        at = ref.shape[0] - META
        given.append(ref[at : at + 1, 0:1].astype(jnp.float32).astype(jnp.int32))
    given.insert(last, rows - sum(given))

    def placement(size, halo):
        lane = lax.broadcasted_iota(jnp.int32, (1, count * size), 1)
        target = jnp.full(lane.shape, -1, jnp.int32)
        for k in range(count):
            step = lane - k * size
            for back in range(halo + 1):
                block = (index ^ k) - back
                start = jnp.zeros((1, 1), jnp.int32)
                length = jnp.zeros((1, 1), jnp.int32)
                for n in range(count):
                    start = start + jnp.where((index ^ n) < block, given[n], 0)
                    length = length + jnp.where((index ^ n) == block, given[n], 0)
                target = jnp.where((step >= 0) & (step < length), start + step, target)
                step = step - length
        return one_hot(rows, target)

    query_out[...] = placement(2 * rows // count, 0)
    key_out[...] = placement(rows, halo)


def place_kernel(count, query_spread, key_spread, *refs):
    ins = refs[:count]
    query_out, key_out, value_out = refs[count : count + 3]
    query_here, key_here, value_here, sems = refs[count + 3 :]
    rows, width = query_here.shape
    depth = key_here.shape[1]
    heads = width // depth
    slot = 2 * rows // count
    copies = []

    def leave(here, out):
        copies.append(pltpu.make_async_copy(here, out, sems.at[len(copies)]))
        copies[-1].start()

    def taken(first, size, pieces):
        return jnp.concatenate(
            [
                jnp.concatenate(
                    [ref[first + n * size : first + (n + 1) * size, :] for n in range(pieces)],
                    axis=1,
                )
                for ref in ins
            ],
            axis=0,
        )

    query_here[...] = contract(query_spread[...], taken(0, slot, heads), 1, 0)
    leave(query_here, query_out)
    both = contract(key_spread[...], taken(heads * slot, rows, 2), 1, 0)
    for n, (here, out) in enumerate(((key_here, key_out), (value_here, value_out))):
        here[...] = both[:, n * depth : (n + 1) * depth]
        leave(here, out)
    for copy in copies:
        copy.wait()


def near_plan(doc_lengths, owners, queries, key_head_rows, value_head_rows, forward_out, grad_out):
    count = lax.axis_size("ctx")
    rows, width = queries.shape
    depth = key_head_rows.shape[1]
    heads = width // depth
    bf16, f32 = jnp.bfloat16, jnp.float32
    columns = heads * rows
    halo = count // 2
    slot = 2 * rows // count
    whole = pl.BlockSpec(memory_space=pltpu.VMEM)
    params = pltpu.CompilerParams(vmem_limit_bytes=40 * 1024 * 1024)

    mark = lax.broadcasted_iota(jnp.int32, (2 * rows + META, rows), 0) - 2 * rows
    packet = jnp.where(
        mark < 0,
        jnp.pad(jnp.concatenate([key_head_rows, value_head_rows], axis=0), ((0, META), (0, 0))),
        (owners[None, :] == mark).astype(bf16),
    )
    near = [lax.ppermute(packet, "ctx", [(i, (i + 1) % count) for i in range(count)])]
    block_shapes = [jax.ShapeDtypeStruct((rows, columns), f32)] * 2
    row_shape = jax.ShapeDtypeStruct((8, columns), f32)
    target_shape = jax.ShapeDtypeStruct((count * rows, rows), bf16)
    filled_shape = jax.ShapeDtypeStruct((8, rows), f32)

    def own_work():
        return pl.pallas_call(
            functools.partial(own_kernel, count, doc_lengths.shape[0]),
            out_shape=[jax.ShapeDtypeStruct((columns, depth), bf16)] * 2
            + block_shapes
            + [row_shape, jax.ShapeDtypeStruct((count * slot, rows), bf16), target_shape, filled_shape],
            in_specs=[pl.BlockSpec(memory_space=pltpu.SMEM)] + [whole] * 4,
            out_specs=[whole] * 8,
            compiler_params=params,
        )(doc_lengths, packet, queries, grad_out, forward_out)

    if halo == 1:
        own = own_work()
    else:
        order = jnp.arange(doc_lengths.shape[0], dtype=jnp.int32)
        ends = jnp.sum(
            jnp.where(order[:, None] <= order[None, :], doc_lengths[:, None], 0), axis=0
        )
        odd = jnp.sum(((ends >= 2 * rows) & (ends <= 3 * rows)).astype(jnp.int32)) == 0

        def far_and_own(part):
            pairs = [(i, (i + 2) % count if i % 2 == part else i) for i in range(count)]
            return lambda: (lax.ppermute(packet, "ctx", pairs), *own_work())

        far, *own = lax.cond(odd, far_and_own(1), far_and_own(0))
        near.append(far)
    query_rows, grad_rows, raised, change, row, spread, target, filled = own
    raised, change, target, given = [raised], [change], [target], filled
    for back in range(1, halo):
        found = pl.pallas_call(
            functools.partial(step_kernel, count, back),
            out_shape=block_shapes + [row_shape, target_shape, filled_shape],
            in_specs=[whole] * 5,
            out_specs=[whole] * 5,
            compiler_params=params,
        )(query_rows, grad_rows, row, filled, near[back - 1])
        raised.append(found[0])
        change.append(found[1])
        row = found[2]
        target.append(found[3])
        filled = found[4]
    sent = pl.pallas_call(
        functools.partial(attend_kernel, count, halo),
        out_shape=[jax.ShapeDtypeStruct((heads * slot + 2 * rows + META, depth), bf16)] * count,
        in_specs=[whole] * (7 + 4 * halo),
        out_specs=[whole] * count,
        compiler_params=params,
    )(query_rows, grad_rows, row, filled, spread, given, *raised, *change, *target, packet, *near)
    received = [sent[0]] + [
        lax.ppermute(sent[k], "ctx", [(i, i ^ k) for i in range(count)]) for k in range(1, count)
    ]
    last = count // 2
    early = [received[k] for k in range(count - 1, 0, -1) if k != last]
    spreads = pl.pallas_call(
        functools.partial(order_kernel, count, halo, last),
        out_shape=[
            jax.ShapeDtypeStruct((rows, count * slot), bf16),
            jax.ShapeDtypeStruct((rows, count * rows), bf16),
        ],
        in_specs=[whole] * (1 + len(early)),
        out_specs=[whole] * 2,
        compiler_params=params,
    )(packet, *early)
    return pl.pallas_call(
        functools.partial(place_kernel, count),
        out_shape=[
            jax.ShapeDtypeStruct((rows, width), f32),
            jax.ShapeDtypeStruct((rows, depth), f32),
            jax.ShapeDtypeStruct((rows, depth), f32),
        ],
        in_specs=[whole] * (2 + count),
        out_specs=[pl.BlockSpec(memory_space=pl.ANY)] * 3,
        scratch_shapes=[
            pltpu.VMEM((rows, width), f32),
            pltpu.VMEM((rows, depth), f32),
            pltpu.VMEM((rows, depth), f32),
            pltpu.SemaphoreType.DMA((3,)),
        ],
        compiler_params=params,
    )(*spreads, *received)


def per_device(*args):
    if lax.axis_size("ctx") in (2, 4):
        return near_plan(*args)
    return ring_plan(*args)


def solution(mesh):
    return jax.shard_map(
        per_device,
        mesh=mesh,
        in_specs=(
            P("groups"),
            P(("groups", "ctx")),
            P(("groups", "ctx"), "head"),
            P(("groups", "ctx"), "head"),
            P(("groups", "ctx"), "head"),
            P(("groups", "ctx"), "head"),
            P(("groups", "ctx"), "head"),
        ),
        out_specs=(
            P(("groups", "ctx"), "head"),
            P(("groups", "ctx"), "head"),
            P(("groups", "ctx"), "head"),
        ),
        check_vma=False,
    )
```

```python
import functools
import math

import jax
import jax.numpy as jnp
from jax import lax
from jax.experimental import pallas as pl
from jax.experimental.pallas import tpu as pltpu
from jax.sharding import PartitionSpec as P

HEAD_WIDTH = 128
GROUP = 4


NEG = -1e30
BLOCK = 512


def shifted(value, axis, by):
    count = lax.axis_size(axis)
    return lax.ppermute(value, axis, [(i, (i + by) % count) for i in range(count)])


def document_of(positions, doc_lengths):
    ends = jnp.cumsum(doc_lengths)
    return jnp.sum((positions[:, None] >= ends[None, :]).astype(jnp.int32), axis=1)


def allowed_between(query_positions, query_docs, key_positions, key_docs):
    return (query_docs[:, None] == key_docs[None, :]) & (
        key_positions[None, :] <= query_positions[:, None]
    )


def head_rows(matrix, group_size, head_dim):
    row_count = matrix.shape[0]
    return matrix.reshape(row_count * group_size, head_dim)


def block_scores(query_flat, key_head, row_count, group_size, head_dim):
    scores = lax.dot_general(
        query_flat, key_head, (((1,), (1,)), ((), ())), preferred_element_type=jnp.float32
    )
    return (scores * (1.0 / math.sqrt(head_dim))).reshape(row_count, group_size, key_head.shape[0])


def update_stats(running, query_local, key_block, allowed, group_size, head_dim):
    running_max, totals = running
    row_count = query_local.shape[0]
    scores = block_scores(
        head_rows(query_local, group_size, head_dim), key_block, row_count, group_size, head_dim
    )
    masked = jnp.where(allowed[:, None, :], scores, NEG)
    new_max = jnp.maximum(running_max, jnp.max(masked, axis=2))
    weights = jnp.where(allowed[:, None, :], jnp.exp(masked - new_max[:, :, None]), 0.0)
    new_totals = [totals * jnp.exp(running_max - new_max) + jnp.sum(weights, axis=2)]
    new_maxima = [new_max]
    return (jnp.concatenate(new_maxima, axis=1), jnp.concatenate(new_totals, axis=1))


def backward_block(
    query_local,
    grad_local,
    log_norm,
    row_delta,
    key_block,
    value_block,
    allowed,
    group_size,
    head_dim,
):
    row_count = query_local.shape[0]
    query_flat = head_rows(query_local, group_size, head_dim)
    grad_flat = head_rows(grad_local, group_size, head_dim)
    scores = block_scores(query_flat, key_block, row_count, group_size, head_dim)
    masked = jnp.where(allowed[:, None, :], scores, NEG)
    weights = jnp.exp(masked - log_norm[:, 0:group_size, None])
    grad_weights = lax.dot_general(
        grad_flat, value_block, (((1,), (1,)), ((), ())), preferred_element_type=jnp.float32
    ).reshape(row_count, group_size, -1)
    grad_scores = weights * (grad_weights - row_delta[:, 0:group_size, None])
    rounded_weights = weights.astype(jnp.bfloat16).reshape(row_count * group_size, -1)
    rounded_grads = grad_scores.astype(jnp.bfloat16).reshape(row_count * group_size, -1)
    value_parts = [
        lax.dot_general(
            rounded_weights, grad_flat, (((0,), (0,)), ((), ())), preferred_element_type=jnp.float32
        )
    ]
    key_parts = [
        lax.dot_general(
            rounded_grads, query_flat, (((0,), (0,)), ((), ())), preferred_element_type=jnp.float32
        )
    ]
    query_parts = [
        jnp.dot(rounded_grads, key_block, preferred_element_type=jnp.float32).reshape(
            row_count, group_size * head_dim
        )
    ]
    return (
        jnp.concatenate(query_parts, axis=1),
        jnp.concatenate(key_parts, axis=1),
        jnp.concatenate(value_parts, axis=1),
    )


def ring_plan(doc_lengths, owners, queries, key_head_rows, value_head_rows, forward_out, grad_out):
    context_size = lax.axis_size("ctx")
    context_index = lax.axis_index("ctx")
    row_count = queries.shape[0]
    head_dim = HEAD_WIDTH
    group_size = GROUP
    query_heads = queries.shape[1] // head_dim
    slot_count = 2 * row_count // context_size
    everyone = lax.all_gather(owners, "ctx", axis=0, tiled=True)
    row_arrangement = jnp.argsort(everyone, stable=True)
    layout_docs = document_of(row_arrangement, doc_lengths)
    own_positions = lax.dynamic_slice_in_dim(
        row_arrangement, context_index * row_count, row_count, 0
    )
    own_documents = lax.dynamic_slice_in_dim(layout_docs, context_index * row_count, row_count, 0)
    owner_ids = jnp.arange(context_size, dtype=jnp.int32)
    owner_hot = (owners[:, None] == owner_ids[None, :]).astype(jnp.int32)
    earlier = jnp.cumsum(owner_hot, axis=0) - owner_hot
    rank_within = jnp.sum(earlier * owner_hot, axis=1)
    slot_rows = owners * slot_count + rank_within

    def packed(matrix):
        empty = jnp.zeros((context_size * slot_count,) + matrix.shape[1:], matrix.dtype)
        return empty.at[slot_rows].set(matrix)

    owner_grid = everyone.reshape(context_size, row_count)
    counts = jnp.sum((owner_grid == context_index).astype(jnp.int32), axis=1)
    count_ends = jnp.cumsum(counts)
    starts = count_ends - counts
    wanted = jnp.arange(row_count, dtype=jnp.int32)
    source = jnp.sum((wanted[:, None] >= count_ends[None, :]).astype(jnp.int32), axis=1)
    source_hot = (source[:, None] == owner_ids[None, :]).astype(jnp.int32)
    take_rows = source * slot_count + wanted - jnp.sum(source_hot * starts[None, :], axis=1)

    def compact(received):
        return jnp.take(received, take_rows, axis=0)

    local_delta = jnp.sum(
        (grad_out.astype(jnp.float32) * forward_out.astype(jnp.float32)).reshape(
            row_count, query_heads, head_dim
        ),
        axis=2,
    )
    arrived = (
        lax.all_to_all(packed(queries), "ctx", split_axis=0, concat_axis=0, tiled=True),
        lax.all_to_all(packed(key_head_rows), "ctx", split_axis=0, concat_axis=0, tiled=True),
        lax.all_to_all(packed(value_head_rows), "ctx", split_axis=0, concat_axis=0, tiled=True),
        lax.all_to_all(packed(grad_out), "ctx", split_axis=0, concat_axis=0, tiled=True),
    )
    query_local, key_local, value_local, grad_local = [compact(received) for received in arrived]
    row_delta = compact(
        lax.all_to_all(packed(local_delta), "ctx", split_axis=0, concat_axis=0, tiled=True)
    )

    def fold_keys(running, shard_rows, first_row):
        piece_count = shard_rows.shape[0]
        step_rows = math.gcd(piece_count, BLOCK) if piece_count > BLOCK else piece_count

        def one_block(partial_value, block_index):
            offset = first_row + block_index * step_rows
            key_block = lax.dynamic_slice_in_dim(shard_rows, block_index * step_rows, step_rows, 0)
            key_positions = lax.dynamic_slice_in_dim(row_arrangement, offset, step_rows, 0)
            key_docs = lax.dynamic_slice_in_dim(layout_docs, offset, step_rows, 0)
            allowed = allowed_between(own_positions, own_documents, key_positions, key_docs)
            return (
                update_stats(partial_value, query_local, key_block, allowed, group_size, head_dim),
                None,
            )

        if piece_count == step_rows:
            return one_block(running, 0)[0]
        return lax.scan(one_block, running, jnp.arange(piece_count // step_rows, dtype=jnp.int32))[
            0
        ]

    start_stats = (
        jnp.full((row_count, query_heads), NEG, jnp.float32),
        jnp.zeros((row_count, query_heads), jnp.float32),
    )
    top_scores, totals = fold_keys(
        start_stats, lax.all_gather(key_local, "ctx", axis=0, tiled=True), jnp.int32(0)
    )
    log_norm = top_scores + jnp.log(totals)

    def block_meta(owner_index, offset, size):
        first = owner_index * row_count + offset
        key_positions = lax.dynamic_slice_in_dim(row_arrangement, first, size, 0)
        key_docs = lax.dynamic_slice_in_dim(layout_docs, first, size, 0)
        return (key_positions, key_docs)

    query_zero = jnp.zeros(query_local.shape, jnp.float32)
    key_zero = jnp.zeros(key_local.shape, jnp.float32)

    def one_turn(turn_index, loop_state):
        key_moving, value_moving, key_grad, value_grad, query_grad = loop_state
        owner_index = (context_index - turn_index) % context_size
        key_positions, key_docs = block_meta(owner_index, 0, row_count)
        allowed = allowed_between(own_positions, own_documents, key_positions, key_docs)
        query_part, key_part, value_part = backward_block(
            query_local,
            grad_local,
            log_norm,
            row_delta,
            key_moving,
            value_moving,
            allowed,
            group_size,
            head_dim,
        )
        return (
            key_moving,
            value_moving,
            key_grad + key_part,
            value_grad + value_part,
            query_grad + query_part,
        )

    def moved_turn(turn_index, loop_state):
        key_moving, value_moving, key_grad, value_grad, query_grad = loop_state
        key_moving, value_moving = shifted((key_moving, value_moving), "ctx", 1)
        key_grad, value_grad = shifted((key_grad, value_grad), "ctx", 1)
        return one_turn(turn_index, (key_moving, value_moving, key_grad, value_grad, query_grad))

    loop_state = one_turn(0, (key_local, value_local, key_zero, key_zero, query_zero))
    loop_state = lax.fori_loop(1, context_size, moved_turn, loop_state)
    key_grad, value_grad = shifted((loop_state[2], loop_state[3]), "ctx", 1)
    query_grad = loop_state[4]
    inverse_root = 1.0 / math.sqrt(head_dim)
    return (query_grad * inverse_root, key_grad * inverse_root, value_grad)


META = 8


def contract(left, right, left_dim, right_dim, **kw):
    return lax.dot_general(
        left,
        right,
        (((left_dim,), (right_dim,)), ((), ())),
        preferred_element_type=jnp.float32,
        **kw,
    )


def one_hot(row_count, target):
    places = lax.broadcasted_iota(jnp.int32, (row_count, target.shape[1]), 0)
    return jnp.where(places == target, 1.0, 0.0).astype(jnp.bfloat16)


def side_by_side(stack, heads):
    rows = stack.shape[0] // heads
    return jnp.concatenate([stack[h * rows : (h + 1) * rows, :] for h in range(heads)], axis=1)


def end_to_end(matrix, heads):
    width = matrix.shape[1] // heads
    return jnp.concatenate([matrix[:, h * width : (h + 1) * width] for h in range(heads)], axis=0)


def runs_of(hot):
    count, rows = hot.shape
    counts = jnp.sum(hot, axis=1, keepdims=True)
    owner = jnp.zeros((1, rows), jnp.int32)
    earlier = jnp.zeros((1, rows), jnp.float32)
    for p in range(count):
        mine = hot[p : p + 1, :] > 0.0
        owner = jnp.where(mine, p, owner)
        for less in range(p):
            earlier = earlier + jnp.where(mine, counts[less : less + 1, :], 0.0)
    lane = lax.broadcasted_iota(jnp.int32, (1, rows), 1)
    return owner, counts, lane - earlier.astype(jnp.int32)


def own_kernel(
    count,
    docs,
    doc_ref,
    packet_ref,
    query_ref,
    grad_ref,
    saved_ref,
    query_out,
    grad_out,
    raised_out,
    change_out,
    row_out,
    spread_out,
    target_out,
    filled_out,
):
    rows, width = query_ref.shape
    depth = packet_ref.shape[1]
    heads = width // depth
    slot = 2 * rows // count
    index = lax.axis_index("ctx")
    lane = lax.broadcasted_iota(jnp.int32, (1, rows), 1)
    position = index * rows + lane
    first = jnp.zeros((1, rows), jnp.int32)
    end = jnp.int32(0)
    for d in range(docs):
        end = end + doc_ref[d]
        first = jnp.where(end <= position, end, first)
    key_position = index * rows + lax.broadcasted_iota(jnp.int32, (rows, rows), 0)
    allowed = (key_position >= first) & (key_position <= position)
    allowed = jnp.concatenate([allowed] * heads, axis=1)

    queries = end_to_end(query_ref[...], heads)
    query_out[...] = queries
    scores = contract(packet_ref[0:rows, :], queries, 1, 1) * (1.0 / math.sqrt(depth))
    scores = jnp.where(allowed, scores, NEG)
    top = jnp.max(scores, axis=0, keepdims=True)
    raised = jnp.exp(scores - top)
    raised_out[...] = raised
    grads = end_to_end(grad_ref[...], heads)
    grad_out[...] = grads
    product = grads.astype(jnp.float32) * end_to_end(saved_ref[...], heads).astype(jnp.float32)
    delta = contract(
        jnp.ones((8, depth), jnp.float32), product, 1, 1, precision=lax.Precision.HIGHEST
    )[0:1, :]
    change_out[...] = contract(packet_ref[rows : 2 * rows, :], grads, 1, 1) - delta
    row_out[0:1, :] = delta
    row_out[1:2, :] = top
    row_out[2:3, :] = jnp.sum(raised, axis=0, keepdims=True)
    row_out[3:4, :] = jnp.concatenate([first.astype(jnp.float32)] * heads, axis=1)
    row_out[4:8, :] = jnp.ones((4, width), jnp.float32)
    owner, counts, rank = runs_of(packet_ref[2 * rows : 2 * rows + count, :].astype(jnp.float32))
    spread_out[...] = one_hot(count * slot, (owner ^ index) * slot + rank)
    target_out[...] = one_hot(count * rows, (owner ^ index) * rows + rank)
    filled_out[0:count, :] = jnp.broadcast_to(counts, (count, rows))
    filled_out[count:, :] = jnp.zeros((8 - count, rows), jnp.float32)


def fold(count, back, packet, queries, grads, row, filled):
    rows = packet.shape[1]
    index = lax.axis_index("ctx")
    delta, top, total = (row[n : n + 1, :] for n in range(3))
    first = row[3:4, :].astype(jnp.int32)
    position = (index - back) * rows + lax.broadcasted_iota(jnp.int32, (rows, row.shape[1]), 0)
    scores = contract(packet[0:rows, :], queries, 1, 1) * (1.0 / math.sqrt(queries.shape[1]))
    scores = jnp.where(position >= first, scores, NEG)
    new_top = jnp.maximum(top, jnp.max(scores, axis=0, keepdims=True))
    raised = jnp.exp(scores - new_top)
    shrink = jnp.exp(top - new_top)
    total = total * shrink + jnp.sum(raised, axis=0, keepdims=True)
    change = contract(packet[rows : 2 * rows, :], grads, 1, 1) - delta
    factors = row[4:8, :] * jnp.where(
        lax.broadcasted_iota(jnp.int32, (4, row.shape[1]), 0) < back, shrink, 1.0
    )
    owner, counts, rank = runs_of(packet[2 * rows : 2 * rows + count, :].astype(jnp.float32))
    base = jnp.zeros((1, rows), jnp.float32)
    for p in range(count):
        base = base + jnp.where(owner == p, filled[p : p + 1, :], 0.0)
    inside = index >= back
    target = jnp.where(inside, (owner ^ index) * rows + base.astype(jnp.int32) + rank, -1)
    filled = filled[0:count, :] + jnp.where(inside, counts, 0.0)
    return raised, change, (new_top, total, factors), one_hot(count * rows, target), filled


def step_kernel(count, back, *refs):
    query_ref, grad_ref, row_ref, filled_ref, packet_ref = refs[:5]
    raised_out, change_out, row_out, target_out, filled_out = refs[5:]
    raised, change, (top, total, factors), target, filled = fold(
        count, back, packet_ref, query_ref[...], grad_ref[...], row_ref, filled_ref
    )
    raised_out[...] = raised
    change_out[...] = change
    row_out[0:1, :] = row_ref[0:1, :]
    row_out[1:2, :] = top
    row_out[2:3, :] = total
    row_out[3:4, :] = row_ref[3:4, :]
    row_out[4:8, :] = factors
    target_out[...] = target
    filled_out[0:count, :] = filled
    filled_out[count:, :] = jnp.zeros_like(filled_out[count:, :])


def attend_kernel(count, halo, *refs):
    query_ref, grad_ref, row_ref, filled_ref, spread_ref = refs[:5]
    raised_refs = refs[5 : 5 + halo]
    change_refs = refs[5 + halo : 5 + 2 * halo]
    target_refs = refs[5 + 2 * halo : 5 + 3 * halo]
    packets = refs[5 + 3 * halo : 6 + 4 * halo]
    outs = refs[6 + 4 * halo :]
    rows = packets[0].shape[1]
    depth = query_ref.shape[1]
    heads = query_ref.shape[0] // rows
    slot = 2 * rows // count
    scale = 1.0 / math.sqrt(depth)
    queries = query_ref[...]
    grads = grad_ref[...]
    raised, change, (_, total, factors), target, _ = fold(
        count, halo, packets[halo], queries, grads, row_ref, filled_ref
    )
    factors = factors * (1.0 / total)
    weights = []
    changes = []
    for block in range(halo + 1):
        mine = raised if block == halo else raised_refs[block][...]
        mine = mine * factors[block : block + 1, :]
        weights.append(mine.astype(jnp.bfloat16))
        mine = mine * (change if block == halo else change_refs[block][...])
        changes.append(mine.astype(jnp.bfloat16))
    weights = jnp.concatenate(weights, axis=0)
    changes = jnp.concatenate(changes, axis=0)
    keys = jnp.concatenate([packet[0:rows, :] for packet in packets], axis=0)
    query_grad = (contract(keys, changes, 0, 0) * scale).astype(jnp.bfloat16)
    key_parts = contract(changes, queries, 1, 0) * scale
    value_parts = contract(weights, grads, 1, 0)
    parts = jnp.concatenate([key_parts, value_parts], axis=1).astype(jnp.bfloat16)

    query_slots = contract(spread_ref[...], end_to_end(query_grad, heads), 1, 1)
    query_slots = query_slots.astype(jnp.bfloat16)
    spread = jnp.concatenate([ref[...] for ref in target_refs] + [target], axis=1)
    part_slots = contract(spread, parts, 1, 0).astype(jnp.bfloat16)
    at = heads * slot
    for k in range(count):
        out = outs[k]
        for h in range(heads):
            out[h * slot : (h + 1) * slot, :] = query_slots[
                k * slot : (k + 1) * slot, h * depth : (h + 1) * depth
            ]
        for n in range(2):
            out[at + n * rows : at + (n + 1) * rows, :] = part_slots[
                k * rows : (k + 1) * rows, n * depth : (n + 1) * depth
            ]


def order_kernel(count, halo, _, *refs):
    packets = refs[: 1 + halo]
    query_out, key_out = refs[1 + halo :]
    rows = query_out.shape[0]
    index = lax.axis_index("ctx")
    given = []
    for ref in packets:
        hot = ref[2 * rows : 2 * rows + count, :].astype(jnp.float32)
        counts = jnp.sum(hot, axis=1, keepdims=True)
        mine = jnp.zeros((1, 1), jnp.float32)
        for p in range(count):
            mine = jnp.where(index == p, counts[p : p + 1, :], mine)
        given.append(mine.astype(jnp.int32))
    if len(given) < count:
        given.append(rows - sum(given))
    giver = [lax.rem(index - d + count, count) for d in range(count)]

    def placement(size, halo):
        lane = lax.broadcasted_iota(jnp.int32, (1, count * size), 1)
        target = jnp.full(lane.shape, -1, jnp.int32)
        for k in range(count):
            step = lane - k * size
            for back in range(halo + 1):
                block = (index ^ k) - back
                start = jnp.zeros((1, 1), jnp.int32)
                length = jnp.zeros((1, 1), jnp.int32)
                for d in range(count):
                    start = start + jnp.where(giver[d] < block, given[d], 0)
                    length = length + jnp.where(giver[d] == block, given[d], 0)
                target = jnp.where((step >= 0) & (step < length), start + step, target)
                step = step - length
        return one_hot(rows, target)

    query_out[...] = placement(2 * rows // count, 0)
    key_out[...] = placement(rows, halo)


def place_kernel(count, query_spread, key_spread, *refs):
    half = (count + 1) // 2
    ins = [refs[k // 2 + half * (k % 2)] for k in range(count)]
    query_out, key_out, value_out = refs[count : count + 3]
    query_here, key_here, value_here, sems = refs[count + 3 :]
    rows, width = query_here.shape
    depth = key_here.shape[1]
    heads = width // depth
    slot = 2 * rows // count
    copies = []

    def leave(here, out):
        copies.append(pltpu.make_async_copy(here, out, sems.at[len(copies)]))
        copies[-1].start()

    def taken(first, size, pieces):
        return jnp.concatenate(
            [
                jnp.concatenate(
                    [ref[first + n * size : first + (n + 1) * size, :] for n in range(pieces)],
                    axis=1,
                )
                for ref in ins
            ],
            axis=0,
        )

    query_here[...] = contract(query_spread[...], taken(0, slot, heads), 1, 0)
    leave(query_here, query_out)
    both = contract(key_spread[...], taken(heads * slot, rows, 2), 1, 0)
    for n, (here, out) in enumerate(((key_here, key_out), (value_here, value_out))):
        here[...] = both[:, n * depth : (n + 1) * depth]
        leave(here, out)
    for copy in copies:
        copy.wait()


def near_plan(doc_lengths, owners, queries, key_head_rows, value_head_rows, forward_out, grad_out):
    count = lax.axis_size("ctx")
    rows, width = queries.shape
    depth = key_head_rows.shape[1]
    heads = width // depth
    bf16, f32 = jnp.bfloat16, jnp.float32
    columns = heads * rows
    halo = count // 2
    slot = 2 * rows // count
    whole = pl.BlockSpec(memory_space=pltpu.VMEM)
    params = pltpu.CompilerParams(vmem_limit_bytes=40 * 1024 * 1024)

    mark = lax.broadcasted_iota(jnp.int32, (2 * rows + META, rows), 0) - 2 * rows
    packet = jnp.where(
        mark < 0,
        jnp.pad(jnp.concatenate([key_head_rows, value_head_rows], axis=0), ((0, META), (0, 0))),
        (owners[None, :] == mark).astype(bf16),
    )
    near = [
        lax.ppermute(packet, "ctx", [(i, (i + back) % count) for i in range(count)])
        for back in range(1, halo + 1)
    ]
    block_shapes = [jax.ShapeDtypeStruct((rows, columns), f32)] * 2
    row_shape = jax.ShapeDtypeStruct((8, columns), f32)
    target_shape = jax.ShapeDtypeStruct((count * rows, rows), bf16)
    filled_shape = jax.ShapeDtypeStruct((8, rows), f32)
    query_rows, grad_rows, raised, change, row, spread, target, filled = pl.pallas_call(
        functools.partial(own_kernel, count, doc_lengths.shape[0]),
        out_shape=[jax.ShapeDtypeStruct((columns, depth), bf16)] * 2
        + block_shapes
        + [row_shape, jax.ShapeDtypeStruct((count * slot, rows), bf16), target_shape, filled_shape],
        in_specs=[pl.BlockSpec(memory_space=pltpu.SMEM)] + [whole] * 4,
        out_specs=[whole] * 8,
        compiler_params=params,
    )(doc_lengths, packet, queries, grad_out, forward_out)
    raised, change, target = [raised], [change], [target]
    for back in range(1, halo):
        found = pl.pallas_call(
            functools.partial(step_kernel, count, back),
            out_shape=block_shapes + [row_shape, target_shape, filled_shape],
            in_specs=[whole] * 5,
            out_specs=[whole] * 5,
            compiler_params=params,
        )(query_rows, grad_rows, row, filled, near[back - 1])
        raised.append(found[0])
        change.append(found[1])
        row = found[2]
        target.append(found[3])
        filled = found[4]
    sent = pl.pallas_call(
        functools.partial(attend_kernel, count, halo),
        out_shape=[jax.ShapeDtypeStruct((heads * slot + 2 * rows, depth), bf16)] * count,
        in_specs=[whole] * (6 + 4 * halo),
        out_specs=[whole] * count,
        compiler_params=params,
    )(query_rows, grad_rows, row, filled, spread, *raised, *change, *target, packet, *near)
    received = [sent[0]] + [
        lax.ppermute(sent[k], "ctx", [(i, i ^ k) for i in range(count)]) for k in range(1, count)
    ]
    spreads = pl.pallas_call(
        functools.partial(order_kernel, count, halo),
        out_shape=[
            jax.ShapeDtypeStruct((rows, count * slot), bf16),
            jax.ShapeDtypeStruct((rows, count * rows), bf16),
        ],
        in_specs=[pl.BlockSpec(memory_space=pl.ANY)] + [whole] * (1 + halo),
        out_specs=[whole] * 2,
        compiler_params=params,
    )(received[-1], packet, *near)
    return pl.pallas_call(
        functools.partial(place_kernel, count),
        out_shape=[
            jax.ShapeDtypeStruct((rows, width), f32),
            jax.ShapeDtypeStruct((rows, depth), f32),
            jax.ShapeDtypeStruct((rows, depth), f32),
        ],
        in_specs=[whole] * (2 + count),
        out_specs=[pl.BlockSpec(memory_space=pl.ANY)] * 3,
        scratch_shapes=[
            pltpu.VMEM((rows, width), f32),
            pltpu.VMEM((rows, depth), f32),
            pltpu.VMEM((rows, depth), f32),
            pltpu.SemaphoreType.DMA((3,)),
        ],
        compiler_params=params,
    )(*spreads, *received[::2], *received[1::2])


def per_device(*args):
    if lax.axis_size("ctx") in (2, 4):
        return near_plan(*args)
    return ring_plan(*args)


def solution(mesh):
    return jax.shard_map(
        per_device,
        mesh=mesh,
        in_specs=(
            P("groups"),
            P(("groups", "ctx")),
            P(("groups", "ctx"), "head"),
            P(("groups", "ctx"), "head"),
            P(("groups", "ctx"), "head"),
            P(("groups", "ctx"), "head"),
            P(("groups", "ctx"), "head"),
        ),
        out_specs=(
            P(("groups", "ctx"), "head"),
            P(("groups", "ctx"), "head"),
            P(("groups", "ctx"), "head"),
        ),
        check_vma=False,
    )
```

```python
import functools
import math

import jax
import jax.numpy as jnp
from jax import lax
from jax.experimental import pallas as pl
from jax.experimental.pallas import tpu as pltpu
from jax.sharding import PartitionSpec as P

HEAD_WIDTH = 128
GROUP = 4


NEG = -1e30
BLOCK = 512


def shifted(value, axis, by):
    count = lax.axis_size(axis)
    return lax.ppermute(value, axis, [(i, (i + by) % count) for i in range(count)])


def document_of(positions, doc_lengths):
    ends = jnp.cumsum(doc_lengths)
    return jnp.sum((positions[:, None] >= ends[None, :]).astype(jnp.int32), axis=1)


def allowed_between(query_positions, query_docs, key_positions, key_docs):
    return (query_docs[:, None] == key_docs[None, :]) & (
        key_positions[None, :] <= query_positions[:, None]
    )


def head_rows(matrix, group_size, head_dim):
    row_count = matrix.shape[0]
    return matrix.reshape(row_count * group_size, head_dim)


def block_scores(query_flat, key_head, row_count, group_size, head_dim):
    scores = lax.dot_general(
        query_flat, key_head, (((1,), (1,)), ((), ())), preferred_element_type=jnp.float32
    )
    return (scores * (1.0 / math.sqrt(head_dim))).reshape(row_count, group_size, key_head.shape[0])


def update_stats(running, query_local, key_block, allowed, group_size, head_dim):
    running_max, totals = running
    row_count = query_local.shape[0]
    scores = block_scores(
        head_rows(query_local, group_size, head_dim), key_block, row_count, group_size, head_dim
    )
    masked = jnp.where(allowed[:, None, :], scores, NEG)
    new_max = jnp.maximum(running_max, jnp.max(masked, axis=2))
    weights = jnp.where(allowed[:, None, :], jnp.exp(masked - new_max[:, :, None]), 0.0)
    new_totals = [totals * jnp.exp(running_max - new_max) + jnp.sum(weights, axis=2)]
    new_maxima = [new_max]
    return (jnp.concatenate(new_maxima, axis=1), jnp.concatenate(new_totals, axis=1))


def backward_block(
    query_local,
    grad_local,
    log_norm,
    row_delta,
    key_block,
    value_block,
    allowed,
    group_size,
    head_dim,
):
    row_count = query_local.shape[0]
    query_flat = head_rows(query_local, group_size, head_dim)
    grad_flat = head_rows(grad_local, group_size, head_dim)
    scores = block_scores(query_flat, key_block, row_count, group_size, head_dim)
    masked = jnp.where(allowed[:, None, :], scores, NEG)
    weights = jnp.exp(masked - log_norm[:, 0:group_size, None])
    grad_weights = lax.dot_general(
        grad_flat, value_block, (((1,), (1,)), ((), ())), preferred_element_type=jnp.float32
    ).reshape(row_count, group_size, -1)
    grad_scores = weights * (grad_weights - row_delta[:, 0:group_size, None])
    rounded_weights = weights.astype(jnp.bfloat16).reshape(row_count * group_size, -1)
    rounded_grads = grad_scores.astype(jnp.bfloat16).reshape(row_count * group_size, -1)
    value_parts = [
        lax.dot_general(
            rounded_weights, grad_flat, (((0,), (0,)), ((), ())), preferred_element_type=jnp.float32
        )
    ]
    key_parts = [
        lax.dot_general(
            rounded_grads, query_flat, (((0,), (0,)), ((), ())), preferred_element_type=jnp.float32
        )
    ]
    query_parts = [
        jnp.dot(rounded_grads, key_block, preferred_element_type=jnp.float32).reshape(
            row_count, group_size * head_dim
        )
    ]
    return (
        jnp.concatenate(query_parts, axis=1),
        jnp.concatenate(key_parts, axis=1),
        jnp.concatenate(value_parts, axis=1),
    )


def ring_plan(doc_lengths, owners, queries, key_head_rows, value_head_rows, forward_out, grad_out):
    context_size = lax.axis_size("ctx")
    context_index = lax.axis_index("ctx")
    row_count = queries.shape[0]
    head_dim = HEAD_WIDTH
    group_size = GROUP
    query_heads = queries.shape[1] // head_dim
    slot_count = 2 * row_count // context_size
    everyone = lax.all_gather(owners, "ctx", axis=0, tiled=True)
    row_arrangement = jnp.argsort(everyone, stable=True)
    layout_docs = document_of(row_arrangement, doc_lengths)
    own_positions = lax.dynamic_slice_in_dim(
        row_arrangement, context_index * row_count, row_count, 0
    )
    own_documents = lax.dynamic_slice_in_dim(layout_docs, context_index * row_count, row_count, 0)
    owner_ids = jnp.arange(context_size, dtype=jnp.int32)
    owner_hot = (owners[:, None] == owner_ids[None, :]).astype(jnp.int32)
    earlier = jnp.cumsum(owner_hot, axis=0) - owner_hot
    rank_within = jnp.sum(earlier * owner_hot, axis=1)
    slot_rows = owners * slot_count + rank_within

    def packed(matrix):
        empty = jnp.zeros((context_size * slot_count,) + matrix.shape[1:], matrix.dtype)
        return empty.at[slot_rows].set(matrix)

    owner_grid = everyone.reshape(context_size, row_count)
    counts = jnp.sum((owner_grid == context_index).astype(jnp.int32), axis=1)
    count_ends = jnp.cumsum(counts)
    starts = count_ends - counts
    wanted = jnp.arange(row_count, dtype=jnp.int32)
    source = jnp.sum((wanted[:, None] >= count_ends[None, :]).astype(jnp.int32), axis=1)
    source_hot = (source[:, None] == owner_ids[None, :]).astype(jnp.int32)
    take_rows = source * slot_count + wanted - jnp.sum(source_hot * starts[None, :], axis=1)

    def compact(received):
        return jnp.take(received, take_rows, axis=0)

    local_delta = jnp.sum(
        (grad_out.astype(jnp.float32) * forward_out.astype(jnp.float32)).reshape(
            row_count, query_heads, head_dim
        ),
        axis=2,
    )
    arrived = (
        lax.all_to_all(packed(queries), "ctx", split_axis=0, concat_axis=0, tiled=True),
        lax.all_to_all(packed(key_head_rows), "ctx", split_axis=0, concat_axis=0, tiled=True),
        lax.all_to_all(packed(value_head_rows), "ctx", split_axis=0, concat_axis=0, tiled=True),
        lax.all_to_all(packed(grad_out), "ctx", split_axis=0, concat_axis=0, tiled=True),
    )
    query_local, key_local, value_local, grad_local = [compact(received) for received in arrived]
    row_delta = compact(
        lax.all_to_all(packed(local_delta), "ctx", split_axis=0, concat_axis=0, tiled=True)
    )

    def fold_keys(running, shard_rows, first_row):
        piece_count = shard_rows.shape[0]
        step_rows = math.gcd(piece_count, BLOCK) if piece_count > BLOCK else piece_count

        def one_block(partial_value, block_index):
            offset = first_row + block_index * step_rows
            key_block = lax.dynamic_slice_in_dim(shard_rows, block_index * step_rows, step_rows, 0)
            key_positions = lax.dynamic_slice_in_dim(row_arrangement, offset, step_rows, 0)
            key_docs = lax.dynamic_slice_in_dim(layout_docs, offset, step_rows, 0)
            allowed = allowed_between(own_positions, own_documents, key_positions, key_docs)
            return (
                update_stats(partial_value, query_local, key_block, allowed, group_size, head_dim),
                None,
            )

        if piece_count == step_rows:
            return one_block(running, 0)[0]
        return lax.scan(one_block, running, jnp.arange(piece_count // step_rows, dtype=jnp.int32))[
            0
        ]

    start_stats = (
        jnp.full((row_count, query_heads), NEG, jnp.float32),
        jnp.zeros((row_count, query_heads), jnp.float32),
    )
    top_scores, totals = fold_keys(
        start_stats, lax.all_gather(key_local, "ctx", axis=0, tiled=True), jnp.int32(0)
    )
    log_norm = top_scores + jnp.log(totals)

    def block_meta(owner_index, offset, size):
        first = owner_index * row_count + offset
        key_positions = lax.dynamic_slice_in_dim(row_arrangement, first, size, 0)
        key_docs = lax.dynamic_slice_in_dim(layout_docs, first, size, 0)
        return (key_positions, key_docs)

    query_zero = jnp.zeros(query_local.shape, jnp.float32)
    key_zero = jnp.zeros(key_local.shape, jnp.float32)

    def one_turn(turn_index, loop_state):
        key_moving, value_moving, key_grad, value_grad, query_grad = loop_state
        owner_index = (context_index - turn_index) % context_size
        key_positions, key_docs = block_meta(owner_index, 0, row_count)
        allowed = allowed_between(own_positions, own_documents, key_positions, key_docs)
        query_part, key_part, value_part = backward_block(
            query_local,
            grad_local,
            log_norm,
            row_delta,
            key_moving,
            value_moving,
            allowed,
            group_size,
            head_dim,
        )
        return (
            key_moving,
            value_moving,
            key_grad + key_part,
            value_grad + value_part,
            query_grad + query_part,
        )

    def moved_turn(turn_index, loop_state):
        key_moving, value_moving, key_grad, value_grad, query_grad = loop_state
        key_moving, value_moving = shifted((key_moving, value_moving), "ctx", 1)
        key_grad, value_grad = shifted((key_grad, value_grad), "ctx", 1)
        return one_turn(turn_index, (key_moving, value_moving, key_grad, value_grad, query_grad))

    loop_state = one_turn(0, (key_local, value_local, key_zero, key_zero, query_zero))
    loop_state = lax.fori_loop(1, context_size, moved_turn, loop_state)
    key_grad, value_grad = shifted((loop_state[2], loop_state[3]), "ctx", 1)
    query_grad = loop_state[4]
    inverse_root = 1.0 / math.sqrt(head_dim)
    return (query_grad * inverse_root, key_grad * inverse_root, value_grad)


META = 8


def contract(left, right, left_dim, right_dim, **kw):
    return lax.dot_general(
        left,
        right,
        (((left_dim,), (right_dim,)), ((), ())),
        preferred_element_type=jnp.float32,
        **kw,
    )


def one_hot(row_count, target):
    places = lax.broadcasted_iota(jnp.int32, (row_count, target.shape[1]), 0)
    return jnp.where(places == target, 1.0, 0.0).astype(jnp.bfloat16)


def side_by_side(stack, heads):
    rows = stack.shape[0] // heads
    return jnp.concatenate([stack[h * rows : (h + 1) * rows, :] for h in range(heads)], axis=1)


def end_to_end(matrix, heads):
    width = matrix.shape[1] // heads
    return jnp.concatenate([matrix[:, h * width : (h + 1) * width] for h in range(heads)], axis=0)


def runs_of(hot):
    count, rows = hot.shape
    counts = jnp.sum(hot, axis=1, keepdims=True)
    owner = jnp.zeros((1, rows), jnp.int32)
    earlier = jnp.zeros((1, rows), jnp.float32)
    for p in range(count):
        mine = hot[p : p + 1, :] > 0.0
        owner = jnp.where(mine, p, owner)
        for less in range(p):
            earlier = earlier + jnp.where(mine, counts[less : less + 1, :], 0.0)
    lane = lax.broadcasted_iota(jnp.int32, (1, rows), 1)
    return owner, counts, lane - earlier.astype(jnp.int32)


def own_kernel(
    count,
    docs,
    doc_ref,
    packet_ref,
    query_ref,
    grad_ref,
    saved_ref,
    query_out,
    grad_out,
    raised_out,
    change_out,
    row_out,
    spread_out,
    target_out,
    filled_out,
):
    rows, width = query_ref.shape
    depth = packet_ref.shape[1]
    heads = width // depth
    slot = 2 * rows // count
    index = lax.axis_index("ctx")
    lane = lax.broadcasted_iota(jnp.int32, (1, rows), 1)
    position = index * rows + lane
    first = jnp.zeros((1, rows), jnp.int32)
    end = jnp.int32(0)
    for d in range(docs):
        end = end + doc_ref[d]
        first = jnp.where(end <= position, end, first)
    key_position = index * rows + lax.broadcasted_iota(jnp.int32, (rows, rows), 0)
    allowed = (key_position >= first) & (key_position <= position)
    allowed = jnp.concatenate([allowed] * heads, axis=1)

    queries = end_to_end(query_ref[...], heads)
    query_out[...] = queries
    scores = contract(packet_ref[0:rows, :], queries, 1, 1) * (1.0 / math.sqrt(depth))
    scores = jnp.where(allowed, scores, NEG)
    top = jnp.max(scores, axis=0, keepdims=True)
    raised = jnp.exp(scores - top)
    raised_out[...] = raised
    grads = end_to_end(grad_ref[...], heads)
    grad_out[...] = grads
    product = grads.astype(jnp.float32) * end_to_end(saved_ref[...], heads).astype(jnp.float32)
    delta = contract(
        jnp.ones((8, depth), jnp.float32), product, 1, 1, precision=lax.Precision.HIGHEST
    )[0:1, :]
    change_out[...] = contract(packet_ref[rows : 2 * rows, :], grads, 1, 1) - delta
    row_out[0:1, :] = delta
    row_out[1:2, :] = top
    row_out[2:3, :] = jnp.sum(raised, axis=0, keepdims=True)
    row_out[3:4, :] = jnp.concatenate([first.astype(jnp.float32)] * heads, axis=1)
    row_out[4:8, :] = jnp.ones((4, width), jnp.float32)
    owner, counts, rank = runs_of(packet_ref[2 * rows : 2 * rows + count, :].astype(jnp.float32))
    spread_out[...] = one_hot(count * slot, (owner ^ index) * slot + rank)
    target_out[...] = one_hot(count * rows, (owner ^ index) * rows + rank)
    filled_out[0:count, :] = jnp.broadcast_to(counts, (count, rows))
    filled_out[count:, :] = jnp.zeros((8 - count, rows), jnp.float32)


def fold(count, back, packet, queries, grads, row, filled):
    rows = packet.shape[1]
    index = lax.axis_index("ctx")
    delta, top, total = (row[n : n + 1, :] for n in range(3))
    first = row[3:4, :].astype(jnp.int32)
    position = (index - back) * rows + lax.broadcasted_iota(jnp.int32, (rows, row.shape[1]), 0)
    scores = contract(packet[0:rows, :], queries, 1, 1) * (1.0 / math.sqrt(queries.shape[1]))
    scores = jnp.where(position >= first, scores, NEG)
    new_top = jnp.maximum(top, jnp.max(scores, axis=0, keepdims=True))
    raised = jnp.exp(scores - new_top)
    shrink = jnp.exp(top - new_top)
    total = total * shrink + jnp.sum(raised, axis=0, keepdims=True)
    change = contract(packet[rows : 2 * rows, :], grads, 1, 1) - delta
    factors = row[4:8, :] * jnp.where(
        lax.broadcasted_iota(jnp.int32, (4, row.shape[1]), 0) < back, shrink, 1.0
    )
    owner, counts, rank = runs_of(packet[2 * rows : 2 * rows + count, :].astype(jnp.float32))
    base = jnp.zeros((1, rows), jnp.float32)
    for p in range(count):
        base = base + jnp.where(owner == p, filled[p : p + 1, :], 0.0)
    inside = index >= back
    target = jnp.where(inside, (owner ^ index) * rows + base.astype(jnp.int32) + rank, -1)
    filled = filled[0:count, :] + jnp.where(inside, counts, 0.0)
    return raised, change, (new_top, total, factors), one_hot(count * rows, target), filled


def step_kernel(count, back, *refs):
    query_ref, grad_ref, row_ref, filled_ref, packet_ref = refs[:5]
    raised_out, change_out, row_out, target_out, filled_out = refs[5:]
    raised, change, (top, total, factors), target, filled = fold(
        count, back, packet_ref, query_ref[...], grad_ref[...], row_ref, filled_ref
    )
    raised_out[...] = raised
    change_out[...] = change
    row_out[0:1, :] = row_ref[0:1, :]
    row_out[1:2, :] = top
    row_out[2:3, :] = total
    row_out[3:4, :] = row_ref[3:4, :]
    row_out[4:8, :] = factors
    target_out[...] = target
    filled_out[0:count, :] = filled
    filled_out[count:, :] = jnp.zeros_like(filled_out[count:, :])


def attend_kernel(count, halo, *refs):
    query_ref, grad_ref, row_ref, filled_ref, spread_ref, given_ref = refs[:6]
    raised_refs = refs[6 : 6 + halo]
    change_refs = refs[6 + halo : 6 + 2 * halo]
    target_refs = refs[6 + 2 * halo : 6 + 3 * halo]
    packets = refs[6 + 3 * halo : 7 + 4 * halo]
    outs = refs[7 + 4 * halo :]
    rows = packets[0].shape[1]
    depth = query_ref.shape[1]
    heads = query_ref.shape[0] // rows
    slot = 2 * rows // count
    scale = 1.0 / math.sqrt(depth)
    queries = query_ref[...]
    grads = grad_ref[...]
    raised, change, (_, total, factors), target, _ = fold(
        count, halo, packets[halo], queries, grads, row_ref, filled_ref
    )
    factors = factors * (1.0 / total)
    weights = []
    changes = []
    for block in range(halo + 1):
        mine = raised if block == halo else raised_refs[block][...]
        mine = mine * factors[block : block + 1, :]
        weights.append(mine.astype(jnp.bfloat16))
        mine = mine * (change if block == halo else change_refs[block][...])
        changes.append(mine.astype(jnp.bfloat16))
    weights = jnp.concatenate(weights, axis=0)
    changes = jnp.concatenate(changes, axis=0)
    keys = jnp.concatenate([packet[0:rows, :] for packet in packets], axis=0)
    query_grad = (contract(keys, changes, 0, 0) * scale).astype(jnp.bfloat16)
    key_parts = contract(changes, queries, 1, 0) * scale
    value_parts = contract(weights, grads, 1, 0)
    parts = jnp.concatenate([key_parts, value_parts], axis=1).astype(jnp.bfloat16)

    query_slots = contract(spread_ref[...], end_to_end(query_grad, heads), 1, 1)
    query_slots = query_slots.astype(jnp.bfloat16)
    spread = jnp.concatenate([ref[...] for ref in target_refs] + [target], axis=1)
    part_slots = contract(spread, parts, 1, 0).astype(jnp.bfloat16)
    at = heads * slot
    for k in range(count):
        out = outs[k]
        for h in range(heads):
            out[h * slot : (h + 1) * slot, :] = query_slots[
                k * slot : (k + 1) * slot, h * depth : (h + 1) * depth
            ]
        for n in range(2):
            out[at + n * rows : at + (n + 1) * rows, :] = part_slots[
                k * rows : (k + 1) * rows, n * depth : (n + 1) * depth
            ]
    half = count // 2
    given = jnp.zeros((1, depth), jnp.float32)
    for p in range(count):
        given = jnp.where((lax.axis_index("ctx") ^ half) == p, given_ref[p : p + 1, 0:depth], given)
    outs[half][at + 2 * rows :, :] = jnp.broadcast_to(given, (META, depth)).astype(jnp.bfloat16)


def order_kernel(count, halo, half_ref, packet_ref, near_ref, query_out, key_out):
    rows = query_out.shape[0]
    index = lax.axis_index("ctx")
    giver = [index, lax.rem(index + count - 1, count)]
    given = []
    for ref in (packet_ref, near_ref):
        hot = ref[2 * rows : 2 * rows + count, :].astype(jnp.float32)
        counts = jnp.sum(hot, axis=1, keepdims=True)
        mine = jnp.zeros((1, 1), jnp.float32)
        for p in range(count):
            mine = jnp.where(index == p, counts[p : p + 1, :], mine)
        given.append(mine.astype(jnp.int32))
    if count == 4:
        at = half_ref.shape[0] - META
        given.append(half_ref[at : at + 1, 0:1].astype(jnp.float32).astype(jnp.int32))
        giver.append(index ^ 2)
        given.append(rows - sum(given))
        giver.append(6 - sum(giver))

    def placement(size, halo):
        lane = lax.broadcasted_iota(jnp.int32, (1, count * size), 1)
        target = jnp.full(lane.shape, -1, jnp.int32)
        for k in range(count):
            step = lane - k * size
            for back in range(halo + 1):
                block = (index ^ k) - back
                start = jnp.zeros((1, 1), jnp.int32)
                length = jnp.zeros((1, 1), jnp.int32)
                for n in range(count):
                    start = start + jnp.where(giver[n] < block, given[n], 0)
                    length = length + jnp.where(giver[n] == block, given[n], 0)
                target = jnp.where((step >= 0) & (step < length), start + step, target)
                step = step - length
        return one_hot(rows, target)

    query_out[...] = placement(2 * rows // count, 0)
    key_out[...] = placement(rows, halo)


def place_kernel(count, query_spread, key_spread, *refs):
    ins = refs[:count]
    query_out, key_out, value_out = refs[count : count + 3]
    query_here, key_here, value_here, sems = refs[count + 3 :]
    rows, width = query_here.shape
    depth = key_here.shape[1]
    heads = width // depth
    slot = 2 * rows // count
    copies = []

    def leave(here, out):
        copies.append(pltpu.make_async_copy(here, out, sems.at[len(copies)]))
        copies[-1].start()

    def taken(first, size, pieces):
        return jnp.concatenate(
            [
                jnp.concatenate(
                    [ref[first + n * size : first + (n + 1) * size, :] for n in range(pieces)],
                    axis=1,
                )
                for ref in ins
            ],
            axis=0,
        )

    query_here[...] = contract(query_spread[...], taken(0, slot, heads), 1, 0)
    leave(query_here, query_out)
    both = contract(key_spread[...], taken(heads * slot, rows, 2), 1, 0)
    for n, (here, out) in enumerate(((key_here, key_out), (value_here, value_out))):
        here[...] = both[:, n * depth : (n + 1) * depth]
        leave(here, out)
    for copy in copies:
        copy.wait()


def near_plan(doc_lengths, owners, queries, key_head_rows, value_head_rows, forward_out, grad_out):
    count = lax.axis_size("ctx")
    rows, width = queries.shape
    depth = key_head_rows.shape[1]
    heads = width // depth
    bf16, f32 = jnp.bfloat16, jnp.float32
    columns = heads * rows
    halo = count // 2
    slot = 2 * rows // count
    whole = pl.BlockSpec(memory_space=pltpu.VMEM)
    params = pltpu.CompilerParams(vmem_limit_bytes=40 * 1024 * 1024)

    mark = lax.broadcasted_iota(jnp.int32, (2 * rows + META, rows), 0) - 2 * rows
    packet = jnp.where(
        mark < 0,
        jnp.pad(jnp.concatenate([key_head_rows, value_head_rows], axis=0), ((0, META), (0, 0))),
        (owners[None, :] == mark).astype(bf16),
    )
    near = [
        lax.ppermute(packet, "ctx", [(i, (i + 1) % count) for i in range(count)])
    ] + [
        lax.ppermute(
            packet,
            "ctx",
            [(i, i + back if i + back < count else count - 1 - i) for i in range(count)],
        )
        for back in range(2, halo + 1)
    ]
    block_shapes = [jax.ShapeDtypeStruct((rows, columns), f32)] * 2
    row_shape = jax.ShapeDtypeStruct((8, columns), f32)
    target_shape = jax.ShapeDtypeStruct((count * rows, rows), bf16)
    filled_shape = jax.ShapeDtypeStruct((8, rows), f32)
    query_rows, grad_rows, raised, change, row, spread, target, filled = pl.pallas_call(
        functools.partial(own_kernel, count, doc_lengths.shape[0]),
        out_shape=[jax.ShapeDtypeStruct((columns, depth), bf16)] * 2
        + block_shapes
        + [row_shape, jax.ShapeDtypeStruct((count * slot, rows), bf16), target_shape, filled_shape],
        in_specs=[pl.BlockSpec(memory_space=pltpu.SMEM)] + [whole] * 4,
        out_specs=[whole] * 8,
        compiler_params=params,
    )(doc_lengths, packet, queries, grad_out, forward_out)
    raised, change, target, given = [raised], [change], [target], filled
    for back in range(1, halo):
        found = pl.pallas_call(
            functools.partial(step_kernel, count, back),
            out_shape=block_shapes + [row_shape, target_shape, filled_shape],
            in_specs=[whole] * 5,
            out_specs=[whole] * 5,
            compiler_params=params,
        )(query_rows, grad_rows, row, filled, near[back - 1])
        raised.append(found[0])
        change.append(found[1])
        row = found[2]
        target.append(found[3])
        filled = found[4]
    sent = pl.pallas_call(
        functools.partial(attend_kernel, count, halo),
        out_shape=[
            jax.ShapeDtypeStruct(
                (heads * slot + 2 * rows + (META if k == count // 2 else 0), depth), bf16
            )
            for k in range(count)
        ],
        in_specs=[whole] * (7 + 4 * halo),
        out_specs=[whole] * count,
        compiler_params=params,
    )(query_rows, grad_rows, row, filled, spread, given, *raised, *change, *target, packet, *near)
    received = [sent[0]] + [
        lax.ppermute(sent[k], "ctx", [(i, i ^ k) for i in range(count)]) for k in range(1, count)
    ]
    spreads = pl.pallas_call(
        functools.partial(order_kernel, count, halo),
        out_shape=[
            jax.ShapeDtypeStruct((rows, count * slot), bf16),
            jax.ShapeDtypeStruct((rows, count * rows), bf16),
        ],
        in_specs=[whole] * 3,
        out_specs=[whole] * 2,
        compiler_params=params,
    )(received[count // 2], packet, near[0])
    return pl.pallas_call(
        functools.partial(place_kernel, count),
        out_shape=[
            jax.ShapeDtypeStruct((rows, width), f32),
            jax.ShapeDtypeStruct((rows, depth), f32),
            jax.ShapeDtypeStruct((rows, depth), f32),
        ],
        in_specs=[whole] * (2 + count),
        out_specs=[pl.BlockSpec(memory_space=pl.ANY)] * 3,
        scratch_shapes=[
            pltpu.VMEM((rows, width), f32),
            pltpu.VMEM((rows, depth), f32),
            pltpu.VMEM((rows, depth), f32),
            pltpu.SemaphoreType.DMA((3,)),
        ],
        compiler_params=params,
    )(*spreads, *received)


def per_device(*args):
    if lax.axis_size("ctx") in (2, 4):
        return near_plan(*args)
    return ring_plan(*args)


def solution(mesh):
    return jax.shard_map(
        per_device,
        mesh=mesh,
        in_specs=(
            P("groups"),
            P(("groups", "ctx")),
            P(("groups", "ctx"), "head"),
            P(("groups", "ctx"), "head"),
            P(("groups", "ctx"), "head"),
            P(("groups", "ctx"), "head"),
            P(("groups", "ctx"), "head"),
        ),
        out_specs=(
            P(("groups", "ctx"), "head"),
            P(("groups", "ctx"), "head"),
            P(("groups", "ctx"), "head"),
        ),
        check_vma=False,
    )
```

```python
import functools
import math

import jax
import jax.numpy as jnp
from jax import lax
from jax.experimental import pallas as pl
from jax.experimental.pallas import tpu as pltpu
from jax.sharding import PartitionSpec as P

HEAD_WIDTH = 128
GROUP = 4


NEG = -1e30
BLOCK = 512


def shifted(value, axis, by):
    count = lax.axis_size(axis)
    return lax.ppermute(value, axis, [(i, (i + by) % count) for i in range(count)])


def document_of(positions, doc_lengths):
    ends = jnp.cumsum(doc_lengths)
    return jnp.sum((positions[:, None] >= ends[None, :]).astype(jnp.int32), axis=1)


def allowed_between(query_positions, query_docs, key_positions, key_docs):
    return (query_docs[:, None] == key_docs[None, :]) & (
        key_positions[None, :] <= query_positions[:, None]
    )


def head_rows(matrix, group_size, head_dim):
    row_count = matrix.shape[0]
    return matrix.reshape(row_count * group_size, head_dim)


def block_scores(query_flat, key_head, row_count, group_size, head_dim):
    scores = lax.dot_general(
        query_flat, key_head, (((1,), (1,)), ((), ())), preferred_element_type=jnp.float32
    )
    return (scores * (1.0 / math.sqrt(head_dim))).reshape(row_count, group_size, key_head.shape[0])


def update_stats(running, query_local, key_block, allowed, group_size, head_dim):
    running_max, totals = running
    row_count = query_local.shape[0]
    scores = block_scores(
        head_rows(query_local, group_size, head_dim), key_block, row_count, group_size, head_dim
    )
    masked = jnp.where(allowed[:, None, :], scores, NEG)
    new_max = jnp.maximum(running_max, jnp.max(masked, axis=2))
    weights = jnp.where(allowed[:, None, :], jnp.exp(masked - new_max[:, :, None]), 0.0)
    new_totals = [totals * jnp.exp(running_max - new_max) + jnp.sum(weights, axis=2)]
    new_maxima = [new_max]
    return (jnp.concatenate(new_maxima, axis=1), jnp.concatenate(new_totals, axis=1))


def backward_block(
    query_local,
    grad_local,
    log_norm,
    row_delta,
    key_block,
    value_block,
    allowed,
    group_size,
    head_dim,
):
    row_count = query_local.shape[0]
    query_flat = head_rows(query_local, group_size, head_dim)
    grad_flat = head_rows(grad_local, group_size, head_dim)
    scores = block_scores(query_flat, key_block, row_count, group_size, head_dim)
    masked = jnp.where(allowed[:, None, :], scores, NEG)
    weights = jnp.exp(masked - log_norm[:, 0:group_size, None])
    grad_weights = lax.dot_general(
        grad_flat, value_block, (((1,), (1,)), ((), ())), preferred_element_type=jnp.float32
    ).reshape(row_count, group_size, -1)
    grad_scores = weights * (grad_weights - row_delta[:, 0:group_size, None])
    rounded_weights = weights.astype(jnp.bfloat16).reshape(row_count * group_size, -1)
    rounded_grads = grad_scores.astype(jnp.bfloat16).reshape(row_count * group_size, -1)
    value_parts = [
        lax.dot_general(
            rounded_weights, grad_flat, (((0,), (0,)), ((), ())), preferred_element_type=jnp.float32
        )
    ]
    key_parts = [
        lax.dot_general(
            rounded_grads, query_flat, (((0,), (0,)), ((), ())), preferred_element_type=jnp.float32
        )
    ]
    query_parts = [
        jnp.dot(rounded_grads, key_block, preferred_element_type=jnp.float32).reshape(
            row_count, group_size * head_dim
        )
    ]
    return (
        jnp.concatenate(query_parts, axis=1),
        jnp.concatenate(key_parts, axis=1),
        jnp.concatenate(value_parts, axis=1),
    )


def ring_plan(doc_lengths, owners, queries, key_head_rows, value_head_rows, forward_out, grad_out):
    context_size = lax.axis_size("ctx")
    context_index = lax.axis_index("ctx")
    row_count = queries.shape[0]
    head_dim = HEAD_WIDTH
    group_size = GROUP
    query_heads = queries.shape[1] // head_dim
    slot_count = 2 * row_count // context_size
    everyone = lax.all_gather(owners, "ctx", axis=0, tiled=True)
    row_arrangement = jnp.argsort(everyone, stable=True)
    layout_docs = document_of(row_arrangement, doc_lengths)
    own_positions = lax.dynamic_slice_in_dim(
        row_arrangement, context_index * row_count, row_count, 0
    )
    own_documents = lax.dynamic_slice_in_dim(layout_docs, context_index * row_count, row_count, 0)
    owner_ids = jnp.arange(context_size, dtype=jnp.int32)
    owner_hot = (owners[:, None] == owner_ids[None, :]).astype(jnp.int32)
    earlier = jnp.cumsum(owner_hot, axis=0) - owner_hot
    rank_within = jnp.sum(earlier * owner_hot, axis=1)
    slot_rows = owners * slot_count + rank_within

    def packed(matrix):
        empty = jnp.zeros((context_size * slot_count,) + matrix.shape[1:], matrix.dtype)
        return empty.at[slot_rows].set(matrix)

    owner_grid = everyone.reshape(context_size, row_count)
    counts = jnp.sum((owner_grid == context_index).astype(jnp.int32), axis=1)
    count_ends = jnp.cumsum(counts)
    starts = count_ends - counts
    wanted = jnp.arange(row_count, dtype=jnp.int32)
    source = jnp.sum((wanted[:, None] >= count_ends[None, :]).astype(jnp.int32), axis=1)
    source_hot = (source[:, None] == owner_ids[None, :]).astype(jnp.int32)
    take_rows = source * slot_count + wanted - jnp.sum(source_hot * starts[None, :], axis=1)

    def compact(received):
        return jnp.take(received, take_rows, axis=0)

    local_delta = jnp.sum(
        (grad_out.astype(jnp.float32) * forward_out.astype(jnp.float32)).reshape(
            row_count, query_heads, head_dim
        ),
        axis=2,
    )
    arrived = (
        lax.all_to_all(packed(queries), "ctx", split_axis=0, concat_axis=0, tiled=True),
        lax.all_to_all(packed(key_head_rows), "ctx", split_axis=0, concat_axis=0, tiled=True),
        lax.all_to_all(packed(value_head_rows), "ctx", split_axis=0, concat_axis=0, tiled=True),
        lax.all_to_all(packed(grad_out), "ctx", split_axis=0, concat_axis=0, tiled=True),
    )
    query_local, key_local, value_local, grad_local = [compact(received) for received in arrived]
    row_delta = compact(
        lax.all_to_all(packed(local_delta), "ctx", split_axis=0, concat_axis=0, tiled=True)
    )

    def fold_keys(running, shard_rows, first_row):
        piece_count = shard_rows.shape[0]
        step_rows = math.gcd(piece_count, BLOCK) if piece_count > BLOCK else piece_count

        def one_block(partial_value, block_index):
            offset = first_row + block_index * step_rows
            key_block = lax.dynamic_slice_in_dim(shard_rows, block_index * step_rows, step_rows, 0)
            key_positions = lax.dynamic_slice_in_dim(row_arrangement, offset, step_rows, 0)
            key_docs = lax.dynamic_slice_in_dim(layout_docs, offset, step_rows, 0)
            allowed = allowed_between(own_positions, own_documents, key_positions, key_docs)
            return (
                update_stats(partial_value, query_local, key_block, allowed, group_size, head_dim),
                None,
            )

        if piece_count == step_rows:
            return one_block(running, 0)[0]
        return lax.scan(one_block, running, jnp.arange(piece_count // step_rows, dtype=jnp.int32))[
            0
        ]

    start_stats = (
        jnp.full((row_count, query_heads), NEG, jnp.float32),
        jnp.zeros((row_count, query_heads), jnp.float32),
    )
    top_scores, totals = fold_keys(
        start_stats, lax.all_gather(key_local, "ctx", axis=0, tiled=True), jnp.int32(0)
    )
    log_norm = top_scores + jnp.log(totals)

    def block_meta(owner_index, offset, size):
        first = owner_index * row_count + offset
        key_positions = lax.dynamic_slice_in_dim(row_arrangement, first, size, 0)
        key_docs = lax.dynamic_slice_in_dim(layout_docs, first, size, 0)
        return (key_positions, key_docs)

    query_zero = jnp.zeros(query_local.shape, jnp.float32)
    key_zero = jnp.zeros(key_local.shape, jnp.float32)

    def one_turn(turn_index, loop_state):
        key_moving, value_moving, key_grad, value_grad, query_grad = loop_state
        owner_index = (context_index - turn_index) % context_size
        key_positions, key_docs = block_meta(owner_index, 0, row_count)
        allowed = allowed_between(own_positions, own_documents, key_positions, key_docs)
        query_part, key_part, value_part = backward_block(
            query_local,
            grad_local,
            log_norm,
            row_delta,
            key_moving,
            value_moving,
            allowed,
            group_size,
            head_dim,
        )
        return (
            key_moving,
            value_moving,
            key_grad + key_part,
            value_grad + value_part,
            query_grad + query_part,
        )

    def moved_turn(turn_index, loop_state):
        key_moving, value_moving, key_grad, value_grad, query_grad = loop_state
        key_moving, value_moving = shifted((key_moving, value_moving), "ctx", 1)
        key_grad, value_grad = shifted((key_grad, value_grad), "ctx", 1)
        return one_turn(turn_index, (key_moving, value_moving, key_grad, value_grad, query_grad))

    loop_state = one_turn(0, (key_local, value_local, key_zero, key_zero, query_zero))
    loop_state = lax.fori_loop(1, context_size, moved_turn, loop_state)
    key_grad, value_grad = shifted((loop_state[2], loop_state[3]), "ctx", 1)
    query_grad = loop_state[4]
    inverse_root = 1.0 / math.sqrt(head_dim)
    return (query_grad * inverse_root, key_grad * inverse_root, value_grad)


META = 8


def contract(left, right, left_dim, right_dim, **kw):
    return lax.dot_general(
        left,
        right,
        (((left_dim,), (right_dim,)), ((), ())),
        preferred_element_type=jnp.float32,
        **kw,
    )


def one_hot(row_count, target):
    places = lax.broadcasted_iota(jnp.int32, (row_count, target.shape[1]), 0)
    return jnp.where(places == target, 1.0, 0.0).astype(jnp.bfloat16)


def side_by_side(stack, heads):
    rows = stack.shape[0] // heads
    return jnp.concatenate([stack[h * rows : (h + 1) * rows, :] for h in range(heads)], axis=1)


def end_to_end(matrix, heads):
    width = matrix.shape[1] // heads
    return jnp.concatenate([matrix[:, h * width : (h + 1) * width] for h in range(heads)], axis=0)


def runs_of(hot):
    count, rows = hot.shape
    counts = jnp.sum(hot, axis=1, keepdims=True)
    owner = jnp.zeros((1, rows), jnp.int32)
    earlier = jnp.zeros((1, rows), jnp.float32)
    for p in range(count):
        mine = hot[p : p + 1, :] > 0.0
        owner = jnp.where(mine, p, owner)
        for less in range(p):
            earlier = earlier + jnp.where(mine, counts[less : less + 1, :], 0.0)
    lane = lax.broadcasted_iota(jnp.int32, (1, rows), 1)
    return owner, counts, lane - earlier.astype(jnp.int32)


def own_scores(count, docs, doc_ref, packet_ref, query_ref, outs):
    query_out, raised_out, row_out, spread_out, target_out, filled_out = outs
    rows, width = query_ref.shape
    depth = packet_ref.shape[1]
    heads = width // depth
    slot = 2 * rows // count
    index = lax.axis_index("ctx")
    lane = lax.broadcasted_iota(jnp.int32, (1, rows), 1)
    position = index * rows + lane
    first = jnp.zeros((1, rows), jnp.int32)
    end = jnp.int32(0)
    for d in range(docs):
        end = end + doc_ref[d]
        first = jnp.where(end <= position, end, first)
    key_position = index * rows + lax.broadcasted_iota(jnp.int32, (rows, rows), 0)
    allowed = (key_position >= first) & (key_position <= position)
    allowed = jnp.concatenate([allowed] * heads, axis=1)

    queries = end_to_end(query_ref[...], heads)
    query_out[...] = queries
    scores = contract(packet_ref[0:rows, :], queries, 1, 1) * (1.0 / math.sqrt(depth))
    scores = jnp.where(allowed, scores, NEG)
    top = jnp.max(scores, axis=0, keepdims=True)
    raised = jnp.exp(scores - top)
    raised_out[...] = raised
    row_out[0:1, :] = jnp.zeros((1, width), jnp.float32)
    row_out[1:2, :] = top
    row_out[2:3, :] = jnp.sum(raised, axis=0, keepdims=True)
    row_out[3:4, :] = jnp.concatenate([first.astype(jnp.float32)] * heads, axis=1)
    row_out[4:8, :] = jnp.ones((4, width), jnp.float32)
    owner, counts, rank = runs_of(packet_ref[2 * rows : 2 * rows + count, :].astype(jnp.float32))
    spread_out[...] = one_hot(count * slot, (owner ^ index) * slot + rank)
    target_out[...] = one_hot(count * rows, (owner ^ index) * rows + rank)
    filled_out[0:count, :] = jnp.broadcast_to(counts, (count, rows))
    filled_out[count:, :] = jnp.zeros((8 - count, rows), jnp.float32)


def odd_kernel(count, docs, doc_ref, packet_ref, query_ref, packet_out, *outs):
    packet_out[...] = packet_ref[...]

    @pl.when(lax.rem(lax.axis_index("ctx"), 2) == 1)
    def _():
        own_scores(count, docs, doc_ref, packet_ref, query_ref, outs)


def own_kernel(count, docs, doc_ref, packet_ref, query_ref, grad_ref, saved_ref, *refs):
    done, outs = refs[:6], refs[6:12]
    grad_out, change_out = refs[12:]
    rows, width = query_ref.shape
    depth = packet_ref.shape[1]
    heads = width // depth
    odd = lax.rem(lax.axis_index("ctx"), 2) == 1

    @pl.when(odd)
    def _():
        for here, out in zip(done, outs, strict=True):
            out[...] = here[...]

    @pl.when(jnp.logical_not(odd))
    def _():
        own_scores(count, docs, doc_ref, packet_ref, query_ref, outs)

    grads = end_to_end(grad_ref[...], heads)
    grad_out[...] = grads
    product = grads.astype(jnp.float32) * end_to_end(saved_ref[...], heads).astype(jnp.float32)
    delta = contract(
        jnp.ones((8, depth), jnp.float32), product, 1, 1, precision=lax.Precision.HIGHEST
    )[0:1, :]
    change_out[...] = contract(packet_ref[rows : 2 * rows, :], grads, 1, 1) - delta
    outs[2][0:1, :] = delta


def fold(count, back, packet, queries, grads, row, filled):
    rows = packet.shape[1]
    index = lax.axis_index("ctx")
    delta, top, total = (row[n : n + 1, :] for n in range(3))
    first = row[3:4, :].astype(jnp.int32)
    position = (index - back) * rows + lax.broadcasted_iota(jnp.int32, (rows, row.shape[1]), 0)
    scores = contract(packet[0:rows, :], queries, 1, 1) * (1.0 / math.sqrt(queries.shape[1]))
    scores = jnp.where(position >= first, scores, NEG)
    new_top = jnp.maximum(top, jnp.max(scores, axis=0, keepdims=True))
    raised = jnp.exp(scores - new_top)
    shrink = jnp.exp(top - new_top)
    total = total * shrink + jnp.sum(raised, axis=0, keepdims=True)
    change = contract(packet[rows : 2 * rows, :], grads, 1, 1) - delta
    factors = row[4:8, :] * jnp.where(
        lax.broadcasted_iota(jnp.int32, (4, row.shape[1]), 0) < back, shrink, 1.0
    )
    owner, counts, rank = runs_of(packet[2 * rows : 2 * rows + count, :].astype(jnp.float32))
    base = jnp.zeros((1, rows), jnp.float32)
    for p in range(count):
        base = base + jnp.where(owner == p, filled[p : p + 1, :], 0.0)
    inside = index >= back
    target = jnp.where(inside, (owner ^ index) * rows + base.astype(jnp.int32) + rank, -1)
    filled = filled[0:count, :] + jnp.where(inside, counts, 0.0)
    return raised, change, (new_top, total, factors), one_hot(count * rows, target), filled


def step_kernel(count, back, *refs):
    query_ref, grad_ref, row_ref, filled_ref, packet_ref = refs[:5]
    raised_out, change_out, row_out, target_out, filled_out = refs[5:]
    raised, change, (top, total, factors), target, filled = fold(
        count, back, packet_ref, query_ref[...], grad_ref[...], row_ref, filled_ref
    )
    raised_out[...] = raised
    change_out[...] = change
    row_out[0:1, :] = row_ref[0:1, :]
    row_out[1:2, :] = top
    row_out[2:3, :] = total
    row_out[3:4, :] = row_ref[3:4, :]
    row_out[4:8, :] = factors
    target_out[...] = target
    filled_out[0:count, :] = filled
    filled_out[count:, :] = jnp.zeros_like(filled_out[count:, :])


def attend_kernel(count, halo, *refs):
    query_ref, grad_ref, row_ref, filled_ref, spread_ref = refs[:5]
    raised_refs = refs[5 : 5 + halo]
    change_refs = refs[5 + halo : 5 + 2 * halo]
    target_refs = refs[5 + 2 * halo : 5 + 3 * halo]
    packets = refs[5 + 3 * halo : 6 + 4 * halo]
    outs = refs[6 + 4 * halo :]
    rows = packets[0].shape[1]
    depth = query_ref.shape[1]
    heads = query_ref.shape[0] // rows
    slot = 2 * rows // count
    scale = 1.0 / math.sqrt(depth)
    queries = query_ref[...]
    grads = grad_ref[...]
    raised, change, (_, total, factors), target, _ = fold(
        count, halo, packets[halo], queries, grads, row_ref, filled_ref
    )
    factors = factors * (1.0 / total)
    weights = []
    changes = []
    for block in range(halo + 1):
        mine = raised if block == halo else raised_refs[block][...]
        mine = mine * factors[block : block + 1, :]
        weights.append(mine.astype(jnp.bfloat16))
        mine = mine * (change if block == halo else change_refs[block][...])
        changes.append(mine.astype(jnp.bfloat16))
    weights = jnp.concatenate(weights, axis=0)
    changes = jnp.concatenate(changes, axis=0)
    keys = jnp.concatenate([packet[0:rows, :] for packet in packets], axis=0)
    query_grad = (contract(keys, changes, 0, 0) * scale).astype(jnp.bfloat16)
    key_parts = contract(changes, queries, 1, 0) * scale
    value_parts = contract(weights, grads, 1, 0)
    parts = jnp.concatenate([key_parts, value_parts], axis=1).astype(jnp.bfloat16)

    query_slots = contract(spread_ref[...], end_to_end(query_grad, heads), 1, 1)
    query_slots = query_slots.astype(jnp.bfloat16)
    spread = jnp.concatenate([ref[...] for ref in target_refs] + [target], axis=1)
    part_slots = contract(spread, parts, 1, 0).astype(jnp.bfloat16)
    at = heads * slot
    for k in range(count):
        out = outs[k]
        for h in range(heads):
            out[h * slot : (h + 1) * slot, :] = query_slots[
                k * slot : (k + 1) * slot, h * depth : (h + 1) * depth
            ]
        for n in range(2):
            out[at + n * rows : at + (n + 1) * rows, :] = part_slots[
                k * rows : (k + 1) * rows, n * depth : (n + 1) * depth
            ]


def order_kernel(count, halo, _, *refs):
    packets = refs[: 1 + halo]
    query_out, key_out = refs[1 + halo :]
    rows = query_out.shape[0]
    index = lax.axis_index("ctx")
    given = []
    for ref in packets:
        hot = ref[2 * rows : 2 * rows + count, :].astype(jnp.float32)
        counts = jnp.sum(hot, axis=1, keepdims=True)
        mine = jnp.zeros((1, 1), jnp.float32)
        for p in range(count):
            mine = jnp.where(index == p, counts[p : p + 1, :], mine)
        given.append(mine.astype(jnp.int32))
    if len(given) < count:
        given.append(rows - sum(given))
    giver = [lax.rem(index - d + count, count) for d in range(count)]

    def placement(size, halo):
        lane = lax.broadcasted_iota(jnp.int32, (1, count * size), 1)
        target = jnp.full(lane.shape, -1, jnp.int32)
        for k in range(count):
            step = lane - k * size
            for back in range(halo + 1):
                block = (index ^ k) - back
                start = jnp.zeros((1, 1), jnp.int32)
                length = jnp.zeros((1, 1), jnp.int32)
                for d in range(count):
                    start = start + jnp.where(giver[d] < block, given[d], 0)
                    length = length + jnp.where(giver[d] == block, given[d], 0)
                target = jnp.where((step >= 0) & (step < length), start + step, target)
                step = step - length
        return one_hot(rows, target)

    query_out[...] = placement(2 * rows // count, 0)
    key_out[...] = placement(rows, halo)


def place_kernel(count, query_spread, key_spread, *refs):
    ins = refs[:count]
    query_out, key_out, value_out = refs[count : count + 3]
    query_here, key_here, value_here, sems = refs[count + 3 :]
    rows, width = query_here.shape
    depth = key_here.shape[1]
    heads = width // depth
    slot = 2 * rows // count
    copies = []

    def leave(here, out):
        copies.append(pltpu.make_async_copy(here, out, sems.at[len(copies)]))
        copies[-1].start()

    def taken(first, size, pieces):
        return jnp.concatenate(
            [
                jnp.concatenate(
                    [ref[first + n * size : first + (n + 1) * size, :] for n in range(pieces)],
                    axis=1,
                )
                for ref in ins
            ],
            axis=0,
        )

    query_here[...] = contract(query_spread[...], taken(0, slot, heads), 1, 0)
    leave(query_here, query_out)
    both = contract(key_spread[...], taken(heads * slot, rows, 2), 1, 0)
    for n, (here, out) in enumerate(((key_here, key_out), (value_here, value_out))):
        here[...] = both[:, n * depth : (n + 1) * depth]
        leave(here, out)
    for copy in copies:
        copy.wait()


def near_plan(doc_lengths, owners, queries, key_head_rows, value_head_rows, forward_out, grad_out):
    count = lax.axis_size("ctx")
    rows, width = queries.shape
    depth = key_head_rows.shape[1]
    heads = width // depth
    bf16, f32 = jnp.bfloat16, jnp.float32
    columns = heads * rows
    halo = count // 2
    slot = 2 * rows // count
    whole = pl.BlockSpec(memory_space=pltpu.VMEM)
    params = pltpu.CompilerParams(vmem_limit_bytes=40 * 1024 * 1024)

    mark = lax.broadcasted_iota(jnp.int32, (2 * rows + META, rows), 0) - 2 * rows
    packet = jnp.where(
        mark < 0,
        jnp.pad(jnp.concatenate([key_head_rows, value_head_rows], axis=0), ((0, META), (0, 0))),
        (owners[None, :] == mark).astype(bf16),
    )
    block_shapes = [jax.ShapeDtypeStruct((rows, columns), f32)] * 2
    row_shape = jax.ShapeDtypeStruct((8, columns), f32)
    target_shape = jax.ShapeDtypeStruct((count * rows, rows), bf16)
    filled_shape = jax.ShapeDtypeStruct((8, rows), f32)
    score_shapes = [
        jax.ShapeDtypeStruct((columns, depth), bf16),
        block_shapes[0],
        row_shape,
        jax.ShapeDtypeStruct((count * slot, rows), bf16),
        target_shape,
        filled_shape,
    ]
    near = [lax.ppermute(packet, "ctx", [(i, (i + 1) % count) for i in range(count)])]
    far, *scored = pl.pallas_call(
        functools.partial(odd_kernel, count, doc_lengths.shape[0]),
        out_shape=[jax.ShapeDtypeStruct(packet.shape, bf16)] + score_shapes,
        in_specs=[pl.BlockSpec(memory_space=pltpu.SMEM)] + [whole] * 2,
        out_specs=[whole] * 7,
        compiler_params=params,
    )(doc_lengths, packet, queries)
    near += [
        lax.ppermute(far, "ctx", [(i, (i + back) % count) for i in range(count)])
        for back in range(2, halo + 1)
    ]
    query_rows, raised, row, spread, target, filled, grad_rows, change = pl.pallas_call(
        functools.partial(own_kernel, count, doc_lengths.shape[0]),
        out_shape=score_shapes + [jax.ShapeDtypeStruct((columns, depth), bf16), block_shapes[1]],
        in_specs=[pl.BlockSpec(memory_space=pltpu.SMEM)] + [whole] * 10,
        out_specs=[whole] * 8,
        compiler_params=params,
    )(doc_lengths, packet, queries, grad_out, forward_out, *scored)
    raised, change, target = [raised], [change], [target]
    for back in range(1, halo):
        found = pl.pallas_call(
            functools.partial(step_kernel, count, back),
            out_shape=block_shapes + [row_shape, target_shape, filled_shape],
            in_specs=[whole] * 5,
            out_specs=[whole] * 5,
            compiler_params=params,
        )(query_rows, grad_rows, row, filled, near[back - 1])
        raised.append(found[0])
        change.append(found[1])
        row = found[2]
        target.append(found[3])
        filled = found[4]
    sent = pl.pallas_call(
        functools.partial(attend_kernel, count, halo),
        out_shape=[jax.ShapeDtypeStruct((heads * slot + 2 * rows, depth), bf16)] * count,
        in_specs=[whole] * (6 + 4 * halo),
        out_specs=[whole] * count,
        compiler_params=params,
    )(query_rows, grad_rows, row, filled, spread, *raised, *change, *target, packet, *near)
    received = [sent[0]] + [
        lax.ppermute(sent[k], "ctx", [(i, i ^ k) for i in range(count)]) for k in range(1, count)
    ]
    spreads = pl.pallas_call(
        functools.partial(order_kernel, count, halo),
        out_shape=[
            jax.ShapeDtypeStruct((rows, count * slot), bf16),
            jax.ShapeDtypeStruct((rows, count * rows), bf16),
        ],
        in_specs=[pl.BlockSpec(memory_space=pl.ANY)] + [whole] * (1 + halo),
        out_specs=[whole] * 2,
        compiler_params=params,
    )(received[-1], packet, *near)
    return pl.pallas_call(
        functools.partial(place_kernel, count),
        out_shape=[
            jax.ShapeDtypeStruct((rows, width), f32),
            jax.ShapeDtypeStruct((rows, depth), f32),
            jax.ShapeDtypeStruct((rows, depth), f32),
        ],
        in_specs=[whole] * (2 + count),
        out_specs=[pl.BlockSpec(memory_space=pl.ANY)] * 3,
        scratch_shapes=[
            pltpu.VMEM((rows, width), f32),
            pltpu.VMEM((rows, depth), f32),
            pltpu.VMEM((rows, depth), f32),
            pltpu.SemaphoreType.DMA((3,)),
        ],
        compiler_params=params,
    )(*spreads, *received)


def per_device(*args):
    if lax.axis_size("ctx") in (2, 4):
        return near_plan(*args)
    return ring_plan(*args)


def solution(mesh):
    return jax.shard_map(
        per_device,
        mesh=mesh,
        in_specs=(
            P("groups"),
            P(("groups", "ctx")),
            P(("groups", "ctx"), "head"),
            P(("groups", "ctx"), "head"),
            P(("groups", "ctx"), "head"),
            P(("groups", "ctx"), "head"),
            P(("groups", "ctx"), "head"),
        ),
        out_specs=(
            P(("groups", "ctx"), "head"),
            P(("groups", "ctx"), "head"),
            P(("groups", "ctx"), "head"),
        ),
        check_vma=False,
    )
```

```python
import functools
import math

import jax
import jax.numpy as jnp
from jax import lax
from jax.experimental import pallas as pl
from jax.experimental.pallas import tpu as pltpu
from jax.sharding import PartitionSpec as P

HEAD_WIDTH = 128
GROUP = 4


NEG = -1e30
BLOCK = 512


def shifted(value, axis, by):
    count = lax.axis_size(axis)
    return lax.ppermute(value, axis, [(i, (i + by) % count) for i in range(count)])


def document_of(positions, doc_lengths):
    ends = jnp.cumsum(doc_lengths)
    return jnp.sum((positions[:, None] >= ends[None, :]).astype(jnp.int32), axis=1)


def allowed_between(query_positions, query_docs, key_positions, key_docs):
    return (query_docs[:, None] == key_docs[None, :]) & (
        key_positions[None, :] <= query_positions[:, None]
    )


def head_rows(matrix, group_size, head_dim):
    row_count = matrix.shape[0]
    return matrix.reshape(row_count * group_size, head_dim)


def block_scores(query_flat, key_head, row_count, group_size, head_dim):
    scores = lax.dot_general(
        query_flat, key_head, (((1,), (1,)), ((), ())), preferred_element_type=jnp.float32
    )
    return (scores * (1.0 / math.sqrt(head_dim))).reshape(row_count, group_size, key_head.shape[0])


def update_stats(running, query_local, key_block, allowed, group_size, head_dim):
    running_max, totals = running
    row_count = query_local.shape[0]
    scores = block_scores(
        head_rows(query_local, group_size, head_dim), key_block, row_count, group_size, head_dim
    )
    masked = jnp.where(allowed[:, None, :], scores, NEG)
    new_max = jnp.maximum(running_max, jnp.max(masked, axis=2))
    weights = jnp.where(allowed[:, None, :], jnp.exp(masked - new_max[:, :, None]), 0.0)
    new_totals = [totals * jnp.exp(running_max - new_max) + jnp.sum(weights, axis=2)]
    new_maxima = [new_max]
    return (jnp.concatenate(new_maxima, axis=1), jnp.concatenate(new_totals, axis=1))


def backward_block(
    query_local,
    grad_local,
    log_norm,
    row_delta,
    key_block,
    value_block,
    allowed,
    group_size,
    head_dim,
):
    row_count = query_local.shape[0]
    query_flat = head_rows(query_local, group_size, head_dim)
    grad_flat = head_rows(grad_local, group_size, head_dim)
    scores = block_scores(query_flat, key_block, row_count, group_size, head_dim)
    masked = jnp.where(allowed[:, None, :], scores, NEG)
    weights = jnp.exp(masked - log_norm[:, 0:group_size, None])
    grad_weights = lax.dot_general(
        grad_flat, value_block, (((1,), (1,)), ((), ())), preferred_element_type=jnp.float32
    ).reshape(row_count, group_size, -1)
    grad_scores = weights * (grad_weights - row_delta[:, 0:group_size, None])
    rounded_weights = weights.astype(jnp.bfloat16).reshape(row_count * group_size, -1)
    rounded_grads = grad_scores.astype(jnp.bfloat16).reshape(row_count * group_size, -1)
    value_parts = [
        lax.dot_general(
            rounded_weights, grad_flat, (((0,), (0,)), ((), ())), preferred_element_type=jnp.float32
        )
    ]
    key_parts = [
        lax.dot_general(
            rounded_grads, query_flat, (((0,), (0,)), ((), ())), preferred_element_type=jnp.float32
        )
    ]
    query_parts = [
        jnp.dot(rounded_grads, key_block, preferred_element_type=jnp.float32).reshape(
            row_count, group_size * head_dim
        )
    ]
    return (
        jnp.concatenate(query_parts, axis=1),
        jnp.concatenate(key_parts, axis=1),
        jnp.concatenate(value_parts, axis=1),
    )


def ring_plan(doc_lengths, owners, queries, key_head_rows, value_head_rows, forward_out, grad_out):
    context_size = lax.axis_size("ctx")
    context_index = lax.axis_index("ctx")
    row_count = queries.shape[0]
    head_dim = HEAD_WIDTH
    group_size = GROUP
    query_heads = queries.shape[1] // head_dim
    slot_count = 2 * row_count // context_size
    everyone = lax.all_gather(owners, "ctx", axis=0, tiled=True)
    row_arrangement = jnp.argsort(everyone, stable=True)
    layout_docs = document_of(row_arrangement, doc_lengths)
    own_positions = lax.dynamic_slice_in_dim(
        row_arrangement, context_index * row_count, row_count, 0
    )
    own_documents = lax.dynamic_slice_in_dim(layout_docs, context_index * row_count, row_count, 0)
    owner_ids = jnp.arange(context_size, dtype=jnp.int32)
    owner_hot = (owners[:, None] == owner_ids[None, :]).astype(jnp.int32)
    earlier = jnp.cumsum(owner_hot, axis=0) - owner_hot
    rank_within = jnp.sum(earlier * owner_hot, axis=1)
    slot_rows = owners * slot_count + rank_within

    def packed(matrix):
        empty = jnp.zeros((context_size * slot_count,) + matrix.shape[1:], matrix.dtype)
        return empty.at[slot_rows].set(matrix)

    owner_grid = everyone.reshape(context_size, row_count)
    counts = jnp.sum((owner_grid == context_index).astype(jnp.int32), axis=1)
    count_ends = jnp.cumsum(counts)
    starts = count_ends - counts
    wanted = jnp.arange(row_count, dtype=jnp.int32)
    source = jnp.sum((wanted[:, None] >= count_ends[None, :]).astype(jnp.int32), axis=1)
    source_hot = (source[:, None] == owner_ids[None, :]).astype(jnp.int32)
    take_rows = source * slot_count + wanted - jnp.sum(source_hot * starts[None, :], axis=1)

    def compact(received):
        return jnp.take(received, take_rows, axis=0)

    local_delta = jnp.sum(
        (grad_out.astype(jnp.float32) * forward_out.astype(jnp.float32)).reshape(
            row_count, query_heads, head_dim
        ),
        axis=2,
    )
    arrived = (
        lax.all_to_all(packed(queries), "ctx", split_axis=0, concat_axis=0, tiled=True),
        lax.all_to_all(packed(key_head_rows), "ctx", split_axis=0, concat_axis=0, tiled=True),
        lax.all_to_all(packed(value_head_rows), "ctx", split_axis=0, concat_axis=0, tiled=True),
        lax.all_to_all(packed(grad_out), "ctx", split_axis=0, concat_axis=0, tiled=True),
    )
    query_local, key_local, value_local, grad_local = [compact(received) for received in arrived]
    row_delta = compact(
        lax.all_to_all(packed(local_delta), "ctx", split_axis=0, concat_axis=0, tiled=True)
    )

    def fold_keys(running, shard_rows, first_row):
        piece_count = shard_rows.shape[0]
        step_rows = math.gcd(piece_count, BLOCK) if piece_count > BLOCK else piece_count

        def one_block(partial_value, block_index):
            offset = first_row + block_index * step_rows
            key_block = lax.dynamic_slice_in_dim(shard_rows, block_index * step_rows, step_rows, 0)
            key_positions = lax.dynamic_slice_in_dim(row_arrangement, offset, step_rows, 0)
            key_docs = lax.dynamic_slice_in_dim(layout_docs, offset, step_rows, 0)
            allowed = allowed_between(own_positions, own_documents, key_positions, key_docs)
            return (
                update_stats(partial_value, query_local, key_block, allowed, group_size, head_dim),
                None,
            )

        if piece_count == step_rows:
            return one_block(running, 0)[0]
        return lax.scan(one_block, running, jnp.arange(piece_count // step_rows, dtype=jnp.int32))[
            0
        ]

    start_stats = (
        jnp.full((row_count, query_heads), NEG, jnp.float32),
        jnp.zeros((row_count, query_heads), jnp.float32),
    )
    top_scores, totals = fold_keys(
        start_stats, lax.all_gather(key_local, "ctx", axis=0, tiled=True), jnp.int32(0)
    )
    log_norm = top_scores + jnp.log(totals)

    def block_meta(owner_index, offset, size):
        first = owner_index * row_count + offset
        key_positions = lax.dynamic_slice_in_dim(row_arrangement, first, size, 0)
        key_docs = lax.dynamic_slice_in_dim(layout_docs, first, size, 0)
        return (key_positions, key_docs)

    query_zero = jnp.zeros(query_local.shape, jnp.float32)
    key_zero = jnp.zeros(key_local.shape, jnp.float32)

    def one_turn(turn_index, loop_state):
        key_moving, value_moving, key_grad, value_grad, query_grad = loop_state
        owner_index = (context_index - turn_index) % context_size
        key_positions, key_docs = block_meta(owner_index, 0, row_count)
        allowed = allowed_between(own_positions, own_documents, key_positions, key_docs)
        query_part, key_part, value_part = backward_block(
            query_local,
            grad_local,
            log_norm,
            row_delta,
            key_moving,
            value_moving,
            allowed,
            group_size,
            head_dim,
        )
        return (
            key_moving,
            value_moving,
            key_grad + key_part,
            value_grad + value_part,
            query_grad + query_part,
        )

    def moved_turn(turn_index, loop_state):
        key_moving, value_moving, key_grad, value_grad, query_grad = loop_state
        key_moving, value_moving = shifted((key_moving, value_moving), "ctx", 1)
        key_grad, value_grad = shifted((key_grad, value_grad), "ctx", 1)
        return one_turn(turn_index, (key_moving, value_moving, key_grad, value_grad, query_grad))

    loop_state = one_turn(0, (key_local, value_local, key_zero, key_zero, query_zero))
    loop_state = lax.fori_loop(1, context_size, moved_turn, loop_state)
    key_grad, value_grad = shifted((loop_state[2], loop_state[3]), "ctx", 1)
    query_grad = loop_state[4]
    inverse_root = 1.0 / math.sqrt(head_dim)
    return (query_grad * inverse_root, key_grad * inverse_root, value_grad)


META = 8


def contract(left, right, left_dim, right_dim, **kw):
    return lax.dot_general(
        left,
        right,
        (((left_dim,), (right_dim,)), ((), ())),
        preferred_element_type=jnp.float32,
        **kw,
    )


def one_hot(row_count, target):
    places = lax.broadcasted_iota(jnp.int32, (row_count, target.shape[1]), 0)
    return jnp.where(places == target, 1.0, 0.0).astype(jnp.bfloat16)


def side_by_side(stack, heads):
    rows = stack.shape[0] // heads
    return jnp.concatenate([stack[h * rows : (h + 1) * rows, :] for h in range(heads)], axis=1)


def end_to_end(matrix, heads):
    width = matrix.shape[1] // heads
    return jnp.concatenate([matrix[:, h * width : (h + 1) * width] for h in range(heads)], axis=0)


def runs_of(hot):
    count, rows = hot.shape
    counts = jnp.sum(hot, axis=1, keepdims=True)
    owner = jnp.zeros((1, rows), jnp.int32)
    earlier = jnp.zeros((1, rows), jnp.float32)
    for p in range(count):
        mine = hot[p : p + 1, :] > 0.0
        owner = jnp.where(mine, p, owner)
        for less in range(p):
            earlier = earlier + jnp.where(mine, counts[less : less + 1, :], 0.0)
    lane = lax.broadcasted_iota(jnp.int32, (1, rows), 1)
    return owner, counts, lane - earlier.astype(jnp.int32)


def own_scores(count, docs, doc_ref, packet_ref, query_ref, outs):
    query_out, raised_out, row_out, spread_out, target_out, filled_out = outs
    rows, width = query_ref.shape
    depth = packet_ref.shape[1]
    heads = width // depth
    slot = 2 * rows // count
    index = lax.axis_index("ctx")
    lane = lax.broadcasted_iota(jnp.int32, (1, rows), 1)
    position = index * rows + lane
    earlier = lax.broadcasted_iota(jnp.int32, (docs, docs), 1) <= lax.broadcasted_iota(
        jnp.int32, (docs, docs), 0
    )
    lengths = doc_ref[...].astype(jnp.float32)
    ends = jnp.sum(jnp.where(earlier, lengths, 0.0), axis=1, keepdims=True).astype(jnp.int32)
    first = jnp.max(jnp.where(ends <= position, ends, 0), axis=0, keepdims=True)
    key_position = index * rows + lax.broadcasted_iota(jnp.int32, (rows, rows), 0)
    allowed = (key_position >= first) & (key_position <= position)
    allowed = jnp.concatenate([allowed] * heads, axis=1)

    queries = end_to_end(query_ref[...], heads)
    query_out[...] = queries
    scores = contract(packet_ref[0:rows, :], queries, 1, 1) * (1.0 / math.sqrt(depth))
    scores = jnp.where(allowed, scores, NEG)
    top = jnp.max(scores, axis=0, keepdims=True)
    raised = jnp.exp(scores - top)
    raised_out[...] = raised
    row_out[0:1, :] = jnp.zeros((1, width), jnp.float32)
    row_out[1:2, :] = top
    row_out[2:3, :] = jnp.sum(raised, axis=0, keepdims=True)
    row_out[3:4, :] = jnp.concatenate([first.astype(jnp.float32)] * heads, axis=1)
    row_out[4:8, :] = jnp.ones((4, width), jnp.float32)
    owner, counts, rank = runs_of(packet_ref[2 * rows : 2 * rows + count, :].astype(jnp.float32))
    spread_out[...] = one_hot(count * slot, (owner ^ index) * slot + rank)
    target_out[...] = one_hot(count * rows, (owner ^ index) * rows + rank)
    filled_out[0:count, :] = jnp.broadcast_to(counts, (count, rows))
    filled_out[count:, :] = jnp.zeros((8 - count, rows), jnp.float32)


def odd_kernel(count, docs, doc_ref, packet_ref, query_ref, packet_out, *outs):
    packet_out[...] = packet_ref[...]

    @pl.when(lax.rem(lax.axis_index("ctx"), 2) == 1)
    def _():
        own_scores(count, docs, doc_ref, packet_ref, query_ref, outs)


def own_kernel(count, docs, doc_ref, packet_ref, query_ref, grad_ref, saved_ref, *refs):
    done, outs = refs[:6], refs[6:12]
    grad_out, change_out = refs[12:]
    rows, width = query_ref.shape
    depth = packet_ref.shape[1]
    heads = width // depth
    odd = lax.rem(lax.axis_index("ctx"), 2) == 1

    @pl.when(odd)
    def _():
        for here, out in zip(done, outs, strict=True):
            out[...] = here[...]

    @pl.when(jnp.logical_not(odd))
    def _():
        own_scores(count, docs, doc_ref, packet_ref, query_ref, outs)

    grads = end_to_end(grad_ref[...], heads)
    grad_out[...] = grads
    product = grads.astype(jnp.float32) * end_to_end(saved_ref[...], heads).astype(jnp.float32)
    delta = contract(
        jnp.ones((8, depth), jnp.float32), product, 1, 1, precision=lax.Precision.HIGHEST
    )[0:1, :]
    change_out[...] = contract(packet_ref[rows : 2 * rows, :], grads, 1, 1) - delta
    outs[2][0:1, :] = delta


def fold(count, back, packet, queries, grads, row, filled):
    rows = packet.shape[1]
    index = lax.axis_index("ctx")
    delta, top, total = (row[n : n + 1, :] for n in range(3))
    first = row[3:4, :].astype(jnp.int32)
    position = (index - back) * rows + lax.broadcasted_iota(jnp.int32, (rows, row.shape[1]), 0)
    scores = contract(packet[0:rows, :], queries, 1, 1) * (1.0 / math.sqrt(queries.shape[1]))
    scores = jnp.where(position >= first, scores, NEG)
    new_top = jnp.maximum(top, jnp.max(scores, axis=0, keepdims=True))
    raised = jnp.exp(scores - new_top)
    shrink = jnp.exp(top - new_top)
    total = total * shrink + jnp.sum(raised, axis=0, keepdims=True)
    change = contract(packet[rows : 2 * rows, :], grads, 1, 1) - delta
    factors = row[4:8, :] * jnp.where(
        lax.broadcasted_iota(jnp.int32, (4, row.shape[1]), 0) < back, shrink, 1.0
    )
    owner, counts, rank = runs_of(packet[2 * rows : 2 * rows + count, :].astype(jnp.float32))
    base = jnp.zeros((1, rows), jnp.float32)
    for p in range(count):
        base = base + jnp.where(owner == p, filled[p : p + 1, :], 0.0)
    inside = index >= back
    target = jnp.where(inside, (owner ^ index) * rows + base.astype(jnp.int32) + rank, -1)
    filled = filled[0:count, :] + jnp.where(inside, counts, 0.0)
    return raised, change, (new_top, total, factors), one_hot(count * rows, target), filled


def step_kernel(count, back, *refs):
    query_ref, grad_ref, row_ref, filled_ref, packet_ref = refs[:5]
    raised_out, change_out, row_out, target_out, filled_out = refs[5:]
    raised, change, (top, total, factors), target, filled = fold(
        count, back, packet_ref, query_ref[...], grad_ref[...], row_ref, filled_ref
    )
    raised_out[...] = raised
    change_out[...] = change
    row_out[0:1, :] = row_ref[0:1, :]
    row_out[1:2, :] = top
    row_out[2:3, :] = total
    row_out[3:4, :] = row_ref[3:4, :]
    row_out[4:8, :] = factors
    target_out[...] = target
    filled_out[0:count, :] = filled
    filled_out[count:, :] = jnp.zeros_like(filled_out[count:, :])


def attend_kernel(count, halo, *refs):
    query_ref, grad_ref, row_ref, filled_ref, spread_ref = refs[:5]
    raised_refs = refs[5 : 5 + halo]
    change_refs = refs[5 + halo : 5 + 2 * halo]
    target_refs = refs[5 + 2 * halo : 5 + 3 * halo]
    packets = refs[5 + 3 * halo : 6 + 4 * halo]
    outs = refs[6 + 4 * halo :]
    rows = packets[0].shape[1]
    depth = query_ref.shape[1]
    heads = query_ref.shape[0] // rows
    slot = 2 * rows // count
    scale = 1.0 / math.sqrt(depth)
    queries = query_ref[...]
    grads = grad_ref[...]
    raised, change, (_, total, factors), target, _ = fold(
        count, halo, packets[halo], queries, grads, row_ref, filled_ref
    )
    factors = factors * (1.0 / total)
    weights = []
    changes = []
    for block in range(halo + 1):
        mine = raised if block == halo else raised_refs[block][...]
        mine = mine * factors[block : block + 1, :]
        weights.append(mine.astype(jnp.bfloat16))
        mine = mine * (change if block == halo else change_refs[block][...])
        changes.append(mine.astype(jnp.bfloat16))
    weights = jnp.concatenate(weights, axis=0)
    changes = jnp.concatenate(changes, axis=0)
    keys = jnp.concatenate([packet[0:rows, :] for packet in packets], axis=0)
    query_grad = (contract(keys, changes, 0, 0) * scale).astype(jnp.bfloat16)
    key_parts = contract(changes, queries, 1, 0) * scale
    value_parts = contract(weights, grads, 1, 0)
    parts = jnp.concatenate([key_parts, value_parts], axis=1).astype(jnp.bfloat16)

    query_slots = contract(spread_ref[...], end_to_end(query_grad, heads), 1, 1)
    query_slots = query_slots.astype(jnp.bfloat16)
    spread = jnp.concatenate([ref[...] for ref in target_refs] + [target], axis=1)
    part_slots = contract(spread, parts, 1, 0).astype(jnp.bfloat16)
    at = heads * slot
    for k in range(count):
        out = outs[k]
        for h in range(heads):
            out[h * slot : (h + 1) * slot, :] = query_slots[
                k * slot : (k + 1) * slot, h * depth : (h + 1) * depth
            ]
        for n in range(2):
            out[at + n * rows : at + (n + 1) * rows, :] = part_slots[
                k * rows : (k + 1) * rows, n * depth : (n + 1) * depth
            ]


def order_kernel(count, halo, _, *refs):
    packets = refs[: 1 + halo]
    query_out, key_out = refs[1 + halo :]
    rows = query_out.shape[0]
    index = lax.axis_index("ctx")
    given = []
    for ref in packets:
        hot = ref[2 * rows : 2 * rows + count, :].astype(jnp.float32)
        counts = jnp.sum(hot, axis=1, keepdims=True)
        mine = jnp.zeros((1, 1), jnp.float32)
        for p in range(count):
            mine = jnp.where(index == p, counts[p : p + 1, :], mine)
        given.append(mine.astype(jnp.int32))
    if len(given) < count:
        given.append(rows - sum(given))
    giver = [lax.rem(index - d + count, count) for d in range(count)]

    def placement(size, halo):
        lane = lax.broadcasted_iota(jnp.int32, (1, count * size), 1)
        target = jnp.full(lane.shape, -1, jnp.int32)
        for k in range(count):
            step = lane - k * size
            for back in range(halo + 1):
                block = (index ^ k) - back
                start = jnp.zeros((1, 1), jnp.int32)
                length = jnp.zeros((1, 1), jnp.int32)
                for d in range(count):
                    start = start + jnp.where(giver[d] < block, given[d], 0)
                    length = length + jnp.where(giver[d] == block, given[d], 0)
                target = jnp.where((step >= 0) & (step < length), start + step, target)
                step = step - length
        return one_hot(rows, target)

    query_out[...] = placement(2 * rows // count, 0)
    key_out[...] = placement(rows, halo)


def place_kernel(count, query_spread, key_spread, *refs):
    query_out, key_out, value_out, query_here, key_here, value_here, sems = refs[-7:]
    even = lax.rem(lax.axis_index("ctx"), 2) == 0
    ins = []
    for k in range(count):
        here = refs[len(ins) + sum(n % 2 == 0 for n in range(1, k)) :]
        ins.append(jnp.where(even, here[1][...], here[0][...]) if k and k % 2 == 0 else here[0])
    rows, width = query_here.shape
    depth = key_here.shape[1]
    heads = width // depth
    slot = 2 * rows // count
    copies = []

    def leave(here, out):
        copies.append(pltpu.make_async_copy(here, out, sems.at[len(copies)]))
        copies[-1].start()

    def taken(first, size, pieces):
        return jnp.concatenate(
            [
                jnp.concatenate(
                    [ref[first + n * size : first + (n + 1) * size, :] for n in range(pieces)],
                    axis=1,
                )
                for ref in ins
            ],
            axis=0,
        )

    query_here[...] = contract(query_spread[...], taken(0, slot, heads), 1, 0)
    leave(query_here, query_out)
    both = contract(key_spread[...], taken(heads * slot, rows, 2), 1, 0)
    for n, (here, out) in enumerate(((key_here, key_out), (value_here, value_out))):
        here[...] = both[:, n * depth : (n + 1) * depth]
        leave(here, out)
    for copy in copies:
        copy.wait()


def near_plan(doc_lengths, owners, queries, key_head_rows, value_head_rows, forward_out, grad_out):
    count = lax.axis_size("ctx")
    rows, width = queries.shape
    depth = key_head_rows.shape[1]
    heads = width // depth
    bf16, f32 = jnp.bfloat16, jnp.float32
    columns = heads * rows
    halo = count // 2
    slot = 2 * rows // count
    whole = pl.BlockSpec(memory_space=pltpu.VMEM)
    params = pltpu.CompilerParams(vmem_limit_bytes=40 * 1024 * 1024)

    mark = lax.broadcasted_iota(jnp.int32, (2 * rows + META, rows), 0) - 2 * rows
    packet = jnp.where(
        mark < 0,
        jnp.pad(jnp.concatenate([key_head_rows, value_head_rows], axis=0), ((0, META), (0, 0))),
        (owners[None, :] == mark).astype(bf16),
    )
    block_shapes = [jax.ShapeDtypeStruct((rows, columns), f32)] * 2
    row_shape = jax.ShapeDtypeStruct((8, columns), f32)
    target_shape = jax.ShapeDtypeStruct((count * rows, rows), bf16)
    filled_shape = jax.ShapeDtypeStruct((8, rows), f32)
    score_shapes = [
        jax.ShapeDtypeStruct((columns, depth), bf16),
        block_shapes[0],
        row_shape,
        jax.ShapeDtypeStruct((count * slot, rows), bf16),
        target_shape,
        filled_shape,
    ]
    near = [lax.ppermute(packet, "ctx", [(i, (i + 1) % count) for i in range(count)])]
    far, *scored = pl.pallas_call(
        functools.partial(odd_kernel, count, doc_lengths.shape[0]),
        out_shape=[jax.ShapeDtypeStruct(packet.shape, bf16)] + score_shapes,
        in_specs=[whole] * 3,
        out_specs=[whole] * 7,
        compiler_params=params,
    )(doc_lengths.reshape(1, -1), packet, queries)
    near += [
        lax.ppermute(far, "ctx", [(i, (i + back) % count) for i in range(count)])
        for back in range(2, halo + 1)
    ]
    query_rows, raised, row, spread, target, filled, grad_rows, change = pl.pallas_call(
        functools.partial(own_kernel, count, doc_lengths.shape[0]),
        out_shape=score_shapes + [jax.ShapeDtypeStruct((columns, depth), bf16), block_shapes[1]],
        in_specs=[whole] * 11,
        out_specs=[whole] * 8,
        compiler_params=params,
    )(doc_lengths.reshape(1, -1), packet, queries, grad_out, forward_out, *scored)
    raised, change, target = [raised], [change], [target]
    for back in range(1, halo):
        found = pl.pallas_call(
            functools.partial(step_kernel, count, back),
            out_shape=block_shapes + [row_shape, target_shape, filled_shape],
            in_specs=[whole] * 5,
            out_specs=[whole] * 5,
            compiler_params=params,
        )(query_rows, grad_rows, row, filled, near[back - 1])
        raised.append(found[0])
        change.append(found[1])
        row = found[2]
        target.append(found[3])
        filled = found[4]
    sent = pl.pallas_call(
        functools.partial(attend_kernel, count, halo),
        out_shape=[jax.ShapeDtypeStruct((heads * slot + 2 * rows, depth), bf16)] * count,
        in_specs=[whole] * (6 + 4 * halo),
        out_specs=[whole] * count,
        compiler_params=params,
    )(query_rows, grad_rows, row, filled, spread, *raised, *change, *target, packet, *near)
    received = [[sent[0]]]
    for k in range(1, count):
        parts = (1, 0) if k % 2 == 0 else (None,)
        received.append(
            [
                lax.ppermute(
                    sent[k], "ctx", [(i, i ^ k if part in (None, i % 2) else i) for i in range(count)]
                )
                for part in parts
            ]
        )
    spreads = pl.pallas_call(
        functools.partial(order_kernel, count, halo),
        out_shape=[
            jax.ShapeDtypeStruct((rows, count * slot), bf16),
            jax.ShapeDtypeStruct((rows, count * rows), bf16),
        ],
        in_specs=[pl.BlockSpec(memory_space=pl.ANY)] + [whole] * (1 + halo),
        out_specs=[whole] * 2,
        compiler_params=params,
    )(received[-1][0], packet, *near)
    return pl.pallas_call(
        functools.partial(place_kernel, count),
        out_shape=[
            jax.ShapeDtypeStruct((rows, width), f32),
            jax.ShapeDtypeStruct((rows, depth), f32),
            jax.ShapeDtypeStruct((rows, depth), f32),
        ],
        in_specs=[whole] * (2 + sum(map(len, received))),
        out_specs=[pl.BlockSpec(memory_space=pl.ANY)] * 3,
        scratch_shapes=[
            pltpu.VMEM((rows, width), f32),
            pltpu.VMEM((rows, depth), f32),
            pltpu.VMEM((rows, depth), f32),
            pltpu.SemaphoreType.DMA((3,)),
        ],
        compiler_params=params,
    )(*spreads, *sum(received, []))


def per_device(*args):
    if lax.axis_size("ctx") in (2, 4):
        return near_plan(*args)
    return ring_plan(*args)


def solution(mesh):
    return jax.shard_map(
        per_device,
        mesh=mesh,
        in_specs=(
            P("groups"),
            P(("groups", "ctx")),
            P(("groups", "ctx"), "head"),
            P(("groups", "ctx"), "head"),
            P(("groups", "ctx"), "head"),
            P(("groups", "ctx"), "head"),
            P(("groups", "ctx"), "head"),
        ),
        out_specs=(
            P(("groups", "ctx"), "head"),
            P(("groups", "ctx"), "head"),
            P(("groups", "ctx"), "head"),
        ),
        check_vma=False,
    )
```

```python
import functools
import math

import jax
import jax.numpy as jnp
from jax import lax
from jax.experimental import pallas as pl
from jax.experimental.pallas import tpu as pltpu
from jax.sharding import PartitionSpec as P

HEAD_WIDTH = 128
GROUP = 4


NEG = -1e30
BLOCK = 512


def shifted(value, axis, by):
    count = lax.axis_size(axis)
    return lax.ppermute(value, axis, [(i, (i + by) % count) for i in range(count)])


def document_of(positions, doc_lengths):
    ends = jnp.cumsum(doc_lengths)
    return jnp.sum((positions[:, None] >= ends[None, :]).astype(jnp.int32), axis=1)


def allowed_between(query_positions, query_docs, key_positions, key_docs):
    return (query_docs[:, None] == key_docs[None, :]) & (
        key_positions[None, :] <= query_positions[:, None]
    )


def head_rows(matrix, group_size, head_dim):
    row_count = matrix.shape[0]
    return matrix.reshape(row_count * group_size, head_dim)


def block_scores(query_flat, key_head, row_count, group_size, head_dim):
    scores = lax.dot_general(
        query_flat, key_head, (((1,), (1,)), ((), ())), preferred_element_type=jnp.float32
    )
    return (scores * (1.0 / math.sqrt(head_dim))).reshape(row_count, group_size, key_head.shape[0])


def update_stats(running, query_local, key_block, allowed, group_size, head_dim):
    running_max, totals = running
    row_count = query_local.shape[0]
    scores = block_scores(
        head_rows(query_local, group_size, head_dim), key_block, row_count, group_size, head_dim
    )
    masked = jnp.where(allowed[:, None, :], scores, NEG)
    new_max = jnp.maximum(running_max, jnp.max(masked, axis=2))
    weights = jnp.where(allowed[:, None, :], jnp.exp(masked - new_max[:, :, None]), 0.0)
    new_totals = [totals * jnp.exp(running_max - new_max) + jnp.sum(weights, axis=2)]
    new_maxima = [new_max]
    return (jnp.concatenate(new_maxima, axis=1), jnp.concatenate(new_totals, axis=1))


def backward_block(
    query_local,
    grad_local,
    log_norm,
    row_delta,
    key_block,
    value_block,
    allowed,
    group_size,
    head_dim,
):
    row_count = query_local.shape[0]
    query_flat = head_rows(query_local, group_size, head_dim)
    grad_flat = head_rows(grad_local, group_size, head_dim)
    scores = block_scores(query_flat, key_block, row_count, group_size, head_dim)
    masked = jnp.where(allowed[:, None, :], scores, NEG)
    weights = jnp.exp(masked - log_norm[:, 0:group_size, None])
    grad_weights = lax.dot_general(
        grad_flat, value_block, (((1,), (1,)), ((), ())), preferred_element_type=jnp.float32
    ).reshape(row_count, group_size, -1)
    grad_scores = weights * (grad_weights - row_delta[:, 0:group_size, None])
    rounded_weights = weights.astype(jnp.bfloat16).reshape(row_count * group_size, -1)
    rounded_grads = grad_scores.astype(jnp.bfloat16).reshape(row_count * group_size, -1)
    value_parts = [
        lax.dot_general(
            rounded_weights, grad_flat, (((0,), (0,)), ((), ())), preferred_element_type=jnp.float32
        )
    ]
    key_parts = [
        lax.dot_general(
            rounded_grads, query_flat, (((0,), (0,)), ((), ())), preferred_element_type=jnp.float32
        )
    ]
    query_parts = [
        jnp.dot(rounded_grads, key_block, preferred_element_type=jnp.float32).reshape(
            row_count, group_size * head_dim
        )
    ]
    return (
        jnp.concatenate(query_parts, axis=1),
        jnp.concatenate(key_parts, axis=1),
        jnp.concatenate(value_parts, axis=1),
    )


def ring_plan(doc_lengths, owners, queries, key_head_rows, value_head_rows, forward_out, grad_out):
    context_size = lax.axis_size("ctx")
    context_index = lax.axis_index("ctx")
    row_count = queries.shape[0]
    head_dim = HEAD_WIDTH
    group_size = GROUP
    query_heads = queries.shape[1] // head_dim
    slot_count = 2 * row_count // context_size
    everyone = lax.all_gather(owners, "ctx", axis=0, tiled=True)
    row_arrangement = jnp.argsort(everyone, stable=True)
    layout_docs = document_of(row_arrangement, doc_lengths)
    own_positions = lax.dynamic_slice_in_dim(
        row_arrangement, context_index * row_count, row_count, 0
    )
    own_documents = lax.dynamic_slice_in_dim(layout_docs, context_index * row_count, row_count, 0)
    owner_ids = jnp.arange(context_size, dtype=jnp.int32)
    owner_hot = (owners[:, None] == owner_ids[None, :]).astype(jnp.int32)
    earlier = jnp.cumsum(owner_hot, axis=0) - owner_hot
    rank_within = jnp.sum(earlier * owner_hot, axis=1)
    slot_rows = owners * slot_count + rank_within

    def packed(matrix):
        empty = jnp.zeros((context_size * slot_count,) + matrix.shape[1:], matrix.dtype)
        return empty.at[slot_rows].set(matrix)

    owner_grid = everyone.reshape(context_size, row_count)
    counts = jnp.sum((owner_grid == context_index).astype(jnp.int32), axis=1)
    count_ends = jnp.cumsum(counts)
    starts = count_ends - counts
    wanted = jnp.arange(row_count, dtype=jnp.int32)
    source = jnp.sum((wanted[:, None] >= count_ends[None, :]).astype(jnp.int32), axis=1)
    source_hot = (source[:, None] == owner_ids[None, :]).astype(jnp.int32)
    take_rows = source * slot_count + wanted - jnp.sum(source_hot * starts[None, :], axis=1)

    def compact(received):
        return jnp.take(received, take_rows, axis=0)

    local_delta = jnp.sum(
        (grad_out.astype(jnp.float32) * forward_out.astype(jnp.float32)).reshape(
            row_count, query_heads, head_dim
        ),
        axis=2,
    )
    arrived = (
        lax.all_to_all(packed(queries), "ctx", split_axis=0, concat_axis=0, tiled=True),
        lax.all_to_all(packed(key_head_rows), "ctx", split_axis=0, concat_axis=0, tiled=True),
        lax.all_to_all(packed(value_head_rows), "ctx", split_axis=0, concat_axis=0, tiled=True),
        lax.all_to_all(packed(grad_out), "ctx", split_axis=0, concat_axis=0, tiled=True),
    )
    query_local, key_local, value_local, grad_local = [compact(received) for received in arrived]
    row_delta = compact(
        lax.all_to_all(packed(local_delta), "ctx", split_axis=0, concat_axis=0, tiled=True)
    )

    def fold_keys(running, shard_rows, first_row):
        piece_count = shard_rows.shape[0]
        step_rows = math.gcd(piece_count, BLOCK) if piece_count > BLOCK else piece_count

        def one_block(partial_value, block_index):
            offset = first_row + block_index * step_rows
            key_block = lax.dynamic_slice_in_dim(shard_rows, block_index * step_rows, step_rows, 0)
            key_positions = lax.dynamic_slice_in_dim(row_arrangement, offset, step_rows, 0)
            key_docs = lax.dynamic_slice_in_dim(layout_docs, offset, step_rows, 0)
            allowed = allowed_between(own_positions, own_documents, key_positions, key_docs)
            return (
                update_stats(partial_value, query_local, key_block, allowed, group_size, head_dim),
                None,
            )

        if piece_count == step_rows:
            return one_block(running, 0)[0]
        return lax.scan(one_block, running, jnp.arange(piece_count // step_rows, dtype=jnp.int32))[
            0
        ]

    start_stats = (
        jnp.full((row_count, query_heads), NEG, jnp.float32),
        jnp.zeros((row_count, query_heads), jnp.float32),
    )
    top_scores, totals = fold_keys(
        start_stats, lax.all_gather(key_local, "ctx", axis=0, tiled=True), jnp.int32(0)
    )
    log_norm = top_scores + jnp.log(totals)

    def block_meta(owner_index, offset, size):
        first = owner_index * row_count + offset
        key_positions = lax.dynamic_slice_in_dim(row_arrangement, first, size, 0)
        key_docs = lax.dynamic_slice_in_dim(layout_docs, first, size, 0)
        return (key_positions, key_docs)

    query_zero = jnp.zeros(query_local.shape, jnp.float32)
    key_zero = jnp.zeros(key_local.shape, jnp.float32)

    def one_turn(turn_index, loop_state):
        key_moving, value_moving, key_grad, value_grad, query_grad = loop_state
        owner_index = (context_index - turn_index) % context_size
        key_positions, key_docs = block_meta(owner_index, 0, row_count)
        allowed = allowed_between(own_positions, own_documents, key_positions, key_docs)
        query_part, key_part, value_part = backward_block(
            query_local,
            grad_local,
            log_norm,
            row_delta,
            key_moving,
            value_moving,
            allowed,
            group_size,
            head_dim,
        )
        return (
            key_moving,
            value_moving,
            key_grad + key_part,
            value_grad + value_part,
            query_grad + query_part,
        )

    def moved_turn(turn_index, loop_state):
        key_moving, value_moving, key_grad, value_grad, query_grad = loop_state
        key_moving, value_moving = shifted((key_moving, value_moving), "ctx", 1)
        key_grad, value_grad = shifted((key_grad, value_grad), "ctx", 1)
        return one_turn(turn_index, (key_moving, value_moving, key_grad, value_grad, query_grad))

    loop_state = one_turn(0, (key_local, value_local, key_zero, key_zero, query_zero))
    loop_state = lax.fori_loop(1, context_size, moved_turn, loop_state)
    key_grad, value_grad = shifted((loop_state[2], loop_state[3]), "ctx", 1)
    query_grad = loop_state[4]
    inverse_root = 1.0 / math.sqrt(head_dim)
    return (query_grad * inverse_root, key_grad * inverse_root, value_grad)


META = 8


def contract(left, right, left_dim, right_dim, **kw):
    return lax.dot_general(
        left,
        right,
        (((left_dim,), (right_dim,)), ((), ())),
        preferred_element_type=jnp.float32,
        **kw,
    )


def one_hot(row_count, target):
    places = lax.broadcasted_iota(jnp.int32, (row_count, target.shape[1]), 0)
    return jnp.where(places == target, 1.0, 0.0).astype(jnp.bfloat16)


def side_by_side(stack, heads):
    rows = stack.shape[0] // heads
    return jnp.concatenate([stack[h * rows : (h + 1) * rows, :] for h in range(heads)], axis=1)


def end_to_end(matrix, heads):
    width = matrix.shape[1] // heads
    return jnp.concatenate([matrix[:, h * width : (h + 1) * width] for h in range(heads)], axis=0)


def target_of(index, k, count):
    if count == 4 and k in (1, 2):
        return (2 * index + 1) % 5 if k == 1 else (3 * index + 2) % 5
    return index ^ k


def source_of(index, k, count):
    return target_of(index, 3 - k if count == 4 and k in (1, 2) else k, count)


def exchange_of(owner, index, count):
    found = jnp.zeros_like(owner)
    for k in range(1, count):
        found = jnp.where(owner == target_of(index, k, count), k, found)
    return found


def runs_of(hot):
    count, rows = hot.shape
    counts = jnp.sum(hot, axis=1, keepdims=True)
    owner = jnp.zeros((1, rows), jnp.int32)
    earlier = jnp.zeros((1, rows), jnp.float32)
    for p in range(count):
        mine = hot[p : p + 1, :] > 0.0
        owner = jnp.where(mine, p, owner)
        for less in range(p):
            earlier = earlier + jnp.where(mine, counts[less : less + 1, :], 0.0)
    lane = lax.broadcasted_iota(jnp.int32, (1, rows), 1)
    return owner, counts, lane - earlier.astype(jnp.int32)


def own_kernel(
    count,
    docs,
    doc_ref,
    packet_ref,
    query_ref,
    grad_ref,
    saved_ref,
    query_out,
    grad_out,
    raised_out,
    change_out,
    row_out,
    spread_out,
    target_out,
    filled_out,
):
    rows, width = query_ref.shape
    depth = packet_ref.shape[1]
    heads = width // depth
    slot = 2 * rows // count
    index = lax.axis_index("ctx")
    lane = lax.broadcasted_iota(jnp.int32, (1, rows), 1)
    position = index * rows + lane
    earlier = lax.broadcasted_iota(jnp.int32, (docs, docs), 1) <= lax.broadcasted_iota(
        jnp.int32, (docs, docs), 0
    )
    lengths = doc_ref[...].astype(jnp.float32)
    ends = jnp.sum(jnp.where(earlier, lengths, 0.0), axis=1, keepdims=True).astype(jnp.int32)
    first = jnp.max(jnp.where(ends <= position, ends, 0), axis=0, keepdims=True)
    key_position = index * rows + lax.broadcasted_iota(jnp.int32, (rows, rows), 0)
    allowed = (key_position >= first) & (key_position <= position)
    allowed = jnp.concatenate([allowed] * heads, axis=1)

    queries = end_to_end(query_ref[...], heads)
    query_out[...] = queries
    scores = contract(packet_ref[0:rows, :], queries, 1, 1) * (1.0 / math.sqrt(depth))
    scores = jnp.where(allowed, scores, NEG)
    top = jnp.max(scores, axis=0, keepdims=True)
    raised = jnp.exp(scores - top)
    raised_out[...] = raised
    grads = end_to_end(grad_ref[...], heads)
    grad_out[...] = grads
    product = grads.astype(jnp.float32) * end_to_end(saved_ref[...], heads).astype(jnp.float32)
    delta = contract(
        jnp.ones((8, depth), jnp.float32), product, 1, 1, precision=lax.Precision.HIGHEST
    )[0:1, :]
    change_out[...] = contract(packet_ref[rows : 2 * rows, :], grads, 1, 1) - delta
    row_out[0:1, :] = delta
    row_out[1:2, :] = top
    row_out[2:3, :] = jnp.sum(raised, axis=0, keepdims=True)
    row_out[3:4, :] = jnp.concatenate([first.astype(jnp.float32)] * heads, axis=1)
    row_out[4:8, :] = jnp.ones((4, width), jnp.float32)
    owner, counts, rank = runs_of(packet_ref[2 * rows : 2 * rows + count, :].astype(jnp.float32))
    at = exchange_of(owner, index, count)
    spread_out[...] = one_hot(count * slot, at * slot + rank)
    target_out[...] = one_hot(count * rows, at * rows + rank)
    filled_out[0:count, :] = jnp.broadcast_to(counts, (count, rows))
    filled_out[count:, :] = jnp.zeros((8 - count, rows), jnp.float32)


def fold(count, back, packet, queries, grads, row, filled):
    rows = packet.shape[1]
    index = lax.axis_index("ctx")
    delta, top, total = (row[n : n + 1, :] for n in range(3))
    first = row[3:4, :].astype(jnp.int32)
    position = (index - back) * rows + lax.broadcasted_iota(jnp.int32, (rows, row.shape[1]), 0)
    scores = contract(packet[0:rows, :], queries, 1, 1) * (1.0 / math.sqrt(queries.shape[1]))
    scores = jnp.where(position >= first, scores, NEG)
    new_top = jnp.maximum(top, jnp.max(scores, axis=0, keepdims=True))
    raised = jnp.exp(scores - new_top)
    shrink = jnp.exp(top - new_top)
    total = total * shrink + jnp.sum(raised, axis=0, keepdims=True)
    change = contract(packet[rows : 2 * rows, :], grads, 1, 1) - delta
    factors = row[4:8, :] * jnp.where(
        lax.broadcasted_iota(jnp.int32, (4, row.shape[1]), 0) < back, shrink, 1.0
    )
    owner, counts, rank = runs_of(packet[2 * rows : 2 * rows + count, :].astype(jnp.float32))
    base = jnp.zeros((1, rows), jnp.float32)
    for p in range(count):
        base = base + jnp.where(owner == p, filled[p : p + 1, :], 0.0)
    inside = index >= back
    at = exchange_of(owner, index, count)
    target = jnp.where(inside, at * rows + base.astype(jnp.int32) + rank, -1)
    filled = filled[0:count, :] + jnp.where(inside, counts, 0.0)
    return raised, change, (new_top, total, factors), one_hot(count * rows, target), filled


def step_kernel(count, back, *refs):
    query_ref, grad_ref, row_ref, filled_ref, packet_ref = refs[:5]
    raised_out, change_out, row_out, target_out, filled_out = refs[5:]
    raised, change, (top, total, factors), target, filled = fold(
        count, back, packet_ref, query_ref[...], grad_ref[...], row_ref, filled_ref
    )
    raised_out[...] = raised
    change_out[...] = change
    row_out[0:1, :] = row_ref[0:1, :]
    row_out[1:2, :] = top
    row_out[2:3, :] = total
    row_out[3:4, :] = row_ref[3:4, :]
    row_out[4:8, :] = factors
    target_out[...] = target
    filled_out[0:count, :] = filled
    filled_out[count:, :] = jnp.zeros_like(filled_out[count:, :])


def attend_kernel(count, halo, *refs):
    query_ref, grad_ref, row_ref, filled_ref, spread_ref = refs[:5]
    raised_refs = refs[5 : 5 + halo]
    change_refs = refs[5 + halo : 5 + 2 * halo]
    target_refs = refs[5 + 2 * halo : 5 + 3 * halo]
    packets = refs[5 + 3 * halo : 6 + 4 * halo]
    outs = refs[6 + 4 * halo :]
    rows = packets[0].shape[1]
    depth = query_ref.shape[1]
    heads = query_ref.shape[0] // rows
    slot = 2 * rows // count
    scale = 1.0 / math.sqrt(depth)
    queries = query_ref[...]
    grads = grad_ref[...]
    raised, change, (_, total, factors), target, _ = fold(
        count, halo, packets[halo], queries, grads, row_ref, filled_ref
    )
    factors = factors * (1.0 / total)
    weights = []
    changes = []
    for block in range(halo + 1):
        mine = raised if block == halo else raised_refs[block][...]
        mine = mine * factors[block : block + 1, :]
        weights.append(mine.astype(jnp.bfloat16))
        mine = mine * (change if block == halo else change_refs[block][...])
        changes.append(mine.astype(jnp.bfloat16))
    weights = jnp.concatenate(weights, axis=0)
    changes = jnp.concatenate(changes, axis=0)
    keys = jnp.concatenate([packet[0:rows, :] for packet in packets], axis=0)
    query_grad = (contract(keys, changes, 0, 0) * scale).astype(jnp.bfloat16)
    key_parts = contract(changes, queries, 1, 0) * scale
    value_parts = contract(weights, grads, 1, 0)
    parts = jnp.concatenate([key_parts, value_parts], axis=1).astype(jnp.bfloat16)

    query_slots = contract(spread_ref[...], end_to_end(query_grad, heads), 1, 1)
    query_slots = query_slots.astype(jnp.bfloat16)
    spread = jnp.concatenate([ref[...] for ref in target_refs] + [target], axis=1)
    part_slots = contract(spread, parts, 1, 0).astype(jnp.bfloat16)
    at = heads * slot
    for k in range(count):
        out = outs[k]
        for h in range(heads):
            out[h * slot : (h + 1) * slot, :] = query_slots[
                k * slot : (k + 1) * slot, h * depth : (h + 1) * depth
            ]
        for n in range(2):
            out[at + n * rows : at + (n + 1) * rows, :] = part_slots[
                k * rows : (k + 1) * rows, n * depth : (n + 1) * depth
            ]


def order_kernel(count, halo, _, *refs):
    packets = refs[: 1 + halo]
    query_out, key_out = refs[1 + halo :]
    rows = query_out.shape[0]
    index = lax.axis_index("ctx")
    given = []
    for ref in packets:
        hot = ref[2 * rows : 2 * rows + count, :].astype(jnp.float32)
        counts = jnp.sum(hot, axis=1, keepdims=True)
        mine = jnp.zeros((1, 1), jnp.float32)
        for p in range(count):
            mine = jnp.where(index == p, counts[p : p + 1, :], mine)
        given.append(mine.astype(jnp.int32))
    if len(given) < count:
        given.append(rows - sum(given))
    giver = [lax.rem(index - d + count, count) for d in range(count)]

    def placement(size, halo):
        lane = lax.broadcasted_iota(jnp.int32, (1, count * size), 1)
        target = jnp.full(lane.shape, -1, jnp.int32)
        for k in range(count):
            step = lane - k * size
            for back in range(halo + 1):
                block = source_of(index, k, count) - back
                start = jnp.zeros((1, 1), jnp.int32)
                length = jnp.zeros((1, 1), jnp.int32)
                for d in range(count):
                    start = start + jnp.where(giver[d] < block, given[d], 0)
                    length = length + jnp.where(giver[d] == block, given[d], 0)
                target = jnp.where((step >= 0) & (step < length), start + step, target)
                step = step - length
        return one_hot(rows, target)

    query_out[...] = placement(2 * rows // count, 0)
    key_out[...] = placement(rows, halo)


def place_kernel(count, query_spread, key_spread, *refs):
    ins = refs[:count]
    query_out, key_out, value_out = refs[count : count + 3]
    query_here, key_here, value_here, sems = refs[count + 3 :]
    rows, width = query_here.shape
    depth = key_here.shape[1]
    heads = width // depth
    slot = 2 * rows // count
    copies = []

    def leave(here, out):
        copies.append(pltpu.make_async_copy(here, out, sems.at[len(copies)]))
        copies[-1].start()

    def taken(first, size, pieces):
        return jnp.concatenate(
            [
                jnp.concatenate(
                    [ref[first + n * size : first + (n + 1) * size, :] for n in range(pieces)],
                    axis=1,
                )
                for ref in ins
            ],
            axis=0,
        )

    query_here[...] = contract(query_spread[...], taken(0, slot, heads), 1, 0)
    leave(query_here, query_out)
    both = contract(key_spread[...], taken(heads * slot, rows, 2), 1, 0)
    for n, (here, out) in enumerate(((key_here, key_out), (value_here, value_out))):
        here[...] = both[:, n * depth : (n + 1) * depth]
        leave(here, out)
    for copy in copies:
        copy.wait()


def near_plan(doc_lengths, owners, queries, key_head_rows, value_head_rows, forward_out, grad_out):
    count = lax.axis_size("ctx")
    rows, width = queries.shape
    depth = key_head_rows.shape[1]
    heads = width // depth
    bf16, f32 = jnp.bfloat16, jnp.float32
    columns = heads * rows
    halo = count // 2
    slot = 2 * rows // count
    whole = pl.BlockSpec(memory_space=pltpu.VMEM)
    params = pltpu.CompilerParams(vmem_limit_bytes=40 * 1024 * 1024)

    mark = lax.broadcasted_iota(jnp.int32, (2 * rows + META, rows), 0) - 2 * rows
    packet = jnp.where(
        mark < 0,
        jnp.pad(jnp.concatenate([key_head_rows, value_head_rows], axis=0), ((0, META), (0, 0))),
        (owners[None, :] == mark).astype(bf16),
    )
    near = [
        lax.ppermute(packet, "ctx", [(i, (i + back) % count) for i in range(count)])
        for back in range(1, halo + 1)
    ]
    block_shapes = [jax.ShapeDtypeStruct((rows, columns), f32)] * 2
    row_shape = jax.ShapeDtypeStruct((8, columns), f32)
    target_shape = jax.ShapeDtypeStruct((count * rows, rows), bf16)
    filled_shape = jax.ShapeDtypeStruct((8, rows), f32)
    query_rows, grad_rows, raised, change, row, spread, target, filled = pl.pallas_call(
        functools.partial(own_kernel, count, doc_lengths.shape[0]),
        out_shape=[jax.ShapeDtypeStruct((columns, depth), bf16)] * 2
        + block_shapes
        + [row_shape, jax.ShapeDtypeStruct((count * slot, rows), bf16), target_shape, filled_shape],
        in_specs=[whole] * 5,
        out_specs=[whole] * 8,
        compiler_params=params,
    )(doc_lengths.reshape(1, -1), packet, queries, grad_out, forward_out)
    raised, change, target = [raised], [change], [target]
    for back in range(1, halo):
        found = pl.pallas_call(
            functools.partial(step_kernel, count, back),
            out_shape=block_shapes + [row_shape, target_shape, filled_shape],
            in_specs=[whole] * 5,
            out_specs=[whole] * 5,
            compiler_params=params,
        )(query_rows, grad_rows, row, filled, near[back - 1])
        raised.append(found[0])
        change.append(found[1])
        row = found[2]
        target.append(found[3])
        filled = found[4]
    sent = pl.pallas_call(
        functools.partial(attend_kernel, count, halo),
        out_shape=[jax.ShapeDtypeStruct((heads * slot + 2 * rows, depth), bf16)] * count,
        in_specs=[whole] * (6 + 4 * halo),
        out_specs=[whole] * count,
        compiler_params=params,
    )(query_rows, grad_rows, row, filled, spread, *raised, *change, *target, packet, *near)
    received = [sent[0]] + [
        lax.ppermute(sent[k], "ctx", [(i, target_of(i, k, count)) for i in range(count)])
        for k in range(1, count)
    ]
    spreads = pl.pallas_call(
        functools.partial(order_kernel, count, halo),
        out_shape=[
            jax.ShapeDtypeStruct((rows, count * slot), bf16),
            jax.ShapeDtypeStruct((rows, count * rows), bf16),
        ],
        in_specs=[pl.BlockSpec(memory_space=pl.ANY)] + [whole] * (1 + halo),
        out_specs=[whole] * 2,
        compiler_params=params,
    )(received[-1], packet, *near)
    return pl.pallas_call(
        functools.partial(place_kernel, count),
        out_shape=[
            jax.ShapeDtypeStruct((rows, width), f32),
            jax.ShapeDtypeStruct((rows, depth), f32),
            jax.ShapeDtypeStruct((rows, depth), f32),
        ],
        in_specs=[whole] * (2 + count),
        out_specs=[pl.BlockSpec(memory_space=pl.ANY)] * 3,
        scratch_shapes=[
            pltpu.VMEM((rows, width), f32),
            pltpu.VMEM((rows, depth), f32),
            pltpu.VMEM((rows, depth), f32),
            pltpu.SemaphoreType.DMA((3,)),
        ],
        compiler_params=params,
    )(*spreads, *received)


def per_device(*args):
    if lax.axis_size("ctx") in (2, 4):
        return near_plan(*args)
    return ring_plan(*args)


def solution(mesh):
    return jax.shard_map(
        per_device,
        mesh=mesh,
        in_specs=(
            P("groups"),
            P(("groups", "ctx")),
            P(("groups", "ctx"), "head"),
            P(("groups", "ctx"), "head"),
            P(("groups", "ctx"), "head"),
            P(("groups", "ctx"), "head"),
            P(("groups", "ctx"), "head"),
        ),
        out_specs=(
            P(("groups", "ctx"), "head"),
            P(("groups", "ctx"), "head"),
            P(("groups", "ctx"), "head"),
        ),
        check_vma=False,
    )
```

```python
import functools
import math

import jax
import jax.numpy as jnp
from jax import lax
from jax.experimental import pallas as pl
from jax.experimental.pallas import tpu as pltpu
from jax.sharding import PartitionSpec as P

HEAD_WIDTH = 128
GROUP = 4


NEG = -1e30
BLOCK = 512


def shifted(value, axis, by):
    count = lax.axis_size(axis)
    return lax.ppermute(value, axis, [(i, (i + by) % count) for i in range(count)])


def document_of(positions, doc_lengths):
    ends = jnp.cumsum(doc_lengths)
    return jnp.sum((positions[:, None] >= ends[None, :]).astype(jnp.int32), axis=1)


def allowed_between(query_positions, query_docs, key_positions, key_docs):
    return (query_docs[:, None] == key_docs[None, :]) & (
        key_positions[None, :] <= query_positions[:, None]
    )


def head_rows(matrix, group_size, head_dim):
    row_count = matrix.shape[0]
    return matrix.reshape(row_count * group_size, head_dim)


def block_scores(query_flat, key_head, row_count, group_size, head_dim):
    scores = lax.dot_general(
        query_flat, key_head, (((1,), (1,)), ((), ())), preferred_element_type=jnp.float32
    )
    return (scores * (1.0 / math.sqrt(head_dim))).reshape(row_count, group_size, key_head.shape[0])


def update_stats(running, query_local, key_block, allowed, group_size, head_dim):
    running_max, totals = running
    row_count = query_local.shape[0]
    scores = block_scores(
        head_rows(query_local, group_size, head_dim), key_block, row_count, group_size, head_dim
    )
    masked = jnp.where(allowed[:, None, :], scores, NEG)
    new_max = jnp.maximum(running_max, jnp.max(masked, axis=2))
    weights = jnp.where(allowed[:, None, :], jnp.exp(masked - new_max[:, :, None]), 0.0)
    new_totals = [totals * jnp.exp(running_max - new_max) + jnp.sum(weights, axis=2)]
    new_maxima = [new_max]
    return (jnp.concatenate(new_maxima, axis=1), jnp.concatenate(new_totals, axis=1))


def backward_block(
    query_local,
    grad_local,
    log_norm,
    row_delta,
    key_block,
    value_block,
    allowed,
    group_size,
    head_dim,
):
    row_count = query_local.shape[0]
    query_flat = head_rows(query_local, group_size, head_dim)
    grad_flat = head_rows(grad_local, group_size, head_dim)
    scores = block_scores(query_flat, key_block, row_count, group_size, head_dim)
    masked = jnp.where(allowed[:, None, :], scores, NEG)
    weights = jnp.exp(masked - log_norm[:, 0:group_size, None])
    grad_weights = lax.dot_general(
        grad_flat, value_block, (((1,), (1,)), ((), ())), preferred_element_type=jnp.float32
    ).reshape(row_count, group_size, -1)
    grad_scores = weights * (grad_weights - row_delta[:, 0:group_size, None])
    rounded_weights = weights.astype(jnp.bfloat16).reshape(row_count * group_size, -1)
    rounded_grads = grad_scores.astype(jnp.bfloat16).reshape(row_count * group_size, -1)
    value_parts = [
        lax.dot_general(
            rounded_weights, grad_flat, (((0,), (0,)), ((), ())), preferred_element_type=jnp.float32
        )
    ]
    key_parts = [
        lax.dot_general(
            rounded_grads, query_flat, (((0,), (0,)), ((), ())), preferred_element_type=jnp.float32
        )
    ]
    query_parts = [
        jnp.dot(rounded_grads, key_block, preferred_element_type=jnp.float32).reshape(
            row_count, group_size * head_dim
        )
    ]
    return (
        jnp.concatenate(query_parts, axis=1),
        jnp.concatenate(key_parts, axis=1),
        jnp.concatenate(value_parts, axis=1),
    )


def ring_plan(doc_lengths, owners, queries, key_head_rows, value_head_rows, forward_out, grad_out):
    context_size = lax.axis_size("ctx")
    context_index = lax.axis_index("ctx")
    row_count = queries.shape[0]
    head_dim = HEAD_WIDTH
    group_size = GROUP
    query_heads = queries.shape[1] // head_dim
    slot_count = 2 * row_count // context_size
    everyone = lax.all_gather(owners, "ctx", axis=0, tiled=True)
    row_arrangement = jnp.argsort(everyone, stable=True)
    layout_docs = document_of(row_arrangement, doc_lengths)
    own_positions = lax.dynamic_slice_in_dim(
        row_arrangement, context_index * row_count, row_count, 0
    )
    own_documents = lax.dynamic_slice_in_dim(layout_docs, context_index * row_count, row_count, 0)
    owner_ids = jnp.arange(context_size, dtype=jnp.int32)
    owner_hot = (owners[:, None] == owner_ids[None, :]).astype(jnp.int32)
    earlier = jnp.cumsum(owner_hot, axis=0) - owner_hot
    rank_within = jnp.sum(earlier * owner_hot, axis=1)
    slot_rows = owners * slot_count + rank_within

    def packed(matrix):
        empty = jnp.zeros((context_size * slot_count,) + matrix.shape[1:], matrix.dtype)
        return empty.at[slot_rows].set(matrix)

    owner_grid = everyone.reshape(context_size, row_count)
    counts = jnp.sum((owner_grid == context_index).astype(jnp.int32), axis=1)
    count_ends = jnp.cumsum(counts)
    starts = count_ends - counts
    wanted = jnp.arange(row_count, dtype=jnp.int32)
    source = jnp.sum((wanted[:, None] >= count_ends[None, :]).astype(jnp.int32), axis=1)
    source_hot = (source[:, None] == owner_ids[None, :]).astype(jnp.int32)
    take_rows = source * slot_count + wanted - jnp.sum(source_hot * starts[None, :], axis=1)

    def compact(received):
        return jnp.take(received, take_rows, axis=0)

    local_delta = jnp.sum(
        (grad_out.astype(jnp.float32) * forward_out.astype(jnp.float32)).reshape(
            row_count, query_heads, head_dim
        ),
        axis=2,
    )
    arrived = (
        lax.all_to_all(packed(queries), "ctx", split_axis=0, concat_axis=0, tiled=True),
        lax.all_to_all(packed(key_head_rows), "ctx", split_axis=0, concat_axis=0, tiled=True),
        lax.all_to_all(packed(value_head_rows), "ctx", split_axis=0, concat_axis=0, tiled=True),
        lax.all_to_all(packed(grad_out), "ctx", split_axis=0, concat_axis=0, tiled=True),
    )
    query_local, key_local, value_local, grad_local = [compact(received) for received in arrived]
    row_delta = compact(
        lax.all_to_all(packed(local_delta), "ctx", split_axis=0, concat_axis=0, tiled=True)
    )

    def fold_keys(running, shard_rows, first_row):
        piece_count = shard_rows.shape[0]
        step_rows = math.gcd(piece_count, BLOCK) if piece_count > BLOCK else piece_count

        def one_block(partial_value, block_index):
            offset = first_row + block_index * step_rows
            key_block = lax.dynamic_slice_in_dim(shard_rows, block_index * step_rows, step_rows, 0)
            key_positions = lax.dynamic_slice_in_dim(row_arrangement, offset, step_rows, 0)
            key_docs = lax.dynamic_slice_in_dim(layout_docs, offset, step_rows, 0)
            allowed = allowed_between(own_positions, own_documents, key_positions, key_docs)
            return (
                update_stats(partial_value, query_local, key_block, allowed, group_size, head_dim),
                None,
            )

        if piece_count == step_rows:
            return one_block(running, 0)[0]
        return lax.scan(one_block, running, jnp.arange(piece_count // step_rows, dtype=jnp.int32))[
            0
        ]

    start_stats = (
        jnp.full((row_count, query_heads), NEG, jnp.float32),
        jnp.zeros((row_count, query_heads), jnp.float32),
    )
    top_scores, totals = fold_keys(
        start_stats, lax.all_gather(key_local, "ctx", axis=0, tiled=True), jnp.int32(0)
    )
    log_norm = top_scores + jnp.log(totals)

    def block_meta(owner_index, offset, size):
        first = owner_index * row_count + offset
        key_positions = lax.dynamic_slice_in_dim(row_arrangement, first, size, 0)
        key_docs = lax.dynamic_slice_in_dim(layout_docs, first, size, 0)
        return (key_positions, key_docs)

    query_zero = jnp.zeros(query_local.shape, jnp.float32)
    key_zero = jnp.zeros(key_local.shape, jnp.float32)

    def one_turn(turn_index, loop_state):
        key_moving, value_moving, key_grad, value_grad, query_grad = loop_state
        owner_index = (context_index - turn_index) % context_size
        key_positions, key_docs = block_meta(owner_index, 0, row_count)
        allowed = allowed_between(own_positions, own_documents, key_positions, key_docs)
        query_part, key_part, value_part = backward_block(
            query_local,
            grad_local,
            log_norm,
            row_delta,
            key_moving,
            value_moving,
            allowed,
            group_size,
            head_dim,
        )
        return (
            key_moving,
            value_moving,
            key_grad + key_part,
            value_grad + value_part,
            query_grad + query_part,
        )

    def moved_turn(turn_index, loop_state):
        key_moving, value_moving, key_grad, value_grad, query_grad = loop_state
        key_moving, value_moving = shifted((key_moving, value_moving), "ctx", 1)
        key_grad, value_grad = shifted((key_grad, value_grad), "ctx", 1)
        return one_turn(turn_index, (key_moving, value_moving, key_grad, value_grad, query_grad))

    loop_state = one_turn(0, (key_local, value_local, key_zero, key_zero, query_zero))
    loop_state = lax.fori_loop(1, context_size, moved_turn, loop_state)
    key_grad, value_grad = shifted((loop_state[2], loop_state[3]), "ctx", 1)
    query_grad = loop_state[4]
    inverse_root = 1.0 / math.sqrt(head_dim)
    return (query_grad * inverse_root, key_grad * inverse_root, value_grad)


META = 8


def contract(left, right, left_dim, right_dim, **kw):
    return lax.dot_general(
        left,
        right,
        (((left_dim,), (right_dim,)), ((), ())),
        preferred_element_type=jnp.float32,
        **kw,
    )


def one_hot(row_count, target):
    places = lax.broadcasted_iota(jnp.int32, (row_count, target.shape[1]), 0)
    return jnp.where(places == target, 1.0, 0.0).astype(jnp.bfloat16)


def side_by_side(stack, heads):
    rows = stack.shape[0] // heads
    return jnp.concatenate([stack[h * rows : (h + 1) * rows, :] for h in range(heads)], axis=1)


def end_to_end(matrix, heads):
    width = matrix.shape[1] // heads
    return jnp.concatenate([matrix[:, h * width : (h + 1) * width] for h in range(heads)], axis=0)


def target_of(index, k, count):
    if count == 4 and k in (1, 2):
        return (2 * index + 1) % 5 if k == 1 else (3 * index + 2) % 5
    return index ^ k


def source_of(index, k, count):
    return target_of(index, 3 - k if count == 4 and k in (1, 2) else k, count)


def exchange_of(owner, index, count):
    found = jnp.zeros_like(owner)
    for k in range(1, count):
        found = jnp.where(owner == target_of(index, k, count), k, found)
    return found


def runs_of(hot):
    count, rows = hot.shape
    counts = jnp.sum(hot, axis=1, keepdims=True)
    owner = jnp.zeros((1, rows), jnp.int32)
    earlier = jnp.zeros((1, rows), jnp.float32)
    for p in range(count):
        mine = hot[p : p + 1, :] > 0.0
        owner = jnp.where(mine, p, owner)
        for less in range(p):
            earlier = earlier + jnp.where(mine, counts[less : less + 1, :], 0.0)
    lane = lax.broadcasted_iota(jnp.int32, (1, rows), 1)
    return owner, counts, lane - earlier.astype(jnp.int32)


def own_scores(count, docs, doc_ref, packet_ref, query_ref, outs):
    query_out, raised_out, row_out, spread_out, target_out, filled_out = outs
    rows, width = query_ref.shape
    depth = packet_ref.shape[1]
    heads = width // depth
    slot = 2 * rows // count
    index = lax.axis_index("ctx")
    lane = lax.broadcasted_iota(jnp.int32, (1, rows), 1)
    position = index * rows + lane
    earlier = lax.broadcasted_iota(jnp.int32, (docs, docs), 1) <= lax.broadcasted_iota(
        jnp.int32, (docs, docs), 0
    )
    lengths = doc_ref[...].astype(jnp.float32)
    ends = jnp.sum(jnp.where(earlier, lengths, 0.0), axis=1, keepdims=True).astype(jnp.int32)
    first = jnp.max(jnp.where(ends <= position, ends, 0), axis=0, keepdims=True)
    key_position = index * rows + lax.broadcasted_iota(jnp.int32, (rows, rows), 0)
    allowed = (key_position >= first) & (key_position <= position)
    allowed = jnp.concatenate([allowed] * heads, axis=1)

    queries = end_to_end(query_ref[...], heads)
    query_out[...] = queries
    scores = contract(packet_ref[0:rows, :], queries, 1, 1) * (1.0 / math.sqrt(depth))
    scores = jnp.where(allowed, scores, NEG)
    top = jnp.max(scores, axis=0, keepdims=True)
    raised = jnp.exp(scores - top)
    raised_out[...] = raised
    row_out[0:1, :] = jnp.zeros((1, width), jnp.float32)
    row_out[1:2, :] = top
    row_out[2:3, :] = jnp.sum(raised, axis=0, keepdims=True)
    row_out[3:4, :] = jnp.concatenate([first.astype(jnp.float32)] * heads, axis=1)
    row_out[4:8, :] = jnp.ones((4, width), jnp.float32)
    owner, counts, rank = runs_of(packet_ref[2 * rows : 2 * rows + count, :].astype(jnp.float32))
    at = exchange_of(owner, index, count)
    spread_out[...] = one_hot(count * slot, at * slot + rank)
    target_out[...] = one_hot(count * rows, at * rows + rank)
    filled_out[0:count, :] = jnp.broadcast_to(counts, (count, rows))
    filled_out[count:, :] = jnp.zeros((8 - count, rows), jnp.float32)


def scores_kernel(count, docs, doc_ref, packet_ref, query_ref, packet_out, *outs):
    packet_out[...] = packet_ref[...]
    own_scores(count, docs, doc_ref, packet_ref, query_ref, outs)


def own_kernel(packet_ref, grad_ref, saved_ref, row_ref, grad_out, change_out, row_out):
    rows, width = grad_ref.shape
    depth = packet_ref.shape[1]
    heads = width // depth
    grads = end_to_end(grad_ref[...], heads)
    grad_out[...] = grads
    product = grads.astype(jnp.float32) * end_to_end(saved_ref[...], heads).astype(jnp.float32)
    delta = contract(
        jnp.ones((8, depth), jnp.float32), product, 1, 1, precision=lax.Precision.HIGHEST
    )[0:1, :]
    change_out[...] = contract(packet_ref[rows : 2 * rows, :], grads, 1, 1) - delta
    row_out[0:1, :] = delta
    row_out[1:, :] = row_ref[1:, :]


def fold(count, back, packet, queries, grads, row, filled):
    rows = packet.shape[1]
    index = lax.axis_index("ctx")
    delta, top, total = (row[n : n + 1, :] for n in range(3))
    first = row[3:4, :].astype(jnp.int32)
    position = (index - back) * rows + lax.broadcasted_iota(jnp.int32, (rows, row.shape[1]), 0)
    scores = contract(packet[0:rows, :], queries, 1, 1) * (1.0 / math.sqrt(queries.shape[1]))
    scores = jnp.where(position >= first, scores, NEG)
    new_top = jnp.maximum(top, jnp.max(scores, axis=0, keepdims=True))
    raised = jnp.exp(scores - new_top)
    shrink = jnp.exp(top - new_top)
    total = total * shrink + jnp.sum(raised, axis=0, keepdims=True)
    change = contract(packet[rows : 2 * rows, :], grads, 1, 1) - delta
    factors = row[4:8, :] * jnp.where(
        lax.broadcasted_iota(jnp.int32, (4, row.shape[1]), 0) < back, shrink, 1.0
    )
    owner, counts, rank = runs_of(packet[2 * rows : 2 * rows + count, :].astype(jnp.float32))
    base = jnp.zeros((1, rows), jnp.float32)
    for p in range(count):
        base = base + jnp.where(owner == p, filled[p : p + 1, :], 0.0)
    inside = index >= back
    at = exchange_of(owner, index, count)
    target = jnp.where(inside, at * rows + base.astype(jnp.int32) + rank, -1)
    filled = filled[0:count, :] + jnp.where(inside, counts, 0.0)
    return raised, change, (new_top, total, factors), one_hot(count * rows, target), filled


def step_kernel(count, back, *refs):
    query_ref, grad_ref, row_ref, filled_ref, packet_ref = refs[:5]
    raised_out, change_out, row_out, target_out, filled_out = refs[5:]
    raised, change, (top, total, factors), target, filled = fold(
        count, back, packet_ref, query_ref[...], grad_ref[...], row_ref, filled_ref
    )
    raised_out[...] = raised
    change_out[...] = change
    row_out[0:1, :] = row_ref[0:1, :]
    row_out[1:2, :] = top
    row_out[2:3, :] = total
    row_out[3:4, :] = row_ref[3:4, :]
    row_out[4:8, :] = factors
    target_out[...] = target
    filled_out[0:count, :] = filled
    filled_out[count:, :] = jnp.zeros_like(filled_out[count:, :])


def attend_kernel(count, halo, *refs):
    query_ref, grad_ref, row_ref, filled_ref, spread_ref = refs[:5]
    raised_refs = refs[5 : 5 + halo]
    change_refs = refs[5 + halo : 5 + 2 * halo]
    target_refs = refs[5 + 2 * halo : 5 + 3 * halo]
    packets = refs[5 + 3 * halo : 6 + 4 * halo]
    outs = refs[6 + 4 * halo :]
    rows = packets[0].shape[1]
    depth = query_ref.shape[1]
    heads = query_ref.shape[0] // rows
    slot = 2 * rows // count
    scale = 1.0 / math.sqrt(depth)
    queries = query_ref[...]
    grads = grad_ref[...]
    raised, change, (_, total, factors), target, _ = fold(
        count, halo, packets[halo], queries, grads, row_ref, filled_ref
    )
    factors = factors * (1.0 / total)
    weights = []
    changes = []
    for block in range(halo + 1):
        mine = raised if block == halo else raised_refs[block][...]
        mine = mine * factors[block : block + 1, :]
        weights.append(mine.astype(jnp.bfloat16))
        mine = mine * (change if block == halo else change_refs[block][...])
        changes.append(mine.astype(jnp.bfloat16))
    weights = jnp.concatenate(weights, axis=0)
    changes = jnp.concatenate(changes, axis=0)
    keys = jnp.concatenate([packet[0:rows, :] for packet in packets], axis=0)
    query_grad = (contract(keys, changes, 0, 0) * scale).astype(jnp.bfloat16)
    key_parts = contract(changes, queries, 1, 0) * scale
    value_parts = contract(weights, grads, 1, 0)
    parts = jnp.concatenate([key_parts, value_parts], axis=1).astype(jnp.bfloat16)

    query_slots = contract(spread_ref[...], end_to_end(query_grad, heads), 1, 1)
    query_slots = query_slots.astype(jnp.bfloat16)
    spread = jnp.concatenate([ref[...] for ref in target_refs] + [target], axis=1)
    part_slots = contract(spread, parts, 1, 0).astype(jnp.bfloat16)
    at = heads * slot
    for k in range(count):
        out = outs[k]
        for h in range(heads):
            out[h * slot : (h + 1) * slot, :] = query_slots[
                k * slot : (k + 1) * slot, h * depth : (h + 1) * depth
            ]
        for n in range(2):
            out[at + n * rows : at + (n + 1) * rows, :] = part_slots[
                k * rows : (k + 1) * rows, n * depth : (n + 1) * depth
            ]


def order_kernel(count, halo, _, *refs):
    packets = refs[: 1 + halo]
    query_out, key_out = refs[1 + halo :]
    rows = query_out.shape[0]
    index = lax.axis_index("ctx")
    given = []
    for ref in packets:
        hot = ref[2 * rows : 2 * rows + count, :].astype(jnp.float32)
        counts = jnp.sum(hot, axis=1, keepdims=True)
        mine = jnp.zeros((1, 1), jnp.float32)
        for p in range(count):
            mine = jnp.where(index == p, counts[p : p + 1, :], mine)
        given.append(mine.astype(jnp.int32))
    if len(given) < count:
        given.append(rows - sum(given))
    giver = [lax.rem(index - d + count, count) for d in range(count)]

    def placement(size, halo):
        lane = lax.broadcasted_iota(jnp.int32, (1, count * size), 1)
        target = jnp.full(lane.shape, -1, jnp.int32)
        for k in range(count):
            step = lane - k * size
            for back in range(halo + 1):
                block = source_of(index, k, count) - back
                start = jnp.zeros((1, 1), jnp.int32)
                length = jnp.zeros((1, 1), jnp.int32)
                for d in range(count):
                    start = start + jnp.where(giver[d] < block, given[d], 0)
                    length = length + jnp.where(giver[d] == block, given[d], 0)
                target = jnp.where((step >= 0) & (step < length), start + step, target)
                step = step - length
        return one_hot(rows, target)

    query_out[...] = placement(2 * rows // count, 0)
    key_out[...] = placement(rows, halo)


def place_kernel(count, query_spread, key_spread, *refs):
    ins = refs[:count]
    query_out, key_out, value_out = refs[count : count + 3]
    query_here, key_here, value_here, sems = refs[count + 3 :]
    rows, width = query_here.shape
    depth = key_here.shape[1]
    heads = width // depth
    slot = 2 * rows // count
    copies = []

    def leave(here, out):
        copies.append(pltpu.make_async_copy(here, out, sems.at[len(copies)]))
        copies[-1].start()

    def taken(first, size, pieces):
        return jnp.concatenate(
            [
                jnp.concatenate(
                    [ref[first + n * size : first + (n + 1) * size, :] for n in range(pieces)],
                    axis=1,
                )
                for ref in ins
            ],
            axis=0,
        )

    query_here[...] = contract(query_spread[...], taken(0, slot, heads), 1, 0)
    leave(query_here, query_out)
    both = contract(key_spread[...], taken(heads * slot, rows, 2), 1, 0)
    for n, (here, out) in enumerate(((key_here, key_out), (value_here, value_out))):
        here[...] = both[:, n * depth : (n + 1) * depth]
        leave(here, out)
    for copy in copies:
        copy.wait()


def near_plan(doc_lengths, owners, queries, key_head_rows, value_head_rows, forward_out, grad_out):
    count = lax.axis_size("ctx")
    rows, width = queries.shape
    depth = key_head_rows.shape[1]
    heads = width // depth
    bf16, f32 = jnp.bfloat16, jnp.float32
    columns = heads * rows
    halo = count // 2
    slot = 2 * rows // count
    whole = pl.BlockSpec(memory_space=pltpu.VMEM)
    params = pltpu.CompilerParams(vmem_limit_bytes=40 * 1024 * 1024)

    mark = lax.broadcasted_iota(jnp.int32, (2 * rows + META, rows), 0) - 2 * rows
    packet = jnp.where(
        mark < 0,
        jnp.pad(jnp.concatenate([key_head_rows, value_head_rows], axis=0), ((0, META), (0, 0))),
        (owners[None, :] == mark).astype(bf16),
    )
    block_shapes = [jax.ShapeDtypeStruct((rows, columns), f32)] * 2
    row_shape = jax.ShapeDtypeStruct((8, columns), f32)
    target_shape = jax.ShapeDtypeStruct((count * rows, rows), bf16)
    filled_shape = jax.ShapeDtypeStruct((8, rows), f32)
    score_shapes = [
        jax.ShapeDtypeStruct((columns, depth), bf16),
        block_shapes[0],
        row_shape,
        jax.ShapeDtypeStruct((count * slot, rows), bf16),
        target_shape,
        filled_shape,
    ]
    near = [lax.ppermute(packet, "ctx", [(i, (i + 1) % count) for i in range(count)])]
    far, *scored = pl.pallas_call(
        functools.partial(scores_kernel, count, doc_lengths.shape[0]),
        out_shape=[jax.ShapeDtypeStruct(packet.shape, bf16)] + score_shapes,
        in_specs=[whole] * 3,
        out_specs=[whole] * 7,
        compiler_params=params,
    )(doc_lengths.reshape(1, -1), packet, queries)
    near += [
        lax.ppermute(far, "ctx", [(i, (i + back) % count) for i in range(count)])
        for back in range(2, halo + 1)
    ]
    query_rows, raised, row, spread, target, filled = scored
    grad_rows, change, row = pl.pallas_call(
        own_kernel,
        out_shape=[jax.ShapeDtypeStruct((columns, depth), bf16), block_shapes[1], row_shape],
        in_specs=[whole] * 4,
        out_specs=[whole] * 3,
        compiler_params=params,
    )(packet, grad_out, forward_out, row)
    raised, change, target = [raised], [change], [target]
    for back in range(1, halo):
        found = pl.pallas_call(
            functools.partial(step_kernel, count, back),
            out_shape=block_shapes + [row_shape, target_shape, filled_shape],
            in_specs=[whole] * 5,
            out_specs=[whole] * 5,
            compiler_params=params,
        )(query_rows, grad_rows, row, filled, near[back - 1])
        raised.append(found[0])
        change.append(found[1])
        row = found[2]
        target.append(found[3])
        filled = found[4]
    sent = pl.pallas_call(
        functools.partial(attend_kernel, count, halo),
        out_shape=[jax.ShapeDtypeStruct((heads * slot + 2 * rows, depth), bf16)] * count,
        in_specs=[whole] * (6 + 4 * halo),
        out_specs=[whole] * count,
        compiler_params=params,
    )(query_rows, grad_rows, row, filled, spread, *raised, *change, *target, packet, *near)
    received = [sent[0]] + [
        lax.ppermute(sent[k], "ctx", [(i, target_of(i, k, count)) for i in range(count)])
        for k in range(1, count)
    ]
    spreads = pl.pallas_call(
        functools.partial(order_kernel, count, halo),
        out_shape=[
            jax.ShapeDtypeStruct((rows, count * slot), bf16),
            jax.ShapeDtypeStruct((rows, count * rows), bf16),
        ],
        in_specs=[pl.BlockSpec(memory_space=pl.ANY)] + [whole] * (1 + halo),
        out_specs=[whole] * 2,
        compiler_params=params,
    )(received[-1], packet, *near)
    return pl.pallas_call(
        functools.partial(place_kernel, count),
        out_shape=[
            jax.ShapeDtypeStruct((rows, width), f32),
            jax.ShapeDtypeStruct((rows, depth), f32),
            jax.ShapeDtypeStruct((rows, depth), f32),
        ],
        in_specs=[whole] * (2 + count),
        out_specs=[pl.BlockSpec(memory_space=pl.ANY)] * 3,
        scratch_shapes=[
            pltpu.VMEM((rows, width), f32),
            pltpu.VMEM((rows, depth), f32),
            pltpu.VMEM((rows, depth), f32),
            pltpu.SemaphoreType.DMA((3,)),
        ],
        compiler_params=params,
    )(*spreads, *received)


def per_device(*args):
    if lax.axis_size("ctx") in (2, 4):
        return near_plan(*args)
    return ring_plan(*args)


def solution(mesh):
    return jax.shard_map(
        per_device,
        mesh=mesh,
        in_specs=(
            P("groups"),
            P(("groups", "ctx")),
            P(("groups", "ctx"), "head"),
            P(("groups", "ctx"), "head"),
            P(("groups", "ctx"), "head"),
            P(("groups", "ctx"), "head"),
            P(("groups", "ctx"), "head"),
        ),
        out_specs=(
            P(("groups", "ctx"), "head"),
            P(("groups", "ctx"), "head"),
            P(("groups", "ctx"), "head"),
        ),
        check_vma=False,
    )
```

```python
import functools
import math

import jax
import jax.numpy as jnp
from jax import lax
from jax.experimental import pallas as pl
from jax.experimental.pallas import tpu as pltpu
from jax.sharding import PartitionSpec as P

HEAD_WIDTH = 128
GROUP = 4


NEG = -1e30
BLOCK = 512


def shifted(value, axis, by):
    count = lax.axis_size(axis)
    return lax.ppermute(value, axis, [(i, (i + by) % count) for i in range(count)])


def document_of(positions, doc_lengths):
    ends = jnp.cumsum(doc_lengths)
    return jnp.sum((positions[:, None] >= ends[None, :]).astype(jnp.int32), axis=1)


def allowed_between(query_positions, query_docs, key_positions, key_docs):
    return (query_docs[:, None] == key_docs[None, :]) & (
        key_positions[None, :] <= query_positions[:, None]
    )


def head_rows(matrix, group_size, head_dim):
    row_count = matrix.shape[0]
    return matrix.reshape(row_count * group_size, head_dim)


def block_scores(query_flat, key_head, row_count, group_size, head_dim):
    scores = lax.dot_general(
        query_flat, key_head, (((1,), (1,)), ((), ())), preferred_element_type=jnp.float32
    )
    return (scores * (1.0 / math.sqrt(head_dim))).reshape(row_count, group_size, key_head.shape[0])


def update_stats(running, query_local, key_block, allowed, group_size, head_dim):
    running_max, totals = running
    row_count = query_local.shape[0]
    scores = block_scores(
        head_rows(query_local, group_size, head_dim), key_block, row_count, group_size, head_dim
    )
    masked = jnp.where(allowed[:, None, :], scores, NEG)
    new_max = jnp.maximum(running_max, jnp.max(masked, axis=2))
    weights = jnp.where(allowed[:, None, :], jnp.exp(masked - new_max[:, :, None]), 0.0)
    new_totals = [totals * jnp.exp(running_max - new_max) + jnp.sum(weights, axis=2)]
    new_maxima = [new_max]
    return (jnp.concatenate(new_maxima, axis=1), jnp.concatenate(new_totals, axis=1))


def backward_block(
    query_local,
    grad_local,
    log_norm,
    row_delta,
    key_block,
    value_block,
    allowed,
    group_size,
    head_dim,
):
    row_count = query_local.shape[0]
    query_flat = head_rows(query_local, group_size, head_dim)
    grad_flat = head_rows(grad_local, group_size, head_dim)
    scores = block_scores(query_flat, key_block, row_count, group_size, head_dim)
    masked = jnp.where(allowed[:, None, :], scores, NEG)
    weights = jnp.exp(masked - log_norm[:, 0:group_size, None])
    grad_weights = lax.dot_general(
        grad_flat, value_block, (((1,), (1,)), ((), ())), preferred_element_type=jnp.float32
    ).reshape(row_count, group_size, -1)
    grad_scores = weights * (grad_weights - row_delta[:, 0:group_size, None])
    rounded_weights = weights.astype(jnp.bfloat16).reshape(row_count * group_size, -1)
    rounded_grads = grad_scores.astype(jnp.bfloat16).reshape(row_count * group_size, -1)
    value_parts = [
        lax.dot_general(
            rounded_weights, grad_flat, (((0,), (0,)), ((), ())), preferred_element_type=jnp.float32
        )
    ]
    key_parts = [
        lax.dot_general(
            rounded_grads, query_flat, (((0,), (0,)), ((), ())), preferred_element_type=jnp.float32
        )
    ]
    query_parts = [
        jnp.dot(rounded_grads, key_block, preferred_element_type=jnp.float32).reshape(
            row_count, group_size * head_dim
        )
    ]
    return (
        jnp.concatenate(query_parts, axis=1),
        jnp.concatenate(key_parts, axis=1),
        jnp.concatenate(value_parts, axis=1),
    )


def ring_plan(doc_lengths, owners, queries, key_head_rows, value_head_rows, forward_out, grad_out):
    context_size = lax.axis_size("ctx")
    context_index = lax.axis_index("ctx")
    row_count = queries.shape[0]
    head_dim = HEAD_WIDTH
    group_size = GROUP
    query_heads = queries.shape[1] // head_dim
    slot_count = 2 * row_count // context_size
    everyone = lax.all_gather(owners, "ctx", axis=0, tiled=True)
    row_arrangement = jnp.argsort(everyone, stable=True)
    layout_docs = document_of(row_arrangement, doc_lengths)
    own_positions = lax.dynamic_slice_in_dim(
        row_arrangement, context_index * row_count, row_count, 0
    )
    own_documents = lax.dynamic_slice_in_dim(layout_docs, context_index * row_count, row_count, 0)
    owner_ids = jnp.arange(context_size, dtype=jnp.int32)
    owner_hot = (owners[:, None] == owner_ids[None, :]).astype(jnp.int32)
    earlier = jnp.cumsum(owner_hot, axis=0) - owner_hot
    rank_within = jnp.sum(earlier * owner_hot, axis=1)
    slot_rows = owners * slot_count + rank_within

    def packed(matrix):
        empty = jnp.zeros((context_size * slot_count,) + matrix.shape[1:], matrix.dtype)
        return empty.at[slot_rows].set(matrix)

    owner_grid = everyone.reshape(context_size, row_count)
    counts = jnp.sum((owner_grid == context_index).astype(jnp.int32), axis=1)
    count_ends = jnp.cumsum(counts)
    starts = count_ends - counts
    wanted = jnp.arange(row_count, dtype=jnp.int32)
    source = jnp.sum((wanted[:, None] >= count_ends[None, :]).astype(jnp.int32), axis=1)
    source_hot = (source[:, None] == owner_ids[None, :]).astype(jnp.int32)
    take_rows = source * slot_count + wanted - jnp.sum(source_hot * starts[None, :], axis=1)

    def compact(received):
        return jnp.take(received, take_rows, axis=0)

    local_delta = jnp.sum(
        (grad_out.astype(jnp.float32) * forward_out.astype(jnp.float32)).reshape(
            row_count, query_heads, head_dim
        ),
        axis=2,
    )
    arrived = (
        lax.all_to_all(packed(queries), "ctx", split_axis=0, concat_axis=0, tiled=True),
        lax.all_to_all(packed(key_head_rows), "ctx", split_axis=0, concat_axis=0, tiled=True),
        lax.all_to_all(packed(value_head_rows), "ctx", split_axis=0, concat_axis=0, tiled=True),
        lax.all_to_all(packed(grad_out), "ctx", split_axis=0, concat_axis=0, tiled=True),
    )
    query_local, key_local, value_local, grad_local = [compact(received) for received in arrived]
    row_delta = compact(
        lax.all_to_all(packed(local_delta), "ctx", split_axis=0, concat_axis=0, tiled=True)
    )

    def fold_keys(running, shard_rows, first_row):
        piece_count = shard_rows.shape[0]
        step_rows = math.gcd(piece_count, BLOCK) if piece_count > BLOCK else piece_count

        def one_block(partial_value, block_index):
            offset = first_row + block_index * step_rows
            key_block = lax.dynamic_slice_in_dim(shard_rows, block_index * step_rows, step_rows, 0)
            key_positions = lax.dynamic_slice_in_dim(row_arrangement, offset, step_rows, 0)
            key_docs = lax.dynamic_slice_in_dim(layout_docs, offset, step_rows, 0)
            allowed = allowed_between(own_positions, own_documents, key_positions, key_docs)
            return (
                update_stats(partial_value, query_local, key_block, allowed, group_size, head_dim),
                None,
            )

        if piece_count == step_rows:
            return one_block(running, 0)[0]
        return lax.scan(one_block, running, jnp.arange(piece_count // step_rows, dtype=jnp.int32))[
            0
        ]

    start_stats = (
        jnp.full((row_count, query_heads), NEG, jnp.float32),
        jnp.zeros((row_count, query_heads), jnp.float32),
    )
    top_scores, totals = fold_keys(
        start_stats, lax.all_gather(key_local, "ctx", axis=0, tiled=True), jnp.int32(0)
    )
    log_norm = top_scores + jnp.log(totals)

    def block_meta(owner_index, offset, size):
        first = owner_index * row_count + offset
        key_positions = lax.dynamic_slice_in_dim(row_arrangement, first, size, 0)
        key_docs = lax.dynamic_slice_in_dim(layout_docs, first, size, 0)
        return (key_positions, key_docs)

    query_zero = jnp.zeros(query_local.shape, jnp.float32)
    key_zero = jnp.zeros(key_local.shape, jnp.float32)

    def one_turn(turn_index, loop_state):
        key_moving, value_moving, key_grad, value_grad, query_grad = loop_state
        owner_index = (context_index - turn_index) % context_size
        key_positions, key_docs = block_meta(owner_index, 0, row_count)
        allowed = allowed_between(own_positions, own_documents, key_positions, key_docs)
        query_part, key_part, value_part = backward_block(
            query_local,
            grad_local,
            log_norm,
            row_delta,
            key_moving,
            value_moving,
            allowed,
            group_size,
            head_dim,
        )
        return (
            key_moving,
            value_moving,
            key_grad + key_part,
            value_grad + value_part,
            query_grad + query_part,
        )

    def moved_turn(turn_index, loop_state):
        key_moving, value_moving, key_grad, value_grad, query_grad = loop_state
        key_moving, value_moving = shifted((key_moving, value_moving), "ctx", 1)
        key_grad, value_grad = shifted((key_grad, value_grad), "ctx", 1)
        return one_turn(turn_index, (key_moving, value_moving, key_grad, value_grad, query_grad))

    loop_state = one_turn(0, (key_local, value_local, key_zero, key_zero, query_zero))
    loop_state = lax.fori_loop(1, context_size, moved_turn, loop_state)
    key_grad, value_grad = shifted((loop_state[2], loop_state[3]), "ctx", 1)
    query_grad = loop_state[4]
    inverse_root = 1.0 / math.sqrt(head_dim)
    return (query_grad * inverse_root, key_grad * inverse_root, value_grad)


META = 8


def contract(left, right, left_dim, right_dim, **kw):
    return lax.dot_general(
        left,
        right,
        (((left_dim,), (right_dim,)), ((), ())),
        preferred_element_type=jnp.float32,
        **kw,
    )


def one_hot(row_count, target):
    places = lax.broadcasted_iota(jnp.int32, (row_count, target.shape[1]), 0)
    return jnp.where(places == target, 1.0, 0.0).astype(jnp.bfloat16)


def side_by_side(stack, heads):
    rows = stack.shape[0] // heads
    return jnp.concatenate([stack[h * rows : (h + 1) * rows, :] for h in range(heads)], axis=1)


def end_to_end(matrix, heads):
    width = matrix.shape[1] // heads
    return jnp.concatenate([matrix[:, h * width : (h + 1) * width] for h in range(heads)], axis=0)


def runs_of(hot):
    count, rows = hot.shape
    counts = jnp.sum(hot, axis=1, keepdims=True)
    owner = jnp.zeros((1, rows), jnp.int32)
    earlier = jnp.zeros((1, rows), jnp.float32)
    for p in range(count):
        mine = hot[p : p + 1, :] > 0.0
        owner = jnp.where(mine, p, owner)
        for less in range(p):
            earlier = earlier + jnp.where(mine, counts[less : less + 1, :], 0.0)
    lane = lax.broadcasted_iota(jnp.int32, (1, rows), 1)
    return owner, counts, lane - earlier.astype(jnp.int32)


def own_kernel(
    count,
    docs,
    doc_ref,
    packet_ref,
    query_ref,
    grad_ref,
    saved_ref,
    query_out,
    grad_out,
    raised_out,
    change_out,
    row_out,
    spread_out,
    target_out,
    filled_out,
):
    rows, width = query_ref.shape
    depth = packet_ref.shape[1]
    heads = width // depth
    slot = 2 * rows // count
    index = lax.axis_index("ctx")
    lane = lax.broadcasted_iota(jnp.int32, (1, rows), 1)
    position = index * rows + lane
    earlier = lax.broadcasted_iota(jnp.int32, (docs, docs), 1) <= lax.broadcasted_iota(
        jnp.int32, (docs, docs), 0
    )
    lengths = doc_ref[...].astype(jnp.float32)
    ends = jnp.sum(jnp.where(earlier, lengths, 0.0), axis=1, keepdims=True).astype(jnp.int32)
    first = jnp.max(jnp.where(ends <= position, ends, 0), axis=0, keepdims=True)
    key_position = index * rows + lax.broadcasted_iota(jnp.int32, (rows, rows), 0)
    allowed = (key_position >= first) & (key_position <= position)
    allowed = jnp.concatenate([allowed] * heads, axis=1)

    queries = end_to_end(query_ref[...], heads)
    query_out[...] = queries
    scores = contract(packet_ref[0:rows, :], queries, 1, 1) * (1.0 / math.sqrt(depth))
    scores = jnp.where(allowed, scores, NEG)
    top = jnp.max(scores, axis=0, keepdims=True)
    raised = jnp.exp(scores - top)
    raised_out[...] = raised
    grads = end_to_end(grad_ref[...], heads)
    grad_out[...] = grads
    product = grads.astype(jnp.float32) * end_to_end(saved_ref[...], heads).astype(jnp.float32)
    delta = contract(
        jnp.ones((8, depth), jnp.float32), product, 1, 1, precision=lax.Precision.HIGHEST
    )[0:1, :]
    change_out[...] = contract(packet_ref[rows : 2 * rows, :], grads, 1, 1) - delta
    row_out[0:1, :] = delta
    row_out[1:2, :] = top
    row_out[2:3, :] = jnp.sum(raised, axis=0, keepdims=True)
    row_out[3:4, :] = jnp.concatenate([first.astype(jnp.float32)] * heads, axis=1)
    row_out[4:8, :] = jnp.ones((4, width), jnp.float32)
    owner, counts, rank = runs_of(packet_ref[2 * rows : 2 * rows + count, :].astype(jnp.float32))
    spread_out[...] = one_hot(count * slot, (owner ^ index) * slot + rank)
    target_out[...] = one_hot(count * rows, (owner ^ index) * rows + rank)
    filled_out[0:count, :] = jnp.broadcast_to(counts, (count, rows))
    filled_out[count:, :] = jnp.zeros((8 - count, rows), jnp.float32)


def fold(count, back, packet, queries, grads, row, filled):
    rows = packet.shape[1]
    index = lax.axis_index("ctx")
    delta, top, total = (row[n : n + 1, :] for n in range(3))
    first = row[3:4, :].astype(jnp.int32)
    position = (index - back) * rows + lax.broadcasted_iota(jnp.int32, (rows, row.shape[1]), 0)
    scores = contract(packet[0:rows, :], queries, 1, 1) * (1.0 / math.sqrt(queries.shape[1]))
    scores = jnp.where(position >= first, scores, NEG)
    new_top = jnp.maximum(top, jnp.max(scores, axis=0, keepdims=True))
    raised = jnp.exp(scores - new_top)
    shrink = jnp.exp(top - new_top)
    total = total * shrink + jnp.sum(raised, axis=0, keepdims=True)
    change = contract(packet[rows : 2 * rows, :], grads, 1, 1) - delta
    factors = row[4:8, :] * jnp.where(
        lax.broadcasted_iota(jnp.int32, (4, row.shape[1]), 0) < back, shrink, 1.0
    )
    owner, counts, rank = runs_of(packet[2 * rows : 2 * rows + count, :].astype(jnp.float32))
    base = jnp.zeros((1, rows), jnp.float32)
    for p in range(count):
        base = base + jnp.where(owner == p, filled[p : p + 1, :], 0.0)
    inside = index >= back
    target = jnp.where(inside, (owner ^ index) * rows + base.astype(jnp.int32) + rank, -1)
    filled = filled[0:count, :] + jnp.where(inside, counts, 0.0)
    return raised, change, (new_top, total, factors), one_hot(count * rows, target), filled


def step_kernel(count, back, *refs):
    query_ref, grad_ref, row_ref, filled_ref, packet_ref = refs[:5]
    raised_out, change_out, row_out, target_out, filled_out = refs[5:]
    raised, change, (top, total, factors), target, filled = fold(
        count, back, packet_ref, query_ref[...], grad_ref[...], row_ref, filled_ref
    )
    raised_out[...] = raised
    change_out[...] = change
    row_out[0:1, :] = row_ref[0:1, :]
    row_out[1:2, :] = top
    row_out[2:3, :] = total
    row_out[3:4, :] = row_ref[3:4, :]
    row_out[4:8, :] = factors
    target_out[...] = target
    filled_out[0:count, :] = filled
    filled_out[count:, :] = jnp.zeros_like(filled_out[count:, :])


def attend_kernel(count, halo, *refs):
    index = lax.axis_index("ctx")
    for blocks in range(1, halo + 2):
        here = index == blocks - 1 if blocks <= halo else index >= halo

        @pl.when(here)
        def _(blocks=blocks):
            attend(count, halo, blocks, refs)


def attend(count, halo, blocks, refs):
    query_ref, grad_ref, row_ref, filled_ref, spread_ref = refs[:5]
    raised_refs = refs[5 : 5 + halo]
    change_refs = refs[5 + halo : 5 + 2 * halo]
    target_refs = refs[5 + 2 * halo : 5 + 3 * halo]
    packets = refs[5 + 3 * halo : 6 + 4 * halo]
    outs = refs[6 + 4 * halo :]
    rows = packets[0].shape[1]
    depth = query_ref.shape[1]
    heads = query_ref.shape[0] // rows
    slot = 2 * rows // count
    scale = 1.0 / math.sqrt(depth)
    queries = query_ref[...]
    grads = grad_ref[...]
    raised = [ref[...] for ref in raised_refs[:blocks]]
    change = [ref[...] for ref in change_refs[:blocks]]
    targets = [ref[...] for ref in target_refs[:blocks]]
    total = row_ref[2:3, :]
    factors = row_ref[4:8, :]
    if blocks > halo:
        raised_far, change_far, (_, total, factors), target_far, _ = fold(
            count, halo, packets[halo], queries, grads, row_ref, filled_ref
        )
        raised.append(raised_far)
        change.append(change_far)
        targets.append(target_far)
    factors = factors * (1.0 / total)
    weights = [raised[n] * factors[n : n + 1, :] for n in range(blocks)]
    changes = [weights[n] * change[n] for n in range(blocks)]
    weights = jnp.concatenate([part.astype(jnp.bfloat16) for part in weights], axis=0)
    changes = jnp.concatenate([part.astype(jnp.bfloat16) for part in changes], axis=0)
    keys = jnp.concatenate([packet[0:rows, :] for packet in packets[:blocks]], axis=0)
    query_grad = (contract(keys, changes, 0, 0) * scale).astype(jnp.bfloat16)
    key_parts = contract(changes, queries, 1, 0) * scale
    value_parts = contract(weights, grads, 1, 0)
    parts = jnp.concatenate([key_parts, value_parts], axis=1).astype(jnp.bfloat16)

    query_slots = contract(spread_ref[...], end_to_end(query_grad, heads), 1, 1)
    query_slots = query_slots.astype(jnp.bfloat16)
    part_slots = contract(jnp.concatenate(targets, axis=1), parts, 1, 0).astype(jnp.bfloat16)
    at = heads * slot
    for k in range(count):
        out = outs[k]
        for h in range(heads):
            out[h * slot : (h + 1) * slot, :] = query_slots[
                k * slot : (k + 1) * slot, h * depth : (h + 1) * depth
            ]
        for n in range(2):
            out[at + n * rows : at + (n + 1) * rows, :] = part_slots[
                k * rows : (k + 1) * rows, n * depth : (n + 1) * depth
            ]


def order_kernel(count, halo, _, *refs):
    packets = refs[: 1 + halo]
    query_out, key_out = refs[1 + halo :]
    rows = query_out.shape[0]
    index = lax.axis_index("ctx")
    given = []
    for ref in packets:
        hot = ref[2 * rows : 2 * rows + count, :].astype(jnp.float32)
        counts = jnp.sum(hot, axis=1, keepdims=True)
        mine = jnp.zeros((1, 1), jnp.float32)
        for p in range(count):
            mine = jnp.where(index == p, counts[p : p + 1, :], mine)
        given.append(mine.astype(jnp.int32))
    if len(given) < count:
        given.append(rows - sum(given))
    giver = [lax.rem(index - d + count, count) for d in range(count)]

    def placement(size, halo):
        lane = lax.broadcasted_iota(jnp.int32, (1, count * size), 1)
        target = jnp.full(lane.shape, -1, jnp.int32)
        for k in range(count):
            step = lane - k * size
            for back in range(halo + 1):
                block = (index ^ k) - back
                start = jnp.zeros((1, 1), jnp.int32)
                length = jnp.zeros((1, 1), jnp.int32)
                for d in range(count):
                    start = start + jnp.where(giver[d] < block, given[d], 0)
                    length = length + jnp.where(giver[d] == block, given[d], 0)
                target = jnp.where((step >= 0) & (step < length), start + step, target)
                step = step - length
        return one_hot(rows, target)

    query_out[...] = placement(2 * rows // count, 0)
    key_out[...] = placement(rows, halo)


def place_kernel(count, query_spread, key_spread, *refs):
    ins = refs[:count]
    query_out, key_out, value_out = refs[count : count + 3]
    query_here, key_here, value_here, sems = refs[count + 3 :]
    rows, width = query_here.shape
    depth = key_here.shape[1]
    heads = width // depth
    slot = 2 * rows // count
    copies = []

    def leave(here, out):
        copies.append(pltpu.make_async_copy(here, out, sems.at[len(copies)]))
        copies[-1].start()

    def taken(first, size, pieces):
        return jnp.concatenate(
            [
                jnp.concatenate(
                    [ref[first + n * size : first + (n + 1) * size, :] for n in range(pieces)],
                    axis=1,
                )
                for ref in ins
            ],
            axis=0,
        )

    query_here[...] = contract(query_spread[...], taken(0, slot, heads), 1, 0)
    leave(query_here, query_out)
    both = contract(key_spread[...], taken(heads * slot, rows, 2), 1, 0)
    for n, (here, out) in enumerate(((key_here, key_out), (value_here, value_out))):
        here[...] = both[:, n * depth : (n + 1) * depth]
        leave(here, out)
    for copy in copies:
        copy.wait()


def near_plan(doc_lengths, owners, queries, key_head_rows, value_head_rows, forward_out, grad_out):
    count = lax.axis_size("ctx")
    rows, width = queries.shape
    depth = key_head_rows.shape[1]
    heads = width // depth
    bf16, f32 = jnp.bfloat16, jnp.float32
    columns = heads * rows
    halo = count // 2
    slot = 2 * rows // count
    whole = pl.BlockSpec(memory_space=pltpu.VMEM)
    params = pltpu.CompilerParams(vmem_limit_bytes=40 * 1024 * 1024)

    mark = lax.broadcasted_iota(jnp.int32, (2 * rows + META, rows), 0) - 2 * rows
    packet = jnp.where(
        mark < 0,
        jnp.pad(jnp.concatenate([key_head_rows, value_head_rows], axis=0), ((0, META), (0, 0))),
        (owners[None, :] == mark).astype(bf16),
    )
    near = [
        lax.ppermute(packet, "ctx", [(i, (i + back) % count) for i in range(count)])
        for back in range(1, halo + 1)
    ]
    block_shapes = [jax.ShapeDtypeStruct((rows, columns), f32)] * 2
    row_shape = jax.ShapeDtypeStruct((8, columns), f32)
    target_shape = jax.ShapeDtypeStruct((count * rows, rows), bf16)
    filled_shape = jax.ShapeDtypeStruct((8, rows), f32)
    query_rows, grad_rows, raised, change, row, spread, target, filled = pl.pallas_call(
        functools.partial(own_kernel, count, doc_lengths.shape[0]),
        out_shape=[jax.ShapeDtypeStruct((columns, depth), bf16)] * 2
        + block_shapes
        + [row_shape, jax.ShapeDtypeStruct((count * slot, rows), bf16), target_shape, filled_shape],
        in_specs=[whole] * 5,
        out_specs=[whole] * 8,
        compiler_params=params,
    )(doc_lengths.reshape(1, -1), packet, queries, grad_out, forward_out)
    raised, change, target = [raised], [change], [target]
    for back in range(1, halo):
        found = pl.pallas_call(
            functools.partial(step_kernel, count, back),
            out_shape=block_shapes + [row_shape, target_shape, filled_shape],
            in_specs=[whole] * 5,
            out_specs=[whole] * 5,
            compiler_params=params,
        )(query_rows, grad_rows, row, filled, near[back - 1])
        raised.append(found[0])
        change.append(found[1])
        row = found[2]
        target.append(found[3])
        filled = found[4]
    sent = pl.pallas_call(
        functools.partial(attend_kernel, count, halo),
        out_shape=[jax.ShapeDtypeStruct((heads * slot + 2 * rows, depth), bf16)] * count,
        in_specs=[whole] * (6 + 4 * halo),
        out_specs=[whole] * count,
        compiler_params=params,
    )(query_rows, grad_rows, row, filled, spread, *raised, *change, *target, packet, *near)
    received = [sent[0]] + [
        lax.ppermute(sent[k], "ctx", [(i, i ^ k) for i in range(count)]) for k in range(1, count)
    ]
    spreads = pl.pallas_call(
        functools.partial(order_kernel, count, halo),
        out_shape=[
            jax.ShapeDtypeStruct((rows, count * slot), bf16),
            jax.ShapeDtypeStruct((rows, count * rows), bf16),
        ],
        in_specs=[pl.BlockSpec(memory_space=pl.ANY)] + [whole] * (1 + halo),
        out_specs=[whole] * 2,
        compiler_params=params,
    )(received[-1], packet, *near)
    return pl.pallas_call(
        functools.partial(place_kernel, count),
        out_shape=[
            jax.ShapeDtypeStruct((rows, width), f32),
            jax.ShapeDtypeStruct((rows, depth), f32),
            jax.ShapeDtypeStruct((rows, depth), f32),
        ],
        in_specs=[whole] * (2 + count),
        out_specs=[pl.BlockSpec(memory_space=pl.ANY)] * 3,
        scratch_shapes=[
            pltpu.VMEM((rows, width), f32),
            pltpu.VMEM((rows, depth), f32),
            pltpu.VMEM((rows, depth), f32),
            pltpu.SemaphoreType.DMA((3,)),
        ],
        compiler_params=params,
    )(*spreads, *received)


def per_device(*args):
    if lax.axis_size("ctx") in (2, 4):
        return near_plan(*args)
    return ring_plan(*args)


def solution(mesh):
    return jax.shard_map(
        per_device,
        mesh=mesh,
        in_specs=(
            P("groups"),
            P(("groups", "ctx")),
            P(("groups", "ctx"), "head"),
            P(("groups", "ctx"), "head"),
            P(("groups", "ctx"), "head"),
            P(("groups", "ctx"), "head"),
            P(("groups", "ctx"), "head"),
        ),
        out_specs=(
            P(("groups", "ctx"), "head"),
            P(("groups", "ctx"), "head"),
            P(("groups", "ctx"), "head"),
        ),
        check_vma=False,
    )
```

```python
import functools
import math

import jax
import jax.numpy as jnp
from jax import lax
from jax.experimental import pallas as pl
from jax.experimental.pallas import tpu as pltpu
from jax.sharding import PartitionSpec as P

HEAD_WIDTH = 128
GROUP = 4


NEG = -1e30
BLOCK = 512


def shifted(value, axis, by):
    count = lax.axis_size(axis)
    return lax.ppermute(value, axis, [(i, (i + by) % count) for i in range(count)])


def document_of(positions, doc_lengths):
    ends = jnp.cumsum(doc_lengths)
    return jnp.sum((positions[:, None] >= ends[None, :]).astype(jnp.int32), axis=1)


def allowed_between(query_positions, query_docs, key_positions, key_docs):
    return (query_docs[:, None] == key_docs[None, :]) & (
        key_positions[None, :] <= query_positions[:, None]
    )


def head_rows(matrix, group_size, head_dim):
    row_count = matrix.shape[0]
    return matrix.reshape(row_count * group_size, head_dim)


def block_scores(query_flat, key_head, row_count, group_size, head_dim):
    scores = lax.dot_general(
        query_flat, key_head, (((1,), (1,)), ((), ())), preferred_element_type=jnp.float32
    )
    return (scores * (1.0 / math.sqrt(head_dim))).reshape(row_count, group_size, key_head.shape[0])


def update_stats(running, query_local, key_block, allowed, group_size, head_dim):
    running_max, totals = running
    row_count = query_local.shape[0]
    scores = block_scores(
        head_rows(query_local, group_size, head_dim), key_block, row_count, group_size, head_dim
    )
    masked = jnp.where(allowed[:, None, :], scores, NEG)
    new_max = jnp.maximum(running_max, jnp.max(masked, axis=2))
    weights = jnp.where(allowed[:, None, :], jnp.exp(masked - new_max[:, :, None]), 0.0)
    new_totals = [totals * jnp.exp(running_max - new_max) + jnp.sum(weights, axis=2)]
    new_maxima = [new_max]
    return (jnp.concatenate(new_maxima, axis=1), jnp.concatenate(new_totals, axis=1))


def backward_block(
    query_local,
    grad_local,
    log_norm,
    row_delta,
    key_block,
    value_block,
    allowed,
    group_size,
    head_dim,
):
    row_count = query_local.shape[0]
    query_flat = head_rows(query_local, group_size, head_dim)
    grad_flat = head_rows(grad_local, group_size, head_dim)
    scores = block_scores(query_flat, key_block, row_count, group_size, head_dim)
    masked = jnp.where(allowed[:, None, :], scores, NEG)
    weights = jnp.exp(masked - log_norm[:, 0:group_size, None])
    grad_weights = lax.dot_general(
        grad_flat, value_block, (((1,), (1,)), ((), ())), preferred_element_type=jnp.float32
    ).reshape(row_count, group_size, -1)
    grad_scores = weights * (grad_weights - row_delta[:, 0:group_size, None])
    rounded_weights = weights.astype(jnp.bfloat16).reshape(row_count * group_size, -1)
    rounded_grads = grad_scores.astype(jnp.bfloat16).reshape(row_count * group_size, -1)
    value_parts = [
        lax.dot_general(
            rounded_weights, grad_flat, (((0,), (0,)), ((), ())), preferred_element_type=jnp.float32
        )
    ]
    key_parts = [
        lax.dot_general(
            rounded_grads, query_flat, (((0,), (0,)), ((), ())), preferred_element_type=jnp.float32
        )
    ]
    query_parts = [
        jnp.dot(rounded_grads, key_block, preferred_element_type=jnp.float32).reshape(
            row_count, group_size * head_dim
        )
    ]
    return (
        jnp.concatenate(query_parts, axis=1),
        jnp.concatenate(key_parts, axis=1),
        jnp.concatenate(value_parts, axis=1),
    )


def ring_plan(doc_lengths, owners, queries, key_head_rows, value_head_rows, forward_out, grad_out):
    context_size = lax.axis_size("ctx")
    context_index = lax.axis_index("ctx")
    row_count = queries.shape[0]
    head_dim = HEAD_WIDTH
    group_size = GROUP
    query_heads = queries.shape[1] // head_dim
    slot_count = 2 * row_count // context_size
    everyone = lax.all_gather(owners, "ctx", axis=0, tiled=True)
    row_arrangement = jnp.argsort(everyone, stable=True)
    layout_docs = document_of(row_arrangement, doc_lengths)
    own_positions = lax.dynamic_slice_in_dim(
        row_arrangement, context_index * row_count, row_count, 0
    )
    own_documents = lax.dynamic_slice_in_dim(layout_docs, context_index * row_count, row_count, 0)
    owner_ids = jnp.arange(context_size, dtype=jnp.int32)
    owner_hot = (owners[:, None] == owner_ids[None, :]).astype(jnp.int32)
    earlier = jnp.cumsum(owner_hot, axis=0) - owner_hot
    rank_within = jnp.sum(earlier * owner_hot, axis=1)
    slot_rows = owners * slot_count + rank_within

    def packed(matrix):
        empty = jnp.zeros((context_size * slot_count,) + matrix.shape[1:], matrix.dtype)
        return empty.at[slot_rows].set(matrix)

    owner_grid = everyone.reshape(context_size, row_count)
    counts = jnp.sum((owner_grid == context_index).astype(jnp.int32), axis=1)
    count_ends = jnp.cumsum(counts)
    starts = count_ends - counts
    wanted = jnp.arange(row_count, dtype=jnp.int32)
    source = jnp.sum((wanted[:, None] >= count_ends[None, :]).astype(jnp.int32), axis=1)
    source_hot = (source[:, None] == owner_ids[None, :]).astype(jnp.int32)
    take_rows = source * slot_count + wanted - jnp.sum(source_hot * starts[None, :], axis=1)

    def compact(received):
        return jnp.take(received, take_rows, axis=0)

    local_delta = jnp.sum(
        (grad_out.astype(jnp.float32) * forward_out.astype(jnp.float32)).reshape(
            row_count, query_heads, head_dim
        ),
        axis=2,
    )
    arrived = (
        lax.all_to_all(packed(queries), "ctx", split_axis=0, concat_axis=0, tiled=True),
        lax.all_to_all(packed(key_head_rows), "ctx", split_axis=0, concat_axis=0, tiled=True),
        lax.all_to_all(packed(value_head_rows), "ctx", split_axis=0, concat_axis=0, tiled=True),
        lax.all_to_all(packed(grad_out), "ctx", split_axis=0, concat_axis=0, tiled=True),
    )
    query_local, key_local, value_local, grad_local = [compact(received) for received in arrived]
    row_delta = compact(
        lax.all_to_all(packed(local_delta), "ctx", split_axis=0, concat_axis=0, tiled=True)
    )

    def fold_keys(running, shard_rows, first_row):
        piece_count = shard_rows.shape[0]
        step_rows = math.gcd(piece_count, BLOCK) if piece_count > BLOCK else piece_count

        def one_block(partial_value, block_index):
            offset = first_row + block_index * step_rows
            key_block = lax.dynamic_slice_in_dim(shard_rows, block_index * step_rows, step_rows, 0)
            key_positions = lax.dynamic_slice_in_dim(row_arrangement, offset, step_rows, 0)
            key_docs = lax.dynamic_slice_in_dim(layout_docs, offset, step_rows, 0)
            allowed = allowed_between(own_positions, own_documents, key_positions, key_docs)
            return (
                update_stats(partial_value, query_local, key_block, allowed, group_size, head_dim),
                None,
            )

        if piece_count == step_rows:
            return one_block(running, 0)[0]
        return lax.scan(one_block, running, jnp.arange(piece_count // step_rows, dtype=jnp.int32))[
            0
        ]

    start_stats = (
        jnp.full((row_count, query_heads), NEG, jnp.float32),
        jnp.zeros((row_count, query_heads), jnp.float32),
    )
    top_scores, totals = fold_keys(
        start_stats, lax.all_gather(key_local, "ctx", axis=0, tiled=True), jnp.int32(0)
    )
    log_norm = top_scores + jnp.log(totals)

    def block_meta(owner_index, offset, size):
        first = owner_index * row_count + offset
        key_positions = lax.dynamic_slice_in_dim(row_arrangement, first, size, 0)
        key_docs = lax.dynamic_slice_in_dim(layout_docs, first, size, 0)
        return (key_positions, key_docs)

    query_zero = jnp.zeros(query_local.shape, jnp.float32)
    key_zero = jnp.zeros(key_local.shape, jnp.float32)

    def one_turn(turn_index, loop_state):
        key_moving, value_moving, key_grad, value_grad, query_grad = loop_state
        owner_index = (context_index - turn_index) % context_size
        key_positions, key_docs = block_meta(owner_index, 0, row_count)
        allowed = allowed_between(own_positions, own_documents, key_positions, key_docs)
        query_part, key_part, value_part = backward_block(
            query_local,
            grad_local,
            log_norm,
            row_delta,
            key_moving,
            value_moving,
            allowed,
            group_size,
            head_dim,
        )
        return (
            key_moving,
            value_moving,
            key_grad + key_part,
            value_grad + value_part,
            query_grad + query_part,
        )

    def moved_turn(turn_index, loop_state):
        key_moving, value_moving, key_grad, value_grad, query_grad = loop_state
        key_moving, value_moving = shifted((key_moving, value_moving), "ctx", 1)
        key_grad, value_grad = shifted((key_grad, value_grad), "ctx", 1)
        return one_turn(turn_index, (key_moving, value_moving, key_grad, value_grad, query_grad))

    loop_state = one_turn(0, (key_local, value_local, key_zero, key_zero, query_zero))
    loop_state = lax.fori_loop(1, context_size, moved_turn, loop_state)
    key_grad, value_grad = shifted((loop_state[2], loop_state[3]), "ctx", 1)
    query_grad = loop_state[4]
    inverse_root = 1.0 / math.sqrt(head_dim)
    return (query_grad * inverse_root, key_grad * inverse_root, value_grad)


META = 8


def contract(left, right, left_dim, right_dim, **kw):
    return lax.dot_general(
        left,
        right,
        (((left_dim,), (right_dim,)), ((), ())),
        preferred_element_type=jnp.float32,
        **kw,
    )


def one_hot(row_count, target):
    places = lax.broadcasted_iota(jnp.int32, (row_count, target.shape[1]), 0)
    return jnp.where(places == target, 1.0, 0.0).astype(jnp.bfloat16)


def side_by_side(stack, heads):
    rows = stack.shape[0] // heads
    return jnp.concatenate([stack[h * rows : (h + 1) * rows, :] for h in range(heads)], axis=1)


def end_to_end(matrix, heads):
    width = matrix.shape[1] // heads
    return jnp.concatenate([matrix[:, h * width : (h + 1) * width] for h in range(heads)], axis=0)


def runs_of(hot):
    count, rows = hot.shape
    counts = jnp.sum(hot, axis=1, keepdims=True)
    owner = jnp.zeros((1, rows), jnp.int32)
    earlier = jnp.zeros((1, rows), jnp.float32)
    for p in range(count):
        mine = hot[p : p + 1, :] > 0.0
        owner = jnp.where(mine, p, owner)
        for less in range(p):
            earlier = earlier + jnp.where(mine, counts[less : less + 1, :], 0.0)
    lane = lax.broadcasted_iota(jnp.int32, (1, rows), 1)
    return owner, counts, lane - earlier.astype(jnp.int32)


def own_kernel(
    count,
    docs,
    doc_ref,
    packet_ref,
    query_ref,
    grad_ref,
    saved_ref,
    query_out,
    grad_out,
    raised_out,
    change_out,
    row_out,
    spread_out,
    target_out,
    filled_out,
):
    rows, width = query_ref.shape
    depth = packet_ref.shape[1]
    heads = width // depth
    slot = 2 * rows // count
    index = lax.axis_index("ctx")
    lane = lax.broadcasted_iota(jnp.int32, (1, rows), 1)
    position = index * rows + lane
    earlier = lax.broadcasted_iota(jnp.int32, (docs, docs), 1) <= lax.broadcasted_iota(
        jnp.int32, (docs, docs), 0
    )
    lengths = doc_ref[...].astype(jnp.float32)
    ends = jnp.sum(jnp.where(earlier, lengths, 0.0), axis=1, keepdims=True).astype(jnp.int32)
    first = jnp.max(jnp.where(ends <= position, ends, 0), axis=0, keepdims=True)
    key_position = index * rows + lax.broadcasted_iota(jnp.int32, (rows, rows), 0)
    allowed = (key_position >= first) & (key_position <= position)
    allowed = jnp.concatenate([allowed] * heads, axis=1)

    queries = end_to_end(query_ref[...], heads)
    query_out[...] = queries
    scores = contract(packet_ref[0:rows, :], queries, 1, 1) * (1.0 / math.sqrt(depth))
    scores = jnp.where(allowed, scores, NEG)
    top = jnp.max(scores, axis=0, keepdims=True)
    raised = jnp.exp(scores - top)
    raised_out[...] = raised
    grads = end_to_end(grad_ref[...], heads)
    grad_out[...] = grads
    product = grads.astype(jnp.float32) * end_to_end(saved_ref[...], heads).astype(jnp.float32)
    delta = contract(
        jnp.ones((8, depth), jnp.float32), product, 1, 1, precision=lax.Precision.HIGHEST
    )[0:1, :]
    change_out[...] = contract(packet_ref[rows : 2 * rows, :], grads, 1, 1) - delta
    row_out[0:1, :] = delta
    row_out[1:2, :] = top
    row_out[2:3, :] = jnp.sum(raised, axis=0, keepdims=True)
    row_out[3:4, :] = jnp.concatenate([first.astype(jnp.float32)] * heads, axis=1)
    row_out[4:8, :] = jnp.ones((4, width), jnp.float32)
    owner, counts, rank = runs_of(packet_ref[2 * rows : 2 * rows + count, :].astype(jnp.float32))
    spread_out[...] = one_hot(count * slot, (owner ^ index) * slot + rank)
    target_out[...] = one_hot(count * rows, (owner ^ index) * rows + rank)
    filled_out[0:count, :] = jnp.broadcast_to(counts, (count, rows))
    filled_out[count:, :] = jnp.zeros((8 - count, rows), jnp.float32)


def fold(count, back, packet, queries, grads, row, filled):
    rows = packet.shape[1]
    index = lax.axis_index("ctx")
    delta, top, total = (row[n : n + 1, :] for n in range(3))
    first = row[3:4, :].astype(jnp.int32)
    position = (index - back) * rows + lax.broadcasted_iota(jnp.int32, (rows, row.shape[1]), 0)
    scores = contract(packet[0:rows, :], queries, 1, 1) * (1.0 / math.sqrt(queries.shape[1]))
    scores = jnp.where(position >= first, scores, NEG)
    new_top = jnp.maximum(top, jnp.max(scores, axis=0, keepdims=True))
    raised = jnp.exp(scores - new_top)
    shrink = jnp.exp(top - new_top)
    total = total * shrink + jnp.sum(raised, axis=0, keepdims=True)
    change = contract(packet[rows : 2 * rows, :], grads, 1, 1) - delta
    factors = row[4:8, :] * jnp.where(
        lax.broadcasted_iota(jnp.int32, (4, row.shape[1]), 0) < back, shrink, 1.0
    )
    owner, counts, rank = runs_of(packet[2 * rows : 2 * rows + count, :].astype(jnp.float32))
    base = jnp.zeros((1, rows), jnp.float32)
    for p in range(count):
        base = base + jnp.where(owner == p, filled[p : p + 1, :], 0.0)
    inside = index >= back
    target = jnp.where(inside, (owner ^ index) * rows + base.astype(jnp.int32) + rank, -1)
    filled = filled[0:count, :] + jnp.where(inside, counts, 0.0)
    return raised, change, (new_top, total, factors), one_hot(count * rows, target), filled


def step_kernel(count, back, *refs):
    query_ref, grad_ref, row_ref, filled_ref, packet_ref = refs[:5]
    raised_out, change_out, row_out, target_out, filled_out, given_out = refs[5:]
    raised, change, (top, total, factors), target, filled = fold(
        count, back, packet_ref, query_ref[...], grad_ref[...], row_ref, filled_ref
    )
    raised_out[...] = raised
    change_out[...] = change
    row_out[0:1, :] = row_ref[0:1, :]
    row_out[1:2, :] = top
    row_out[2:3, :] = total
    row_out[3:4, :] = row_ref[3:4, :]
    row_out[4:8, :] = factors
    target_out[...] = target
    filled_out[0:count, :] = filled
    filled_out[count:, :] = jnp.zeros_like(filled_out[count:, :])
    rows = packet_ref.shape[1]
    hot = packet_ref[2 * rows : 2 * rows + count, :].astype(jnp.float32)
    given_out[0:count, :] = jnp.broadcast_to(jnp.sum(hot, axis=1, keepdims=True), (count, rows))
    given_out[count:, :] = jnp.zeros_like(given_out[count:, :])


def attend_kernel(count, halo, given_ref, *refs):
    index = lax.axis_index("ctx")
    last = refs[-1]
    given = jnp.zeros((1, last.shape[1]), jnp.float32)
    for p in range(count):
        given = jnp.where((index ^ (count - 1)) == p, given_ref[p : p + 1, 0 : last.shape[1]], given)
    last[last.shape[0] - META :, :] = jnp.broadcast_to(given, (META, last.shape[1])).astype(
        jnp.bfloat16
    )
    for blocks in range(1, halo + 2):
        here = index == blocks - 1 if blocks <= halo else index >= halo

        @pl.when(here)
        def _(blocks=blocks):
            attend(count, halo, blocks, refs)


def attend(count, halo, blocks, refs):
    query_ref, grad_ref, row_ref, filled_ref, spread_ref = refs[:5]
    raised_refs = refs[5 : 5 + halo]
    change_refs = refs[5 + halo : 5 + 2 * halo]
    target_refs = refs[5 + 2 * halo : 5 + 3 * halo]
    packets = refs[5 + 3 * halo : 6 + 4 * halo]
    outs = refs[6 + 4 * halo :]
    rows = packets[0].shape[1]
    depth = query_ref.shape[1]
    heads = query_ref.shape[0] // rows
    slot = 2 * rows // count
    scale = 1.0 / math.sqrt(depth)
    queries = query_ref[...]
    grads = grad_ref[...]
    raised = [ref[...] for ref in raised_refs[:blocks]]
    change = [ref[...] for ref in change_refs[:blocks]]
    targets = [ref[...] for ref in target_refs[:blocks]]
    total = row_ref[2:3, :]
    factors = row_ref[4:8, :]
    if blocks > halo:
        raised_far, change_far, (_, total, factors), target_far, _ = fold(
            count, halo, packets[halo], queries, grads, row_ref, filled_ref
        )
        raised.append(raised_far)
        change.append(change_far)
        targets.append(target_far)
    factors = factors * (1.0 / total)
    weights = [raised[n] * factors[n : n + 1, :] for n in range(blocks)]
    changes = [weights[n] * change[n] for n in range(blocks)]
    weights = jnp.concatenate([part.astype(jnp.bfloat16) for part in weights], axis=0)
    changes = jnp.concatenate([part.astype(jnp.bfloat16) for part in changes], axis=0)
    keys = jnp.concatenate([packet[0:rows, :] for packet in packets[:blocks]], axis=0)
    query_grad = (contract(keys, changes, 0, 0) * scale).astype(jnp.bfloat16)
    key_parts = contract(changes, queries, 1, 0) * scale
    value_parts = contract(weights, grads, 1, 0)
    parts = jnp.concatenate([key_parts, value_parts], axis=1).astype(jnp.bfloat16)

    query_slots = contract(spread_ref[...], end_to_end(query_grad, heads), 1, 1)
    query_slots = query_slots.astype(jnp.bfloat16)
    part_slots = contract(jnp.concatenate(targets, axis=1), parts, 1, 0).astype(jnp.bfloat16)
    at = heads * slot
    for k in range(count):
        out = outs[k]
        for h in range(heads):
            out[h * slot : (h + 1) * slot, :] = query_slots[
                k * slot : (k + 1) * slot, h * depth : (h + 1) * depth
            ]
        for n in range(2):
            out[at + n * rows : at + (n + 1) * rows, :] = part_slots[
                k * rows : (k + 1) * rows, n * depth : (n + 1) * depth
            ]


def order_kernel(count, halo, last_ref, *refs):
    packets = refs[: 1 + halo]
    query_out, key_out = refs[1 + halo :]
    rows = query_out.shape[0]
    index = lax.axis_index("ctx")
    giver = [index, lax.rem(index + count - 1, count)]
    given = []
    for ref in packets:
        hot = ref[2 * rows : 2 * rows + count, :].astype(jnp.float32)
        counts = jnp.sum(hot, axis=1, keepdims=True)
        mine = jnp.zeros((1, 1), jnp.float32)
        for p in range(count):
            mine = jnp.where(index == p, counts[p : p + 1, :], mine)
        given.append(mine.astype(jnp.int32))
    if count == 4:
        at = last_ref.shape[0] - META
        told = last_ref[at : at + 1, 0:1].astype(jnp.float32).astype(jnp.int32)
        even = lax.rem(index, 2) == 0
        given[2] = jnp.where(even, told, given[2])
        giver.append(jnp.where(even, lax.rem((index ^ 3) + 3, 4), jnp.where(index == 1, 2, 1)))
        given.append(rows - sum(given))
        giver.append(6 - sum(giver))

    def placement(size, halo):
        lane = lax.broadcasted_iota(jnp.int32, (1, count * size), 1)
        target = jnp.full(lane.shape, -1, jnp.int32)
        for k in range(count):
            step = lane - k * size
            for back in range(halo + 1):
                block = (index ^ k) - back
                start = jnp.zeros((1, 1), jnp.int32)
                length = jnp.zeros((1, 1), jnp.int32)
                for d in range(count):
                    start = start + jnp.where(giver[d] < block, given[d], 0)
                    length = length + jnp.where(giver[d] == block, given[d], 0)
                target = jnp.where((step >= 0) & (step < length), start + step, target)
                step = step - length
        return one_hot(rows, target)

    query_out[...] = placement(2 * rows // count, 0)
    key_out[...] = placement(rows, halo)


def place_kernel(count, query_spread, key_spread, *refs):
    ins = refs[:count]
    query_out, key_out, value_out = refs[count : count + 3]
    query_here, key_here, value_here, sems = refs[count + 3 :]
    rows, width = query_here.shape
    depth = key_here.shape[1]
    heads = width // depth
    slot = 2 * rows // count
    copies = []

    def leave(here, out):
        copies.append(pltpu.make_async_copy(here, out, sems.at[len(copies)]))
        copies[-1].start()

    def taken(first, size, pieces):
        return jnp.concatenate(
            [
                jnp.concatenate(
                    [ref[first + n * size : first + (n + 1) * size, :] for n in range(pieces)],
                    axis=1,
                )
                for ref in ins
            ],
            axis=0,
        )

    query_here[...] = contract(query_spread[...], taken(0, slot, heads), 1, 0)
    leave(query_here, query_out)
    both = contract(key_spread[...], taken(heads * slot, rows, 2), 1, 0)
    for n, (here, out) in enumerate(((key_here, key_out), (value_here, value_out))):
        here[...] = both[:, n * depth : (n + 1) * depth]
        leave(here, out)
    for copy in copies:
        copy.wait()


def near_plan(doc_lengths, owners, queries, key_head_rows, value_head_rows, forward_out, grad_out):
    count = lax.axis_size("ctx")
    rows, width = queries.shape
    depth = key_head_rows.shape[1]
    heads = width // depth
    bf16, f32 = jnp.bfloat16, jnp.float32
    columns = heads * rows
    halo = count // 2
    slot = 2 * rows // count
    whole = pl.BlockSpec(memory_space=pltpu.VMEM)
    params = pltpu.CompilerParams(vmem_limit_bytes=40 * 1024 * 1024)

    mark = lax.broadcasted_iota(jnp.int32, (2 * rows + META, rows), 0) - 2 * rows
    packet = jnp.where(
        mark < 0,
        jnp.pad(jnp.concatenate([key_head_rows, value_head_rows], axis=0), ((0, META), (0, 0))),
        (owners[None, :] == mark).astype(bf16),
    )
    near = [
        lax.ppermute(packet, "ctx", [(i, (i + 1) % count) for i in range(count)])
    ] + [
        lax.ppermute(
            packet,
            "ctx",
            [(i, i + back if i + back < count else count - 1 - i) for i in range(count)],
        )
        for back in range(2, halo + 1)
    ]
    block_shapes = [jax.ShapeDtypeStruct((rows, columns), f32)] * 2
    row_shape = jax.ShapeDtypeStruct((8, columns), f32)
    target_shape = jax.ShapeDtypeStruct((count * rows, rows), bf16)
    filled_shape = jax.ShapeDtypeStruct((8, rows), f32)
    query_rows, grad_rows, raised, change, row, spread, target, filled = pl.pallas_call(
        functools.partial(own_kernel, count, doc_lengths.shape[0]),
        out_shape=[jax.ShapeDtypeStruct((columns, depth), bf16)] * 2
        + block_shapes
        + [row_shape, jax.ShapeDtypeStruct((count * slot, rows), bf16), target_shape, filled_shape],
        in_specs=[whole] * 5,
        out_specs=[whole] * 8,
        compiler_params=params,
    )(doc_lengths.reshape(1, -1), packet, queries, grad_out, forward_out)
    raised, change, target, given = [raised], [change], [target], filled
    for back in range(1, halo):
        found = pl.pallas_call(
            functools.partial(step_kernel, count, back),
            out_shape=block_shapes + [row_shape, target_shape, filled_shape, filled_shape],
            in_specs=[whole] * 5,
            out_specs=[whole] * 6,
            compiler_params=params,
        )(query_rows, grad_rows, row, filled, near[back - 1])
        raised.append(found[0])
        change.append(found[1])
        row = found[2]
        target.append(found[3])
        filled, given = found[4:]
    sent = pl.pallas_call(
        functools.partial(attend_kernel, count, halo),
        out_shape=[
            jax.ShapeDtypeStruct(
                (heads * slot + 2 * rows + (META if k == count - 1 else 0), depth), bf16
            )
            for k in range(count)
        ],
        in_specs=[whole] * (7 + 4 * halo),
        out_specs=[whole] * count,
        compiler_params=params,
    )(given, query_rows, grad_rows, row, filled, spread, *raised, *change, *target, packet, *near)
    received = [sent[0]] + [
        lax.ppermute(sent[k], "ctx", [(i, i ^ k) for i in range(count)]) for k in range(1, count)
    ]
    spreads = pl.pallas_call(
        functools.partial(order_kernel, count, halo),
        out_shape=[
            jax.ShapeDtypeStruct((rows, count * slot), bf16),
            jax.ShapeDtypeStruct((rows, count * rows), bf16),
        ],
        in_specs=[whole] * (2 + halo),
        out_specs=[whole] * 2,
        compiler_params=params,
    )(received[-1], packet, *near)
    return pl.pallas_call(
        functools.partial(place_kernel, count),
        out_shape=[
            jax.ShapeDtypeStruct((rows, width), f32),
            jax.ShapeDtypeStruct((rows, depth), f32),
            jax.ShapeDtypeStruct((rows, depth), f32),
        ],
        in_specs=[whole] * (2 + count),
        out_specs=[pl.BlockSpec(memory_space=pl.ANY)] * 3,
        scratch_shapes=[
            pltpu.VMEM((rows, width), f32),
            pltpu.VMEM((rows, depth), f32),
            pltpu.VMEM((rows, depth), f32),
            pltpu.SemaphoreType.DMA((3,)),
        ],
        compiler_params=params,
    )(*spreads, *received)


def per_device(*args):
    if lax.axis_size("ctx") in (2, 4):
        return near_plan(*args)
    return ring_plan(*args)


def solution(mesh):
    return jax.shard_map(
        per_device,
        mesh=mesh,
        in_specs=(
            P("groups"),
            P(("groups", "ctx")),
            P(("groups", "ctx"), "head"),
            P(("groups", "ctx"), "head"),
            P(("groups", "ctx"), "head"),
            P(("groups", "ctx"), "head"),
            P(("groups", "ctx"), "head"),
        ),
        out_specs=(
            P(("groups", "ctx"), "head"),
            P(("groups", "ctx"), "head"),
            P(("groups", "ctx"), "head"),
        ),
        check_vma=False,
    )
```

```python
import functools
import math

import jax
import jax.numpy as jnp
from jax import lax
from jax.experimental import pallas as pl
from jax.experimental.pallas import tpu as pltpu
from jax.sharding import PartitionSpec as P

HEAD_WIDTH = 128
GROUP = 4


NEG = -1e30
BLOCK = 512


def shifted(value, axis, by):
    count = lax.axis_size(axis)
    return lax.ppermute(value, axis, [(i, (i + by) % count) for i in range(count)])


def document_of(positions, doc_lengths):
    ends = jnp.cumsum(doc_lengths)
    return jnp.sum((positions[:, None] >= ends[None, :]).astype(jnp.int32), axis=1)


def allowed_between(query_positions, query_docs, key_positions, key_docs):
    return (query_docs[:, None] == key_docs[None, :]) & (
        key_positions[None, :] <= query_positions[:, None]
    )


def head_rows(matrix, group_size, head_dim):
    row_count = matrix.shape[0]
    return matrix.reshape(row_count * group_size, head_dim)


def block_scores(query_flat, key_head, row_count, group_size, head_dim):
    scores = lax.dot_general(
        query_flat, key_head, (((1,), (1,)), ((), ())), preferred_element_type=jnp.float32
    )
    return (scores * (1.0 / math.sqrt(head_dim))).reshape(row_count, group_size, key_head.shape[0])


def update_stats(running, query_local, key_block, allowed, group_size, head_dim):
    running_max, totals = running
    row_count = query_local.shape[0]
    scores = block_scores(
        head_rows(query_local, group_size, head_dim), key_block, row_count, group_size, head_dim
    )
    masked = jnp.where(allowed[:, None, :], scores, NEG)
    new_max = jnp.maximum(running_max, jnp.max(masked, axis=2))
    weights = jnp.where(allowed[:, None, :], jnp.exp(masked - new_max[:, :, None]), 0.0)
    new_totals = [totals * jnp.exp(running_max - new_max) + jnp.sum(weights, axis=2)]
    new_maxima = [new_max]
    return (jnp.concatenate(new_maxima, axis=1), jnp.concatenate(new_totals, axis=1))


def backward_block(
    query_local,
    grad_local,
    log_norm,
    row_delta,
    key_block,
    value_block,
    allowed,
    group_size,
    head_dim,
):
    row_count = query_local.shape[0]
    query_flat = head_rows(query_local, group_size, head_dim)
    grad_flat = head_rows(grad_local, group_size, head_dim)
    scores = block_scores(query_flat, key_block, row_count, group_size, head_dim)
    masked = jnp.where(allowed[:, None, :], scores, NEG)
    weights = jnp.exp(masked - log_norm[:, 0:group_size, None])
    grad_weights = lax.dot_general(
        grad_flat, value_block, (((1,), (1,)), ((), ())), preferred_element_type=jnp.float32
    ).reshape(row_count, group_size, -1)
    grad_scores = weights * (grad_weights - row_delta[:, 0:group_size, None])
    rounded_weights = weights.astype(jnp.bfloat16).reshape(row_count * group_size, -1)
    rounded_grads = grad_scores.astype(jnp.bfloat16).reshape(row_count * group_size, -1)
    value_parts = [
        lax.dot_general(
            rounded_weights, grad_flat, (((0,), (0,)), ((), ())), preferred_element_type=jnp.float32
        )
    ]
    key_parts = [
        lax.dot_general(
            rounded_grads, query_flat, (((0,), (0,)), ((), ())), preferred_element_type=jnp.float32
        )
    ]
    query_parts = [
        jnp.dot(rounded_grads, key_block, preferred_element_type=jnp.float32).reshape(
            row_count, group_size * head_dim
        )
    ]
    return (
        jnp.concatenate(query_parts, axis=1),
        jnp.concatenate(key_parts, axis=1),
        jnp.concatenate(value_parts, axis=1),
    )


def ring_plan(doc_lengths, owners, queries, key_head_rows, value_head_rows, forward_out, grad_out):
    context_size = lax.axis_size("ctx")
    context_index = lax.axis_index("ctx")
    row_count = queries.shape[0]
    head_dim = HEAD_WIDTH
    group_size = GROUP
    query_heads = queries.shape[1] // head_dim
    slot_count = 2 * row_count // context_size
    everyone = lax.all_gather(owners, "ctx", axis=0, tiled=True)
    row_arrangement = jnp.argsort(everyone, stable=True)
    layout_docs = document_of(row_arrangement, doc_lengths)
    own_positions = lax.dynamic_slice_in_dim(
        row_arrangement, context_index * row_count, row_count, 0
    )
    own_documents = lax.dynamic_slice_in_dim(layout_docs, context_index * row_count, row_count, 0)
    owner_ids = jnp.arange(context_size, dtype=jnp.int32)
    owner_hot = (owners[:, None] == owner_ids[None, :]).astype(jnp.int32)
    earlier = jnp.cumsum(owner_hot, axis=0) - owner_hot
    rank_within = jnp.sum(earlier * owner_hot, axis=1)
    slot_rows = owners * slot_count + rank_within

    def packed(matrix):
        empty = jnp.zeros((context_size * slot_count,) + matrix.shape[1:], matrix.dtype)
        return empty.at[slot_rows].set(matrix)

    owner_grid = everyone.reshape(context_size, row_count)
    counts = jnp.sum((owner_grid == context_index).astype(jnp.int32), axis=1)
    count_ends = jnp.cumsum(counts)
    starts = count_ends - counts
    wanted = jnp.arange(row_count, dtype=jnp.int32)
    source = jnp.sum((wanted[:, None] >= count_ends[None, :]).astype(jnp.int32), axis=1)
    source_hot = (source[:, None] == owner_ids[None, :]).astype(jnp.int32)
    take_rows = source * slot_count + wanted - jnp.sum(source_hot * starts[None, :], axis=1)

    def compact(received):
        return jnp.take(received, take_rows, axis=0)

    local_delta = jnp.sum(
        (grad_out.astype(jnp.float32) * forward_out.astype(jnp.float32)).reshape(
            row_count, query_heads, head_dim
        ),
        axis=2,
    )
    arrived = (
        lax.all_to_all(packed(queries), "ctx", split_axis=0, concat_axis=0, tiled=True),
        lax.all_to_all(packed(key_head_rows), "ctx", split_axis=0, concat_axis=0, tiled=True),
        lax.all_to_all(packed(value_head_rows), "ctx", split_axis=0, concat_axis=0, tiled=True),
        lax.all_to_all(packed(grad_out), "ctx", split_axis=0, concat_axis=0, tiled=True),
    )
    query_local, key_local, value_local, grad_local = [compact(received) for received in arrived]
    row_delta = compact(
        lax.all_to_all(packed(local_delta), "ctx", split_axis=0, concat_axis=0, tiled=True)
    )

    def fold_keys(running, shard_rows, first_row):
        piece_count = shard_rows.shape[0]
        step_rows = math.gcd(piece_count, BLOCK) if piece_count > BLOCK else piece_count

        def one_block(partial_value, block_index):
            offset = first_row + block_index * step_rows
            key_block = lax.dynamic_slice_in_dim(shard_rows, block_index * step_rows, step_rows, 0)
            key_positions = lax.dynamic_slice_in_dim(row_arrangement, offset, step_rows, 0)
            key_docs = lax.dynamic_slice_in_dim(layout_docs, offset, step_rows, 0)
            allowed = allowed_between(own_positions, own_documents, key_positions, key_docs)
            return (
                update_stats(partial_value, query_local, key_block, allowed, group_size, head_dim),
                None,
            )

        if piece_count == step_rows:
            return one_block(running, 0)[0]
        return lax.scan(one_block, running, jnp.arange(piece_count // step_rows, dtype=jnp.int32))[
            0
        ]

    start_stats = (
        jnp.full((row_count, query_heads), NEG, jnp.float32),
        jnp.zeros((row_count, query_heads), jnp.float32),
    )
    top_scores, totals = fold_keys(
        start_stats, lax.all_gather(key_local, "ctx", axis=0, tiled=True), jnp.int32(0)
    )
    log_norm = top_scores + jnp.log(totals)

    def block_meta(owner_index, offset, size):
        first = owner_index * row_count + offset
        key_positions = lax.dynamic_slice_in_dim(row_arrangement, first, size, 0)
        key_docs = lax.dynamic_slice_in_dim(layout_docs, first, size, 0)
        return (key_positions, key_docs)

    query_zero = jnp.zeros(query_local.shape, jnp.float32)
    key_zero = jnp.zeros(key_local.shape, jnp.float32)

    def one_turn(turn_index, loop_state):
        key_moving, value_moving, key_grad, value_grad, query_grad = loop_state
        owner_index = (context_index - turn_index) % context_size
        key_positions, key_docs = block_meta(owner_index, 0, row_count)
        allowed = allowed_between(own_positions, own_documents, key_positions, key_docs)
        query_part, key_part, value_part = backward_block(
            query_local,
            grad_local,
            log_norm,
            row_delta,
            key_moving,
            value_moving,
            allowed,
            group_size,
            head_dim,
        )
        return (
            key_moving,
            value_moving,
            key_grad + key_part,
            value_grad + value_part,
            query_grad + query_part,
        )

    def moved_turn(turn_index, loop_state):
        key_moving, value_moving, key_grad, value_grad, query_grad = loop_state
        key_moving, value_moving = shifted((key_moving, value_moving), "ctx", 1)
        key_grad, value_grad = shifted((key_grad, value_grad), "ctx", 1)
        return one_turn(turn_index, (key_moving, value_moving, key_grad, value_grad, query_grad))

    loop_state = one_turn(0, (key_local, value_local, key_zero, key_zero, query_zero))
    loop_state = lax.fori_loop(1, context_size, moved_turn, loop_state)
    key_grad, value_grad = shifted((loop_state[2], loop_state[3]), "ctx", 1)
    query_grad = loop_state[4]
    inverse_root = 1.0 / math.sqrt(head_dim)
    return (query_grad * inverse_root, key_grad * inverse_root, value_grad)


META = 8


def contract(left, right, left_dim, right_dim, **kw):
    return lax.dot_general(
        left,
        right,
        (((left_dim,), (right_dim,)), ((), ())),
        preferred_element_type=jnp.float32,
        **kw,
    )


def one_hot(row_count, target):
    places = lax.broadcasted_iota(jnp.int32, (row_count, target.shape[1]), 0)
    return jnp.where(places == target, 1.0, 0.0).astype(jnp.bfloat16)


def side_by_side(stack, heads):
    rows = stack.shape[0] // heads
    return jnp.concatenate([stack[h * rows : (h + 1) * rows, :] for h in range(heads)], axis=1)


def end_to_end(matrix, heads):
    width = matrix.shape[1] // heads
    return jnp.concatenate([matrix[:, h * width : (h + 1) * width] for h in range(heads)], axis=0)


def runs_of(hot):
    count, rows = hot.shape
    counts = jnp.sum(hot, axis=1, keepdims=True)
    owner = jnp.zeros((1, rows), jnp.int32)
    earlier = jnp.zeros((1, rows), jnp.float32)
    for p in range(count):
        mine = hot[p : p + 1, :] > 0.0
        owner = jnp.where(mine, p, owner)
        for less in range(p):
            earlier = earlier + jnp.where(mine, counts[less : less + 1, :], 0.0)
    lane = lax.broadcasted_iota(jnp.int32, (1, rows), 1)
    return owner, counts, lane - earlier.astype(jnp.int32)


def own_kernel(
    count,
    docs,
    doc_ref,
    packet_ref,
    query_ref,
    grad_ref,
    saved_ref,
    query_out,
    grad_out,
    raised_out,
    change_out,
    row_out,
    spread_out,
    target_out,
    filled_out,
):
    rows, width = query_ref.shape
    depth = packet_ref.shape[1]
    heads = width // depth
    slot = 2 * rows // count
    index = lax.axis_index("ctx")
    lane = lax.broadcasted_iota(jnp.int32, (1, rows), 1)
    position = index * rows + lane
    earlier = lax.broadcasted_iota(jnp.int32, (docs, docs), 1) <= lax.broadcasted_iota(
        jnp.int32, (docs, docs), 0
    )
    lengths = doc_ref[...].astype(jnp.float32)
    ends = jnp.sum(jnp.where(earlier, lengths, 0.0), axis=1, keepdims=True).astype(jnp.int32)
    first = jnp.max(jnp.where(ends <= position, ends, 0), axis=0, keepdims=True)
    key_position = index * rows + lax.broadcasted_iota(jnp.int32, (rows, rows), 0)
    allowed = (key_position >= first) & (key_position <= position)
    allowed = jnp.concatenate([allowed] * heads, axis=1)

    queries = end_to_end(query_ref[...], heads)
    query_out[...] = queries
    scores = contract(packet_ref[0:rows, :], queries, 1, 1) * (1.0 / math.sqrt(depth))
    scores = jnp.where(allowed, scores, NEG)
    top = jnp.max(scores, axis=0, keepdims=True)
    raised = jnp.exp(scores - top)
    raised_out[...] = raised
    grads = end_to_end(grad_ref[...], heads)
    grad_out[...] = grads
    product = grads.astype(jnp.float32) * end_to_end(saved_ref[...], heads).astype(jnp.float32)
    delta = contract(
        jnp.ones((8, depth), jnp.float32), product, 1, 1, precision=lax.Precision.HIGHEST
    )[0:1, :]
    change_out[...] = contract(packet_ref[rows : 2 * rows, :], grads, 1, 1) - delta
    row_out[0:1, :] = delta
    row_out[1:2, :] = top
    row_out[2:3, :] = jnp.sum(raised, axis=0, keepdims=True)
    row_out[3:4, :] = jnp.concatenate([first.astype(jnp.float32)] * heads, axis=1)
    row_out[4:8, :] = jnp.ones((4, width), jnp.float32)
    owner, counts, rank = runs_of(packet_ref[2 * rows : 2 * rows + count, :].astype(jnp.float32))
    spread_out[...] = one_hot(count * slot, (owner ^ index) * slot + rank)
    target_out[...] = one_hot(count * rows, (owner ^ index) * rows + rank)
    filled_out[0:count, :] = jnp.broadcast_to(counts, (count, rows))
    filled_out[count:, :] = jnp.zeros((8 - count, rows), jnp.float32)


def fold(count, back, packet, queries, grads, row, filled):
    rows = packet.shape[1]
    index = lax.axis_index("ctx")
    delta, top, total = (row[n : n + 1, :] for n in range(3))
    first = row[3:4, :].astype(jnp.int32)
    position = (index - back) * rows + lax.broadcasted_iota(jnp.int32, (rows, row.shape[1]), 0)
    scores = contract(packet[0:rows, :], queries, 1, 1) * (1.0 / math.sqrt(queries.shape[1]))
    scores = jnp.where(position >= first, scores, NEG)
    new_top = jnp.maximum(top, jnp.max(scores, axis=0, keepdims=True))
    raised = jnp.exp(scores - new_top)
    shrink = jnp.exp(top - new_top)
    total = total * shrink + jnp.sum(raised, axis=0, keepdims=True)
    change = contract(packet[rows : 2 * rows, :], grads, 1, 1) - delta
    factors = row[4:8, :] * jnp.where(
        lax.broadcasted_iota(jnp.int32, (4, row.shape[1]), 0) < back, shrink, 1.0
    )
    owner, counts, rank = runs_of(packet[2 * rows : 2 * rows + count, :].astype(jnp.float32))
    base = jnp.zeros((1, rows), jnp.float32)
    for p in range(count):
        base = base + jnp.where(owner == p, filled[p : p + 1, :], 0.0)
    inside = index >= back
    target = jnp.where(inside, (owner ^ index) * rows + base.astype(jnp.int32) + rank, -1)
    filled = filled[0:count, :] + jnp.where(inside, counts, 0.0)
    return raised, change, (new_top, total, factors), one_hot(count * rows, target), filled


def step_kernel(count, back, *refs):
    query_ref, grad_ref, row_ref, filled_ref, packet_ref = refs[:5]
    raised_out, change_out, row_out, target_out, filled_out = refs[5:]
    raised, change, (top, total, factors), target, filled = fold(
        count, back, packet_ref, query_ref[...], grad_ref[...], row_ref, filled_ref
    )
    raised_out[...] = raised
    change_out[...] = change
    row_out[0:1, :] = row_ref[0:1, :]
    row_out[1:2, :] = top
    row_out[2:3, :] = total
    row_out[3:4, :] = row_ref[3:4, :]
    row_out[4:8, :] = factors
    target_out[...] = target
    filled_out[0:count, :] = filled
    filled_out[count:, :] = jnp.zeros_like(filled_out[count:, :])


def attend_kernel(count, halo, *refs):
    index = lax.axis_index("ctx")
    for blocks in range(1, halo + 2):
        here = index == blocks - 1 if blocks <= halo else index >= halo

        @pl.when(here)
        def _(blocks=blocks):
            attend(count, halo, blocks, refs)


def attend(count, halo, blocks, refs):
    query_ref, grad_ref, row_ref, filled_ref, spread_ref = refs[:5]
    raised_refs = refs[5 : 5 + halo]
    change_refs = refs[5 + halo : 5 + 2 * halo]
    target_refs = refs[5 + 2 * halo : 5 + 3 * halo]
    packets = refs[5 + 3 * halo : 6 + 4 * halo]
    outs = refs[6 + 4 * halo :]
    rows = packets[0].shape[1]
    depth = query_ref.shape[1]
    heads = query_ref.shape[0] // rows
    slot = 2 * rows // count
    scale = 1.0 / math.sqrt(depth)
    queries = query_ref[...]
    grads = grad_ref[...]
    raised = [ref[...] for ref in raised_refs[:blocks]]
    change = [ref[...] for ref in change_refs[:blocks]]
    targets = [ref[...] for ref in target_refs[:blocks]]
    total = row_ref[2:3, :]
    factors = row_ref[4:8, :]
    if blocks > halo:
        raised_far, change_far, (_, total, factors), target_far, _ = fold(
            count, halo, packets[halo], queries, grads, row_ref, filled_ref
        )
        raised.append(raised_far)
        change.append(change_far)
        targets.append(target_far)
    factors = factors * (1.0 / total)
    weights = [raised[n] * factors[n : n + 1, :] for n in range(blocks)]
    changes = [weights[n] * change[n] for n in range(blocks)]
    weights = jnp.concatenate([part.astype(jnp.bfloat16) for part in weights], axis=0)
    changes = jnp.concatenate([part.astype(jnp.bfloat16) for part in changes], axis=0)
    keys = jnp.concatenate([packet[0:rows, :] for packet in packets[:blocks]], axis=0)
    query_grad = (contract(keys, changes, 0, 0) * scale).astype(jnp.bfloat16)
    key_parts = contract(changes, queries, 1, 0) * scale
    value_parts = contract(weights, grads, 1, 0)
    parts = jnp.concatenate([key_parts, value_parts], axis=1).astype(jnp.bfloat16)

    query_slots = contract(spread_ref[...], end_to_end(query_grad, heads), 1, 1)
    query_slots = query_slots.astype(jnp.bfloat16)
    part_slots = contract(jnp.concatenate(targets, axis=1), parts, 1, 0).astype(jnp.bfloat16)
    at = heads * slot
    for k in range(count):
        out = outs[k]
        for h in range(heads):
            out[h * slot : (h + 1) * slot, :] = query_slots[
                k * slot : (k + 1) * slot, h * depth : (h + 1) * depth
            ]
        for n in range(2):
            out[at + n * rows : at + (n + 1) * rows, :] = part_slots[
                k * rows : (k + 1) * rows, n * depth : (n + 1) * depth
            ]


def slots_of(refs, first, size, pieces):
    return jnp.concatenate(
        [
            jnp.concatenate(
                [ref[first + n * size : first + (n + 1) * size, :] for n in range(pieces)], axis=1
            )
            for ref in refs
        ],
        axis=0,
    )


def order_kernel(count, halo, early, late, *refs):
    ins, packets = refs[: len(early)], refs[len(early) : len(early) + 1 + halo]
    query_out, key_out, query_base, key_base = refs[-4:]
    rows, width = query_base.shape
    depth = ins[0].shape[1]
    heads = width // depth
    slot = 2 * rows // count
    index = lax.axis_index("ctx")
    given = []
    for ref in packets:
        hot = ref[2 * rows : 2 * rows + count, :].astype(jnp.float32)
        counts = jnp.sum(hot, axis=1, keepdims=True)
        mine = jnp.zeros((1, 1), jnp.float32)
        for p in range(count):
            mine = jnp.where(index == p, counts[p : p + 1, :], mine)
        given.append(mine.astype(jnp.int32))
    if len(given) < count:
        given.append(rows - sum(given))
    giver = [lax.rem(index - d + count, count) for d in range(count)]

    def placement(size, halo, exchanges):
        lane = lax.broadcasted_iota(jnp.int32, (1, len(exchanges) * size), 1)
        target = jnp.full(lane.shape, -1, jnp.int32)
        for n, k in enumerate(exchanges):
            step = lane - n * size
            for back in range(halo + 1):
                block = (index ^ k) - back
                start = jnp.zeros((1, 1), jnp.int32)
                length = jnp.zeros((1, 1), jnp.int32)
                for d in range(count):
                    start = start + jnp.where(giver[d] < block, given[d], 0)
                    length = length + jnp.where(giver[d] == block, given[d], 0)
                target = jnp.where((step >= 0) & (step < length), start + step, target)
                step = step - length
        return one_hot(rows, target)

    query_out[...] = placement(slot, 0, late)
    key_out[...] = placement(rows, halo, late)
    query_base[...] = contract(placement(slot, 0, early), slots_of(ins, 0, slot, heads), 1, 0)
    key_base[...] = contract(
        placement(rows, halo, early), slots_of(ins, heads * slot, rows, 2), 1, 0
    )


def place_kernel(count, query_spread, key_spread, query_base, key_base, *refs):
    ins = refs[:-7]
    query_out, key_out, value_out, query_here, key_here, value_here, sems = refs[-7:]
    rows, width = query_here.shape
    depth = key_here.shape[1]
    heads = width // depth
    slot = 2 * rows // count
    copies = []

    def leave(here, out):
        copies.append(pltpu.make_async_copy(here, out, sems.at[len(copies)]))
        copies[-1].start()

    query_here[...] = query_base[...] + contract(
        query_spread[...], slots_of(ins, 0, slot, heads), 1, 0
    )
    leave(query_here, query_out)
    both = key_base[...] + contract(
        key_spread[...], slots_of(ins, heads * slot, rows, 2), 1, 0
    )
    for n, (here, out) in enumerate(((key_here, key_out), (value_here, value_out))):
        here[...] = both[:, n * depth : (n + 1) * depth]
        leave(here, out)
    for copy in copies:
        copy.wait()


def near_plan(doc_lengths, owners, queries, key_head_rows, value_head_rows, forward_out, grad_out):
    count = lax.axis_size("ctx")
    rows, width = queries.shape
    depth = key_head_rows.shape[1]
    heads = width // depth
    bf16, f32 = jnp.bfloat16, jnp.float32
    columns = heads * rows
    halo = count // 2
    slot = 2 * rows // count
    whole = pl.BlockSpec(memory_space=pltpu.VMEM)
    params = pltpu.CompilerParams(vmem_limit_bytes=40 * 1024 * 1024)

    mark = lax.broadcasted_iota(jnp.int32, (2 * rows + META, rows), 0) - 2 * rows
    packet = jnp.where(
        mark < 0,
        jnp.pad(jnp.concatenate([key_head_rows, value_head_rows], axis=0), ((0, META), (0, 0))),
        (owners[None, :] == mark).astype(bf16),
    )
    near = [
        lax.ppermute(packet, "ctx", [(i, (i + back) % count) for i in range(count)])
        for back in range(1, halo + 1)
    ]
    block_shapes = [jax.ShapeDtypeStruct((rows, columns), f32)] * 2
    row_shape = jax.ShapeDtypeStruct((8, columns), f32)
    target_shape = jax.ShapeDtypeStruct((count * rows, rows), bf16)
    filled_shape = jax.ShapeDtypeStruct((8, rows), f32)
    query_rows, grad_rows, raised, change, row, spread, target, filled = pl.pallas_call(
        functools.partial(own_kernel, count, doc_lengths.shape[0]),
        out_shape=[jax.ShapeDtypeStruct((columns, depth), bf16)] * 2
        + block_shapes
        + [row_shape, jax.ShapeDtypeStruct((count * slot, rows), bf16), target_shape, filled_shape],
        in_specs=[whole] * 5,
        out_specs=[whole] * 8,
        compiler_params=params,
    )(doc_lengths.reshape(1, -1), packet, queries, grad_out, forward_out)
    raised, change, target = [raised], [change], [target]
    for back in range(1, halo):
        found = pl.pallas_call(
            functools.partial(step_kernel, count, back),
            out_shape=block_shapes + [row_shape, target_shape, filled_shape],
            in_specs=[whole] * 5,
            out_specs=[whole] * 5,
            compiler_params=params,
        )(query_rows, grad_rows, row, filled, near[back - 1])
        raised.append(found[0])
        change.append(found[1])
        row = found[2]
        target.append(found[3])
        filled = found[4]
    sent = pl.pallas_call(
        functools.partial(attend_kernel, count, halo),
        out_shape=[jax.ShapeDtypeStruct((heads * slot + 2 * rows, depth), bf16)] * count,
        in_specs=[whole] * (6 + 4 * halo),
        out_specs=[whole] * count,
        compiler_params=params,
    )(query_rows, grad_rows, row, filled, spread, *raised, *change, *target, packet, *near)
    received = [sent[0]] + [
        lax.ppermute(sent[k], "ctx", [(i, i ^ k) for i in range(count)]) for k in range(1, count)
    ]
    early = (0, 3) if count == 4 else (0,)
    late = tuple(k for k in range(count) if k not in early)
    placed = pl.pallas_call(
        functools.partial(order_kernel, count, halo, early, late),
        out_shape=[
            jax.ShapeDtypeStruct((rows, len(late) * slot), bf16),
            jax.ShapeDtypeStruct((rows, len(late) * rows), bf16),
            jax.ShapeDtypeStruct((rows, width), f32),
            jax.ShapeDtypeStruct((rows, 2 * depth), f32),
        ],
        in_specs=[whole] * (len(early) + 1 + halo),
        out_specs=[whole] * 4,
        compiler_params=params,
    )(*[received[k] for k in early], packet, *near)
    return pl.pallas_call(
        functools.partial(place_kernel, count),
        out_shape=[
            jax.ShapeDtypeStruct((rows, width), f32),
            jax.ShapeDtypeStruct((rows, depth), f32),
            jax.ShapeDtypeStruct((rows, depth), f32),
        ],
        in_specs=[whole] * (4 + len(late)),
        out_specs=[pl.BlockSpec(memory_space=pl.ANY)] * 3,
        scratch_shapes=[
            pltpu.VMEM((rows, width), f32),
            pltpu.VMEM((rows, depth), f32),
            pltpu.VMEM((rows, depth), f32),
            pltpu.SemaphoreType.DMA((3,)),
        ],
        compiler_params=params,
    )(*placed, *[received[k] for k in late])


def per_device(*args):
    if lax.axis_size("ctx") in (2, 4):
        return near_plan(*args)
    return ring_plan(*args)


def solution(mesh):
    return jax.shard_map(
        per_device,
        mesh=mesh,
        in_specs=(
            P("groups"),
            P(("groups", "ctx")),
            P(("groups", "ctx"), "head"),
            P(("groups", "ctx"), "head"),
            P(("groups", "ctx"), "head"),
            P(("groups", "ctx"), "head"),
            P(("groups", "ctx"), "head"),
        ),
        out_specs=(
            P(("groups", "ctx"), "head"),
            P(("groups", "ctx"), "head"),
            P(("groups", "ctx"), "head"),
        ),
        check_vma=False,
    )
```

```python
import functools
import math

import jax
import jax.numpy as jnp
from jax import lax
from jax.experimental import pallas as pl
from jax.experimental.pallas import tpu as pltpu
from jax.sharding import PartitionSpec as P

HEAD_WIDTH = 128
GROUP = 4


NEG = -1e30
BLOCK = 512


def shifted(value, axis, by):
    count = lax.axis_size(axis)
    return lax.ppermute(value, axis, [(i, (i + by) % count) for i in range(count)])


def document_of(positions, doc_lengths):
    ends = jnp.cumsum(doc_lengths)
    return jnp.sum((positions[:, None] >= ends[None, :]).astype(jnp.int32), axis=1)


def allowed_between(query_positions, query_docs, key_positions, key_docs):
    return (query_docs[:, None] == key_docs[None, :]) & (
        key_positions[None, :] <= query_positions[:, None]
    )


def head_rows(matrix, group_size, head_dim):
    row_count = matrix.shape[0]
    return matrix.reshape(row_count * group_size, head_dim)


def block_scores(query_flat, key_head, row_count, group_size, head_dim):
    scores = lax.dot_general(
        query_flat, key_head, (((1,), (1,)), ((), ())), preferred_element_type=jnp.float32
    )
    return (scores * (1.0 / math.sqrt(head_dim))).reshape(row_count, group_size, key_head.shape[0])


def update_stats(running, query_local, key_block, allowed, group_size, head_dim):
    running_max, totals = running
    row_count = query_local.shape[0]
    scores = block_scores(
        head_rows(query_local, group_size, head_dim), key_block, row_count, group_size, head_dim
    )
    masked = jnp.where(allowed[:, None, :], scores, NEG)
    new_max = jnp.maximum(running_max, jnp.max(masked, axis=2))
    weights = jnp.where(allowed[:, None, :], jnp.exp(masked - new_max[:, :, None]), 0.0)
    new_totals = [totals * jnp.exp(running_max - new_max) + jnp.sum(weights, axis=2)]
    new_maxima = [new_max]
    return (jnp.concatenate(new_maxima, axis=1), jnp.concatenate(new_totals, axis=1))


def backward_block(
    query_local,
    grad_local,
    log_norm,
    row_delta,
    key_block,
    value_block,
    allowed,
    group_size,
    head_dim,
):
    row_count = query_local.shape[0]
    query_flat = head_rows(query_local, group_size, head_dim)
    grad_flat = head_rows(grad_local, group_size, head_dim)
    scores = block_scores(query_flat, key_block, row_count, group_size, head_dim)
    masked = jnp.where(allowed[:, None, :], scores, NEG)
    weights = jnp.exp(masked - log_norm[:, 0:group_size, None])
    grad_weights = lax.dot_general(
        grad_flat, value_block, (((1,), (1,)), ((), ())), preferred_element_type=jnp.float32
    ).reshape(row_count, group_size, -1)
    grad_scores = weights * (grad_weights - row_delta[:, 0:group_size, None])
    rounded_weights = weights.astype(jnp.bfloat16).reshape(row_count * group_size, -1)
    rounded_grads = grad_scores.astype(jnp.bfloat16).reshape(row_count * group_size, -1)
    value_parts = [
        lax.dot_general(
            rounded_weights, grad_flat, (((0,), (0,)), ((), ())), preferred_element_type=jnp.float32
        )
    ]
    key_parts = [
        lax.dot_general(
            rounded_grads, query_flat, (((0,), (0,)), ((), ())), preferred_element_type=jnp.float32
        )
    ]
    query_parts = [
        jnp.dot(rounded_grads, key_block, preferred_element_type=jnp.float32).reshape(
            row_count, group_size * head_dim
        )
    ]
    return (
        jnp.concatenate(query_parts, axis=1),
        jnp.concatenate(key_parts, axis=1),
        jnp.concatenate(value_parts, axis=1),
    )


def ring_plan(doc_lengths, owners, queries, key_head_rows, value_head_rows, forward_out, grad_out):
    context_size = lax.axis_size("ctx")
    context_index = lax.axis_index("ctx")
    row_count = queries.shape[0]
    head_dim = HEAD_WIDTH
    group_size = GROUP
    query_heads = queries.shape[1] // head_dim
    slot_count = 2 * row_count // context_size
    everyone = lax.all_gather(owners, "ctx", axis=0, tiled=True)
    row_arrangement = jnp.argsort(everyone, stable=True)
    layout_docs = document_of(row_arrangement, doc_lengths)
    own_positions = lax.dynamic_slice_in_dim(
        row_arrangement, context_index * row_count, row_count, 0
    )
    own_documents = lax.dynamic_slice_in_dim(layout_docs, context_index * row_count, row_count, 0)
    owner_ids = jnp.arange(context_size, dtype=jnp.int32)
    owner_hot = (owners[:, None] == owner_ids[None, :]).astype(jnp.int32)
    earlier = jnp.cumsum(owner_hot, axis=0) - owner_hot
    rank_within = jnp.sum(earlier * owner_hot, axis=1)
    slot_rows = owners * slot_count + rank_within

    def packed(matrix):
        empty = jnp.zeros((context_size * slot_count,) + matrix.shape[1:], matrix.dtype)
        return empty.at[slot_rows].set(matrix)

    owner_grid = everyone.reshape(context_size, row_count)
    counts = jnp.sum((owner_grid == context_index).astype(jnp.int32), axis=1)
    count_ends = jnp.cumsum(counts)
    starts = count_ends - counts
    wanted = jnp.arange(row_count, dtype=jnp.int32)
    source = jnp.sum((wanted[:, None] >= count_ends[None, :]).astype(jnp.int32), axis=1)
    source_hot = (source[:, None] == owner_ids[None, :]).astype(jnp.int32)
    take_rows = source * slot_count + wanted - jnp.sum(source_hot * starts[None, :], axis=1)

    def compact(received):
        return jnp.take(received, take_rows, axis=0)

    local_delta = jnp.sum(
        (grad_out.astype(jnp.float32) * forward_out.astype(jnp.float32)).reshape(
            row_count, query_heads, head_dim
        ),
        axis=2,
    )
    arrived = (
        lax.all_to_all(packed(queries), "ctx", split_axis=0, concat_axis=0, tiled=True),
        lax.all_to_all(packed(key_head_rows), "ctx", split_axis=0, concat_axis=0, tiled=True),
        lax.all_to_all(packed(value_head_rows), "ctx", split_axis=0, concat_axis=0, tiled=True),
        lax.all_to_all(packed(grad_out), "ctx", split_axis=0, concat_axis=0, tiled=True),
    )
    query_local, key_local, value_local, grad_local = [compact(received) for received in arrived]
    row_delta = compact(
        lax.all_to_all(packed(local_delta), "ctx", split_axis=0, concat_axis=0, tiled=True)
    )

    def fold_keys(running, shard_rows, first_row):
        piece_count = shard_rows.shape[0]
        step_rows = math.gcd(piece_count, BLOCK) if piece_count > BLOCK else piece_count

        def one_block(partial_value, block_index):
            offset = first_row + block_index * step_rows
            key_block = lax.dynamic_slice_in_dim(shard_rows, block_index * step_rows, step_rows, 0)
            key_positions = lax.dynamic_slice_in_dim(row_arrangement, offset, step_rows, 0)
            key_docs = lax.dynamic_slice_in_dim(layout_docs, offset, step_rows, 0)
            allowed = allowed_between(own_positions, own_documents, key_positions, key_docs)
            return (
                update_stats(partial_value, query_local, key_block, allowed, group_size, head_dim),
                None,
            )

        if piece_count == step_rows:
            return one_block(running, 0)[0]
        return lax.scan(one_block, running, jnp.arange(piece_count // step_rows, dtype=jnp.int32))[
            0
        ]

    start_stats = (
        jnp.full((row_count, query_heads), NEG, jnp.float32),
        jnp.zeros((row_count, query_heads), jnp.float32),
    )
    top_scores, totals = fold_keys(
        start_stats, lax.all_gather(key_local, "ctx", axis=0, tiled=True), jnp.int32(0)
    )
    log_norm = top_scores + jnp.log(totals)

    def block_meta(owner_index, offset, size):
        first = owner_index * row_count + offset
        key_positions = lax.dynamic_slice_in_dim(row_arrangement, first, size, 0)
        key_docs = lax.dynamic_slice_in_dim(layout_docs, first, size, 0)
        return (key_positions, key_docs)

    query_zero = jnp.zeros(query_local.shape, jnp.float32)
    key_zero = jnp.zeros(key_local.shape, jnp.float32)

    def one_turn(turn_index, loop_state):
        key_moving, value_moving, key_grad, value_grad, query_grad = loop_state
        owner_index = (context_index - turn_index) % context_size
        key_positions, key_docs = block_meta(owner_index, 0, row_count)
        allowed = allowed_between(own_positions, own_documents, key_positions, key_docs)
        query_part, key_part, value_part = backward_block(
            query_local,
            grad_local,
            log_norm,
            row_delta,
            key_moving,
            value_moving,
            allowed,
            group_size,
            head_dim,
        )
        return (
            key_moving,
            value_moving,
            key_grad + key_part,
            value_grad + value_part,
            query_grad + query_part,
        )

    def moved_turn(turn_index, loop_state):
        key_moving, value_moving, key_grad, value_grad, query_grad = loop_state
        key_moving, value_moving = shifted((key_moving, value_moving), "ctx", 1)
        key_grad, value_grad = shifted((key_grad, value_grad), "ctx", 1)
        return one_turn(turn_index, (key_moving, value_moving, key_grad, value_grad, query_grad))

    loop_state = one_turn(0, (key_local, value_local, key_zero, key_zero, query_zero))
    loop_state = lax.fori_loop(1, context_size, moved_turn, loop_state)
    key_grad, value_grad = shifted((loop_state[2], loop_state[3]), "ctx", 1)
    query_grad = loop_state[4]
    inverse_root = 1.0 / math.sqrt(head_dim)
    return (query_grad * inverse_root, key_grad * inverse_root, value_grad)


META = 8


def contract(left, right, left_dim, right_dim, **kw):
    return lax.dot_general(
        left,
        right,
        (((left_dim,), (right_dim,)), ((), ())),
        preferred_element_type=jnp.float32,
        **kw,
    )


def one_hot(row_count, target):
    places = lax.broadcasted_iota(jnp.int32, (row_count, target.shape[1]), 0)
    return jnp.where(places == target, 1.0, 0.0).astype(jnp.bfloat16)


def side_by_side(stack, heads):
    rows = stack.shape[0] // heads
    return jnp.concatenate([stack[h * rows : (h + 1) * rows, :] for h in range(heads)], axis=1)


def end_to_end(matrix, heads):
    width = matrix.shape[1] // heads
    return jnp.concatenate([matrix[:, h * width : (h + 1) * width] for h in range(heads)], axis=0)


def runs_of(hot):
    count, rows = hot.shape
    counts = jnp.sum(hot, axis=1, keepdims=True)
    owner = jnp.zeros((1, rows), jnp.int32)
    earlier = jnp.zeros((1, rows), jnp.float32)
    for p in range(count):
        mine = hot[p : p + 1, :] > 0.0
        owner = jnp.where(mine, p, owner)
        for less in range(p):
            earlier = earlier + jnp.where(mine, counts[less : less + 1, :], 0.0)
    lane = lax.broadcasted_iota(jnp.int32, (1, rows), 1)
    return owner, counts, lane - earlier.astype(jnp.int32)


def own_kernel(
    count,
    docs,
    doc_ref,
    packet_ref,
    query_ref,
    grad_ref,
    saved_ref,
    query_out,
    grad_out,
    raised_out,
    change_out,
    row_out,
    spread_out,
    target_out,
    filled_out,
):
    rows, width = query_ref.shape
    depth = packet_ref.shape[1]
    heads = width // depth
    slot = 2 * rows // count
    index = lax.axis_index("ctx")
    lane = lax.broadcasted_iota(jnp.int32, (1, rows), 1)
    position = index * rows + lane
    earlier = lax.broadcasted_iota(jnp.int32, (docs, docs), 1) <= lax.broadcasted_iota(
        jnp.int32, (docs, docs), 0
    )
    lengths = doc_ref[...].astype(jnp.float32)
    ends = jnp.sum(jnp.where(earlier, lengths, 0.0), axis=1, keepdims=True).astype(jnp.int32)
    first = jnp.max(jnp.where(ends <= position, ends, 0), axis=0, keepdims=True)
    key_position = index * rows + lax.broadcasted_iota(jnp.int32, (rows, rows), 0)
    allowed = (key_position >= first) & (key_position <= position)
    allowed = jnp.concatenate([allowed] * heads, axis=1)

    queries = end_to_end(query_ref[...], heads)
    query_out[...] = queries
    scores = contract(packet_ref[0:rows, :], queries, 1, 1) * (1.0 / math.sqrt(depth))
    scores = jnp.where(allowed, scores, NEG)
    top = jnp.max(scores, axis=0, keepdims=True)
    raised = jnp.exp(scores - top)
    raised_out[...] = raised
    grads = end_to_end(grad_ref[...], heads)
    grad_out[...] = grads
    product = grads.astype(jnp.float32) * end_to_end(saved_ref[...], heads).astype(jnp.float32)
    delta = contract(
        jnp.ones((8, depth), jnp.float32), product, 1, 1, precision=lax.Precision.HIGHEST
    )[0:1, :]
    change_out[...] = contract(packet_ref[rows : 2 * rows, :], grads, 1, 1) - delta
    row_out[0:1, :] = delta
    row_out[1:2, :] = top
    row_out[2:3, :] = jnp.sum(raised, axis=0, keepdims=True)
    row_out[3:4, :] = jnp.concatenate([first.astype(jnp.float32)] * heads, axis=1)
    row_out[4:8, :] = jnp.ones((4, width), jnp.float32)
    owner, counts, rank = runs_of(packet_ref[2 * rows : 2 * rows + count, :].astype(jnp.float32))
    spread_out[...] = one_hot(count * slot, (owner ^ index) * slot + rank)
    target_out[...] = one_hot(count * rows, (owner ^ index) * rows + rank)
    filled_out[0:count, :] = jnp.broadcast_to(counts, (count, rows))
    filled_out[count:, :] = jnp.zeros((8 - count, rows), jnp.float32)


def fold(count, back, packet, queries, grads, row, filled):
    rows = packet.shape[1]
    index = lax.axis_index("ctx")
    delta, top, total = (row[n : n + 1, :] for n in range(3))
    first = row[3:4, :].astype(jnp.int32)
    position = (index - back) * rows + lax.broadcasted_iota(jnp.int32, (rows, row.shape[1]), 0)
    scores = contract(packet[0:rows, :], queries, 1, 1) * (1.0 / math.sqrt(queries.shape[1]))
    scores = jnp.where(position >= first, scores, NEG)
    new_top = jnp.maximum(top, jnp.max(scores, axis=0, keepdims=True))
    raised = jnp.exp(scores - new_top)
    shrink = jnp.exp(top - new_top)
    total = total * shrink + jnp.sum(raised, axis=0, keepdims=True)
    change = contract(packet[rows : 2 * rows, :], grads, 1, 1) - delta
    factors = row[4:8, :] * jnp.where(
        lax.broadcasted_iota(jnp.int32, (4, row.shape[1]), 0) < back, shrink, 1.0
    )
    owner, counts, rank = runs_of(packet[2 * rows : 2 * rows + count, :].astype(jnp.float32))
    base = jnp.zeros((1, rows), jnp.float32)
    for p in range(count):
        base = base + jnp.where(owner == p, filled[p : p + 1, :], 0.0)
    inside = index >= back
    target = jnp.where(inside, (owner ^ index) * rows + base.astype(jnp.int32) + rank, -1)
    filled = filled[0:count, :] + jnp.where(inside, counts, 0.0)
    return raised, change, (new_top, total, factors), one_hot(count * rows, target), filled


def step_kernel(count, halo, back, *refs):
    query_ref, grad_ref, row_ref, filled_ref, spread_ref = refs[:5]
    raised_refs = refs[5 : 5 + back]
    change_refs = refs[5 + back : 5 + 2 * back]
    target_refs = refs[5 + 2 * back : 5 + 3 * back]
    packets = refs[5 + 3 * back : 6 + 4 * back]
    raised_out, change_out, row_out, target_out, filled_out = refs[6 + 4 * back : 11 + 4 * back]
    outs = refs[11 + 4 * back :]
    raised, change, (top, total, factors), target, filled = fold(
        count, back, packets[back], query_ref[...], grad_ref[...], row_ref, filled_ref
    )
    raised_out[...] = raised
    change_out[...] = change
    row_out[0:1, :] = row_ref[0:1, :]
    row_out[1:2, :] = top
    row_out[2:3, :] = total
    row_out[3:4, :] = row_ref[3:4, :]
    row_out[4:8, :] = factors
    target_out[...] = target
    filled_out[0:count, :] = filled
    filled_out[count:, :] = jnp.zeros_like(filled_out[count:, :])
    if outs:
        attend_first(
            count,
            halo,
            (query_ref, grad_ref, row_out, filled_out, spread_ref)
            + (*raised_refs, raised_out, *change_refs, change_out, *target_refs, target_out)
            + (*packets, None, *outs),
        )


def attend_first(count, halo, refs):
    for blocks in range(1, halo + 1):

        @pl.when(lax.axis_index("ctx") == blocks - 1)
        def _(blocks=blocks):
            attend(count, halo, blocks, refs)


def attend_kernel(count, halo, *refs):
    ready, refs = refs[: count * (halo > 1)], refs[count * (halo > 1) :]
    held = lax.axis_index("ctx") >= halo

    @pl.when(held)
    def _():
        attend(count, halo, halo + 1, refs)

    if not ready:
        return attend_first(count, halo, refs)

    @pl.when(jnp.logical_not(held))
    def _():
        for here, out in zip(ready, refs[-count:], strict=True):
            out[...] = here[...]


def attend(count, halo, blocks, refs):
    query_ref, grad_ref, row_ref, filled_ref, spread_ref = refs[:5]
    raised_refs = refs[5 : 5 + halo]
    change_refs = refs[5 + halo : 5 + 2 * halo]
    target_refs = refs[5 + 2 * halo : 5 + 3 * halo]
    packets = refs[5 + 3 * halo : 6 + 4 * halo]
    outs = refs[6 + 4 * halo :]
    rows = packets[0].shape[1]
    depth = query_ref.shape[1]
    heads = query_ref.shape[0] // rows
    slot = 2 * rows // count
    scale = 1.0 / math.sqrt(depth)
    queries = query_ref[...]
    grads = grad_ref[...]
    raised = [ref[...] for ref in raised_refs[:blocks]]
    change = [ref[...] for ref in change_refs[:blocks]]
    targets = [ref[...] for ref in target_refs[:blocks]]
    total = row_ref[2:3, :]
    factors = row_ref[4:8, :]
    if blocks > halo:
        raised_far, change_far, (_, total, factors), target_far, _ = fold(
            count, halo, packets[halo], queries, grads, row_ref, filled_ref
        )
        raised.append(raised_far)
        change.append(change_far)
        targets.append(target_far)
    factors = factors * (1.0 / total)
    weights = [raised[n] * factors[n : n + 1, :] for n in range(blocks)]
    changes = [weights[n] * change[n] for n in range(blocks)]
    weights = jnp.concatenate([part.astype(jnp.bfloat16) for part in weights], axis=0)
    changes = jnp.concatenate([part.astype(jnp.bfloat16) for part in changes], axis=0)
    keys = jnp.concatenate([packet[0:rows, :] for packet in packets[:blocks]], axis=0)
    query_grad = (contract(keys, changes, 0, 0) * scale).astype(jnp.bfloat16)
    key_parts = contract(changes, queries, 1, 0) * scale
    value_parts = contract(weights, grads, 1, 0)
    parts = jnp.concatenate([key_parts, value_parts], axis=1).astype(jnp.bfloat16)

    query_slots = contract(spread_ref[...], end_to_end(query_grad, heads), 1, 1)
    query_slots = query_slots.astype(jnp.bfloat16)
    part_slots = contract(jnp.concatenate(targets, axis=1), parts, 1, 0).astype(jnp.bfloat16)
    at = heads * slot
    for k in range(count):
        out = outs[k]
        for h in range(heads):
            out[h * slot : (h + 1) * slot, :] = query_slots[
                k * slot : (k + 1) * slot, h * depth : (h + 1) * depth
            ]
        for n in range(2):
            out[at + n * rows : at + (n + 1) * rows, :] = part_slots[
                k * rows : (k + 1) * rows, n * depth : (n + 1) * depth
            ]


def slots_of(refs, first, size, pieces):
    return jnp.concatenate(
        [
            jnp.concatenate(
                [ref[first + n * size : first + (n + 1) * size, :] for n in range(pieces)], axis=1
            )
            for ref in refs
        ],
        axis=0,
    )


def order_kernel(count, halo, early, late, *refs):
    ins, packets = refs[: len(early)], refs[len(early) : len(early) + 1 + halo]
    query_out, key_out, query_base, key_base = refs[-4:]
    rows, width = query_base.shape
    depth = ins[0].shape[1]
    heads = width // depth
    slot = 2 * rows // count
    index = lax.axis_index("ctx")
    given = []
    for ref in packets:
        hot = ref[2 * rows : 2 * rows + count, :].astype(jnp.float32)
        counts = jnp.sum(hot, axis=1, keepdims=True)
        mine = jnp.zeros((1, 1), jnp.float32)
        for p in range(count):
            mine = jnp.where(index == p, counts[p : p + 1, :], mine)
        given.append(mine.astype(jnp.int32))
    if len(given) < count:
        given.append(rows - sum(given))
    giver = [lax.rem(index - d + count, count) for d in range(count)]

    def placement(size, halo, exchanges):
        lane = lax.broadcasted_iota(jnp.int32, (1, len(exchanges) * size), 1)
        target = jnp.full(lane.shape, -1, jnp.int32)
        for n, k in enumerate(exchanges):
            step = lane - n * size
            for back in range(halo + 1):
                block = (index ^ k) - back
                start = jnp.zeros((1, 1), jnp.int32)
                length = jnp.zeros((1, 1), jnp.int32)
                for d in range(count):
                    start = start + jnp.where(giver[d] < block, given[d], 0)
                    length = length + jnp.where(giver[d] == block, given[d], 0)
                target = jnp.where((step >= 0) & (step < length), start + step, target)
                step = step - length
        return one_hot(rows, target)

    query_out[...] = placement(slot, 0, late)
    key_out[...] = placement(rows, halo, late)
    query_base[...] = contract(placement(slot, 0, early), slots_of(ins, 0, slot, heads), 1, 0)
    key_base[...] = contract(
        placement(rows, halo, early), slots_of(ins, heads * slot, rows, 2), 1, 0
    )


def place_kernel(count, query_spread, key_spread, query_base, key_base, *refs):
    ins = refs[:-7]
    query_out, key_out, value_out, query_here, key_here, value_here, sems = refs[-7:]
    rows, width = query_here.shape
    depth = key_here.shape[1]
    heads = width // depth
    slot = 2 * rows // count
    copies = []

    def leave(here, out):
        copies.append(pltpu.make_async_copy(here, out, sems.at[len(copies)]))
        copies[-1].start()

    query_here[...] = query_base[...] + contract(
        query_spread[...], slots_of(ins, 0, slot, heads), 1, 0
    )
    leave(query_here, query_out)
    both = key_base[...] + contract(
        key_spread[...], slots_of(ins, heads * slot, rows, 2), 1, 0
    )
    for n, (here, out) in enumerate(((key_here, key_out), (value_here, value_out))):
        here[...] = both[:, n * depth : (n + 1) * depth]
        leave(here, out)
    for copy in copies:
        copy.wait()


def near_plan(doc_lengths, owners, queries, key_head_rows, value_head_rows, forward_out, grad_out):
    count = lax.axis_size("ctx")
    rows, width = queries.shape
    depth = key_head_rows.shape[1]
    heads = width // depth
    bf16, f32 = jnp.bfloat16, jnp.float32
    columns = heads * rows
    halo = count // 2
    slot = 2 * rows // count
    whole = pl.BlockSpec(memory_space=pltpu.VMEM)
    params = pltpu.CompilerParams(vmem_limit_bytes=40 * 1024 * 1024)

    mark = lax.broadcasted_iota(jnp.int32, (2 * rows + META, rows), 0) - 2 * rows
    packet = jnp.where(
        mark < 0,
        jnp.pad(jnp.concatenate([key_head_rows, value_head_rows], axis=0), ((0, META), (0, 0))),
        (owners[None, :] == mark).astype(bf16),
    )
    near = [
        lax.ppermute(packet, "ctx", [(i, (i + back) % count) for i in range(count)])
        for back in range(1, halo + 1)
    ]
    block_shapes = [jax.ShapeDtypeStruct((rows, columns), f32)] * 2
    row_shape = jax.ShapeDtypeStruct((8, columns), f32)
    target_shape = jax.ShapeDtypeStruct((count * rows, rows), bf16)
    filled_shape = jax.ShapeDtypeStruct((8, rows), f32)
    query_rows, grad_rows, raised, change, row, spread, target, filled = pl.pallas_call(
        functools.partial(own_kernel, count, doc_lengths.shape[0]),
        out_shape=[jax.ShapeDtypeStruct((columns, depth), bf16)] * 2
        + block_shapes
        + [row_shape, jax.ShapeDtypeStruct((count * slot, rows), bf16), target_shape, filled_shape],
        in_specs=[whole] * 5,
        out_specs=[whole] * 8,
        compiler_params=params,
    )(doc_lengths.reshape(1, -1), packet, queries, grad_out, forward_out)
    raised, change, target = [raised], [change], [target]
    slot_shapes = [jax.ShapeDtypeStruct((heads * slot + 2 * rows, depth), bf16)] * count
    ready = []
    for back in range(1, halo):
        found = pl.pallas_call(
            functools.partial(step_kernel, count, halo, back),
            out_shape=block_shapes
            + [row_shape, target_shape, filled_shape]
            + slot_shapes * (back == halo - 1),
            in_specs=[whole] * (6 + 4 * back),
            out_specs=[whole] * (5 + count * (back == halo - 1)),
            compiler_params=params,
        )(query_rows, grad_rows, row, filled, spread, *raised, *change, *target, packet, *near[:back])
        raised.append(found[0])
        change.append(found[1])
        row = found[2]
        target.append(found[3])
        filled = found[4]
        ready = found[5:]
    sent = pl.pallas_call(
        functools.partial(attend_kernel, count, halo),
        out_shape=slot_shapes,
        in_specs=[whole] * (len(ready) + 6 + 4 * halo),
        out_specs=[whole] * count,
        compiler_params=params,
    )(*ready, query_rows, grad_rows, row, filled, spread, *raised, *change, *target, packet, *near)
    received = [sent[0]] + [
        lax.ppermute(sent[k], "ctx", [(i, i ^ k) for i in range(count)]) for k in range(1, count)
    ]
    early = (0, 3) if count == 4 else (0,)
    late = tuple(k for k in range(count) if k not in early)
    placed = pl.pallas_call(
        functools.partial(order_kernel, count, halo, early, late),
        out_shape=[
            jax.ShapeDtypeStruct((rows, len(late) * slot), bf16),
            jax.ShapeDtypeStruct((rows, len(late) * rows), bf16),
            jax.ShapeDtypeStruct((rows, width), f32),
            jax.ShapeDtypeStruct((rows, 2 * depth), f32),
        ],
        in_specs=[whole] * (len(early) + 1 + halo),
        out_specs=[whole] * 4,
        compiler_params=params,
    )(*[received[k] for k in early], packet, *near)
    return pl.pallas_call(
        functools.partial(place_kernel, count),
        out_shape=[
            jax.ShapeDtypeStruct((rows, width), f32),
            jax.ShapeDtypeStruct((rows, depth), f32),
            jax.ShapeDtypeStruct((rows, depth), f32),
        ],
        in_specs=[whole] * (4 + len(late)),
        out_specs=[pl.BlockSpec(memory_space=pl.ANY)] * 3,
        scratch_shapes=[
            pltpu.VMEM((rows, width), f32),
            pltpu.VMEM((rows, depth), f32),
            pltpu.VMEM((rows, depth), f32),
            pltpu.SemaphoreType.DMA((3,)),
        ],
        compiler_params=params,
    )(*placed, *[received[k] for k in late])


def per_device(*args):
    if lax.axis_size("ctx") in (2, 4):
        return near_plan(*args)
    return ring_plan(*args)


def solution(mesh):
    return jax.shard_map(
        per_device,
        mesh=mesh,
        in_specs=(
            P("groups"),
            P(("groups", "ctx")),
            P(("groups", "ctx"), "head"),
            P(("groups", "ctx"), "head"),
            P(("groups", "ctx"), "head"),
            P(("groups", "ctx"), "head"),
            P(("groups", "ctx"), "head"),
        ),
        out_specs=(
            P(("groups", "ctx"), "head"),
            P(("groups", "ctx"), "head"),
            P(("groups", "ctx"), "head"),
        ),
        check_vma=False,
    )
```

```python
import functools
import math

import jax
import jax.numpy as jnp
from jax import lax
from jax.experimental import pallas as pl
from jax.experimental.pallas import tpu as pltpu
from jax.sharding import PartitionSpec as P

HEAD_WIDTH = 128
GROUP = 4


NEG = -1e30
BLOCK = 512


def shifted(value, axis, by):
    count = lax.axis_size(axis)
    return lax.ppermute(value, axis, [(i, (i + by) % count) for i in range(count)])


def document_of(positions, doc_lengths):
    ends = jnp.cumsum(doc_lengths)
    return jnp.sum((positions[:, None] >= ends[None, :]).astype(jnp.int32), axis=1)


def allowed_between(query_positions, query_docs, key_positions, key_docs):
    return (query_docs[:, None] == key_docs[None, :]) & (
        key_positions[None, :] <= query_positions[:, None]
    )


def head_rows(matrix, group_size, head_dim):
    row_count = matrix.shape[0]
    return matrix.reshape(row_count * group_size, head_dim)


def block_scores(query_flat, key_head, row_count, group_size, head_dim):
    scores = lax.dot_general(
        query_flat, key_head, (((1,), (1,)), ((), ())), preferred_element_type=jnp.float32
    )
    return (scores * (1.0 / math.sqrt(head_dim))).reshape(row_count, group_size, key_head.shape[0])


def update_stats(running, query_local, key_block, allowed, group_size, head_dim):
    running_max, totals = running
    row_count = query_local.shape[0]
    scores = block_scores(
        head_rows(query_local, group_size, head_dim), key_block, row_count, group_size, head_dim
    )
    masked = jnp.where(allowed[:, None, :], scores, NEG)
    new_max = jnp.maximum(running_max, jnp.max(masked, axis=2))
    weights = jnp.where(allowed[:, None, :], jnp.exp(masked - new_max[:, :, None]), 0.0)
    new_totals = [totals * jnp.exp(running_max - new_max) + jnp.sum(weights, axis=2)]
    new_maxima = [new_max]
    return (jnp.concatenate(new_maxima, axis=1), jnp.concatenate(new_totals, axis=1))


def backward_block(
    query_local,
    grad_local,
    log_norm,
    row_delta,
    key_block,
    value_block,
    allowed,
    group_size,
    head_dim,
):
    row_count = query_local.shape[0]
    query_flat = head_rows(query_local, group_size, head_dim)
    grad_flat = head_rows(grad_local, group_size, head_dim)
    scores = block_scores(query_flat, key_block, row_count, group_size, head_dim)
    masked = jnp.where(allowed[:, None, :], scores, NEG)
    weights = jnp.exp(masked - log_norm[:, 0:group_size, None])
    grad_weights = lax.dot_general(
        grad_flat, value_block, (((1,), (1,)), ((), ())), preferred_element_type=jnp.float32
    ).reshape(row_count, group_size, -1)
    grad_scores = weights * (grad_weights - row_delta[:, 0:group_size, None])
    rounded_weights = weights.astype(jnp.bfloat16).reshape(row_count * group_size, -1)
    rounded_grads = grad_scores.astype(jnp.bfloat16).reshape(row_count * group_size, -1)
    value_parts = [
        lax.dot_general(
            rounded_weights, grad_flat, (((0,), (0,)), ((), ())), preferred_element_type=jnp.float32
        )
    ]
    key_parts = [
        lax.dot_general(
            rounded_grads, query_flat, (((0,), (0,)), ((), ())), preferred_element_type=jnp.float32
        )
    ]
    query_parts = [
        jnp.dot(rounded_grads, key_block, preferred_element_type=jnp.float32).reshape(
            row_count, group_size * head_dim
        )
    ]
    return (
        jnp.concatenate(query_parts, axis=1),
        jnp.concatenate(key_parts, axis=1),
        jnp.concatenate(value_parts, axis=1),
    )


def ring_plan(doc_lengths, owners, queries, key_head_rows, value_head_rows, forward_out, grad_out):
    context_size = lax.axis_size("ctx")
    context_index = lax.axis_index("ctx")
    row_count = queries.shape[0]
    head_dim = HEAD_WIDTH
    group_size = GROUP
    query_heads = queries.shape[1] // head_dim
    slot_count = 2 * row_count // context_size
    everyone = lax.all_gather(owners, "ctx", axis=0, tiled=True)
    row_arrangement = jnp.argsort(everyone, stable=True)
    layout_docs = document_of(row_arrangement, doc_lengths)
    own_positions = lax.dynamic_slice_in_dim(
        row_arrangement, context_index * row_count, row_count, 0
    )
    own_documents = lax.dynamic_slice_in_dim(layout_docs, context_index * row_count, row_count, 0)
    owner_ids = jnp.arange(context_size, dtype=jnp.int32)
    owner_hot = (owners[:, None] == owner_ids[None, :]).astype(jnp.int32)
    earlier = jnp.cumsum(owner_hot, axis=0) - owner_hot
    rank_within = jnp.sum(earlier * owner_hot, axis=1)
    slot_rows = owners * slot_count + rank_within

    def packed(matrix):
        empty = jnp.zeros((context_size * slot_count,) + matrix.shape[1:], matrix.dtype)
        return empty.at[slot_rows].set(matrix)

    owner_grid = everyone.reshape(context_size, row_count)
    counts = jnp.sum((owner_grid == context_index).astype(jnp.int32), axis=1)
    count_ends = jnp.cumsum(counts)
    starts = count_ends - counts
    wanted = jnp.arange(row_count, dtype=jnp.int32)
    source = jnp.sum((wanted[:, None] >= count_ends[None, :]).astype(jnp.int32), axis=1)
    source_hot = (source[:, None] == owner_ids[None, :]).astype(jnp.int32)
    take_rows = source * slot_count + wanted - jnp.sum(source_hot * starts[None, :], axis=1)

    def compact(received):
        return jnp.take(received, take_rows, axis=0)

    local_delta = jnp.sum(
        (grad_out.astype(jnp.float32) * forward_out.astype(jnp.float32)).reshape(
            row_count, query_heads, head_dim
        ),
        axis=2,
    )
    arrived = (
        lax.all_to_all(packed(queries), "ctx", split_axis=0, concat_axis=0, tiled=True),
        lax.all_to_all(packed(key_head_rows), "ctx", split_axis=0, concat_axis=0, tiled=True),
        lax.all_to_all(packed(value_head_rows), "ctx", split_axis=0, concat_axis=0, tiled=True),
        lax.all_to_all(packed(grad_out), "ctx", split_axis=0, concat_axis=0, tiled=True),
    )
    query_local, key_local, value_local, grad_local = [compact(received) for received in arrived]
    row_delta = compact(
        lax.all_to_all(packed(local_delta), "ctx", split_axis=0, concat_axis=0, tiled=True)
    )

    def fold_keys(running, shard_rows, first_row):
        piece_count = shard_rows.shape[0]
        step_rows = math.gcd(piece_count, BLOCK) if piece_count > BLOCK else piece_count

        def one_block(partial_value, block_index):
            offset = first_row + block_index * step_rows
            key_block = lax.dynamic_slice_in_dim(shard_rows, block_index * step_rows, step_rows, 0)
            key_positions = lax.dynamic_slice_in_dim(row_arrangement, offset, step_rows, 0)
            key_docs = lax.dynamic_slice_in_dim(layout_docs, offset, step_rows, 0)
            allowed = allowed_between(own_positions, own_documents, key_positions, key_docs)
            return (
                update_stats(partial_value, query_local, key_block, allowed, group_size, head_dim),
                None,
            )

        if piece_count == step_rows:
            return one_block(running, 0)[0]
        return lax.scan(one_block, running, jnp.arange(piece_count // step_rows, dtype=jnp.int32))[
            0
        ]

    start_stats = (
        jnp.full((row_count, query_heads), NEG, jnp.float32),
        jnp.zeros((row_count, query_heads), jnp.float32),
    )
    top_scores, totals = fold_keys(
        start_stats, lax.all_gather(key_local, "ctx", axis=0, tiled=True), jnp.int32(0)
    )
    log_norm = top_scores + jnp.log(totals)

    def block_meta(owner_index, offset, size):
        first = owner_index * row_count + offset
        key_positions = lax.dynamic_slice_in_dim(row_arrangement, first, size, 0)
        key_docs = lax.dynamic_slice_in_dim(layout_docs, first, size, 0)
        return (key_positions, key_docs)

    query_zero = jnp.zeros(query_local.shape, jnp.float32)
    key_zero = jnp.zeros(key_local.shape, jnp.float32)

    def one_turn(turn_index, loop_state):
        key_moving, value_moving, key_grad, value_grad, query_grad = loop_state
        owner_index = (context_index - turn_index) % context_size
        key_positions, key_docs = block_meta(owner_index, 0, row_count)
        allowed = allowed_between(own_positions, own_documents, key_positions, key_docs)
        query_part, key_part, value_part = backward_block(
            query_local,
            grad_local,
            log_norm,
            row_delta,
            key_moving,
            value_moving,
            allowed,
            group_size,
            head_dim,
        )
        return (
            key_moving,
            value_moving,
            key_grad + key_part,
            value_grad + value_part,
            query_grad + query_part,
        )

    def moved_turn(turn_index, loop_state):
        key_moving, value_moving, key_grad, value_grad, query_grad = loop_state
        key_moving, value_moving = shifted((key_moving, value_moving), "ctx", 1)
        key_grad, value_grad = shifted((key_grad, value_grad), "ctx", 1)
        return one_turn(turn_index, (key_moving, value_moving, key_grad, value_grad, query_grad))

    loop_state = one_turn(0, (key_local, value_local, key_zero, key_zero, query_zero))
    loop_state = lax.fori_loop(1, context_size, moved_turn, loop_state)
    key_grad, value_grad = shifted((loop_state[2], loop_state[3]), "ctx", 1)
    query_grad = loop_state[4]
    inverse_root = 1.0 / math.sqrt(head_dim)
    return (query_grad * inverse_root, key_grad * inverse_root, value_grad)


META = 8


def contract(left, right, left_dim, right_dim, **kw):
    return lax.dot_general(
        left,
        right,
        (((left_dim,), (right_dim,)), ((), ())),
        preferred_element_type=jnp.float32,
        **kw,
    )


def one_hot(row_count, target):
    places = lax.broadcasted_iota(jnp.int32, (row_count, target.shape[1]), 0)
    return jnp.where(places == target, 1.0, 0.0).astype(jnp.bfloat16)


def side_by_side(stack, heads):
    rows = stack.shape[0] // heads
    return jnp.concatenate([stack[h * rows : (h + 1) * rows, :] for h in range(heads)], axis=1)


def end_to_end(matrix, heads):
    width = matrix.shape[1] // heads
    return jnp.concatenate([matrix[:, h * width : (h + 1) * width] for h in range(heads)], axis=0)


def runs_of(hot):
    count, rows = hot.shape
    counts = jnp.sum(hot, axis=1, keepdims=True)
    owner = jnp.zeros((1, rows), jnp.int32)
    earlier = jnp.zeros((1, rows), jnp.float32)
    for p in range(count):
        mine = hot[p : p + 1, :] > 0.0
        owner = jnp.where(mine, p, owner)
        for less in range(p):
            earlier = earlier + jnp.where(mine, counts[less : less + 1, :], 0.0)
    lane = lax.broadcasted_iota(jnp.int32, (1, rows), 1)
    return owner, counts, lane - earlier.astype(jnp.int32)


def own_kernel(
    count,
    docs,
    doc_ref,
    packet_ref,
    query_ref,
    grad_ref,
    saved_ref,
    query_out,
    grad_out,
    raised_out,
    change_out,
    row_out,
    spread_out,
    target_out,
    filled_out,
):
    rows, width = query_ref.shape
    depth = packet_ref.shape[1]
    heads = width // depth
    slot = 2 * rows // count
    index = lax.axis_index("ctx")
    lane = lax.broadcasted_iota(jnp.int32, (1, rows), 1)
    position = index * rows + lane
    earlier = lax.broadcasted_iota(jnp.int32, (docs, docs), 1) <= lax.broadcasted_iota(
        jnp.int32, (docs, docs), 0
    )
    lengths = doc_ref[...].astype(jnp.float32)
    ends = jnp.sum(jnp.where(earlier, lengths, 0.0), axis=1, keepdims=True).astype(jnp.int32)
    first = jnp.max(jnp.where(ends <= position, ends, 0), axis=0, keepdims=True)
    key_position = index * rows + lax.broadcasted_iota(jnp.int32, (rows, rows), 0)
    allowed = (key_position >= first) & (key_position <= position)
    allowed = jnp.concatenate([allowed] * heads, axis=1)

    queries = end_to_end(query_ref[...], heads)
    query_out[...] = queries
    scores = contract(packet_ref[0:rows, :], queries, 1, 1) * (1.0 / math.sqrt(depth))
    scores = jnp.where(allowed, scores, NEG)
    top = jnp.max(scores, axis=0, keepdims=True)
    raised = jnp.exp(scores - top)
    raised_out[...] = raised
    grads = end_to_end(grad_ref[...], heads)
    grad_out[...] = grads
    product = grads.astype(jnp.float32) * end_to_end(saved_ref[...], heads).astype(jnp.float32)
    delta = contract(
        jnp.ones((8, depth), jnp.float32), product, 1, 1, precision=lax.Precision.HIGHEST
    )[0:1, :]
    change_out[...] = contract(packet_ref[rows : 2 * rows, :], grads, 1, 1) - delta
    row_out[0:1, :] = delta
    row_out[1:2, :] = top
    row_out[2:3, :] = jnp.sum(raised, axis=0, keepdims=True)
    row_out[3:4, :] = jnp.concatenate([first.astype(jnp.float32)] * heads, axis=1)
    row_out[4:8, :] = jnp.ones((4, width), jnp.float32)
    owner, counts, rank = runs_of(packet_ref[2 * rows : 2 * rows + count, :].astype(jnp.float32))
    spread_out[...] = one_hot(count * slot, (owner ^ index) * slot + rank)
    target_out[...] = one_hot(count * rows, (owner ^ index) * rows + rank)
    filled_out[0:count, :] = jnp.broadcast_to(counts, (count, rows))
    filled_out[count:, :] = jnp.zeros((8 - count, rows), jnp.float32)


def fold(count, back, packet, queries, grads, row, filled):
    rows = packet.shape[1]
    index = lax.axis_index("ctx")
    delta, top, total = (row[n : n + 1, :] for n in range(3))
    first = row[3:4, :].astype(jnp.int32)
    position = (index - back) * rows + lax.broadcasted_iota(jnp.int32, (rows, row.shape[1]), 0)
    scores = contract(packet[0:rows, :], queries, 1, 1) * (1.0 / math.sqrt(queries.shape[1]))
    scores = jnp.where(position >= first, scores, NEG)
    new_top = jnp.maximum(top, jnp.max(scores, axis=0, keepdims=True))
    raised = jnp.exp(scores - new_top)
    shrink = jnp.exp(top - new_top)
    total = total * shrink + jnp.sum(raised, axis=0, keepdims=True)
    change = contract(packet[rows : 2 * rows, :], grads, 1, 1) - delta
    factors = row[4:8, :] * jnp.where(
        lax.broadcasted_iota(jnp.int32, (4, row.shape[1]), 0) < back, shrink, 1.0
    )
    owner, counts, rank = runs_of(packet[2 * rows : 2 * rows + count, :].astype(jnp.float32))
    base = jnp.zeros((1, rows), jnp.float32)
    for p in range(count):
        base = base + jnp.where(owner == p, filled[p : p + 1, :], 0.0)
    inside = index >= back
    target = jnp.where(inside, (owner ^ index) * rows + base.astype(jnp.int32) + rank, -1)
    filled = filled[0:count, :] + jnp.where(inside, counts, 0.0)
    return raised, change, (new_top, total, factors), one_hot(count * rows, target), filled


def step_kernel(count, halo, back, *refs):
    query_ref, grad_ref, row_ref, filled_ref, spread_ref = refs[:5]
    raised_refs = refs[5 : 5 + back]
    change_refs = refs[5 + back : 5 + 2 * back]
    target_refs = refs[5 + 2 * back : 5 + 3 * back]
    packets = refs[5 + 3 * back : 6 + 4 * back]
    raised_out, change_out, row_out, target_out, filled_out = refs[6 + 4 * back : 11 + 4 * back]
    outs = refs[11 + 4 * back :]
    raised, change, (top, total, factors), target, filled = fold(
        count, back, packets[back], query_ref[...], grad_ref[...], row_ref, filled_ref
    )
    raised_out[...] = raised
    change_out[...] = change
    row_out[0:1, :] = row_ref[0:1, :]
    row_out[1:2, :] = top
    row_out[2:3, :] = total
    row_out[3:4, :] = row_ref[3:4, :]
    row_out[4:8, :] = factors
    target_out[...] = target
    filled_out[0:count, :] = filled
    filled_out[count:, :] = jnp.zeros_like(filled_out[count:, :])
    if outs:
        attend_first(
            count,
            (1,),
            (query_ref, grad_ref, row_out, filled_out, spread_ref)
            + (*raised_refs, raised_out, *change_refs, change_out, *target_refs, target_out)
            + (*packets, None, *outs),
        )


def attend_first(count, several, refs):
    halo = count // 2
    for blocks in several:

        @pl.when(lax.axis_index("ctx") == blocks - 1)
        def _(blocks=blocks):
            attend(count, halo, blocks, refs)


def attend_kernel(count, halo, *refs):
    ready, refs = refs[: count * (halo > 1)], refs[count * (halo > 1) :]
    held = lax.axis_index("ctx") >= halo

    @pl.when(held)
    def _():
        attend(count, halo, halo + 1, refs)

    attend_first(count, range(2 if ready else 1, halo + 1), refs)
    if not ready:
        return

    @pl.when(lax.axis_index("ctx") == 0)
    def _():
        for here, out in zip(ready, refs[-count:], strict=True):
            out[...] = here[...]


def attend(count, halo, blocks, refs):
    query_ref, grad_ref, row_ref, filled_ref, spread_ref = refs[:5]
    raised_refs = refs[5 : 5 + halo]
    change_refs = refs[5 + halo : 5 + 2 * halo]
    target_refs = refs[5 + 2 * halo : 5 + 3 * halo]
    packets = refs[5 + 3 * halo : 6 + 4 * halo]
    outs = refs[6 + 4 * halo :]
    rows = packets[0].shape[1]
    depth = query_ref.shape[1]
    heads = query_ref.shape[0] // rows
    slot = 2 * rows // count
    scale = 1.0 / math.sqrt(depth)
    queries = query_ref[...]
    grads = grad_ref[...]
    raised = [ref[...] for ref in raised_refs[:blocks]]
    change = [ref[...] for ref in change_refs[:blocks]]
    targets = [ref[...] for ref in target_refs[:blocks]]
    total = row_ref[2:3, :]
    factors = row_ref[4:8, :]
    if blocks > halo:
        raised_far, change_far, (_, total, factors), target_far, _ = fold(
            count, halo, packets[halo], queries, grads, row_ref, filled_ref
        )
        raised.append(raised_far)
        change.append(change_far)
        targets.append(target_far)
    factors = factors * (1.0 / total)
    weights = [raised[n] * factors[n : n + 1, :] for n in range(blocks)]
    changes = [weights[n] * change[n] for n in range(blocks)]
    weights = jnp.concatenate([part.astype(jnp.bfloat16) for part in weights], axis=0)
    changes = jnp.concatenate([part.astype(jnp.bfloat16) for part in changes], axis=0)
    keys = jnp.concatenate([packet[0:rows, :] for packet in packets[:blocks]], axis=0)
    query_grad = (contract(keys, changes, 0, 0) * scale).astype(jnp.bfloat16)
    key_parts = contract(changes, queries, 1, 0) * scale
    value_parts = contract(weights, grads, 1, 0)
    parts = jnp.concatenate([key_parts, value_parts], axis=1).astype(jnp.bfloat16)

    query_slots = contract(spread_ref[...], end_to_end(query_grad, heads), 1, 1)
    query_slots = query_slots.astype(jnp.bfloat16)
    part_slots = contract(jnp.concatenate(targets, axis=1), parts, 1, 0).astype(jnp.bfloat16)
    at = heads * slot
    for k in range(count):
        out = outs[k]
        for h in range(heads):
            out[h * slot : (h + 1) * slot, :] = query_slots[
                k * slot : (k + 1) * slot, h * depth : (h + 1) * depth
            ]
        for n in range(2):
            out[at + n * rows : at + (n + 1) * rows, :] = part_slots[
                k * rows : (k + 1) * rows, n * depth : (n + 1) * depth
            ]


def slots_of(refs, first, size, pieces):
    return jnp.concatenate(
        [
            jnp.concatenate(
                [ref[first + n * size : first + (n + 1) * size, :] for n in range(pieces)], axis=1
            )
            for ref in refs
        ],
        axis=0,
    )


def order_kernel(count, halo, early, late, *refs):
    ins, packets = refs[: len(early)], refs[len(early) : len(early) + 1 + halo]
    query_out, key_out, query_base, key_base = refs[-4:]
    rows, width = query_base.shape
    depth = ins[0].shape[1]
    heads = width // depth
    slot = 2 * rows // count
    index = lax.axis_index("ctx")
    given = []
    for ref in packets:
        hot = ref[2 * rows : 2 * rows + count, :].astype(jnp.float32)
        counts = jnp.sum(hot, axis=1, keepdims=True)
        mine = jnp.zeros((1, 1), jnp.float32)
        for p in range(count):
            mine = jnp.where(index == p, counts[p : p + 1, :], mine)
        given.append(mine.astype(jnp.int32))
    if len(given) < count:
        given.append(rows - sum(given))
    giver = [lax.rem(index - d + count, count) for d in range(count)]

    def placement(size, halo, exchanges):
        lane = lax.broadcasted_iota(jnp.int32, (1, len(exchanges) * size), 1)
        target = jnp.full(lane.shape, -1, jnp.int32)
        for n, k in enumerate(exchanges):
            step = lane - n * size
            for back in range(halo + 1):
                block = (index ^ k) - back
                start = jnp.zeros((1, 1), jnp.int32)
                length = jnp.zeros((1, 1), jnp.int32)
                for d in range(count):
                    start = start + jnp.where(giver[d] < block, given[d], 0)
                    length = length + jnp.where(giver[d] == block, given[d], 0)
                target = jnp.where((step >= 0) & (step < length), start + step, target)
                step = step - length
        return one_hot(rows, target)

    query_out[...] = placement(slot, 0, late)
    key_out[...] = placement(rows, halo, late)
    query_base[...] = contract(placement(slot, 0, early), slots_of(ins, 0, slot, heads), 1, 0)
    key_base[...] = contract(
        placement(rows, halo, early), slots_of(ins, heads * slot, rows, 2), 1, 0
    )


def place_kernel(count, query_spread, key_spread, query_base, key_base, *refs):
    ins = refs[:-7]
    query_out, key_out, value_out, query_here, key_here, value_here, sems = refs[-7:]
    rows, width = query_here.shape
    depth = key_here.shape[1]
    heads = width // depth
    slot = 2 * rows // count
    copies = []

    def leave(here, out):
        copies.append(pltpu.make_async_copy(here, out, sems.at[len(copies)]))
        copies[-1].start()

    query_here[...] = query_base[...] + contract(
        query_spread[...], slots_of(ins, 0, slot, heads), 1, 0
    )
    leave(query_here, query_out)
    both = key_base[...] + contract(
        key_spread[...], slots_of(ins, heads * slot, rows, 2), 1, 0
    )
    for n, (here, out) in enumerate(((key_here, key_out), (value_here, value_out))):
        here[...] = both[:, n * depth : (n + 1) * depth]
        leave(here, out)
    for copy in copies:
        copy.wait()


def near_plan(doc_lengths, owners, queries, key_head_rows, value_head_rows, forward_out, grad_out):
    count = lax.axis_size("ctx")
    rows, width = queries.shape
    depth = key_head_rows.shape[1]
    heads = width // depth
    bf16, f32 = jnp.bfloat16, jnp.float32
    columns = heads * rows
    halo = count // 2
    slot = 2 * rows // count
    whole = pl.BlockSpec(memory_space=pltpu.VMEM)
    params = pltpu.CompilerParams(vmem_limit_bytes=40 * 1024 * 1024)

    mark = lax.broadcasted_iota(jnp.int32, (2 * rows + META, rows), 0) - 2 * rows
    packet = jnp.where(
        mark < 0,
        jnp.pad(jnp.concatenate([key_head_rows, value_head_rows], axis=0), ((0, META), (0, 0))),
        (owners[None, :] == mark).astype(bf16),
    )
    near = [
        lax.ppermute(packet, "ctx", [(i, (i + back) % count) for i in range(count)])
        for back in range(1, halo + 1)
    ]
    block_shapes = [jax.ShapeDtypeStruct((rows, columns), f32)] * 2
    row_shape = jax.ShapeDtypeStruct((8, columns), f32)
    target_shape = jax.ShapeDtypeStruct((count * rows, rows), bf16)
    filled_shape = jax.ShapeDtypeStruct((8, rows), f32)
    query_rows, grad_rows, raised, change, row, spread, target, filled = pl.pallas_call(
        functools.partial(own_kernel, count, doc_lengths.shape[0]),
        out_shape=[jax.ShapeDtypeStruct((columns, depth), bf16)] * 2
        + block_shapes
        + [row_shape, jax.ShapeDtypeStruct((count * slot, rows), bf16), target_shape, filled_shape],
        in_specs=[whole] * 5,
        out_specs=[whole] * 8,
        compiler_params=params,
    )(doc_lengths.reshape(1, -1), packet, queries, grad_out, forward_out)
    raised, change, target = [raised], [change], [target]
    slot_shapes = [jax.ShapeDtypeStruct((heads * slot + 2 * rows, depth), bf16)] * count
    ready = []
    for back in range(1, halo):
        found = pl.pallas_call(
            functools.partial(step_kernel, count, halo, back),
            out_shape=block_shapes
            + [row_shape, target_shape, filled_shape]
            + slot_shapes * (back == halo - 1),
            in_specs=[whole] * (6 + 4 * back),
            out_specs=[whole] * (5 + count * (back == halo - 1)),
            compiler_params=params,
        )(query_rows, grad_rows, row, filled, spread, *raised, *change, *target, packet, *near[:back])
        raised.append(found[0])
        change.append(found[1])
        row = found[2]
        target.append(found[3])
        filled = found[4]
        ready = found[5:]
    sent = pl.pallas_call(
        functools.partial(attend_kernel, count, halo),
        out_shape=slot_shapes,
        in_specs=[whole] * (len(ready) + 6 + 4 * halo),
        out_specs=[whole] * count,
        compiler_params=params,
    )(*ready, query_rows, grad_rows, row, filled, spread, *raised, *change, *target, packet, *near)
    received = [sent[0]] + [
        lax.ppermute(sent[k], "ctx", [(i, i ^ k) for i in range(count)]) for k in range(1, count)
    ]
    early = (0, 3) if count == 4 else (0,)
    late = tuple(k for k in range(count) if k not in early)
    placed = pl.pallas_call(
        functools.partial(order_kernel, count, halo, early, late),
        out_shape=[
            jax.ShapeDtypeStruct((rows, len(late) * slot), bf16),
            jax.ShapeDtypeStruct((rows, len(late) * rows), bf16),
            jax.ShapeDtypeStruct((rows, width), f32),
            jax.ShapeDtypeStruct((rows, 2 * depth), f32),
        ],
        in_specs=[whole] * (len(early) + 1 + halo),
        out_specs=[whole] * 4,
        compiler_params=params,
    )(*[received[k] for k in early], packet, *near)
    return pl.pallas_call(
        functools.partial(place_kernel, count),
        out_shape=[
            jax.ShapeDtypeStruct((rows, width), f32),
            jax.ShapeDtypeStruct((rows, depth), f32),
            jax.ShapeDtypeStruct((rows, depth), f32),
        ],
        in_specs=[whole] * (4 + len(late)),
        out_specs=[pl.BlockSpec(memory_space=pl.ANY)] * 3,
        scratch_shapes=[
            pltpu.VMEM((rows, width), f32),
            pltpu.VMEM((rows, depth), f32),
            pltpu.VMEM((rows, depth), f32),
            pltpu.SemaphoreType.DMA((3,)),
        ],
        compiler_params=params,
    )(*placed, *[received[k] for k in late])


def per_device(*args):
    if lax.axis_size("ctx") in (2, 4):
        return near_plan(*args)
    return ring_plan(*args)


def solution(mesh):
    return jax.shard_map(
        per_device,
        mesh=mesh,
        in_specs=(
            P("groups"),
            P(("groups", "ctx")),
            P(("groups", "ctx"), "head"),
            P(("groups", "ctx"), "head"),
            P(("groups", "ctx"), "head"),
            P(("groups", "ctx"), "head"),
            P(("groups", "ctx"), "head"),
        ),
        out_specs=(
            P(("groups", "ctx"), "head"),
            P(("groups", "ctx"), "head"),
            P(("groups", "ctx"), "head"),
        ),
        check_vma=False,
    )
```

```python
import functools
import math

import jax
import jax.numpy as jnp
from jax import lax
from jax.experimental import pallas as pl
from jax.experimental.pallas import tpu as pltpu
from jax.sharding import PartitionSpec as P

HEAD_WIDTH = 128
GROUP = 4


NEG = -1e30
BLOCK = 512


def shifted(value, axis, by):
    count = lax.axis_size(axis)
    return lax.ppermute(value, axis, [(i, (i + by) % count) for i in range(count)])


def document_of(positions, doc_lengths):
    ends = jnp.cumsum(doc_lengths)
    return jnp.sum((positions[:, None] >= ends[None, :]).astype(jnp.int32), axis=1)


def allowed_between(query_positions, query_docs, key_positions, key_docs):
    return (query_docs[:, None] == key_docs[None, :]) & (
        key_positions[None, :] <= query_positions[:, None]
    )


def head_rows(matrix, group_size, head_dim):
    row_count = matrix.shape[0]
    return matrix.reshape(row_count * group_size, head_dim)


def block_scores(query_flat, key_head, row_count, group_size, head_dim):
    scores = lax.dot_general(
        query_flat, key_head, (((1,), (1,)), ((), ())), preferred_element_type=jnp.float32
    )
    return (scores * (1.0 / math.sqrt(head_dim))).reshape(row_count, group_size, key_head.shape[0])


def update_stats(running, query_local, key_block, allowed, group_size, head_dim):
    running_max, totals = running
    row_count = query_local.shape[0]
    scores = block_scores(
        head_rows(query_local, group_size, head_dim), key_block, row_count, group_size, head_dim
    )
    masked = jnp.where(allowed[:, None, :], scores, NEG)
    new_max = jnp.maximum(running_max, jnp.max(masked, axis=2))
    weights = jnp.where(allowed[:, None, :], jnp.exp(masked - new_max[:, :, None]), 0.0)
    new_totals = [totals * jnp.exp(running_max - new_max) + jnp.sum(weights, axis=2)]
    new_maxima = [new_max]
    return (jnp.concatenate(new_maxima, axis=1), jnp.concatenate(new_totals, axis=1))


def backward_block(
    query_local,
    grad_local,
    log_norm,
    row_delta,
    key_block,
    value_block,
    allowed,
    group_size,
    head_dim,
):
    row_count = query_local.shape[0]
    query_flat = head_rows(query_local, group_size, head_dim)
    grad_flat = head_rows(grad_local, group_size, head_dim)
    scores = block_scores(query_flat, key_block, row_count, group_size, head_dim)
    masked = jnp.where(allowed[:, None, :], scores, NEG)
    weights = jnp.exp(masked - log_norm[:, 0:group_size, None])
    grad_weights = lax.dot_general(
        grad_flat, value_block, (((1,), (1,)), ((), ())), preferred_element_type=jnp.float32
    ).reshape(row_count, group_size, -1)
    grad_scores = weights * (grad_weights - row_delta[:, 0:group_size, None])
    rounded_weights = weights.astype(jnp.bfloat16).reshape(row_count * group_size, -1)
    rounded_grads = grad_scores.astype(jnp.bfloat16).reshape(row_count * group_size, -1)
    value_parts = [
        lax.dot_general(
            rounded_weights, grad_flat, (((0,), (0,)), ((), ())), preferred_element_type=jnp.float32
        )
    ]
    key_parts = [
        lax.dot_general(
            rounded_grads, query_flat, (((0,), (0,)), ((), ())), preferred_element_type=jnp.float32
        )
    ]
    query_parts = [
        jnp.dot(rounded_grads, key_block, preferred_element_type=jnp.float32).reshape(
            row_count, group_size * head_dim
        )
    ]
    return (
        jnp.concatenate(query_parts, axis=1),
        jnp.concatenate(key_parts, axis=1),
        jnp.concatenate(value_parts, axis=1),
    )


def ring_plan(doc_lengths, owners, queries, key_head_rows, value_head_rows, forward_out, grad_out):
    context_size = lax.axis_size("ctx")
    context_index = lax.axis_index("ctx")
    row_count = queries.shape[0]
    head_dim = HEAD_WIDTH
    group_size = GROUP
    query_heads = queries.shape[1] // head_dim
    slot_count = 2 * row_count // context_size
    everyone = lax.all_gather(owners, "ctx", axis=0, tiled=True)
    row_arrangement = jnp.argsort(everyone, stable=True)
    layout_docs = document_of(row_arrangement, doc_lengths)
    own_positions = lax.dynamic_slice_in_dim(
        row_arrangement, context_index * row_count, row_count, 0
    )
    own_documents = lax.dynamic_slice_in_dim(layout_docs, context_index * row_count, row_count, 0)
    owner_ids = jnp.arange(context_size, dtype=jnp.int32)
    owner_hot = (owners[:, None] == owner_ids[None, :]).astype(jnp.int32)
    earlier = jnp.cumsum(owner_hot, axis=0) - owner_hot
    rank_within = jnp.sum(earlier * owner_hot, axis=1)
    slot_rows = owners * slot_count + rank_within

    def packed(matrix):
        empty = jnp.zeros((context_size * slot_count,) + matrix.shape[1:], matrix.dtype)
        return empty.at[slot_rows].set(matrix)

    owner_grid = everyone.reshape(context_size, row_count)
    counts = jnp.sum((owner_grid == context_index).astype(jnp.int32), axis=1)
    count_ends = jnp.cumsum(counts)
    starts = count_ends - counts
    wanted = jnp.arange(row_count, dtype=jnp.int32)
    source = jnp.sum((wanted[:, None] >= count_ends[None, :]).astype(jnp.int32), axis=1)
    source_hot = (source[:, None] == owner_ids[None, :]).astype(jnp.int32)
    take_rows = source * slot_count + wanted - jnp.sum(source_hot * starts[None, :], axis=1)

    def compact(received):
        return jnp.take(received, take_rows, axis=0)

    local_delta = jnp.sum(
        (grad_out.astype(jnp.float32) * forward_out.astype(jnp.float32)).reshape(
            row_count, query_heads, head_dim
        ),
        axis=2,
    )
    arrived = (
        lax.all_to_all(packed(queries), "ctx", split_axis=0, concat_axis=0, tiled=True),
        lax.all_to_all(packed(key_head_rows), "ctx", split_axis=0, concat_axis=0, tiled=True),
        lax.all_to_all(packed(value_head_rows), "ctx", split_axis=0, concat_axis=0, tiled=True),
        lax.all_to_all(packed(grad_out), "ctx", split_axis=0, concat_axis=0, tiled=True),
    )
    query_local, key_local, value_local, grad_local = [compact(received) for received in arrived]
    row_delta = compact(
        lax.all_to_all(packed(local_delta), "ctx", split_axis=0, concat_axis=0, tiled=True)
    )

    def fold_keys(running, shard_rows, first_row):
        piece_count = shard_rows.shape[0]
        step_rows = math.gcd(piece_count, BLOCK) if piece_count > BLOCK else piece_count

        def one_block(partial_value, block_index):
            offset = first_row + block_index * step_rows
            key_block = lax.dynamic_slice_in_dim(shard_rows, block_index * step_rows, step_rows, 0)
            key_positions = lax.dynamic_slice_in_dim(row_arrangement, offset, step_rows, 0)
            key_docs = lax.dynamic_slice_in_dim(layout_docs, offset, step_rows, 0)
            allowed = allowed_between(own_positions, own_documents, key_positions, key_docs)
            return (
                update_stats(partial_value, query_local, key_block, allowed, group_size, head_dim),
                None,
            )

        if piece_count == step_rows:
            return one_block(running, 0)[0]
        return lax.scan(one_block, running, jnp.arange(piece_count // step_rows, dtype=jnp.int32))[
            0
        ]

    start_stats = (
        jnp.full((row_count, query_heads), NEG, jnp.float32),
        jnp.zeros((row_count, query_heads), jnp.float32),
    )
    top_scores, totals = fold_keys(
        start_stats, lax.all_gather(key_local, "ctx", axis=0, tiled=True), jnp.int32(0)
    )
    log_norm = top_scores + jnp.log(totals)

    def block_meta(owner_index, offset, size):
        first = owner_index * row_count + offset
        key_positions = lax.dynamic_slice_in_dim(row_arrangement, first, size, 0)
        key_docs = lax.dynamic_slice_in_dim(layout_docs, first, size, 0)
        return (key_positions, key_docs)

    query_zero = jnp.zeros(query_local.shape, jnp.float32)
    key_zero = jnp.zeros(key_local.shape, jnp.float32)

    def one_turn(turn_index, loop_state):
        key_moving, value_moving, key_grad, value_grad, query_grad = loop_state
        owner_index = (context_index - turn_index) % context_size
        key_positions, key_docs = block_meta(owner_index, 0, row_count)
        allowed = allowed_between(own_positions, own_documents, key_positions, key_docs)
        query_part, key_part, value_part = backward_block(
            query_local,
            grad_local,
            log_norm,
            row_delta,
            key_moving,
            value_moving,
            allowed,
            group_size,
            head_dim,
        )
        return (
            key_moving,
            value_moving,
            key_grad + key_part,
            value_grad + value_part,
            query_grad + query_part,
        )

    def moved_turn(turn_index, loop_state):
        key_moving, value_moving, key_grad, value_grad, query_grad = loop_state
        key_moving, value_moving = shifted((key_moving, value_moving), "ctx", 1)
        key_grad, value_grad = shifted((key_grad, value_grad), "ctx", 1)
        return one_turn(turn_index, (key_moving, value_moving, key_grad, value_grad, query_grad))

    loop_state = one_turn(0, (key_local, value_local, key_zero, key_zero, query_zero))
    loop_state = lax.fori_loop(1, context_size, moved_turn, loop_state)
    key_grad, value_grad = shifted((loop_state[2], loop_state[3]), "ctx", 1)
    query_grad = loop_state[4]
    inverse_root = 1.0 / math.sqrt(head_dim)
    return (query_grad * inverse_root, key_grad * inverse_root, value_grad)


META = 8


def contract(left, right, left_dim, right_dim, **kw):
    return lax.dot_general(
        left,
        right,
        (((left_dim,), (right_dim,)), ((), ())),
        preferred_element_type=jnp.float32,
        **kw,
    )


def one_hot(row_count, target):
    places = lax.broadcasted_iota(jnp.int32, (row_count, target.shape[1]), 0)
    return jnp.where(places == target, 1.0, 0.0).astype(jnp.bfloat16)


def side_by_side(stack, heads):
    rows = stack.shape[0] // heads
    return jnp.concatenate([stack[h * rows : (h + 1) * rows, :] for h in range(heads)], axis=1)


def end_to_end(matrix, heads):
    width = matrix.shape[1] // heads
    return jnp.concatenate([matrix[:, h * width : (h + 1) * width] for h in range(heads)], axis=0)


def runs_of(hot):
    count, rows = hot.shape
    counts = jnp.sum(hot, axis=1, keepdims=True)
    owner = jnp.zeros((1, rows), jnp.int32)
    earlier = jnp.zeros((1, rows), jnp.float32)
    for p in range(count):
        mine = hot[p : p + 1, :] > 0.0
        owner = jnp.where(mine, p, owner)
        for less in range(p):
            earlier = earlier + jnp.where(mine, counts[less : less + 1, :], 0.0)
    lane = lax.broadcasted_iota(jnp.int32, (1, rows), 1)
    return owner, counts, lane - earlier.astype(jnp.int32)


def own_kernel(
    count,
    docs,
    doc_ref,
    packet_ref,
    query_ref,
    grad_ref,
    saved_ref,
    query_out,
    grad_out,
    raised_out,
    change_out,
    row_out,
    spread_out,
    target_out,
    filled_out,
):
    rows, width = query_ref.shape
    depth = packet_ref.shape[1]
    heads = width // depth
    slot = 2 * rows // count
    index = lax.axis_index("ctx")
    lane = lax.broadcasted_iota(jnp.int32, (1, rows), 1)
    position = index * rows + lane
    earlier = lax.broadcasted_iota(jnp.int32, (docs, docs), 1) <= lax.broadcasted_iota(
        jnp.int32, (docs, docs), 0
    )
    lengths = doc_ref[...].astype(jnp.float32)
    ends = jnp.sum(jnp.where(earlier, lengths, 0.0), axis=1, keepdims=True).astype(jnp.int32)
    first = jnp.max(jnp.where(ends <= position, ends, 0), axis=0, keepdims=True)
    key_position = index * rows + lax.broadcasted_iota(jnp.int32, (rows, rows), 0)
    allowed = (key_position >= first) & (key_position <= position)
    allowed = jnp.concatenate([allowed] * heads, axis=1)

    queries = end_to_end(query_ref[...], heads)
    query_out[...] = queries
    scores = contract(packet_ref[0:rows, :], queries, 1, 1) * (1.0 / math.sqrt(depth))
    scores = jnp.where(allowed, scores, NEG)
    top = jnp.max(scores, axis=0, keepdims=True)
    raised = jnp.exp(scores - top)
    raised_out[...] = raised
    grads = end_to_end(grad_ref[...], heads)
    grad_out[...] = grads
    product = grads.astype(jnp.float32) * end_to_end(saved_ref[...], heads).astype(jnp.float32)
    delta = contract(
        jnp.ones((8, depth), jnp.float32), product, 1, 1, precision=lax.Precision.HIGHEST
    )[0:1, :]
    change_out[...] = contract(packet_ref[rows : 2 * rows, :], grads, 1, 1) - delta
    row_out[0:1, :] = delta
    row_out[1:2, :] = top
    row_out[2:3, :] = jnp.sum(raised, axis=0, keepdims=True)
    row_out[3:4, :] = jnp.concatenate([first.astype(jnp.float32)] * heads, axis=1)
    row_out[4:8, :] = jnp.ones((4, width), jnp.float32)
    owner, counts, rank = runs_of(packet_ref[2 * rows : 2 * rows + count, :].astype(jnp.float32))
    spread_out[...] = one_hot(count * slot, (owner ^ index) * slot + rank)
    target_out[...] = one_hot(count * rows, (owner ^ index) * rows + rank)
    filled_out[0:count, :] = jnp.broadcast_to(counts, (count, rows))
    filled_out[count:, :] = jnp.zeros((8 - count, rows), jnp.float32)


def fold(count, back, packet, queries, grads, row, filled):
    rows = packet.shape[1]
    index = lax.axis_index("ctx")
    delta, top, total = (row[n : n + 1, :] for n in range(3))
    first = row[3:4, :].astype(jnp.int32)
    position = (index - back) * rows + lax.broadcasted_iota(jnp.int32, (rows, row.shape[1]), 0)
    scores = contract(packet[0:rows, :], queries, 1, 1) * (1.0 / math.sqrt(queries.shape[1]))
    scores = jnp.where(position >= first, scores, NEG)
    new_top = jnp.maximum(top, jnp.max(scores, axis=0, keepdims=True))
    raised = jnp.exp(scores - new_top)
    shrink = jnp.exp(top - new_top)
    total = total * shrink + jnp.sum(raised, axis=0, keepdims=True)
    change = contract(packet[rows : 2 * rows, :], grads, 1, 1) - delta
    factors = row[4:8, :] * jnp.where(
        lax.broadcasted_iota(jnp.int32, (4, row.shape[1]), 0) < back, shrink, 1.0
    )
    owner, counts, rank = runs_of(packet[2 * rows : 2 * rows + count, :].astype(jnp.float32))
    base = jnp.zeros((1, rows), jnp.float32)
    for p in range(count):
        base = base + jnp.where(owner == p, filled[p : p + 1, :], 0.0)
    inside = index >= back
    target = jnp.where(inside, (owner ^ index) * rows + base.astype(jnp.int32) + rank, -1)
    filled = filled[0:count, :] + jnp.where(inside, counts, 0.0)
    return raised, change, (new_top, total, factors), one_hot(count * rows, target), filled


def step_kernel(count, halo, back, *refs):
    query_ref, grad_ref, row_ref, filled_ref, spread_ref = refs[:5]
    raised_refs = refs[5 : 5 + back]
    change_refs = refs[5 + back : 5 + 2 * back]
    target_refs = refs[5 + 2 * back : 5 + 3 * back]
    packets = refs[5 + 3 * back : 6 + 4 * back]
    raised_out, change_out, row_out, target_out, filled_out = refs[6 + 4 * back : 11 + 4 * back]
    outs = refs[11 + 4 * back :]
    raised, change, (top, total, factors), target, filled = fold(
        count, back, packets[back], query_ref[...], grad_ref[...], row_ref, filled_ref
    )
    raised_out[...] = raised
    change_out[...] = change
    row_out[0:1, :] = row_ref[0:1, :]
    row_out[1:2, :] = top
    row_out[2:3, :] = total
    row_out[3:4, :] = row_ref[3:4, :]
    row_out[4:8, :] = factors
    target_out[...] = target
    filled_out[0:count, :] = filled
    filled_out[count:, :] = jnp.zeros_like(filled_out[count:, :])
    if outs:
        attend_first(
            count,
            (halo,),
            (query_ref, grad_ref, row_out, filled_out, spread_ref)
            + (*raised_refs, raised_out, *change_refs, change_out, *target_refs, target_out)
            + (*packets, None, *outs),
        )


def attend_first(count, several, refs):
    halo = count // 2
    for blocks in several:

        @pl.when(lax.axis_index("ctx") == blocks - 1)
        def _(blocks=blocks):
            attend(count, halo, blocks, refs)


def attend_kernel(count, halo, *refs):
    ready, refs = refs[: count * (halo > 1)], refs[count * (halo > 1) :]
    held = lax.axis_index("ctx") >= halo

    @pl.when(held)
    def _():
        attend(count, halo, halo + 1, refs)

    attend_first(count, range(1, halo + (not ready)), refs)
    if not ready:
        return

    @pl.when(lax.axis_index("ctx") == halo - 1)
    def _():
        for here, out in zip(ready, refs[-count:], strict=True):
            out[...] = here[...]


def attend(count, halo, blocks, refs):
    query_ref, grad_ref, row_ref, filled_ref, spread_ref = refs[:5]
    raised_refs = refs[5 : 5 + halo]
    change_refs = refs[5 + halo : 5 + 2 * halo]
    target_refs = refs[5 + 2 * halo : 5 + 3 * halo]
    packets = refs[5 + 3 * halo : 6 + 4 * halo]
    outs = refs[6 + 4 * halo :]
    rows = packets[0].shape[1]
    depth = query_ref.shape[1]
    heads = query_ref.shape[0] // rows
    slot = 2 * rows // count
    scale = 1.0 / math.sqrt(depth)
    queries = query_ref[...]
    grads = grad_ref[...]
    raised = [ref[...] for ref in raised_refs[:blocks]]
    change = [ref[...] for ref in change_refs[:blocks]]
    targets = [ref[...] for ref in target_refs[:blocks]]
    total = row_ref[2:3, :]
    factors = row_ref[4:8, :]
    if blocks > halo:
        raised_far, change_far, (_, total, factors), target_far, _ = fold(
            count, halo, packets[halo], queries, grads, row_ref, filled_ref
        )
        raised.append(raised_far)
        change.append(change_far)
        targets.append(target_far)
    factors = factors * (1.0 / total)
    weights = [raised[n] * factors[n : n + 1, :] for n in range(blocks)]
    changes = [weights[n] * change[n] for n in range(blocks)]
    weights = jnp.concatenate([part.astype(jnp.bfloat16) for part in weights], axis=0)
    changes = jnp.concatenate([part.astype(jnp.bfloat16) for part in changes], axis=0)
    keys = jnp.concatenate([packet[0:rows, :] for packet in packets[:blocks]], axis=0)
    query_grad = (contract(keys, changes, 0, 0) * scale).astype(jnp.bfloat16)
    key_parts = contract(changes, queries, 1, 0) * scale
    value_parts = contract(weights, grads, 1, 0)
    parts = jnp.concatenate([key_parts, value_parts], axis=1).astype(jnp.bfloat16)

    query_slots = contract(spread_ref[...], end_to_end(query_grad, heads), 1, 1)
    query_slots = query_slots.astype(jnp.bfloat16)
    part_slots = contract(jnp.concatenate(targets, axis=1), parts, 1, 0).astype(jnp.bfloat16)
    at = heads * slot
    for k in range(count):
        out = outs[k]
        for h in range(heads):
            out[h * slot : (h + 1) * slot, :] = query_slots[
                k * slot : (k + 1) * slot, h * depth : (h + 1) * depth
            ]
        for n in range(2):
            out[at + n * rows : at + (n + 1) * rows, :] = part_slots[
                k * rows : (k + 1) * rows, n * depth : (n + 1) * depth
            ]


def slots_of(refs, first, size, pieces):
    return jnp.concatenate(
        [
            jnp.concatenate(
                [ref[first + n * size : first + (n + 1) * size, :] for n in range(pieces)], axis=1
            )
            for ref in refs
        ],
        axis=0,
    )


def order_kernel(count, halo, early, late, *refs):
    ins, packets = refs[: len(early)], refs[len(early) : len(early) + 1 + halo]
    query_out, key_out, query_base, key_base = refs[-4:]
    rows, width = query_base.shape
    depth = ins[0].shape[1]
    heads = width // depth
    slot = 2 * rows // count
    index = lax.axis_index("ctx")
    given = []
    for ref in packets:
        hot = ref[2 * rows : 2 * rows + count, :].astype(jnp.float32)
        counts = jnp.sum(hot, axis=1, keepdims=True)
        mine = jnp.zeros((1, 1), jnp.float32)
        for p in range(count):
            mine = jnp.where(index == p, counts[p : p + 1, :], mine)
        given.append(mine.astype(jnp.int32))
    if len(given) < count:
        given.append(rows - sum(given))
    giver = [lax.rem(index - d + count, count) for d in range(count)]

    def placement(size, halo, exchanges):
        lane = lax.broadcasted_iota(jnp.int32, (1, len(exchanges) * size), 1)
        target = jnp.full(lane.shape, -1, jnp.int32)
        for n, k in enumerate(exchanges):
            step = lane - n * size
            for back in range(halo + 1):
                block = (index ^ k) - back
                start = jnp.zeros((1, 1), jnp.int32)
                length = jnp.zeros((1, 1), jnp.int32)
                for d in range(count):
                    start = start + jnp.where(giver[d] < block, given[d], 0)
                    length = length + jnp.where(giver[d] == block, given[d], 0)
                target = jnp.where((step >= 0) & (step < length), start + step, target)
                step = step - length
        return one_hot(rows, target)

    query_out[...] = placement(slot, 0, late)
    key_out[...] = placement(rows, halo, late)
    query_base[...] = contract(placement(slot, 0, early), slots_of(ins, 0, slot, heads), 1, 0)
    key_base[...] = contract(
        placement(rows, halo, early), slots_of(ins, heads * slot, rows, 2), 1, 0
    )


def place_kernel(count, query_spread, key_spread, query_base, key_base, *refs):
    ins = refs[:-7]
    query_out, key_out, value_out, query_here, key_here, value_here, sems = refs[-7:]
    rows, width = query_here.shape
    depth = key_here.shape[1]
    heads = width // depth
    slot = 2 * rows // count
    copies = []

    def leave(here, out):
        copies.append(pltpu.make_async_copy(here, out, sems.at[len(copies)]))
        copies[-1].start()

    query_here[...] = query_base[...] + contract(
        query_spread[...], slots_of(ins, 0, slot, heads), 1, 0
    )
    leave(query_here, query_out)
    both = key_base[...] + contract(
        key_spread[...], slots_of(ins, heads * slot, rows, 2), 1, 0
    )
    for n, (here, out) in enumerate(((key_here, key_out), (value_here, value_out))):
        here[...] = both[:, n * depth : (n + 1) * depth]
        leave(here, out)
    for copy in copies:
        copy.wait()


def near_plan(doc_lengths, owners, queries, key_head_rows, value_head_rows, forward_out, grad_out):
    count = lax.axis_size("ctx")
    rows, width = queries.shape
    depth = key_head_rows.shape[1]
    heads = width // depth
    bf16, f32 = jnp.bfloat16, jnp.float32
    columns = heads * rows
    halo = count // 2
    slot = 2 * rows // count
    whole = pl.BlockSpec(memory_space=pltpu.VMEM)
    params = pltpu.CompilerParams(vmem_limit_bytes=40 * 1024 * 1024)

    mark = lax.broadcasted_iota(jnp.int32, (2 * rows + META, rows), 0) - 2 * rows
    packet = jnp.where(
        mark < 0,
        jnp.pad(jnp.concatenate([key_head_rows, value_head_rows], axis=0), ((0, META), (0, 0))),
        (owners[None, :] == mark).astype(bf16),
    )
    near = [
        lax.ppermute(packet, "ctx", [(i, (i + back) % count) for i in range(count)])
        for back in range(1, halo + 1)
    ]
    block_shapes = [jax.ShapeDtypeStruct((rows, columns), f32)] * 2
    row_shape = jax.ShapeDtypeStruct((8, columns), f32)
    target_shape = jax.ShapeDtypeStruct((count * rows, rows), bf16)
    filled_shape = jax.ShapeDtypeStruct((8, rows), f32)
    query_rows, grad_rows, raised, change, row, spread, target, filled = pl.pallas_call(
        functools.partial(own_kernel, count, doc_lengths.shape[0]),
        out_shape=[jax.ShapeDtypeStruct((columns, depth), bf16)] * 2
        + block_shapes
        + [row_shape, jax.ShapeDtypeStruct((count * slot, rows), bf16), target_shape, filled_shape],
        in_specs=[whole] * 5,
        out_specs=[whole] * 8,
        compiler_params=params,
    )(doc_lengths.reshape(1, -1), packet, queries, grad_out, forward_out)
    raised, change, target = [raised], [change], [target]
    slot_shapes = [jax.ShapeDtypeStruct((heads * slot + 2 * rows, depth), bf16)] * count
    ready = []
    for back in range(1, halo):
        found = pl.pallas_call(
            functools.partial(step_kernel, count, halo, back),
            out_shape=block_shapes
            + [row_shape, target_shape, filled_shape]
            + slot_shapes * (back == halo - 1),
            in_specs=[whole] * (6 + 4 * back),
            out_specs=[whole] * (5 + count * (back == halo - 1)),
            compiler_params=params,
        )(query_rows, grad_rows, row, filled, spread, *raised, *change, *target, packet, *near[:back])
        raised.append(found[0])
        change.append(found[1])
        row = found[2]
        target.append(found[3])
        filled = found[4]
        ready = found[5:]
    sent = pl.pallas_call(
        functools.partial(attend_kernel, count, halo),
        out_shape=slot_shapes,
        in_specs=[whole] * (len(ready) + 6 + 4 * halo),
        out_specs=[whole] * count,
        compiler_params=params,
    )(*ready, query_rows, grad_rows, row, filled, spread, *raised, *change, *target, packet, *near)
    received = [sent[0]] + [
        lax.ppermute(sent[k], "ctx", [(i, i ^ k) for i in range(count)]) for k in range(1, count)
    ]
    early = (0, 3) if count == 4 else (0,)
    late = tuple(k for k in range(count) if k not in early)
    placed = pl.pallas_call(
        functools.partial(order_kernel, count, halo, early, late),
        out_shape=[
            jax.ShapeDtypeStruct((rows, len(late) * slot), bf16),
            jax.ShapeDtypeStruct((rows, len(late) * rows), bf16),
            jax.ShapeDtypeStruct((rows, width), f32),
            jax.ShapeDtypeStruct((rows, 2 * depth), f32),
        ],
        in_specs=[whole] * (len(early) + 1 + halo),
        out_specs=[whole] * 4,
        compiler_params=params,
    )(*[received[k] for k in early], packet, *near)
    return pl.pallas_call(
        functools.partial(place_kernel, count),
        out_shape=[
            jax.ShapeDtypeStruct((rows, width), f32),
            jax.ShapeDtypeStruct((rows, depth), f32),
            jax.ShapeDtypeStruct((rows, depth), f32),
        ],
        in_specs=[whole] * (4 + len(late)),
        out_specs=[pl.BlockSpec(memory_space=pl.ANY)] * 3,
        scratch_shapes=[
            pltpu.VMEM((rows, width), f32),
            pltpu.VMEM((rows, depth), f32),
            pltpu.VMEM((rows, depth), f32),
            pltpu.SemaphoreType.DMA((3,)),
        ],
        compiler_params=params,
    )(*placed, *[received[k] for k in late])


def per_device(*args):
    if lax.axis_size("ctx") in (2, 4):
        return near_plan(*args)
    return ring_plan(*args)


def solution(mesh):
    return jax.shard_map(
        per_device,
        mesh=mesh,
        in_specs=(
            P("groups"),
            P(("groups", "ctx")),
            P(("groups", "ctx"), "head"),
            P(("groups", "ctx"), "head"),
            P(("groups", "ctx"), "head"),
            P(("groups", "ctx"), "head"),
            P(("groups", "ctx"), "head"),
        ),
        out_specs=(
            P(("groups", "ctx"), "head"),
            P(("groups", "ctx"), "head"),
            P(("groups", "ctx"), "head"),
        ),
        check_vma=False,
    )
```
